32 devices in a mesh: blk: 16 (over z, y, core), fsdp: 2 (over x).
Axes of the slice: x: 2, y: 2, z: 4, core: 2. Of those that a mesh axis runs over, the one named last changes fastest.
Arguments:
- tokens: bfloat16 [2, 4096, 512], P('fsdp', 'blk'), may hold values from -6 to 6
- ln1_gain: bfloat16 [512], P(('blk', 'fsdp')), may hold values from 0.25 to 1.75
- ln1_bias: bfloat16 [512], P(('blk', 'fsdp')), may hold values from -3 to 3
- qkv_weight: bfloat16 [512, 1536], P(('blk', 'fsdp')), may hold values from -0.25 to 0.25
- query_bias: bfloat16 [512], P(('blk', 'fsdp')), may hold values from -3 to 3
- value_bias: bfloat16 [512], P(('blk', 'fsdp')), may hold values from -0.29882812 to 0.29882812
- out_weight: bfloat16 [512, 512], P(('blk', 'fsdp')), may hold values from -6 to 6
- out_bias: bfloat16 [512], P(('blk', 'fsdp')), may hold values from -3 to 3
- ln2_gain: bfloat16 [512], P(('blk', 'fsdp')), may hold values from 0.25 to 1.75
- ln2_bias: bfloat16 [512], P(('blk', 'fsdp')), may hold values from -3 to 3
- up_weight: bfloat16 [512, 2048], P(('blk', 'fsdp')), may hold values from -0.25 to 0.25
- up_bias: bfloat16 [2048], P(('blk', 'fsdp')), may hold values from -3 to 3
- down_weight: bfloat16 [2048, 512], P(('blk', 'fsdp')), may hold values from -0.125 to 0.125
- down_bias: bfloat16 [512], P(('blk', 'fsdp')), may hold values from -3 to 3
- table_lengths: int32 [2, 8], P('fsdp'), may hold values from 1 to 3879, as said below
- support_lengths: int32 [2, 8], P('fsdp'), may hold values from 1 to 2910, as said below
- cotangent: bfloat16 [2, 4096, 512], P('fsdp', 'blk'), may hold values from -6 to 6
Outputs:
- block_out: bfloat16 [2, 4096, 512], P('fsdp', 'blk')
- grad_tokens: bfloat16 [2, 4096, 512], P('fsdp', 'blk')
- grad_ln1_gain: float32 [512], P(('blk', 'fsdp'))
- grad_ln1_bias: float32 [512], P(('blk', 'fsdp'))
- grad_qkv_weight: float32 [512, 1536], P(('blk', 'fsdp'))
- grad_query_bias: float32 [512], P(('blk', 'fsdp'))
- grad_value_bias: float32 [512], P(('blk', 'fsdp'))
- grad_out_weight: float32 [512, 512], P(('blk', 'fsdp'))
- grad_out_bias: float32 [512], P(('blk', 'fsdp'))
- grad_ln2_gain: float32 [512], P(('blk', 'fsdp'))
- grad_ln2_bias: float32 [512], P(('blk', 'fsdp'))
- grad_up_weight: float32 [512, 2048], P(('blk', 'fsdp'))
- grad_up_bias: float32 [2048], P(('blk', 'fsdp'))
- grad_down_weight: float32 [2048, 512], P(('blk', 'fsdp'))
- grad_down_bias: float32 [512], P(('blk', 'fsdp'))
The draws below stay inside these ranges and needn't reach their ends.
Inputs may be any that keep to these rules, and one draw needn't show every extreme that they name: `table_lengths`: in each bucket the 8 lengths sum to 4096; one table of each bucket has exactly the largest length. Entry by entry, support_lengths is at most table_lengths; the longest table of each bucket has the largest support.
All inputs are finite; a program needn't handle non-finite values.
Results may differ from the reference program's by a relative error of at most 0.012.
Values may be sent and summed in bfloat16 or wider, within the bound.
A program may use at most 128 MiB of HBM per device.

```python
import math
import jax
import jax.numpy as jnp
from jax import lax

D = 512
H = 4
FF = 2048
ROWS_DEV = 256
NTAB = 8
ROWS = 4096
BUCKETS = 2


def draw_layout(key):
    pick_key, small_key, share_key = jax.random.split(key, 3)
    most = max((ROWS_DEV - 1) // (NTAB - 1), 1)
    fixed_total = (NTAB - 2) * most + 1
    small = jax.random.randint(small_key, (BUCKETS, NTAB), 1, most + 1, dtype=jnp.int32)
    chosen_slot = jax.random.randint(pick_key, (BUCKETS, 1), 0, NTAB, dtype=jnp.int32)
    adjust_slot = (chosen_slot + 1) % NTAB
    slots = jnp.arange(NTAB, dtype=jnp.int32)[None, :]
    chosen = slots == chosen_slot
    adjusted = slots == adjust_slot
    rest = jnp.sum(jnp.where(chosen | adjusted, 0, small), axis=1, keepdims=True)
    lengths = jnp.where(chosen, ROWS - fixed_total, jnp.where(adjusted, fixed_total - rest, small)).astype(jnp.int32)
    extra = jax.random.randint(share_key, (BUCKETS, NTAB), 0, lengths, dtype=jnp.int32)
    support = jnp.where(chosen, lengths - lengths // 4, 1 + extra).astype(jnp.int32)
    return (lengths, support)


def draw_table_lengths(key, part):
    lengths, support = draw_layout(key)
    return lengths


def draw_support_lengths(key, part):
    lengths, support = draw_layout(key)
    return support


def raised(entries, rng, source, target, parts, factor):
    owner, partner = [(jnp.arange(entries.shape[position]) // (entries.shape[position] // parts)).reshape([-1 if axis == position else 1 for axis in range(entries.ndim)]) for position in (source, target)]
    chosen = jax.random.permutation(rng, parts)[partner]
    strong = (owner == chosen) | (owner == (partner + parts // 2) % parts)
    return jnp.where(strong, factor * entries, entries)


def shard_levels(own_key, extent, pieces, low, high):
    level = 1.0
    for axis_at, shards_of in pieces:
        draws = jax.random.uniform(jax.random.fold_in(jax.random.fold_in(own_key, 6), axis_at), (shards_of,), jnp.float32, low / len(pieces), high / len(pieces))
        level = level * jnp.repeat(jnp.exp(draws), extent[axis_at] // shards_of).reshape((-1,) + (1,) * (len(extent) - 1 - axis_at))
    return level


def bell_draw(stream_key, extent, scale, reach, cuts=(), kind=jnp.bfloat16):
    result = scale * jax.random.normal(stream_key, extent, jnp.float32)
    if cuts:
        result = result * shard_levels(stream_key, extent, cuts, -0.22, 0.18)
    return jnp.clip(result, -reach, reach).astype(kind)


def gaussian_with(rng, extent, deviation, bound, pieces, heavy, kind=jnp.bfloat16):
    entries = deviation * jax.random.normal(rng, extent, jnp.float32)
    if pieces:
        entries = entries * shard_levels(rng, extent, pieces, -0.22, 0.18)
    return jnp.clip(raised(entries, jax.random.fold_in(rng, 3), *heavy), -bound, bound).astype(kind)


def setup_inputs(seed: int = 0) -> dict:
    splits = jax.random.split(jax.random.key(seed), 18)
    tokens = bell_draw(splits[0], (BUCKETS, ROWS, D), 1.0, 6.0, ((0, 2), (1, 16)))
    ln1_gain = jnp.clip(1.0 + 0.15 * jax.random.normal(splits[1], (D,), jnp.float32), 0.25, 1.75).astype(jnp.bfloat16)
    ln1_bias = bell_draw(splits[2], (D,), 0.3, 3.0, ((0, 32),))
    qkv_weight = bell_draw(splits[3], (D, 3 * D), D ** -0.5, 0.25, ((0, 32),))
    query_bias = bell_draw(splits[4], (D,), 0.3, 3.0, ((0, 32),))
    value_bias = bell_draw(splits[5], (D,), 0.03, 0.29882812, ((0, 32),))
    out_weight = bell_draw(splits[6], (D, D), 1 ** -0.5, 6.0, ((0, 32),))
    out_bias = bell_draw(splits[7], (D,), 0.3, 3.0, ((0, 32),))
    ln2_gain = jnp.clip(1.0 + 0.15 * jax.random.normal(splits[8], (D,), jnp.float32), 0.25, 1.75).astype(jnp.bfloat16)
    ln2_bias = bell_draw(splits[9], (D,), 0.3, 3.0, ((0, 32),))
    up_weight = bell_draw(splits[10], (D, FF), D ** -0.5, 0.25, ((0, 32),))
    up_bias = bell_draw(splits[11], (FF,), 0.3, 3.0, ((0, 32),))
    down_weight = bell_draw(splits[12], (FF, D), FF ** -0.5, 0.125, ((0, 32),))
    down_bias = bell_draw(splits[13], (D,), 0.3, 3.0, ((0, 32),))
    table_lengths = draw_table_lengths(jax.random.fold_in(splits[17], 71), 0)
    support_lengths = draw_support_lengths(jax.random.fold_in(splits[17], 71), 0)
    cotangent = gaussian_with(splits[16], (BUCKETS, ROWS, D), 1.0, 6.0, ((0, 2), (1, 16)), (1, 2, 16, 2.0))
    return {"tokens": tokens, "ln1_gain": ln1_gain, "ln1_bias": ln1_bias, "qkv_weight": qkv_weight, "query_bias": query_bias, "value_bias": value_bias, "out_weight": out_weight, "out_bias": out_bias, "ln2_gain": ln2_gain, "ln2_bias": ln2_bias, "up_weight": up_weight, "up_bias": up_bias, "down_weight": down_weight, "down_bias": down_bias, "table_lengths": table_lengths, "support_lengths": support_lengths, "cotangent": cotangent}


EPSILON = 1e-05
MASKED = -1e+30
PRECISE = lax.Precision.HIGHEST

@jax.custom_vjp
def low(v):
    return lax.optimization_barrier(v.astype(jnp.bfloat16)).astype(jnp.float32)

@jax.custom_vjp
def low_back(v):
    return v

def low_keep(v):
    return (low(v), None)

def low_pass(kept, grad):
    return (grad,)

def back_keep(v):
    return (v, None)

def back_low(kept, grad):
    return (low(grad),)
low.defvjp(low_keep, low_pass)
low_back.defvjp(back_keep, back_low)

def normalize(values, norm_gain, norm_bias):
    row_mean = lax.optimization_barrier(jnp.mean(values, axis=-1, keepdims=True))
    centered = values - row_mean
    variance = lax.optimization_barrier(jnp.mean(centered * centered, axis=-1, keepdims=True))
    return centered * lax.rsqrt(variance + EPSILON) * norm_gain + norm_bias

def row_codes(lengths, support, positions):
    table_ends = jnp.cumsum(lengths).astype(jnp.int32)
    table_ids = lax.optimization_barrier(jnp.sum((positions[:, None] >= table_ends[None, :]).astype(jnp.int32), axis=1))
    starts = table_ends - lengths
    chosen = (table_ids[:, None] == jnp.arange(lengths.shape[0], dtype=jnp.int32)[None, :]).astype(jnp.int32)
    support_end = lax.optimization_barrier(jnp.sum(chosen * (starts + support)[None, :], axis=1))
    key_codes = jnp.where(positions < support_end, table_ids, -1)
    return (table_ids, key_codes)

def bucket_layer(params, float_tokens, lengths, support):
    gain_first, bias_first, w_qkv, q_shift, v_shift, w_out, b_out, gain_second, bias_second, w_up, b_up, w_down, b_down = params
    row_total = float_tokens.shape[0]
    head_size = D // H
    score_scale = head_size ** (-0.5)
    positions = jnp.arange(row_total, dtype=jnp.int32)
    table_ids, key_codes = row_codes(lengths, support, positions)
    normed_first = low(normalize(float_tokens, gain_first, bias_first))
    projected = jnp.dot(normed_first, w_qkv, precision=PRECISE)
    queries = low(low_back(projected[:, :D] + q_shift)).reshape(row_total, H, head_size)
    key_heads = low(low_back(projected[:, D:2 * D])).reshape(row_total, H, head_size)
    value_heads = low(low_back(projected[:, 2 * D:] + v_shift)).reshape(row_total, H, head_size)

    def attend(block):
        block_queries, block_tables = block
        scores = low_back(jnp.einsum('qhd,khd->hqk', block_queries, key_heads, precision=PRECISE) * score_scale)
        allowed = block_tables[:, None] == key_codes[None, :]
        scores = jnp.where(allowed[None], scores, MASKED)
        shifted = scores - lax.optimization_barrier(jnp.max(scores, axis=-1, keepdims=True))
        expos = jnp.exp(shifted)
        probs = low(expos / lax.optimization_barrier(jnp.sum(expos, axis=-1, keepdims=True)))
        return jnp.einsum('hqk,khd->qhd', probs, value_heads, precision=PRECISE)
    block_size = math.gcd(row_total, 512)
    block_count = row_total // block_size
    attended = lax.map(jax.checkpoint(attend), (queries.reshape(block_count, block_size, H, head_size), table_ids.reshape(block_count, block_size)))
    attended = low(low_back(attended.reshape(row_total, D)))
    branch = low_back(jnp.dot(attended, w_out, precision=PRECISE) + b_out)
    hidden = float_tokens + branch
    normed_second = low(normalize(hidden, gain_second, bias_second))
    pre_act = low_back(jnp.dot(normed_second, w_up, precision=PRECISE) + b_up)
    activated = low(jax.nn.gelu(pre_act, approximate=False))
    return hidden + jnp.dot(activated, w_down, precision=PRECISE) + b_down

def reference(tokens, ln1_gain, ln1_bias, qkv_weight, query_bias, value_bias, out_weight, out_bias, ln2_gain, ln2_bias, up_weight, up_bias, down_weight, down_bias, table_lengths, support_lengths, cotangent):
    params = tuple((member.astype(jnp.float32) for member in (ln1_gain, ln1_bias, qkv_weight, query_bias, value_bias, out_weight, out_bias, ln2_gain, ln2_bias, up_weight, up_bias, down_weight, down_bias)))
    float_tokens = tokens.astype(jnp.float32)

    def forward(weights, inputs):

        def one_bucket(bucket_item):
            return jax.checkpoint(bucket_layer)(weights, bucket_item[0], bucket_item[1], bucket_item[2])
        return lax.map(one_bucket, (inputs, table_lengths, support_lengths))
    output, pullback = jax.vjp(forward, params, float_tokens)
    grad_params, grad_inputs = pullback(cotangent.astype(jnp.float32))
    return (output.astype(jnp.bfloat16), grad_inputs.astype(jnp.bfloat16), grad_params[0], grad_params[1], grad_params[2], grad_params[3], grad_params[4], grad_params[5], grad_params[6], grad_params[7], grad_params[8], grad_params[9], grad_params[10], grad_params[11], grad_params[12])
```

```python
import functools
import math

import jax
import jax.numpy as jnp
from jax import lax
from jax.experimental import pallas as pl
from jax.experimental.pallas import tpu as pltpu
from jax.sharding import PartitionSpec as P

H = 4
HD = 128
SLAB = 16
EPSILON = 1e-05
MASKED = -1e30
LN2 = math.log(2.0)
MESH = pl.DeviceIdType.MESH
F32 = jnp.float32
BF16 = jnp.bfloat16


def dot_nn(a, b):
    return lax.dot_general(a, b, (((1,), (0,)), ((), ())), preferred_element_type=F32)


def dot_nt(a, b):
    return lax.dot_general(a, b, (((1,), (1,)), ((), ())), preferred_element_type=F32)


def dot_tn(a, b):
    return lax.dot_general(a, b, (((0,), (0,)), ((), ())), preferred_element_type=F32)


def moments(v):
    mean = jnp.mean(v, axis=-1, keepdims=True)
    centered = v - mean
    rstd = lax.rsqrt(jnp.mean(centered * centered, axis=-1, keepdims=True) + EPSILON)
    return mean, centered, rstd


def norm_back(g, n, r):
    return r * (g - jnp.mean(g, axis=-1, keepdims=True) - n * jnp.mean(g * n, axis=-1, keepdims=True))


def three_terms(v):
    first = v.astype(BF16)
    rest = v - first.astype(F32)
    second = rest.astype(BF16)
    third = (rest - second.astype(F32)).astype(BF16)
    return first.astype(F32), second.astype(F32), third.astype(F32)


def col_sum(v):
    return jnp.sum(v, axis=0, keepdims=True)


def fold_rows(v):
    return jnp.sum(v.reshape(v.shape[0] // 8, 8, v.shape[1]), axis=0)


def body(
    Z, FK, R, D, NT,
    tok_ref, cot_ref, wq_ref, wo_ref, wu_ref, wd_ref, sm_ref, len_ref, sup_ref,
    out_ref, gtok_ref, gqkv_ref, gout_ref, gup_ref, gdown_ref, gsm_ref,
    tokb, kb, vb, eb, stat, w0, w1, w2, g0, g1, g2,
    c0, c1, c2, x0, x1, x2, y0, y1, y2, z0, z1, z2,
    crf, yrf, zrf, par, upb, qt, dot_, qs, dos, ot, mrun, dqt,
    nrm2, hid, acc, gsec, xg, dwkv, lacc, upg, xown,
    sg, src, srx, sry, srz,
    s_tz, s_ty, s_tc, r_t,
    s_wz, r_wz, s_wy, r_wy, s_wx, r_wx, s_wc, r_wc,
    s_gc, r_gc, s_gx, r_gx, s_gy, r_gy, s_gz, r_gz,
    s_pc, r_pc, s_py, r_py, s_pz, r_pz,
    s_sc, r_sc, s_sx, r_sx, s_sy, r_sy, s_sz, r_sz,
):
    i = lax.axis_index("blk")
    f = lax.axis_index("fsdp")
    c = lax.rem(i, 2)
    y = lax.rem(i // 2, 2)
    z = i // 4
    oc = 1 - c
    oy = 1 - y
    CH = 4 * FK * SLAB * 4
    FF = Z * CH
    NSH = Z * 4 * FK
    KEEP = Z <= 4

    def dev(zz, yy, cc, ff):
        return ((zz * 2 + yy) * 2 + cc, ff)

    d_core = dev(z, y, oc, f)
    d_y = dev(z, oy, c, f)

    def zplus(k):
        return lax.rem(z + k, Z)

    def fplus(k):
        return lax.rem(f + k, FK)

    def d_z(zz):
        return dev(zz, y, c, f)

    def d_f(ff):
        return (i, ff)

    def cp(s, d, ss, rs, to):
        return pltpu.make_async_remote_copy(
            src_ref=s, dst_ref=d, send_sem=ss, recv_sem=rs, device_id=to, device_id_type=MESH
        )

    def push(s, d, ss, rs, to):
        cp(s, d, ss, rs, to).start()

    def got(d, rs):
        cp(d, d, rs, rs, d_core).wait_recv()

    def sent(s, ss):
        cp(s, s, ss, ss, d_core).wait_send()

    bar = pltpu.get_barrier_semaphore()
    partners = [d_core, d_y] + [d_z(zplus(k)) for k in range(1, Z)] + [d_f(fplus(k)) for k in range(1, FK)]
    for to in partners:
        pl.semaphore_signal(bar, inc=1, device_id=to, device_id_type=MESH)
    pl.semaphore_wait(bar, len(partners))

    def tok_push(zz, ss_z, to):
        t = tokb.at[zz, y, c]
        push(t, t, ss_z, r_t.at[zz, y, c], to)

    def tok_side(zz):
        t = tokb.at[zz, y, c]
        push(t, t, s_ty.at[zz], r_t.at[zz, y, c], d_y)
        push(t, t, s_tc.at[zz, 0], r_t.at[zz, y, c], d_core)

    def tok_right(zz):
        @pl.when(z < Z - 1)
        def _():
            tok_push(zz, s_tz.at[0, zz], d_z(z + 1))

    def tok_left(zz):
        @pl.when(z > 0)
        def _():
            tok_push(zz, s_tz.at[1, zz], d_z(z - 1))

    def tok_z(k):
        @pl.when(z - k >= 0)
        def _():
            zz = z - k
            got(tokb.at[zz, y, c], r_t.at[zz, y, c])
            tok_right(zz)
            tok_side(zz)

        @pl.when(z + k < Z)
        def _():
            zz = z + k
            got(tokb.at[zz, y, c], r_t.at[zz, y, c])
            tok_left(zz)
            tok_side(zz)

    def tok_y_one(zz):
        t = tokb.at[zz, oy, c]
        got(t, r_t.at[zz, oy, c])
        push(t, t, s_tc.at[zz, 1], r_t.at[zz, oy, c], d_core)

    def tok_y(k):
        if k == 0:
            tok_y_one(z)
        else:
            @pl.when(z - k >= 0)
            def _():
                tok_y_one(z - k)

            @pl.when(z + k < Z)
            def _():
                tok_y_one(z + k)

    wb = (w0, w1, w2)

    def w_side(g, zz, yy):
        for k in range(1, FK):
            ff = fplus(k)
            t = wb[g].at[zz, yy, c, f]
            push(t, t, s_wx.at[g, ff, zz, yy], r_wx.at[g, f, zz, yy], d_f(ff))

    def w_own(g):
        t = wb[g].at[z, y, c, f]
        for k in range(1, Z):
            zz = zplus(k)
            push(t, t, s_wz.at[g, zz], r_wz.at[g, z], d_z(zz))
        push(t, t, s_wy.at[g, z], r_wy.at[g, z], d_y)
        w_side(g, z, y)

    def w_z(g):
        for k in range(1, Z):
            zz = zplus(k)
            t = wb[g].at[zz, y, c, f]
            got(t, r_wz.at[g, zz])
            push(t, t, s_wy.at[g, zz], r_wy.at[g, zz], d_y)
            w_side(g, zz, y)

    def w_core(g, ff, n):
        t = wb[g].at[:, :, c, ff]
        push(t, t, s_wc.at[g, n], r_wc.at[g, n], d_core)

    def w_y(g):
        for k in range(Z):
            zz = zplus(k)
            got(wb[g].at[zz, oy, c, f], r_wy.at[g, zz])
            w_side(g, zz, oy)
        w_core(g, f, 0)

    def w_x(g):
        for k in range(1, FK):
            ff = fplus(k)
            for zz in range(Z):
                for yy in range(2):
                    got(wb[g].at[zz, yy, c, ff], r_wx.at[g, ff, zz, yy])
            w_core(g, ff, k)

    def w_c(g):
        for k in range(FK):
            got(wb[g].at[:, :, oc, fplus(k)], r_wc.at[g, k])

    tokb[z, y, c] = tok_ref[...]
    w0[z, y, c, f, :, 0 : 3 * D] = wq_ref[...]
    w0[z, y, c, f, :, 3 * D : 3 * D + 128] = sm_ref[...]
    w1[z, y, c, f, :, 0:D] = wo_ref[...]
    w1[z, y, c, f, :, D : D + FF] = wu_ref[...]
    w2[z, y, c, f] = wd_ref[...]

    w_own(0)
    tok_right(z)
    tok_left(z)
    tok_side(z)
    w_own(1)
    w_own(2)

    starts, ends, stops = [], [], []
    total = jnp.int32(0)
    for t in range(NT):
        starts.append(total)
        stops.append(total + sup_ref[0, t])
        total = total + len_ref[0, t]
        ends.append(total)

    lane = lax.broadcasted_iota(jnp.int32, (1, 128), 1)
    lane_start = jnp.zeros((1, 128), jnp.int32)
    lane_stop = jnp.zeros((1, 128), jnp.int32)
    for t in range(NT):
        lane_start = jnp.where(lane == t, starts[t], lane_start)
        lane_stop = jnp.where(lane == t, stops[t], lane_stop)
    lane_ones = jnp.where((lane >= NT) & (lane < NT + 3), 1.0, 0.0)

    def mask_of(n):
        pos = n * R + lax.broadcasted_iota(jnp.int32, (R, 128), 0)
        seen = (pos >= lane_start) & (pos < lane_stop)
        extra = jnp.where(lane < NT, jnp.where(seen, 0.0, MASKED), lane_ones)
        return extra.astype(BF16)

    def mask_block(n, carry):
        eb[n] = mask_of(n)
        return carry

    if KEEP:
        lax.fori_loop(0, 4 * Z, mask_block, 0)

    row = lax.broadcasted_iota(jnp.int32, (128, R), 0)
    qpos = i * R + lax.broadcasted_iota(jnp.int32, (128, R), 1)
    onehot = jnp.zeros((128, R), F32)
    for t in range(NT):
        onehot = jnp.where((row == t) & (qpos >= starts[t]) & (qpos < ends[t]), 1.0, onehot)

    tok_z(1)
    w_z(0)
    tok_y(0)
    for k in range(2, Z):
        tok_z(k)
        if k == 2:
            w_y(0)
            w_z(1)
        tok_y(k - 1)
    w_x(0)
    tok_y(Z - 1)
    w_z(2)
    w_c(0)

    piece = D // NSH
    small = w0[:, :, :, :, :, 3 * D : 3 * D + 128].reshape(NSH * SLAB, 128)
    spread = (
        lax.rem(lax.broadcasted_iota(jnp.int32, (128, D), 1), piece)
        == lax.broadcasted_iota(jnp.int32, (128, D), 0)
    )
    wide = dot_nn(small, spread.astype(BF16))
    mine = (
        lax.broadcasted_iota(jnp.int32, (NSH * SLAB, D), 1) // piece
        == lax.broadcasted_iota(jnp.int32, (NSH * SLAB, D), 0) // SLAB
    )
    wide = jnp.where(mine, wide, 0.0)
    par[...] = jnp.sum(wide.reshape(NSH, SLAB, D), axis=0)
    pick = (
        lax.broadcasted_iota(jnp.int32, (NSH, NSH * SLAB), 1)
        == lax.broadcasted_iota(jnp.int32, (NSH, NSH * SLAB), 0) * SLAB + 8
    )
    ups = dot_nn(pick.astype(BF16), small).astype(BF16)
    spread = (
        lax.rem(lax.broadcasted_iota(jnp.int32, (128, FF), 1), 4 * piece)
        == lax.broadcasted_iota(jnp.int32, (128, FF), 0)
    )
    wide = dot_nn(ups, spread.astype(BF16))
    mine = (
        lax.broadcasted_iota(jnp.int32, (NSH, FF), 1) // (4 * piece)
        == lax.broadcasted_iota(jnp.int32, (NSH, FF), 0)
    )
    upb[...] = col_sum(jnp.where(mine, wide, 0.0))
    ln1g, ln1b = par[0:1, :], par[1:2, :]

    tokens = tok_ref[...].astype(F32)
    mean, centered, rstd = moments(tokens)
    own = (centered * rstd * ln1g + ln1b).astype(BF16)
    xown[...] = own
    wq = w0[:, :, :, :, :, 0:D].reshape(D, D)
    qscale = HD ** (-0.5) / LN2
    qs[...] = ((dot_nn(own, wq) + par[2:3, :]) * qscale).astype(BF16)
    for h in range(H):
        qt[h, 0:HD, :] = qs[:, h * HD : (h + 1) * HD].T
        qt[h, HD : 2 * HD, :] = onehot.astype(BF16)
        ot[h] = jnp.zeros((2 * HD, R), F32)
        mrun[h] = jnp.full((1, R), MASKED, F32)

    def place(n):
        zz = zplus(n // 4)
        part = lax.rem(n, 4)
        yy = lax.rem(y + part // 2, 2)
        cc = lax.rem(c + part, 2)
        return zz, yy, cc

    def ahead(n, carry):
        zz, yy, cc = place(n)

        @pl.when(lax.rem(n, 2) == 1)
        def _():
            got(tokb.at[zz, yy, cc], r_t.at[zz, yy, cc])

        b = (zz * 2 + yy) * 2 + cc
        mean, centered, rstd = moments(tokb[zz, yy, cc].astype(F32))
        if KEEP:
            stat[b] = jnp.where(lax.broadcasted_iota(jnp.int32, (R, 128), 1) == 0, mean, rstd)
        x = (centered * rstd * par[0:1, :] + par[1:2, :]).astype(BF16)
        kv = dot_nn(x, w0[:, :, :, :, :, D : 3 * D].reshape(D, 2 * D))
        keys = kv[:, 0:D].astype(BF16)
        values = (kv[:, D : 2 * D] + par[3:4, :]).astype(BF16)
        kb[b] = keys
        vb[b] = values
        extra = eb[b] if KEEP else mask_of(b)
        for h in range(H):
            cols = slice(h * HD, (h + 1) * HD)
            s = dot_nn(jnp.concatenate([keys[:, cols], extra], axis=1), qt[h])
            before = mrun[h]
            top = jnp.maximum(before, jnp.ceil(jnp.max(s, axis=0, keepdims=True)))
            e = jnp.exp2(s - top).astype(BF16)
            grown = dot_tn(jnp.concatenate([values[:, cols], extra], axis=1), e)
            ot[h] = ot[h] * jnp.exp2(before - top) + grown
            mrun[h] = top
        return carry

    lax.fori_loop(0, 4 * Z, ahead, 0)

    w_y(1)
    w_y(2)
    w_x(1)
    w_x(2)
    w_c(1)
    w_c(2)

    parts = []
    for h in range(H):
        inverse = 1.0 / ot[h, HD + NT : HD + NT + 1, :]
        attended = ot[h, 0:HD, :] * inverse
        ot[h, 0:HD, :] = attended
        dot_[h, HD : HD + 1, :] = inverse.astype(BF16)
        ot[h, HD : HD + 1, :] = inverse
        parts.append(attended.T.astype(BF16))
        m1, m2, m3 = three_terms(mrun[h])
        tail = jnp.where(row == NT, -m1, jnp.where(row == NT + 1, -m2, jnp.where(row == NT + 2, -m3, onehot)))
        qt[h, HD : 2 * HD, :] = tail.astype(BF16)
    attn_low = jnp.concatenate(parts, axis=1)
    w_out = w1[:, :, :, :, :, 0:D].reshape(D, D)
    hidden = tokens + (dot_nn(attn_low, w_out) + par[4:5, :])
    hid[...] = hidden
    mean2, centered, rstd2 = moments(hidden)
    n2 = centered * rstd2
    nrm2[...] = (n2 * par[5:6, :] + par[6:7, :]).astype(BF16)
    acc[...] = hidden + par[7:8, :]
    gsec[...] = jnp.zeros((R, D), F32)

    def chunk(j, carry):
        cols = pl.ds(pl.multiple_of(D + j * CH, 128), CH)
        bcols = pl.ds(pl.multiple_of(j * CH, 128), CH)
        up = w1[:, :, :, :, :, cols].reshape(D, CH)
        down = w2[j].reshape(CH, D)
        normed = nrm2[...]
        cot = cot_ref[...]
        pre = dot_nn(normed, up) + upb[:, bcols]
        phi = 0.5 * (1.0 + lax.erf(pre * (0.5**0.5)))
        act = (pre * phi).astype(BF16)
        slope = phi + pre * (jnp.exp2(pre * pre * (-0.5 / LN2)) * ((2.0 * math.pi) ** -0.5))
        acc[...] += dot_nn(act, down)
        gpre32 = dot_nt(cot, down) * slope
        gpre = gpre32.astype(BF16)
        gsec[...] += dot_nt(gpre, up)
        upg[:, bcols] = col_sum(gpre.astype(F32))
        g1[:, :, :, :, :, cols] = dot_tn(normed, gpre).astype(BF16).reshape(Z, 2, 2, FK, SLAB, CH)
        g2[j] = dot_tn(act, cot).astype(BF16).reshape(2, 2, FK, 4 * SLAB, D)
        return carry

    lax.fori_loop(0, Z, chunk, 0)
    out_ref[...] = acc[...].astype(BF16)

    gb = (g0, g1, g2)
    cb = (c0, c1, c2)
    xb = (x0, x1, x2)
    yb = (y0, y1, y2)
    zb = (z0, z1, z2)

    def r_c(g):
        push(gb[g].at[:, :, oc], cb[g], s_gc.at[g], r_gc.at[g], d_core)

    def r_x(g):
        got(cb[g], r_gc.at[g])

        def one(zz, carry):
            t = gb[g][zz, :, c].astype(F32) + cb[g][zz].astype(F32)
            gb[g][zz, :, c] = t.astype(BF16)
            return carry

        lax.fori_loop(0, Z, one, 0)
        for k in range(1, FK):
            ff = fplus(k)
            push(gb[g].at[:, :, c, ff], xb[g].at[f], s_gx.at[g, ff], r_gx.at[g, f], d_f(ff))

    def r_y(g):
        for k in range(1, FK):
            got(xb[g].at[fplus(k)], r_gx.at[g, fplus(k)])

        if FK > 1:
            def one(zz, carry):
                t = gb[g][zz, :, c, f].astype(F32)
                for k in range(1, FK):
                    t = t + xb[g][fplus(k), zz].astype(F32)
                gb[g][zz, :, c, f] = t.astype(BF16)
                return carry

            lax.fori_loop(0, Z, one, 0)
        push(gb[g].at[:, oy, c, f], yb[g], s_gy.at[g], r_gy.at[g], d_y)

    def r_z(g):
        got(yb[g], r_gy.at[g])

        def one(zz, carry):
            t = gb[g][zz, y, c, f].astype(F32) + yb[g][zz].astype(F32)
            gb[g][zz, y, c, f] = t.astype(BF16)
            return carry

        lax.fori_loop(0, Z, one, 0)
        for k in range(1, Z):
            zz = zplus(k)
            push(gb[g].at[zz, y, c, f], zb[g].at[z], s_gz.at[g, zz], r_gz.at[g, z], d_z(zz))

    def r_end(g):
        t = gb[g][z, y, c, f].astype(F32)
        for k in range(1, Z):
            zz = zplus(k)
            got(zb[g].at[zz], r_gz.at[g, zz])
            t = t + zb[g][zz].astype(F32)
        return t

    def r_sent(g):
        sent(gb[g].at[:, :, oc], s_gc.at[g])
        for k in range(1, FK):
            sent(gb[g].at[:, :, c, fplus(k)], s_gx.at[g, fplus(k)])
        sent(gb[g].at[:, oy, c, f], s_gy.at[g])
        for k in range(1, Z):
            sent(gb[g].at[zplus(k), y, c, f], s_gz.at[g, zplus(k)])

    r_c(2)

    g_second = gsec[...]
    n2 = (hid[...] - mean2) * rstd2
    ln2g = par[5:6, :]
    cot32 = cot_ref[...].astype(F32)
    grad_hidden = cot32 + norm_back(g_second * ln2g, n2, rstd2)
    hid[...] = grad_hidden
    g_branch = grad_hidden.astype(BF16)
    g1[:, :, :, :, :, 0:D] = dot_tn(attn_low, g_branch).astype(BF16).reshape(Z, 2, 2, FK, SLAB, D)
    r_c(1)
    zero = jnp.zeros((1, D), F32)
    for r in range(SLAB):
        sg[0, r : r + 1, :] = zero
    sg[0, 4:5, :] = col_sum(g_branch.astype(F32))
    sg[0, 5:6, :] = col_sum(g_second * n2)
    sg[0, 6:7, :] = col_sum(g_second)
    sg[0, 7:8, :] = col_sum(cot32)
    for r in range(FF // D):
        sg[0, 8 + r : 9 + r, :] = upg[:, r * D : (r + 1) * D]

    for h in range(H):
        rows = slice(h * HD, (h + 1) * HD)
        w_head = w1[:, :, :, :, :, 0:D].reshape(D, D)[rows, :]
        ga = dot_nt(w_head, g_branch).astype(BF16).astype(F32)
        low = (ga * ot[h, HD : HD + 1, :]).astype(BF16)
        delta = col_sum(low.astype(F32) * ot[h, 0:HD, :])
        d1, d2, d3 = three_terms(delta)
        tail = jnp.where(row == NT, -d1, jnp.where(row == NT + 1, -d2, jnp.where(row == NT + 2, -d3, 0.0)))
        dot_[h, 0:HD, :] = low
        dot_[h, HD : 2 * HD, :] = tail.astype(BF16)
        dos[:, rows] = low.T
        dqt[h] = jnp.zeros((HD, R), F32)

    def tok_sent():
        @pl.when(z < Z - 1)
        def _():
            for k in range(Z):
                @pl.when(z - k >= 0)
                def _():
                    sent(tokb.at[z - k, y, c], s_tz.at[0, z - k])

        @pl.when(z > 0)
        def _():
            for k in range(Z):
                @pl.when(z + k < Z)
                def _():
                    sent(tokb.at[z + k, y, c], s_tz.at[1, z + k])

        for zz in range(Z):
            sent(tokb.at[zz, y, c], s_ty.at[zz])
            sent(tokb.at[zz, y, c], s_tc.at[zz, 0])
            sent(tokb.at[zz, oy, c], s_tc.at[zz, 1])

    tok_sent()

    dwkv[...] = jnp.zeros((D, 2 * D), F32)
    lacc[...] = jnp.zeros((3, 8, D), F32)

    def p_c(zz, yy):
        push(tokb.at[zz, yy, oc], crf.at[zz, yy], s_pc.at[zz, yy], r_pc.at[zz, yy], d_core)

    def p_y(zz):
        got(crf.at[zz, oy], r_pc.at[zz, oy])
        t = tokb[zz, oy, c].astype(F32) + crf[zz, oy].astype(F32)
        tokb[zz, oy, c] = t.astype(BF16)
        push(tokb.at[zz, oy, c], yrf.at[zz], s_py.at[zz], r_py.at[zz], d_y)

    def p_sum(zz):
        got(crf.at[zz, y], r_pc.at[zz, y])
        got(yrf.at[zz], r_py.at[zz])
        return tokb[zz, y, c].astype(F32) + crf[zz, y].astype(F32) + yrf[zz].astype(F32)

    def p_z(zz):
        tokb[zz, y, c] = p_sum(zz).astype(BF16)
        push(tokb.at[zz, y, c], zrf.at[z], s_pz.at[zz], r_pz.at[z], d_z(zz))

    def back_place(n):
        zz = zplus(1 + n // 4)
        part = lax.rem(n, 4)
        yy = lax.rem(y + 1 + part // 2, 2)
        cc = lax.rem(c + 1 + part, 2)
        return zz, yy, cc

    timed = {3: (r_x, 2), 7: (r_x, 1), 13: (r_y, 2)}

    def behind(n, carry):
        zz, yy, cc = back_place(n)
        part = lax.rem(n, 4)

        for at, (step, g) in timed.items():
            @pl.when(n == at)
            def _():
                step(g)

        @pl.when((part == 0) & (n >= 8))
        def _():
            p_z(zplus(n // 4 - 1))

        @pl.when(part == 3)
        def _():
            p_y(zz)

        b = (zz * 2 + yy) * 2 + cc
        keys, values, extra = kb[b], vb[b], eb[b] if KEEP else mask_of(b)
        dks, dvs = [], []
        for h in range(H):
            cols = slice(h * HD, (h + 1) * HD)
            s = dot_nn(jnp.concatenate([keys[:, cols], extra], axis=1), qt[h])
            dp = dot_nn(jnp.concatenate([values[:, cols], extra], axis=1), dot_[h])
            e = jnp.exp2(s).astype(BF16)
            ds = (e.astype(F32) * dp).astype(BF16)
            dvs.append(dot_nn(e, dos[:, cols]))
            dks.append(dot_nn(ds, qs[:, cols]) * LN2)
            dqt[h] += dot_tn(keys[:, cols], ds)
        dv = jnp.concatenate(dvs, axis=1)
        dkv = jnp.concatenate(dks + [dv], axis=1).astype(BF16)
        kb[b] = dkv[:, 0:D]
        vb[b] = dkv[:, D : 2 * D]
        gp = dot_nt(dkv, w0[:, :, :, :, :, D : 3 * D].reshape(D, 2 * D))
        if KEEP:
            norm = (tokb[zz, yy, cc].astype(F32) - stat[b, :, 0:1]) * stat[b, :, 1:2]
        else:
            mean, centered, rstd = moments(tokb[zz, yy, cc].astype(F32))
            norm = centered * rstd
        span = pl.ds(pl.multiple_of((yy * 2 + cc) * R, R), R)
        xg[span, :] = (norm * par[0:1, :] + par[1:2, :]).astype(BF16)
        lacc[0] += fold_rows(gp * norm)
        lacc[1] += fold_rows(gp)
        lacc[2] += fold_rows(dv)
        tokb[zz, yy, cc] = gp.astype(BF16)

        @pl.when(lax.rem(part, 2) == 0)
        def _():
            p_c(zz, yy)

        @pl.when(part == 3)
        def _():
            xs = xg[...]
            four = pl.ds(pl.multiple_of(zz * 4, 4), 4)
            dwkv[:, 0:D] += dot_tn(xs, kb[four].reshape(4 * R, D))
            dwkv[:, D : 2 * D] += dot_tn(xs, vb[four].reshape(4 * R, D))

        return carry

    lax.fori_loop(0, 4 * Z, behind, 0)

    dq = jnp.concatenate([(dqt[h] * (HD**-0.5)).T for h in range(H)], axis=1).astype(BF16)
    own = xown[...]
    g0[:, :, :, :, :, 0:D] = dot_tn(own, dq).astype(BF16).reshape(Z, 2, 2, FK, SLAB, D)
    g0[:, :, :, :, :, D : 3 * D] = dwkv[...].astype(BF16).reshape(Z, 2, 2, FK, SLAB, 2 * D)
    r_c(0)
    gq = dot_nt(dq, w0[:, :, :, :, :, 0:D].reshape(D, D))
    mean, centered, rstd1 = moments(tok_ref[...].astype(F32))
    n1 = centered * rstd1
    sg[0, 0:1, :] = col_sum(lacc[0]) + col_sum(gq * n1)
    sg[0, 1:2, :] = col_sum(lacc[1]) + col_sum(gq)
    sg[0, 2:3, :] = col_sum(dq.astype(F32))
    sg[0, 3:4, :] = col_sum(lacc[2])
    push(sg.at[0], src, s_sc, r_sc, d_core)

    if Z >= 2:
        p_z(zplus(Z - 1))
    r_x(0)
    got(src, r_sc)
    sg[1] = sg[0] + src[...]
    for k in range(1, FK):
        ff = fplus(k)
        push(sg.at[1], srx.at[f], s_sx.at[ff], r_sx.at[f], d_f(ff))
    r_y(1)
    r_z(2)
    acc[...] = p_sum(z) + gq
    r_y(0)
    t = sg[1]
    for k in range(1, FK):
        got(srx.at[fplus(k)], r_sx.at[fplus(k)])
        t = t + srx[fplus(k)]
    sg[2] = t
    push(sg.at[2], sry, s_sy, r_sy, d_y)
    r_z(1)
    r_z(0)
    got(sry, r_sy)
    sg[3] = sg[2] + sry[...]
    for k in range(1, Z):
        zz = zplus(k)
        push(sg.at[3], srz.at[z], s_sz.at[zz], r_sz.at[z], d_z(zz))

    t = acc[...]
    for k in range(1, Z):
        zz = zplus(k)
        got(zrf.at[zz], r_pz.at[zz])
        t = t + zrf[zz].astype(F32)
    gtok_ref[...] = (hid[...] + norm_back(t * par[0:1, :], n1, rstd1)).astype(BF16)

    gdown_ref[...] = r_end(2)
    t = r_end(1)
    gout_ref[...] = t[:, 0:D]
    gup_ref[...] = t[:, D : D + FF]
    gqkv_ref[...] = r_end(0)
    t = sg[3]
    for k in range(1, Z):
        zz = zplus(k)
        got(srz.at[zz], r_sz.at[zz])
        t = t + srz[zz]
    gsm_ref[...] = t

    for g in range(3):
        t = wb[g].at[z, y, c, f]
        for k in range(1, Z):
            sent(t, s_wz.at[g, zplus(k)])
        for zz in range(Z):
            sent(wb[g].at[zz, y, c, f], s_wy.at[g, zz])
            for k in range(1, FK):
                for yy in range(2):
                    sent(wb[g].at[zz, yy, c, f], s_wx.at[g, fplus(k), zz, yy])
        for k in range(FK):
            sent(wb[g].at[:, :, c, fplus(k)], s_wc.at[g, k])
        r_sent(g)
    for zz in range(Z):
        for yy in range(2):
            sent(tokb.at[zz, yy, oc], s_pc.at[zz, yy])
        sent(tokb.at[zz, oy, c], s_py.at[zz])
    for k in range(1, Z):
        sent(tokb.at[zplus(k), y, c], s_pz.at[zplus(k)])
        sent(sg.at[3], s_sz.at[zplus(k)])
    sent(sg.at[0], s_sc)
    for k in range(1, FK):
        sent(sg.at[1], s_sx.at[fplus(k)])
    sent(sg.at[2], s_sy)


def layer(Z, FK, R, D, FF, NT, operands):
    vm = lambda shape, dtype: pltpu.VMEM(shape, dtype)
    dma = lambda *shape: pltpu.SemaphoreType.DMA(shape)
    lead = (Z, 2, 2, FK)
    half = (Z, 2, FK)
    slabs = ((SLAB, 3 * D + 128), (SLAB, D + FF), (4 * SLAB, D))
    gslabs = ((SLAB, 3 * D), (SLAB, D + FF), (4 * SLAB, D))
    scratch = [
        vm((Z, 2, 2, R, D), BF16),
        vm((4 * Z, R, D), BF16),
        vm((4 * Z, R, D), BF16),
        vm((4 * Z if Z <= 4 else 1, R, 128), BF16),
        vm((4 * Z if Z <= 4 else 1, R, 128), F32),
        *[vm(lead + s, BF16) for s in slabs],
        *[vm(lead + s, BF16) for s in gslabs],
        *[vm(half + s, BF16) for s in gslabs],
        *[vm((FK, Z, 2) + s if FK > 1 else (SLAB, 128), BF16) for s in gslabs],
        *[vm((Z,) + s, BF16) for s in gslabs],
        *[vm((Z,) + s, BF16) for s in gslabs],
        vm((Z, 2, R, D), BF16),
        vm((Z, R, D), BF16),
        vm((Z, R, D), BF16),
        vm((SLAB, D), F32),
        vm((1, FF), F32),
        vm((H, 2 * HD, R), BF16),
        vm((H, 2 * HD, R), BF16),
        vm((R, D), BF16),
        vm((R, D), BF16),
        vm((H, 2 * HD, R), F32),
        vm((H, 1, R), F32),
        vm((H, HD, R), F32),
        vm((R, D), BF16),
        vm((R, D), F32),
        vm((R, D), F32),
        vm((R, D), F32),
        vm((4 * R, D), BF16),
        vm((D, 2 * D), F32),
        vm((3, 8, D), F32),
        vm((1, FF), F32),
        vm((R, D), BF16),
        vm((4, SLAB, D), F32),
        vm((SLAB, D), F32),
        vm((FK, SLAB, D), F32),
        vm((SLAB, D), F32),
        vm((Z, SLAB, D), F32),
        dma(2, Z), dma(Z), dma(Z, 2), dma(Z, 2, 2),
        dma(3, Z), dma(3, Z), dma(3, Z), dma(3, Z),
        dma(3, FK, Z, 2), dma(3, FK, Z, 2), dma(3, FK), dma(3, FK),
        dma(3), dma(3), dma(3, FK), dma(3, FK), dma(3), dma(3), dma(3, Z), dma(3, Z),
        dma(Z, 2), dma(Z, 2), dma(Z), dma(Z), dma(Z), dma(Z),
        pltpu.SemaphoreType.DMA, pltpu.SemaphoreType.DMA,
        dma(FK), dma(FK),
        pltpu.SemaphoreType.DMA, pltpu.SemaphoreType.DMA,
        dma(Z), dma(Z),
    ]
    vmem = pl.BlockSpec(memory_space=pltpu.VMEM)
    smem = pl.BlockSpec(memory_space=pltpu.SMEM)
    shape = jax.ShapeDtypeStruct
    return pl.pallas_call(
        functools.partial(body, Z, FK, R, D, NT),
        out_shape=(
            shape((R, D), BF16),
            shape((R, D), BF16),
            shape((SLAB, 3 * D), F32),
            shape((SLAB, D), F32),
            shape((SLAB, FF), F32),
            shape((4 * SLAB, D), F32),
            shape((SLAB, D), F32),
        ),
        in_specs=[vmem] * 7 + [smem] * 2,
        out_specs=[vmem] * 7,
        scratch_shapes=scratch,
        compiler_params=pltpu.CompilerParams(
            collective_id=0, has_side_effects=True, vmem_limit_bytes=63 * 2**20
        ),
        name="layer",
    )(*operands)


def shards(
    blocks, fsdp,
    tokens, ln1_gain, ln1_bias, qkv_weight, query_bias, value_bias, out_weight, out_bias,
    ln2_gain, ln2_bias, up_weight, up_bias, down_weight, down_bias,
    table_lengths, support_lengths, cotangent,
):
    R, D = tokens.shape[1:]
    FF = up_weight.shape[1]
    NT = table_lengths.shape[1]
    smalls = (ln1_gain, ln1_bias, query_bias, value_bias, out_bias, ln2_gain, ln2_bias, down_bias, up_bias)
    weights = (qkv_weight, out_weight, up_weight, down_weight)
    inside = qkv_weight.shape[0] == SLAB
    FK = fsdp if inside else 1
    if not inside:
        whole = lambda v: lax.all_gather(v, "fsdp", axis=0, tiled=True)
        smalls = tuple(whole(v) for v in smalls)
        weights = tuple(whole(v) for v in weights)
    rows = [jnp.pad(v[None], ((0, 0), (0, 128 - v.shape[0]))) for v in smalls]
    rows.append(jnp.zeros((SLAB - len(rows), 128), BF16))
    small_tile = jnp.concatenate(rows, axis=0)
    block_out, grad_tokens, g_qkv, g_out, g_up, g_down, g_small = layer(
        blocks // 4, FK, R, D, FF, NT,
        (tokens[0], cotangent[0], *weights, small_tile, table_lengths, support_lengths),
    )
    at = lax.axis_index("blk") * FK + (lax.axis_index("fsdp") if inside else 0)
    piece = D // (blocks * FK)
    cut = lax.dynamic_slice(g_small, (0, at * piece), (8, piece))
    up_cut = lax.dynamic_slice(g_small[8 : 8 + FF // D].reshape(FF), (at * 4 * piece,), (4 * piece,))
    small_grads = [cut[r] for r in range(8)] + [up_cut]
    weight_grads = [g_qkv, g_out, g_up, g_down]
    if not inside:
        spread = lambda v: lax.psum_scatter(v, "fsdp", scatter_dimension=0, tiled=True)
        small_grads = [spread(v) for v in small_grads]
        weight_grads = [spread(v) for v in weight_grads]
    g_ln1g, g_ln1b, g_qb, g_vb, g_ob, g_ln2g, g_ln2b, g_db, g_ub = small_grads
    g_qkv, g_out, g_up, g_down = weight_grads
    return (
        block_out[None], grad_tokens[None], g_ln1g, g_ln1b, g_qkv, g_qb, g_vb, g_out, g_ob,
        g_ln2g, g_ln2b, g_up, g_ub, g_down, g_db,
    )


def solution(mesh):
    both = ("blk", "fsdp")
    vec, mat, rows = P(both), P(both, None), P("fsdp", "blk", None)
    return jax.shard_map(
        functools.partial(shards, mesh.shape["blk"], mesh.shape["fsdp"]),
        mesh=mesh,
        in_specs=(
            rows, vec, vec, mat, vec, vec, mat, vec, vec, vec, mat, vec, mat, vec,
            P("fsdp", None), P("fsdp", None), rows,
        ),
        out_specs=(rows, rows, vec, vec, mat, vec, vec, mat, vec, vec, vec, mat, vec, mat, vec),
        check_vma=False,
    )
```

```python
import functools
import math

import jax
import jax.numpy as jnp
from jax import lax
from jax.experimental import pallas as pl
from jax.experimental.pallas import tpu as pltpu
from jax.sharding import PartitionSpec as P

H = 4
HD = 128
SLAB = 16
EPSILON = 1e-05
MASKED = -1e30
LN2 = math.log(2.0)
MESH = pl.DeviceIdType.MESH
F32 = jnp.float32
BF16 = jnp.bfloat16


def dot_nn(a, b):
    return lax.dot_general(a, b, (((1,), (0,)), ((), ())), preferred_element_type=F32)


def dot_nt(a, b):
    return lax.dot_general(a, b, (((1,), (1,)), ((), ())), preferred_element_type=F32)


def dot_tn(a, b):
    return lax.dot_general(a, b, (((0,), (0,)), ((), ())), preferred_element_type=F32)


def moments(v):
    mean = jnp.mean(v, axis=-1, keepdims=True)
    centered = v - mean
    rstd = lax.rsqrt(jnp.mean(centered * centered, axis=-1, keepdims=True) + EPSILON)
    return mean, centered, rstd


def norm_back(g, n, r):
    return r * (g - jnp.mean(g, axis=-1, keepdims=True) - n * jnp.mean(g * n, axis=-1, keepdims=True))


def three_terms(v):
    first = v.astype(BF16)
    rest = v - first.astype(F32)
    second = rest.astype(BF16)
    third = (rest - second.astype(F32)).astype(BF16)
    return first.astype(F32), second.astype(F32), third.astype(F32)


def col_sum(v):
    return jnp.sum(v, axis=0, keepdims=True)


def fold_rows(v):
    return jnp.sum(v.reshape(v.shape[0] // 8, 8, v.shape[1]), axis=0)


def body(
    Z, FK, R, D, NT,
    tok_ref, cot_ref, wq_ref, wo_ref, wu_ref, wd_ref,
    v0, v1, v2, v3, v4, v5, v6, v7, v8, len_ref, sup_ref,
    out_ref, gtok_ref, gqkv_ref, gout_ref, gup_ref, gdown_ref, gsm_ref,
    tokb, kb, vb, eb, stat, w0, w1, w2, g0, g1, g2,
    c0, c1, c2, x0, x1, x2, y0, y1, y2, z0, z1, z2,
    crf, yrf, zrf, par, upb, qt, dot_, qs, dos, ot, mrun, dqt,
    nrm2, hid, acc, gsec, xg, dwkv, lacc, upg, xown,
    sg, src, srx, sry, srz, tile,
    s_tz, s_ty, s_tc, r_t,
    s_wz, r_wz, s_wy, r_wy, s_wx, r_wx, s_wc, r_wc,
    s_gc, r_gc, s_gx, r_gx, s_gy, r_gy, s_gz, r_gz,
    s_pc, r_pc, s_py, r_py, s_pz, r_pz,
    s_sc, r_sc, s_sx, r_sx, s_sy, r_sy, s_sz, r_sz,
):
    i = lax.axis_index("blk")
    f = lax.axis_index("fsdp")
    c = lax.rem(i, 2)
    y = lax.rem(i // 2, 2)
    z = i // 4
    oc = 1 - c
    oy = 1 - y
    CH = 4 * FK * SLAB * 4
    FF = Z * CH
    NSH = Z * 4 * FK
    KEEP = Z <= 4

    def dev(zz, yy, cc, ff):
        return ((zz * 2 + yy) * 2 + cc, ff)

    d_core = dev(z, y, oc, f)
    d_y = dev(z, oy, c, f)

    def zplus(k):
        return lax.rem(z + k, Z)

    def fplus(k):
        return lax.rem(f + k, FK)

    def d_z(zz):
        return dev(zz, y, c, f)

    def d_f(ff):
        return (i, ff)

    def cp(s, d, ss, rs, to):
        return pltpu.make_async_remote_copy(
            src_ref=s, dst_ref=d, send_sem=ss, recv_sem=rs, device_id=to, device_id_type=MESH
        )

    def push(s, d, ss, rs, to):
        cp(s, d, ss, rs, to).start()

    def got(d, rs):
        cp(d, d, rs, rs, d_core).wait_recv()

    def sent(s, ss):
        cp(s, s, ss, ss, d_core).wait_send()

    bar = pltpu.get_barrier_semaphore()
    partners = [d_core, d_y] + [d_z(zplus(k)) for k in range(1, Z)] + [d_f(fplus(k)) for k in range(1, FK)]
    for to in partners:
        pl.semaphore_signal(bar, inc=1, device_id=to, device_id_type=MESH)
    pl.semaphore_wait(bar, len(partners))

    def tok_push(zz, ss_z, to):
        t = tokb.at[zz, y, c]
        push(t, t, ss_z, r_t.at[zz, y, c], to)

    def tok_side(zz):
        t = tokb.at[zz, y, c]
        push(t, t, s_ty.at[zz], r_t.at[zz, y, c], d_y)
        push(t, t, s_tc.at[zz, 0], r_t.at[zz, y, c], d_core)

    def tok_right(zz):
        @pl.when(z < Z - 1)
        def _():
            tok_push(zz, s_tz.at[0, zz], d_z(z + 1))

    def tok_left(zz):
        @pl.when(z > 0)
        def _():
            tok_push(zz, s_tz.at[1, zz], d_z(z - 1))

    def tok_z(k):
        @pl.when(z - k >= 0)
        def _():
            zz = z - k
            got(tokb.at[zz, y, c], r_t.at[zz, y, c])
            tok_right(zz)
            tok_side(zz)

        @pl.when(z + k < Z)
        def _():
            zz = z + k
            got(tokb.at[zz, y, c], r_t.at[zz, y, c])
            tok_left(zz)
            tok_side(zz)

    def tok_y_one(zz):
        t = tokb.at[zz, oy, c]
        got(t, r_t.at[zz, oy, c])
        push(t, t, s_tc.at[zz, 1], r_t.at[zz, oy, c], d_core)

    def tok_y(k):
        if k == 0:
            tok_y_one(z)
        else:
            @pl.when(z - k >= 0)
            def _():
                tok_y_one(z - k)

            @pl.when(z + k < Z)
            def _():
                tok_y_one(z + k)

    wb = (w0, w1, w2)

    def w_side(g, zz, yy):
        for k in range(1, FK):
            ff = fplus(k)
            t = wb[g].at[zz, yy, c, f]
            push(t, t, s_wx.at[g, ff, zz, yy], r_wx.at[g, f, zz, yy], d_f(ff))

    def w_out_z(g):
        t = wb[g].at[z, y, c, f]
        for k in range(1, Z):
            zz = zplus(k)
            push(t, t, s_wz.at[g, zz], r_wz.at[g, z], d_z(zz))

    def w_own(g):
        t = wb[g].at[z, y, c, f]
        push(t, t, s_wy.at[g, z], r_wy.at[g, z], d_y)
        w_side(g, z, y)

    def w_z(g):
        for k in range(1, Z):
            zz = zplus(k)
            t = wb[g].at[zz, y, c, f]
            got(t, r_wz.at[g, zz])
            push(t, t, s_wy.at[g, zz], r_wy.at[g, zz], d_y)
            w_side(g, zz, y)

    def w_core(g, ff, n):
        t = wb[g].at[:, :, c, ff]
        push(t, t, s_wc.at[g, n], r_wc.at[g, n], d_core)

    def w_y(g):
        for k in range(Z):
            zz = zplus(k)
            got(wb[g].at[zz, oy, c, f], r_wy.at[g, zz])
            w_side(g, zz, oy)
        w_core(g, f, 0)

    def w_x(g):
        for k in range(1, FK):
            ff = fplus(k)
            for zz in range(Z):
                for yy in range(2):
                    got(wb[g].at[zz, yy, c, ff], r_wx.at[g, ff, zz, yy])
            w_core(g, ff, k)

    def w_c(g):
        for k in range(FK):
            got(wb[g].at[:, :, oc, fplus(k)], r_wc.at[g, k])

    tokb[z, y, c] = tok_ref[...]
    w0[z, y, c, f, :, 0 : 3 * D] = wq_ref[...]
    tile[...] = jnp.zeros((SLAB, 128), F32)
    for r, v in enumerate((v0, v1, v2, v3, v4, v5, v6, v7, v8)):
        tile[r : r + 1, 0 : v.shape[1]] = v[...].astype(F32)
    w0[z, y, c, f, :, 3 * D : 3 * D + 128] = tile[...].astype(BF16)
    w1[z, y, c, f, :, 0:D] = wo_ref[...]
    w1[z, y, c, f, :, D : D + FF] = wu_ref[...]
    w2[z, y, c, f] = wd_ref[...]

    w_out_z(0)
    tok_right(z)
    tok_left(z)
    tok_side(z)
    w_own(0)
    w_out_z(1)
    w_own(1)
    w_own(2)

    starts, ends, stops = [], [], []
    total = jnp.int32(0)
    for t in range(NT):
        starts.append(total)
        stops.append(total + sup_ref[0, t])
        total = total + len_ref[0, t]
        ends.append(total)

    lane = lax.broadcasted_iota(jnp.int32, (1, 128), 1)
    lane_start = jnp.zeros((1, 128), jnp.int32)
    lane_stop = jnp.zeros((1, 128), jnp.int32)
    for t in range(NT):
        lane_start = jnp.where(lane == t, starts[t], lane_start)
        lane_stop = jnp.where(lane == t, stops[t], lane_stop)
    lane_ones = jnp.where((lane >= NT) & (lane < NT + 3), 1.0, 0.0)

    def mask_of(n):
        pos = n * R + lax.broadcasted_iota(jnp.int32, (R, 128), 0)
        seen = (pos >= lane_start) & (pos < lane_stop)
        extra = jnp.where(lane < NT, jnp.where(seen, 0.0, MASKED), lane_ones)
        return extra.astype(BF16)

    def mask_block(n, carry):
        eb[n] = mask_of(n)
        return carry

    if KEEP:
        lax.fori_loop(0, 4 * Z, mask_block, 0)

    row = lax.broadcasted_iota(jnp.int32, (128, R), 0)
    qpos = i * R + lax.broadcasted_iota(jnp.int32, (128, R), 1)
    onehot = jnp.zeros((128, R), F32)
    for t in range(NT):
        onehot = jnp.where((row == t) & (qpos >= starts[t]) & (qpos < ends[t]), 1.0, onehot)

    w_z(0)
    tok_y(0)
    tok_z(1)
    w_out_z(2)
    w_y(0)
    w_z(1)
    w_x(0)
    tok_y(1)
    w_c(0)

    piece = D // NSH
    small = w0[:, :, :, :, :, 3 * D : 3 * D + 128].reshape(NSH * SLAB, 128)
    spread = (
        lax.rem(lax.broadcasted_iota(jnp.int32, (128, D), 1), piece)
        == lax.broadcasted_iota(jnp.int32, (128, D), 0)
    )
    wide = dot_nn(small, spread.astype(BF16))
    mine = (
        lax.broadcasted_iota(jnp.int32, (NSH * SLAB, D), 1) // piece
        == lax.broadcasted_iota(jnp.int32, (NSH * SLAB, D), 0) // SLAB
    )
    wide = jnp.where(mine, wide, 0.0)
    par[...] = jnp.sum(wide.reshape(NSH, SLAB, D), axis=0)
    pick = (
        lax.broadcasted_iota(jnp.int32, (NSH, NSH * SLAB), 1)
        == lax.broadcasted_iota(jnp.int32, (NSH, NSH * SLAB), 0) * SLAB + 8
    )
    ups = dot_nn(pick.astype(BF16), small).astype(BF16)
    spread = (
        lax.rem(lax.broadcasted_iota(jnp.int32, (128, FF), 1), 4 * piece)
        == lax.broadcasted_iota(jnp.int32, (128, FF), 0)
    )
    wide = dot_nn(ups, spread.astype(BF16))
    mine = (
        lax.broadcasted_iota(jnp.int32, (NSH, FF), 1) // (4 * piece)
        == lax.broadcasted_iota(jnp.int32, (NSH, FF), 0)
    )
    upb[...] = col_sum(jnp.where(mine, wide, 0.0))
    ln1g, ln1b = par[0:1, :], par[1:2, :]

    tokens = tok_ref[...].astype(F32)
    mean, centered, rstd = moments(tokens)
    own = (centered * rstd * ln1g + ln1b).astype(BF16)
    xown[...] = own
    wq = w0[:, :, :, :, :, 0:D].reshape(D, D)
    qscale = HD ** (-0.5) / LN2
    qs[...] = ((dot_nn(own, wq) + par[2:3, :]) * qscale).astype(BF16)
    for h in range(H):
        qt[h, 0:HD, :] = qs[:, h * HD : (h + 1) * HD].T
        qt[h, HD : 2 * HD, :] = onehot.astype(BF16)
        ot[h] = jnp.zeros((2 * HD, R), F32)
        mrun[h] = jnp.full((1, R), MASKED, F32)

    def near(s):
        inner = jnp.minimum(z, Z - 1 - z)
        odd = lax.rem(s, 2)
        paired = z + (1 - 2 * odd) * ((s + 1) // 2)
        rest = jnp.where(z < Z - 1 - z, s, Z - 1 - s)
        return jnp.where(s <= 2 * inner, paired, rest)

    def place(n):
        zz = near(n // 4)
        part = lax.rem(n, 4)
        yy = lax.rem(y + part // 2, 2)
        cc = lax.rem(c + part, 2)
        return zz, yy, cc

    arrivals = {2: [lambda: tok_z(2)], 4: [lambda: w_y(1)], 5: [lambda: w_z(2)], 8: [lambda: tok_y(2), lambda: w_x(1)]}
    for k in range(3, Z):
        arrivals.setdefault(4 * k - 3, []).append(lambda k=k: tok_z(k))
        arrivals.setdefault(4 * k + 2, []).append(lambda k=k: tok_y(k))
    arrivals.setdefault(12, []).append(lambda: w_y(2))

    def ahead(n, carry):
        zz, yy, cc = place(n)

        for at in sorted(arrivals):
            @pl.when(n == at)
            def _():
                for step in arrivals[at]:
                    step()

        @pl.when(lax.rem(n, 2) == 1)
        def _():
            got(tokb.at[zz, yy, cc], r_t.at[zz, yy, cc])

        b = (zz * 2 + yy) * 2 + cc
        mean, centered, rstd = moments(tokb[zz, yy, cc].astype(F32))
        if KEEP:
            stat[b] = jnp.where(lax.broadcasted_iota(jnp.int32, (R, 128), 1) == 0, mean, rstd)
        x = (centered * rstd * par[0:1, :] + par[1:2, :]).astype(BF16)
        kv = dot_nn(x, w0[:, :, :, :, :, D : 3 * D].reshape(D, 2 * D))
        keys = kv[:, 0:D].astype(BF16)
        values = (kv[:, D : 2 * D] + par[3:4, :]).astype(BF16)
        kb[b] = keys
        vb[b] = values
        extra = eb[b] if KEEP else mask_of(b)
        for h in range(H):
            cols = slice(h * HD, (h + 1) * HD)
            s = dot_nn(jnp.concatenate([keys[:, cols], extra], axis=1), qt[h])
            before = mrun[h]
            top = jnp.maximum(before, jnp.ceil(jnp.max(s, axis=0, keepdims=True)))
            e = jnp.exp2(s - top).astype(BF16)
            grown = dot_tn(jnp.concatenate([values[:, cols], extra], axis=1), e)
            ot[h] = ot[h] * jnp.exp2(before - top) + grown
            mrun[h] = top
        return carry

    lax.fori_loop(0, 4 * Z, ahead, 0)

    w_x(2)
    w_c(1)
    w_c(2)

    parts = []
    for h in range(H):
        inverse = 1.0 / ot[h, HD + NT : HD + NT + 1, :]
        attended = ot[h, 0:HD, :] * inverse
        ot[h, 0:HD, :] = attended
        dot_[h, HD : HD + 1, :] = inverse.astype(BF16)
        ot[h, HD : HD + 1, :] = inverse
        parts.append(attended.T.astype(BF16))
        m1, m2, m3 = three_terms(mrun[h])
        tail = jnp.where(row == NT, -m1, jnp.where(row == NT + 1, -m2, jnp.where(row == NT + 2, -m3, onehot)))
        qt[h, HD : 2 * HD, :] = tail.astype(BF16)
    attn_low = jnp.concatenate(parts, axis=1)
    w_out = w1[:, :, :, :, :, 0:D].reshape(D, D)
    hidden = tokens + (dot_nn(attn_low, w_out) + par[4:5, :])
    hid[...] = hidden
    mean2, centered, rstd2 = moments(hidden)
    n2 = centered * rstd2
    nrm2[...] = (n2 * par[5:6, :] + par[6:7, :]).astype(BF16)
    acc[...] = hidden + par[7:8, :]
    gsec[...] = jnp.zeros((R, D), F32)

    def chunk(j, carry):
        cols = pl.ds(pl.multiple_of(D + j * CH, 128), CH)
        bcols = pl.ds(pl.multiple_of(j * CH, 128), CH)
        up = w1[:, :, :, :, :, cols].reshape(D, CH)
        down = w2[j].reshape(CH, D)
        normed = nrm2[...]
        cot = cot_ref[...]
        pre = dot_nn(normed, up) + upb[:, bcols]
        phi = 0.5 * (1.0 + lax.erf(pre * (0.5**0.5)))
        act = (pre * phi).astype(BF16)
        slope = phi + pre * (jnp.exp2(pre * pre * (-0.5 / LN2)) * ((2.0 * math.pi) ** -0.5))
        acc[...] += dot_nn(act, down)
        gpre32 = dot_nt(cot, down) * slope
        gpre = gpre32.astype(BF16)
        gsec[...] += dot_nt(gpre, up)
        upg[:, bcols] = col_sum(gpre.astype(F32))
        g1[:, :, :, :, :, cols] = dot_tn(normed, gpre).astype(BF16).reshape(Z, 2, 2, FK, SLAB, CH)
        g2[j] = dot_tn(act, cot).astype(BF16).reshape(2, 2, FK, 4 * SLAB, D)
        return carry

    lax.fori_loop(0, Z, chunk, 0)
    out_ref[...] = acc[...].astype(BF16)

    gb = (g0, g1, g2)
    cb = (c0, c1, c2)
    xb = (x0, x1, x2)
    yb = (y0, y1, y2)
    zb = (z0, z1, z2)

    def r_c(g):
        push(gb[g].at[:, :, oc], cb[g], s_gc.at[g], r_gc.at[g], d_core)

    def r_x(g):
        got(cb[g], r_gc.at[g])

        def one(zz, carry):
            t = gb[g][zz, :, c].astype(F32) + cb[g][zz].astype(F32)
            gb[g][zz, :, c] = t.astype(BF16)
            return carry

        lax.fori_loop(0, Z, one, 0)
        for k in range(1, FK):
            ff = fplus(k)
            push(gb[g].at[:, :, c, ff], xb[g].at[f], s_gx.at[g, ff], r_gx.at[g, f], d_f(ff))

    def r_y(g):
        for k in range(1, FK):
            got(xb[g].at[fplus(k)], r_gx.at[g, fplus(k)])

        if FK > 1:
            def one(zz, carry):
                t = gb[g][zz, :, c, f].astype(F32)
                for k in range(1, FK):
                    t = t + xb[g][fplus(k), zz].astype(F32)
                gb[g][zz, :, c, f] = t.astype(BF16)
                return carry

            lax.fori_loop(0, Z, one, 0)
        push(gb[g].at[:, oy, c, f], yb[g], s_gy.at[g], r_gy.at[g], d_y)

    def r_z(g):
        got(yb[g], r_gy.at[g])

        def one(zz, carry):
            t = gb[g][zz, y, c, f].astype(F32) + yb[g][zz].astype(F32)
            gb[g][zz, y, c, f] = t.astype(BF16)
            return carry

        lax.fori_loop(0, Z, one, 0)
        for k in range(1, Z):
            zz = zplus(k)
            push(gb[g].at[zz, y, c, f], zb[g].at[z], s_gz.at[g, zz], r_gz.at[g, z], d_z(zz))

    def r_end(g):
        t = gb[g][z, y, c, f].astype(F32)
        for k in range(1, Z):
            zz = zplus(k)
            got(zb[g].at[zz], r_gz.at[g, zz])
            t = t + zb[g][zz].astype(F32)
        return t

    def r_sent(g):
        sent(gb[g].at[:, :, oc], s_gc.at[g])
        for k in range(1, FK):
            sent(gb[g].at[:, :, c, fplus(k)], s_gx.at[g, fplus(k)])
        sent(gb[g].at[:, oy, c, f], s_gy.at[g])
        for k in range(1, Z):
            sent(gb[g].at[zplus(k), y, c, f], s_gz.at[g, zplus(k)])

    r_c(2)

    g_second = gsec[...]
    n2 = (hid[...] - mean2) * rstd2
    ln2g = par[5:6, :]
    cot32 = cot_ref[...].astype(F32)
    grad_hidden = cot32 + norm_back(g_second * ln2g, n2, rstd2)
    hid[...] = grad_hidden
    g_branch = grad_hidden.astype(BF16)
    g1[:, :, :, :, :, 0:D] = dot_tn(attn_low, g_branch).astype(BF16).reshape(Z, 2, 2, FK, SLAB, D)
    r_c(1)
    zero = jnp.zeros((1, D), F32)
    for r in range(SLAB):
        sg[0, r : r + 1, :] = zero
    sg[0, 4:5, :] = col_sum(g_branch.astype(F32))
    sg[0, 5:6, :] = col_sum(g_second * n2)
    sg[0, 6:7, :] = col_sum(g_second)
    sg[0, 7:8, :] = col_sum(cot32)
    for r in range(FF // D):
        sg[0, 8 + r : 9 + r, :] = upg[:, r * D : (r + 1) * D]

    for h in range(H):
        rows = slice(h * HD, (h + 1) * HD)
        w_head = w1[:, :, :, :, :, 0:D].reshape(D, D)[rows, :]
        ga = dot_nt(w_head, g_branch).astype(BF16).astype(F32)
        low = (ga * ot[h, HD : HD + 1, :]).astype(BF16)
        delta = col_sum(low.astype(F32) * ot[h, 0:HD, :])
        d1, d2, d3 = three_terms(delta)
        tail = jnp.where(row == NT, -d1, jnp.where(row == NT + 1, -d2, jnp.where(row == NT + 2, -d3, 0.0)))
        dot_[h, 0:HD, :] = low
        dot_[h, HD : 2 * HD, :] = tail.astype(BF16)
        dos[:, rows] = low.T
        dqt[h] = jnp.zeros((HD, R), F32)

    def tok_sent():
        @pl.when(z < Z - 1)
        def _():
            for k in range(Z):
                @pl.when(z - k >= 0)
                def _():
                    sent(tokb.at[z - k, y, c], s_tz.at[0, z - k])

        @pl.when(z > 0)
        def _():
            for k in range(Z):
                @pl.when(z + k < Z)
                def _():
                    sent(tokb.at[z + k, y, c], s_tz.at[1, z + k])

        for zz in range(Z):
            sent(tokb.at[zz, y, c], s_ty.at[zz])
            sent(tokb.at[zz, y, c], s_tc.at[zz, 0])
            sent(tokb.at[zz, oy, c], s_tc.at[zz, 1])

    tok_sent()

    dwkv[...] = jnp.zeros((D, 2 * D), F32)
    lacc[...] = jnp.zeros((3, 8, D), F32)

    def p_c(zz, yy):
        push(tokb.at[zz, yy, oc], crf.at[zz, yy], s_pc.at[zz, yy], r_pc.at[zz, yy], d_core)

    def p_y(zz):
        got(crf.at[zz, oy], r_pc.at[zz, oy])
        t = tokb[zz, oy, c].astype(F32) + crf[zz, oy].astype(F32)
        tokb[zz, oy, c] = t.astype(BF16)
        push(tokb.at[zz, oy, c], yrf.at[zz], s_py.at[zz], r_py.at[zz], d_y)

    def p_sum(zz):
        got(crf.at[zz, y], r_pc.at[zz, y])
        got(yrf.at[zz], r_py.at[zz])
        return tokb[zz, y, c].astype(F32) + crf[zz, y].astype(F32) + yrf[zz].astype(F32)

    def p_z(zz):
        tokb[zz, y, c] = p_sum(zz).astype(BF16)
        push(tokb.at[zz, y, c], zrf.at[z], s_pz.at[zz], r_pz.at[z], d_z(zz))

    def back_place(n):
        zz = zplus(1 + n // 4)
        part = lax.rem(n, 4)
        yy = lax.rem(y + 1 + part // 2, 2)
        cc = lax.rem(c + 1 + part, 2)
        return zz, yy, cc

    timed = {3: (r_x, 2), 7: (r_x, 1), 13: (r_y, 2)}

    def behind(n, carry):
        zz, yy, cc = back_place(n)
        part = lax.rem(n, 4)

        for at, (step, g) in timed.items():
            @pl.when(n == at)
            def _():
                step(g)

        @pl.when((part == 0) & (n >= 8))
        def _():
            p_z(zplus(n // 4 - 1))

        @pl.when(part == 3)
        def _():
            p_y(zz)

        b = (zz * 2 + yy) * 2 + cc
        keys, values, extra = kb[b], vb[b], eb[b] if KEEP else mask_of(b)
        dks, dvs = [], []
        for h in range(H):
            cols = slice(h * HD, (h + 1) * HD)
            s = dot_nn(jnp.concatenate([keys[:, cols], extra], axis=1), qt[h])
            dp = dot_nn(jnp.concatenate([values[:, cols], extra], axis=1), dot_[h])
            e = jnp.exp2(s).astype(BF16)
            ds = (e.astype(F32) * dp).astype(BF16)
            dvs.append(dot_nn(e, dos[:, cols]))
            dks.append(dot_nn(ds, qs[:, cols]) * LN2)
            dqt[h] += dot_tn(keys[:, cols], ds)
        dv = jnp.concatenate(dvs, axis=1)
        dkv = jnp.concatenate(dks + [dv], axis=1).astype(BF16)
        kb[b] = dkv[:, 0:D]
        vb[b] = dkv[:, D : 2 * D]
        gp = dot_nt(dkv, w0[:, :, :, :, :, D : 3 * D].reshape(D, 2 * D))
        if KEEP:
            norm = (tokb[zz, yy, cc].astype(F32) - stat[b, :, 0:1]) * stat[b, :, 1:2]
        else:
            mean, centered, rstd = moments(tokb[zz, yy, cc].astype(F32))
            norm = centered * rstd
        span = pl.ds(pl.multiple_of((yy * 2 + cc) * R, R), R)
        xg[span, :] = (norm * par[0:1, :] + par[1:2, :]).astype(BF16)
        lacc[0] += fold_rows(gp * norm)
        lacc[1] += fold_rows(gp)
        lacc[2] += fold_rows(dv)
        tokb[zz, yy, cc] = gp.astype(BF16)

        @pl.when(lax.rem(part, 2) == 0)
        def _():
            p_c(zz, yy)

        @pl.when(part == 3)
        def _():
            xs = xg[...]
            four = pl.ds(pl.multiple_of(zz * 4, 4), 4)
            dwkv[:, 0:D] += dot_tn(xs, kb[four].reshape(4 * R, D))
            dwkv[:, D : 2 * D] += dot_tn(xs, vb[four].reshape(4 * R, D))

        return carry

    lax.fori_loop(0, 4 * Z, behind, 0)

    dq = jnp.concatenate([(dqt[h] * (HD**-0.5)).T for h in range(H)], axis=1).astype(BF16)
    own = xown[...]
    g0[:, :, :, :, :, 0:D] = dot_tn(own, dq).astype(BF16).reshape(Z, 2, 2, FK, SLAB, D)
    g0[:, :, :, :, :, D : 3 * D] = dwkv[...].astype(BF16).reshape(Z, 2, 2, FK, SLAB, 2 * D)
    r_c(0)
    gq = dot_nt(dq, w0[:, :, :, :, :, 0:D].reshape(D, D))
    mean, centered, rstd1 = moments(tok_ref[...].astype(F32))
    n1 = centered * rstd1
    sg[0, 0:1, :] = col_sum(lacc[0]) + col_sum(gq * n1)
    sg[0, 1:2, :] = col_sum(lacc[1]) + col_sum(gq)
    sg[0, 2:3, :] = col_sum(dq.astype(F32))
    sg[0, 3:4, :] = col_sum(lacc[2])
    push(sg.at[0], src, s_sc, r_sc, d_core)

    if Z >= 2:
        p_z(zplus(Z - 1))
    r_x(0)
    got(src, r_sc)
    sg[1] = sg[0] + src[...]
    for k in range(1, FK):
        ff = fplus(k)
        push(sg.at[1], srx.at[f], s_sx.at[ff], r_sx.at[f], d_f(ff))
    r_y(1)
    r_z(2)
    acc[...] = p_sum(z) + gq
    r_y(0)
    t = sg[1]
    for k in range(1, FK):
        got(srx.at[fplus(k)], r_sx.at[fplus(k)])
        t = t + srx[fplus(k)]
    sg[2] = t
    push(sg.at[2], sry, s_sy, r_sy, d_y)
    r_z(1)
    r_z(0)
    got(sry, r_sy)
    sg[3] = sg[2] + sry[...]
    for k in range(1, Z):
        zz = zplus(k)
        push(sg.at[3], srz.at[z], s_sz.at[zz], r_sz.at[z], d_z(zz))

    t = acc[...]
    for k in range(1, Z):
        zz = zplus(k)
        got(zrf.at[zz], r_pz.at[zz])
        t = t + zrf[zz].astype(F32)
    gtok_ref[...] = (hid[...] + norm_back(t * par[0:1, :], n1, rstd1)).astype(BF16)

    gdown_ref[...] = r_end(2)
    t = r_end(1)
    gout_ref[...] = t[:, 0:D]
    gup_ref[...] = t[:, D : D + FF]
    gqkv_ref[...] = r_end(0)
    t = sg[3]
    for k in range(1, Z):
        zz = zplus(k)
        got(srz.at[zz], r_sz.at[zz])
        t = t + srz[zz]
    gsm_ref[...] = t

    for g in range(3):
        t = wb[g].at[z, y, c, f]
        for k in range(1, Z):
            sent(t, s_wz.at[g, zplus(k)])
        for zz in range(Z):
            sent(wb[g].at[zz, y, c, f], s_wy.at[g, zz])
            for k in range(1, FK):
                for yy in range(2):
                    sent(wb[g].at[zz, yy, c, f], s_wx.at[g, fplus(k), zz, yy])
        for k in range(FK):
            sent(wb[g].at[:, :, c, fplus(k)], s_wc.at[g, k])
        r_sent(g)
    for zz in range(Z):
        for yy in range(2):
            sent(tokb.at[zz, yy, oc], s_pc.at[zz, yy])
        sent(tokb.at[zz, oy, c], s_py.at[zz])
    for k in range(1, Z):
        sent(tokb.at[zplus(k), y, c], s_pz.at[zplus(k)])
        sent(sg.at[3], s_sz.at[zplus(k)])
    sent(sg.at[0], s_sc)
    for k in range(1, FK):
        sent(sg.at[1], s_sx.at[fplus(k)])
    sent(sg.at[2], s_sy)


def layer(Z, FK, R, D, FF, NT, operands):
    vm = lambda shape, dtype: pltpu.VMEM(shape, dtype)
    dma = lambda *shape: pltpu.SemaphoreType.DMA(shape)
    lead = (Z, 2, 2, FK)
    half = (Z, 2, FK)
    slabs = ((SLAB, 3 * D + 128), (SLAB, D + FF), (4 * SLAB, D))
    gslabs = ((SLAB, 3 * D), (SLAB, D + FF), (4 * SLAB, D))
    scratch = [
        vm((Z, 2, 2, R, D), BF16),
        vm((4 * Z, R, D), BF16),
        vm((4 * Z, R, D), BF16),
        vm((4 * Z if Z <= 4 else 1, R, 128), BF16),
        vm((4 * Z if Z <= 4 else 1, R, 128), F32),
        *[vm(lead + s, BF16) for s in slabs],
        *[vm(lead + s, BF16) for s in gslabs],
        *[vm(half + s, BF16) for s in gslabs],
        *[vm((FK, Z, 2) + s if FK > 1 else (SLAB, 128), BF16) for s in gslabs],
        *[vm((Z,) + s, BF16) for s in gslabs],
        *[vm((Z,) + s, BF16) for s in gslabs],
        vm((Z, 2, R, D), BF16),
        vm((Z, R, D), BF16),
        vm((Z, R, D), BF16),
        vm((SLAB, D), F32),
        vm((1, FF), F32),
        vm((H, 2 * HD, R), BF16),
        vm((H, 2 * HD, R), BF16),
        vm((R, D), BF16),
        vm((R, D), BF16),
        vm((H, 2 * HD, R), F32),
        vm((H, 1, R), F32),
        vm((H, HD, R), F32),
        vm((R, D), BF16),
        vm((R, D), F32),
        vm((R, D), F32),
        vm((R, D), F32),
        vm((4 * R, D), BF16),
        vm((D, 2 * D), F32),
        vm((3, 8, D), F32),
        vm((1, FF), F32),
        vm((R, D), BF16),
        vm((4, SLAB, D), F32),
        vm((SLAB, D), F32),
        vm((FK, SLAB, D), F32),
        vm((SLAB, D), F32),
        vm((Z, SLAB, D), F32),
        vm((SLAB, 128), F32),
        dma(2, Z), dma(Z), dma(Z, 2), dma(Z, 2, 2),
        dma(3, Z), dma(3, Z), dma(3, Z), dma(3, Z),
        dma(3, FK, Z, 2), dma(3, FK, Z, 2), dma(3, FK), dma(3, FK),
        dma(3), dma(3), dma(3, FK), dma(3, FK), dma(3), dma(3), dma(3, Z), dma(3, Z),
        dma(Z, 2), dma(Z, 2), dma(Z), dma(Z), dma(Z), dma(Z),
        pltpu.SemaphoreType.DMA, pltpu.SemaphoreType.DMA,
        dma(FK), dma(FK),
        pltpu.SemaphoreType.DMA, pltpu.SemaphoreType.DMA,
        dma(Z), dma(Z),
    ]
    vmem = pl.BlockSpec(memory_space=pltpu.VMEM)
    smem = pl.BlockSpec(memory_space=pltpu.SMEM)
    shape = jax.ShapeDtypeStruct
    return pl.pallas_call(
        functools.partial(body, Z, FK, R, D, NT),
        out_shape=(
            shape((R, D), BF16),
            shape((R, D), BF16),
            shape((SLAB, 3 * D), F32),
            shape((SLAB, D), F32),
            shape((SLAB, FF), F32),
            shape((4 * SLAB, D), F32),
            shape((SLAB, D), F32),
        ),
        in_specs=[vmem] * 15 + [smem] * 2,
        out_specs=[vmem] * 7,
        scratch_shapes=scratch,
        compiler_params=pltpu.CompilerParams(
            collective_id=0, has_side_effects=True, vmem_limit_bytes=63 * 2**20
        ),
        name="layer",
    )(*operands)


def finish(NSH, FK, *refs):
    big_in, small_in, big_out, small_out = refs[0:6], refs[6], refs[7:13], refs[13:22]
    for a, b in zip(big_in, big_out):
        b[...] = a[...]
    at = lax.axis_index("blk") * FK
    if FK > 1:
        at = at + lax.axis_index("fsdp")
    D = small_in.shape[1]
    piece = D // NSH
    lane = lax.broadcasted_iota(jnp.int32, (128, D), 1)
    take = lax.broadcasted_iota(jnp.int32, (128, D), 0)
    full = small_in[...]
    for r in range(8):
        chosen = jnp.where(lane == at * piece + take, full[r : r + 1, :], 0.0)
        small_out[r][...] = jnp.sum(chosen, axis=1).reshape(1, 128)[:, 0:piece]
    FF = D * 4
    total = jnp.zeros((128,), F32)
    for r in range(4):
        chosen = jnp.where(lane + r * D == at * 4 * piece + take, full[8 + r : 9 + r, :], 0.0)
        total = total + jnp.sum(chosen, axis=1)
    small_out[8][...] = total.reshape(1, 128)[:, 0 : 4 * piece]


def hand_over(NSH, FK, FF, results):
    *big, small = results
    D = small.shape[1]
    vmem = pl.BlockSpec(memory_space=pltpu.VMEM)
    shape = jax.ShapeDtypeStruct
    return pl.pallas_call(
        functools.partial(finish, NSH, FK),
        out_shape=(
            *[shape(v.shape, v.dtype) for v in big],
            *[shape((1, D // NSH), F32) for _ in range(8)],
            shape((1, FF // NSH), F32),
        ),
        in_specs=[vmem] * 7,
        out_specs=[vmem] * 15,
        name="finish",
    )(*results)


def shards(
    blocks, fsdp,
    tokens, ln1_gain, ln1_bias, qkv_weight, query_bias, value_bias, out_weight, out_bias,
    ln2_gain, ln2_bias, up_weight, up_bias, down_weight, down_bias,
    table_lengths, support_lengths, cotangent,
):
    R, D = tokens.shape[1:]
    FF = up_weight.shape[1]
    NT = table_lengths.shape[1]
    smalls = (ln1_gain, ln1_bias, query_bias, value_bias, out_bias, ln2_gain, ln2_bias, down_bias, up_bias)
    weights = (qkv_weight, out_weight, up_weight, down_weight)
    inside = qkv_weight.shape[0] == SLAB
    FK = fsdp if inside else 1
    if not inside:
        whole = lambda v: lax.all_gather(v, "fsdp", axis=0, tiled=True)
        smalls = tuple(whole(v) for v in smalls)
        weights = tuple(whole(v) for v in weights)
    results = layer(
        blocks // 4, FK, R, D, FF, NT,
        (tokens[0], cotangent[0], *weights, *[v[None] for v in smalls], table_lengths, support_lengths),
    )
    block_out, grad_tokens, g_qkv, g_out, g_up, g_down, *small_grads = hand_over(
        blocks * FK, FK, FF, results
    )
    small_grads = [v[0] for v in small_grads]
    weight_grads = [g_qkv, g_out, g_up, g_down]
    if not inside:
        spread = lambda v: lax.psum_scatter(v, "fsdp", scatter_dimension=0, tiled=True)
        small_grads = [spread(v) for v in small_grads]
        weight_grads = [spread(v) for v in weight_grads]
    g_ln1g, g_ln1b, g_qb, g_vb, g_ob, g_ln2g, g_ln2b, g_db, g_ub = small_grads
    g_qkv, g_out, g_up, g_down = weight_grads
    return (
        block_out[None], grad_tokens[None], g_ln1g, g_ln1b, g_qkv, g_qb, g_vb, g_out, g_ob,
        g_ln2g, g_ln2b, g_up, g_ub, g_down, g_db,
    )


def solution(mesh):
    both = ("blk", "fsdp")
    vec, mat, rows = P(both), P(both, None), P("fsdp", "blk", None)
    return jax.shard_map(
        functools.partial(shards, mesh.shape["blk"], mesh.shape["fsdp"]),
        mesh=mesh,
        in_specs=(
            rows, vec, vec, mat, vec, vec, mat, vec, vec, vec, mat, vec, mat, vec,
            P("fsdp", None), P("fsdp", None), rows,
        ),
        out_specs=(rows, rows, vec, vec, mat, vec, vec, mat, vec, vec, vec, mat, vec, mat, vec),
        check_vma=False,
    )
```

```python
import functools
import math

import jax
import jax.numpy as jnp
from jax import lax
from jax.experimental import pallas as pl
from jax.experimental.pallas import tpu as pltpu
from jax.sharding import PartitionSpec as P

H = 4
HD = 128
SLAB = 16
EPSILON = 1e-05
MASKED = -1e30
LN2 = math.log(2.0)
MESH = pl.DeviceIdType.MESH
F32 = jnp.float32
BF16 = jnp.bfloat16


def dot_nn(a, b):
    return lax.dot_general(a, b, (((1,), (0,)), ((), ())), preferred_element_type=F32)


def dot_nt(a, b):
    return lax.dot_general(a, b, (((1,), (1,)), ((), ())), preferred_element_type=F32)


def dot_tn(a, b):
    return lax.dot_general(a, b, (((0,), (0,)), ((), ())), preferred_element_type=F32)


def moments(v):
    mean = jnp.mean(v, axis=-1, keepdims=True)
    centered = v - mean
    rstd = lax.rsqrt(jnp.mean(centered * centered, axis=-1, keepdims=True) + EPSILON)
    return mean, centered, rstd


def norm_back(g, n, r):
    return r * (g - jnp.mean(g, axis=-1, keepdims=True) - n * jnp.mean(g * n, axis=-1, keepdims=True))


def three_terms(v):
    first = v.astype(BF16)
    rest = v - first.astype(F32)
    second = rest.astype(BF16)
    third = (rest - second.astype(F32)).astype(BF16)
    return first.astype(F32), second.astype(F32), third.astype(F32)


def col_sum(v):
    return jnp.sum(v, axis=0, keepdims=True)


def fold_rows(v):
    return jnp.sum(v.reshape(v.shape[0] // 8, 8, v.shape[1]), axis=0)


def body(
    Z, FK, R, D, NT,
    tok_ref, cot_ref, wq_ref, wo_ref, wu_ref, wd_ref,
    v0, v1, v2, v3, v4, v5, v6, v7, v8, len_ref, sup_ref,
    out_ref, gtok_ref, gqkv_ref, gout_ref, gup_ref, gdown_ref, gsm_ref,
    tokb, tokp, kb, vb, eb, stat, w0, w1, w2, gs, gu, gd,
    cs, cu, cd, xs, xu, xd, ys, yu, yd, zs, zu, zd,
    crf, zrf, par, upb, qt, dot_, qs, dos, ot, mrun, dqt,
    oh, ol, ml, ohr, olr, mlr, gqs, gqr,
    nrm2, hid, acc, gsec, dwkv, lacc, upg, xq,
    sg, src, srx, sry, srz, tile,
    s_tz, s_tc, r_t, s_tp, r_tp,
    s_wz, r_wz, s_wy, r_wy, s_wx, r_wx, s_wc, r_wc,
    s_gc, r_gc, s_gx, r_gx, s_gy, r_gy, s_gz, r_gz,
    s_pc, r_pc, s_pz, r_pz, s_y, r_y,
    s_sc, r_sc, s_sx, r_sx, s_sy, r_sy, s_sz, r_sz,
):
    i = lax.axis_index("blk")
    f = lax.axis_index("fsdp")
    c = lax.rem(i, 2)
    y = lax.rem(i // 2, 2)
    z = i // 4
    oc = 1 - c
    oy = 1 - y
    CH = 4 * FK * SLAB * 4
    FF = Z * CH
    NSH = Z * 4 * FK

    def dev(zz, yy, cc, ff):
        return ((zz * 2 + yy) * 2 + cc, ff)

    d_core = dev(z, y, oc, f)
    d_y = dev(z, oy, c, f)

    def zplus(k):
        return lax.rem(z + k, Z)

    def zxor(m):
        out, bit = z, 1
        while bit < Z:
            out = out + bit * ((m // bit) % 2) * (1 - 2 * lax.rem(z // bit, 2))
            bit *= 2
        return out

    def fplus(k):
        return lax.rem(f + k, FK)

    def d_z(zz):
        return dev(zz, y, c, f)

    def d_f(ff):
        return (i, ff)

    def cp(s, d, ss, rs, to):
        return pltpu.make_async_remote_copy(
            src_ref=s, dst_ref=d, send_sem=ss, recv_sem=rs, device_id=to, device_id_type=MESH
        )

    def push(s, d, ss, rs, to):
        cp(s, d, ss, rs, to).start()

    def got(d, rs):
        cp(d, d, rs, rs, d_core).wait_recv()

    def sent(s, ss):
        cp(s, s, ss, ss, d_core).wait_send()

    bar = pltpu.get_barrier_semaphore()
    partners = [d_core, d_y] + [d_z(zplus(k)) for k in range(1, Z)] + [d_f(fplus(k)) for k in range(1, FK)]
    for to in partners:
        pl.semaphore_signal(bar, inc=1, device_id=to, device_id_type=MESH)
    pl.semaphore_wait(bar, len(partners))

    def tok_push(zz, ss_z, to):
        t = tokb.at[zz, c]
        push(t, t, ss_z, r_t.at[zz, c], to)

    def tok_core(zz):
        t = tokb.at[zz, c]
        push(t, t, s_tc.at[zz], r_t.at[zz, c], d_core)

    def tok_right(zz):
        @pl.when(z < Z - 1)
        def _():
            tok_push(zz, s_tz.at[0, zz], d_z(z + 1))

    def tok_left(zz):
        @pl.when(z > 0)
        def _():
            tok_push(zz, s_tz.at[1, zz], d_z(z - 1))

    def tok_z(k):
        @pl.when(z - k >= 0)
        def _():
            zz = z - k
            got(tokb.at[zz, c], r_t.at[zz, c])
            tok_right(zz)
            tok_core(zz)

        @pl.when(z + k < Z)
        def _():
            zz = z + k
            got(tokb.at[zz, c], r_t.at[zz, c])
            tok_left(zz)
            tok_core(zz)

    wb = (w0, w1, w2)

    x_first = {2}

    def w_push_x(g, zz, yy):
        for k in range(1, FK):
            ff = fplus(k)
            t = wb[g].at[zz, yy, c, f]
            push(t, t, s_wx.at[g, ff, zz, yy], r_wx.at[g, f, zz, yy], d_f(ff))

    def w_push_y(g, zz, ff):
        t = wb[g].at[zz, y, c, ff]
        push(t, t, s_wy.at[g, zz, ff], r_wy.at[g, zz, ff], d_y)

    def w_out_z(g):
        t = wb[g].at[z, y, c, f]
        for k in range(1, Z):
            zz = zplus(k)
            push(t, t, s_wz.at[g, zz], r_wz.at[g, z], d_z(zz))

    def w_own_y(g):
        w_push_y(g, z, f)

    def w_own_x(g):
        w_push_x(g, z, y)

    def w_z(g):
        for k in range(1, Z):
            zz = zplus(k)
            got(wb[g].at[zz, y, c, f], r_wz.at[g, zz])
            w_push_x(g, zz, y)
            w_push_y(g, zz, f)

    def w_to_core(g, n):
        if g in x_first:
            t = wb[g].at[:, y if n == 0 else oy, c]
        else:
            t = wb[g].at[:, :, c, fplus(n)]
        push(t, t, s_wc.at[g, n], r_wc.at[g, n], d_core)

    def w_m(g):
        if g in x_first:
            for zz in range(Z):
                for k in range(1, FK):
                    ff = fplus(k)
                    got(wb[g].at[zz, y, c, ff], r_wx.at[g, ff, zz, y])
                    w_push_y(g, zz, ff)
        else:
            for zz in range(Z):
                got(wb[g].at[zz, oy, c, f], r_wy.at[g, zz, f])
                w_push_x(g, zz, oy)
        w_to_core(g, 0)

    def w_l(g):
        if g in x_first:
            for zz in range(Z):
                for ff in range(FK):
                    got(wb[g].at[zz, oy, c, ff], r_wy.at[g, zz, ff])
            w_to_core(g, 1)
        else:
            for k in range(1, FK):
                ff = fplus(k)
                for zz in range(Z):
                    for yy in range(2):
                        got(wb[g].at[zz, yy, c, ff], r_wx.at[g, ff, zz, yy])
                w_to_core(g, k)

    def w_parts(g):
        return 2 if g in x_first else FK

    def w_c(g):
        for n in range(w_parts(g)):
            if g in x_first:
                got(wb[g].at[:, y if n == 0 else oy, oc], r_wc.at[g, n])
            else:
                got(wb[g].at[:, :, oc, fplus(n)], r_wc.at[g, n])

    tokb[z, c] = tok_ref[...]
    w0[z, y, c, f, :, 0 : 3 * D] = wq_ref[...]
    tile[...] = jnp.zeros((SLAB, 128), F32)
    for r, v in enumerate((v0, v1, v2, v3, v4, v5, v6, v7, v8)):
        tile[r : r + 1, 0 : v.shape[1]] = v[...].astype(F32)
    w0[z, y, c, f, :, 3 * D : 3 * D + 128] = tile[...].astype(BF16)
    w1[z, y, c, f, :, 0:D] = wo_ref[...]
    w1[z, y, c, f, :, D : D + FF] = wu_ref[...]
    w2[z, y, c, f] = wd_ref[...]

    w_out_z(0)
    w_own_y(0)
    w_own_x(0)
    tok_right(z)
    tok_left(z)
    w_out_z(1)
    w_own_y(1)
    w_own_x(1)
    w_own_x(2)
    push(tokb.at[z, c], tokp, s_tp, r_tp, d_y)
    tok_core(z)
    w_own_y(2)

    starts, ends, stops = [], [], []
    total = jnp.int32(0)
    for t in range(NT):
        starts.append(total)
        stops.append(total + sup_ref[0, t])
        total = total + len_ref[0, t]
        ends.append(total)

    lane = lax.broadcasted_iota(jnp.int32, (1, 128), 1)
    lane_start = jnp.zeros((1, 128), jnp.int32)
    lane_stop = jnp.zeros((1, 128), jnp.int32)
    for t in range(NT):
        lane_start = jnp.where(lane == t, starts[t], lane_start)
        lane_stop = jnp.where(lane == t, stops[t], lane_stop)
    lane_ones = jnp.where((lane >= NT) & (lane < NT + 3), 1.0, 0.0)

    def mask_of(n):
        pos = (n * 2 + y) * 2 * R + lax.broadcasted_iota(jnp.int32, (2 * R, 128), 0)
        seen = (pos >= lane_start) & (pos < lane_stop)
        extra = jnp.where(lane < NT, jnp.where(seen, 0.0, MASKED), lane_ones)
        return extra.astype(BF16)

    def mask_block(n, carry):
        eb[n] = mask_of(n)
        return carry

    lax.fori_loop(0, Z, mask_block, 0)

    row = lax.broadcasted_iota(jnp.int32, (HD, 2 * R), 0)
    col = lax.broadcasted_iota(jnp.int32, (HD, 2 * R), 1)
    qpos = jnp.where(col < R, i * R + col, ((z * 2 + oy) * 2 + c - 1) * R + col)
    onehot = jnp.zeros((HD, 2 * R), F32)
    for t in range(NT):
        onehot = jnp.where((row == t) & (qpos >= starts[t]) & (qpos < ends[t]), 1.0, onehot)
    for h in range(H):
        qt[h, HD : 2 * HD, :] = onehot.astype(BF16)
        dot_[h, HD + SLAB : 2 * HD, :] = jnp.zeros((HD - SLAB, 2 * R), BF16)
        ot[h] = jnp.zeros((2 * HD, 2 * R), F32)
        mrun[h] = jnp.full((1, 2 * R), MASKED, F32)

    w_z(0)
    w_m(0)
    tok_z(1)
    w_out_z(2)
    w_l(0)
    w_z(1)
    w_c(0)

    piece = D // NSH
    small = w0[:, :, :, :, :, 3 * D : 3 * D + 128].reshape(NSH * SLAB, 128)
    spread = (
        lax.rem(lax.broadcasted_iota(jnp.int32, (128, D), 1), piece)
        == lax.broadcasted_iota(jnp.int32, (128, D), 0)
    )
    wide = dot_nn(small, spread.astype(BF16))
    mine = (
        lax.broadcasted_iota(jnp.int32, (NSH * SLAB, D), 1) // piece
        == lax.broadcasted_iota(jnp.int32, (NSH * SLAB, D), 0) // SLAB
    )
    wide = jnp.where(mine, wide, 0.0)
    par[...] = jnp.sum(wide.reshape(NSH, SLAB, D), axis=0)
    pick = (
        lax.broadcasted_iota(jnp.int32, (NSH, NSH * SLAB), 1)
        == lax.broadcasted_iota(jnp.int32, (NSH, NSH * SLAB), 0) * SLAB + 8
    )
    ups = dot_nn(pick.astype(BF16), small).astype(BF16)
    spread = (
        lax.rem(lax.broadcasted_iota(jnp.int32, (128, FF), 1), 4 * piece)
        == lax.broadcasted_iota(jnp.int32, (128, FF), 0)
    )
    wide = dot_nn(ups, spread.astype(BF16))
    mine = (
        lax.broadcasted_iota(jnp.int32, (NSH, FF), 1) // (4 * piece)
        == lax.broadcasted_iota(jnp.int32, (NSH, FF), 0)
    )
    upb[...] = col_sum(jnp.where(mine, wide, 0.0))
    ln1g, ln1b = par[0:1, :], par[1:2, :]

    got(tokp, r_tp)
    tokens = tok_ref[...].astype(F32)
    mean, centered, rstd = moments(tokens)
    xq[0:R, :] = (centered * rstd * ln1g + ln1b).astype(BF16)
    mean, centered, rstd = moments(tokp[...].astype(F32))
    xq[R : 2 * R, :] = (centered * rstd * ln1g + ln1b).astype(BF16)
    wq = w0[:, :, :, :, :, 0:D].reshape(D, D)
    qscale = HD ** (-0.5) / LN2
    qs[...] = ((dot_nn(xq[...], wq) + par[2:3, :]) * qscale).astype(BF16)
    for h in range(H):
        qt[h, 0:HD, :] = qs[:, h * HD : (h + 1) * HD].T

    def near(s):
        inner = jnp.minimum(z, Z - 1 - z)
        odd = lax.rem(s, 2)
        paired = z + (1 - 2 * odd) * ((s + 1) // 2)
        rest = jnp.where(z < Z - 1 - z, s, Z - 1 - s)
        return jnp.where(s <= 2 * inner, paired, rest)

    if Z == 4:
        arrivals = {
            1: [(tok_z, 2)],
            2: [(w_m, 1), (w_z, 2)],
            3: [(tok_z, 3)],
            4: [(w_m, 2)],
            6: [(w_l, 1)],
        }
    else:
        arrivals = {n: [(tok_z, n + 1)] for n in range(1, Z - 1)}
        arrivals[Z] = [(w_m, 1), (w_z, 2), (w_l, 1), (w_m, 2)]

    def run(table, n):
        for at in sorted(table):
            @pl.when(n == at)
            def _():
                for step, which in table[at]:
                    step(which)

    def attend(h, keys, values, extra, span):
        cols = slice(h * HD, (h + 1) * HD)
        s = dot_nn(jnp.concatenate([keys[:, cols], extra], axis=1), qt[h, :, span])
        top0 = mrun[h, :, span]
        top = jnp.maximum(top0, jnp.ceil(jnp.max(s, axis=0, keepdims=True)))
        e = jnp.exp2(s - top).astype(BF16)
        grown = dot_tn(jnp.concatenate([values[:, cols], extra], axis=1), e)
        ot[h, :, span] = ot[h, :, span] * jnp.exp2(top0 - top) + grown
        mrun[h, :, span] = top

    def ahead(n, carry):
        zz = near(n)
        run(arrivals, n)
        got(tokb.at[zz, oc], r_t.at[zz, oc])
        mean, centered, rstd = moments(tokb[zz].reshape(2 * R, D).astype(F32))
        stat[zz] = jnp.where(lax.broadcasted_iota(jnp.int32, (2 * R, 128), 1) == 0, mean, rstd)
        x = (centered * rstd * par[0:1, :] + par[1:2, :]).astype(BF16)
        kv = dot_nn(x, w0[:, :, :, :, :, D : 3 * D].reshape(D, 2 * D))
        keys = kv[:, 0:D].astype(BF16)
        values = (kv[:, D : 2 * D] + par[3:4, :]).astype(BF16)
        kb[zz] = keys
        vb[zz] = values
        extra = eb[zz]
        for h in range(H):
            attend(h, keys, values, extra, slice(R, 2 * R))
        return carry

    lax.fori_loop(0, Z, ahead, 0)

    for h in range(H):
        t = ot[h, 0:HD, R : 2 * R]
        first_part = t.astype(BF16)
        oh[h] = first_part
        ol[h] = (t - first_part.astype(F32)).astype(BF16)
        ml[h : h + 1, :] = mrun[h, :, R : 2 * R]
        ml[H + h : H + h + 1, :] = ot[h, HD + NT : HD + NT + 1, R : 2 * R]
    push(oh, ohr, s_y.at[0], r_y.at[0], d_y)
    push(ml, mlr, s_y.at[1], r_y.at[1], d_y)

    def ahead_own(n, carry):
        zz = near(n)
        run(arrivals, Z + n)
        for h in range(H):
            attend(h, kb[zz], vb[zz], eb[zz], slice(0, R))
        return carry

    lax.fori_loop(0, Z, ahead_own, 0)
    w_l(2)
    w_c(1)
    push(ol, olr, s_y.at[2], r_y.at[2], d_y)

    got(ohr, r_y.at[0])
    got(mlr, r_y.at[1])
    parts = []
    row_tail = lax.broadcasted_iota(jnp.int32, (SLAB, R), 0)
    for h in range(H):
        m_own, m_far = mrun[h, :, 0:R], mlr[h : h + 1, :]
        top = jnp.maximum(m_own, m_far)
        a_own, a_far = jnp.exp2(m_own - top), jnp.exp2(m_far - top)
        total = a_own * ot[h, HD + NT : HD + NT + 1, 0:R] + a_far * mlr[H + h : H + h + 1, :]
        inverse = 1.0 / total
        attended = ot[h, 0:HD, 0:R] * (a_own * inverse) + ohr[h].astype(F32) * (a_far * inverse)
        ot[h, 0:HD, 0:R] = attended
        ot[h, HD : HD + 1, 0:R] = inverse
        ot[h, HD + 1 : HD + 2, 0:R] = a_far * inverse
        parts.append(attended.T.astype(BF16))
        m1, m2, m3 = three_terms(top)
        tail = jnp.where(
            row_tail == NT, -m1,
            jnp.where(row_tail == NT + 1, -m2, jnp.where(row_tail == NT + 2, -m3, onehot[0:SLAB, 0:R])),
        )
        qt[h, HD : HD + SLAB, 0:R] = tail.astype(BF16)
    push(qt.at[:, HD : HD + SLAB, 0:R], qt.at[:, HD : HD + SLAB, R : 2 * R], s_y.at[3], r_y.at[3], d_y)
    attn_low = jnp.concatenate(parts, axis=1)
    w_out = w1[:, :, :, :, :, 0:D].reshape(D, D)
    hidden = tokens + (dot_nn(attn_low, w_out) + par[4:5, :])
    hid[...] = hidden
    mean2, centered, rstd2 = moments(hidden)
    n2 = centered * rstd2
    nrm2[...] = (n2 * par[5:6, :] + par[6:7, :]).astype(BF16)
    acc[...] = hidden + par[7:8, :]
    gsec[...] = jnp.zeros((R, D), F32)
    w_c(2)

    HF = FF // 2
    store = (gs, gs, gs, gs, gu, gu, gd, gd)
    from_core = (cs, cs, cs, cs, cu, cu, cd, cd)
    from_x = (xs, xs, xs, xs, xu, xu, xd, xd)
    from_y = (ys, ys, ys, ys, yu, yu, yd, yd)
    from_z = (zs, zs, zs, zs, zu, zu, zd, zd)
    lead = (0, 1, 2, 3, 0, 1, 0, 1)
    Q, K, V, O, UA, UB, DA, DB = range(8)
    y_first = {V, DB}
    straight = {Q, K, V}

    def r_c(g):
        n = lead[g]
        push(store[g].at[n, :, :, oc], from_core[g].at[n], s_gc.at[g], r_gc.at[g], d_core)

    def r_push_x(g, whole):
        n = lead[g]
        for k in range(1, FK):
            ff = fplus(k)
            if whole:
                push(store[g].at[n, :, :, c, ff], from_x[g].at[n, f], s_gx.at[g, ff], r_gx.at[g, f], d_f(ff))
            else:
                push(store[g].at[n, :, y, c, ff], from_x[g].at[n, f, :, 0], s_gx.at[g, ff], r_gx.at[g, f], d_f(ff))

    def r_push_y(g, whole):
        n = lead[g]
        if whole:
            push(store[g].at[n, :, oy, c], from_y[g].at[n], s_gy.at[g], r_gy.at[g], d_y)
        else:
            push(store[g].at[n, :, oy, c, f], from_y[g].at[n, :, 0], s_gy.at[g], r_gy.at[g], d_y)

    def over_z(one):
        def step(zz, carry):
            one(zz)
            return carry

        lax.fori_loop(0, Z, step, 0)

    def r_1(g):
        n = lead[g]
        got(from_core[g].at[n], r_gc.at[g])

        def one(zz):
            t = store[g][n, zz, :, c].astype(F32) + from_core[g][n, zz].astype(F32)
            store[g][n, zz, :, c] = t.astype(BF16)

        over_z(one)
        if g in y_first:
            r_push_y(g, True)
        else:
            r_push_x(g, True)

    def r_2(g):
        n = lead[g]
        if g in y_first:
            got(from_y[g].at[n], r_gy.at[g])

            def one(zz):
                t = store[g][n, zz, y, c].astype(F32) + from_y[g][n, zz].astype(F32)
                store[g][n, zz, y, c] = t.astype(BF16)

            over_z(one)
            r_push_x(g, False)
        else:
            for k in range(1, FK):
                got(from_x[g].at[n, fplus(k)], r_gx.at[g, fplus(k)])

            def one(zz):
                t = store[g][n, zz, :, c, f].astype(F32)
                for k in range(1, FK):
                    t = t + from_x[g][n, fplus(k), zz].astype(F32)
                store[g][n, zz, :, c, f] = t.astype(BF16)

            if FK > 1:
                over_z(one)
            r_push_y(g, False)

    def r_z(g):
        n = lead[g]
        if g in y_first:
            for k in range(1, FK):
                got(from_x[g].at[n, fplus(k), :, 0], r_gx.at[g, fplus(k)])

            def one(zz):
                t = store[g][n, zz, y, c, f].astype(F32)
                for k in range(1, FK):
                    t = t + from_x[g][n, fplus(k), zz, 0].astype(F32)
                store[g][n, zz, y, c, f] = t.astype(BF16)

            if FK > 1:
                over_z(one)
        else:
            got(from_y[g].at[n, :, 0], r_gy.at[g])

            def one(zz):
                t = store[g][n, zz, y, c, f].astype(F32) + from_y[g][n, zz, 0].astype(F32)
                store[g][n, zz, y, c, f] = t.astype(BF16)

            over_z(one)
        if g in straight:
            for k in range(1, Z):
                zz = zplus(k)
                push(store[g].at[n, zz, y, c, f], from_z[g].at[n, z], s_gz.at[g, zz], r_gz.at[g, z], d_z(zz))
        else:
            r_fold(g, 1)

    def r_fold(g, bit):
        n = lead[g]
        for m in range(bit, Z, 2 * bit):
            push(
                store[g].at[n, zxor(m), y, c, f], from_z[g].at[n, zxor(bit ^ (m - 1))],
                s_gz.at[g, zxor(m)], r_gz.at[g, zxor(bit ^ (m - 1))], d_z(zxor(bit)),
            )

    def r_zz(g):
        n = lead[g]
        bit = 1
        while 2 * bit < Z:
            for m in range(0, Z, 2 * bit):
                zz, at = zxor(m), zxor(m + bit - 1)
                got(from_z[g].at[n, at], r_gz.at[g, at])
                t = store[g][n, zz, y, c, f].astype(F32) + from_z[g][n, at].astype(F32)
                store[g][n, zz, y, c, f] = t.astype(BF16)
            bit *= 2
            r_fold(g, bit)

    def r_end(g):
        n = lead[g]
        t = store[g][n, z, y, c, f].astype(F32)
        if g in straight:
            for k in range(1, Z):
                zz = zplus(k)
                got(from_z[g].at[n, zz], r_gz.at[g, zz])
                t = t + from_z[g][n, zz].astype(F32)
        else:
            at = zxor(Z // 2 - 1)
            got(from_z[g].at[n, at], r_gz.at[g, at])
            t = t + from_z[g][n, at].astype(F32)
        if g <= V:
            gqkv_ref[:, g * D : (g + 1) * D] = t
        elif g == O:
            gout_ref[...] = t
        elif g <= UB:
            gup_ref[:, (g - UA) * HF : (g - UA + 1) * HF] = t
        else:
            gdown_ref[(g - DA) * 2 * SLAB : (g - DA + 1) * 2 * SLAB, :] = t

    def r_sent(g):
        n = lead[g]
        sent(store[g].at[n, :, :, oc], s_gc.at[g])
        for k in range(1, FK):
            ff = fplus(k)
            if g in y_first:
                sent(store[g].at[n, :, y, c, ff], s_gx.at[g, ff])
            else:
                sent(store[g].at[n, :, :, c, ff], s_gx.at[g, ff])
        if g in y_first:
            sent(store[g].at[n, :, oy, c], s_gy.at[g])
        else:
            sent(store[g].at[n, :, oy, c, f], s_gy.at[g])
        for k in range(1, Z):
            sent(store[g].at[n, zplus(k), y, c, f], s_gz.at[g, zplus(k)])

    def half(hh):
        def chunk(j, carry):
            cols = pl.ds(pl.multiple_of(D + j * CH, 128), CH)
            bcols = pl.ds(pl.multiple_of(j * CH, 128), CH)
            hcols = pl.ds(pl.multiple_of((j - hh * (Z // 2)) * CH, 128), CH)
            up = w1[:, :, :, :, :, cols].reshape(D, CH)
            down = w2[j].reshape(CH, D)
            normed = nrm2[...]
            cot = cot_ref[...]
            pre = dot_nn(normed, up) + upb[:, bcols]
            phi = 0.5 * (1.0 + lax.erf(pre * (0.5**0.5)))
            act = (pre * phi).astype(BF16)
            slope = phi + pre * (jnp.exp2(pre * pre * (-0.5 / LN2)) * ((2.0 * math.pi) ** -0.5))
            acc[...] += dot_nn(act, down)
            gpre32 = dot_nt(cot, down) * slope
            gpre = gpre32.astype(BF16)
            gsec[...] += dot_nt(gpre, up)
            upg[:, bcols] = col_sum(gpre.astype(F32))
            gu[hh, :, :, :, :, :, hcols] = dot_tn(normed, gpre).astype(BF16).reshape(Z, 2, 2, FK, SLAB, CH)
            g_down = dot_tn(act, cot).astype(BF16).reshape(2, 2, FK, 4 * SLAB, D)
            gd[0, j] = g_down[:, :, :, 0 : 2 * SLAB]
            gd[1, j] = g_down[:, :, :, 2 * SLAB : 4 * SLAB]
            return carry

        lax.fori_loop(hh * (Z // 2), (hh + 1) * (Z // 2), chunk, 0)

    half(0)
    r_c(UA)
    half(1)
    r_1(UA)
    out_ref[...] = acc[...].astype(BF16)

    g_second = gsec[...]
    n2 = (hid[...] - mean2) * rstd2
    ln2g = par[5:6, :]
    cot32 = cot_ref[...].astype(F32)
    grad_hidden = cot32 + norm_back(g_second * ln2g, n2, rstd2)
    hid[...] = grad_hidden
    g_branch = grad_hidden.astype(BF16)
    gs[O] = dot_tn(attn_low, g_branch).astype(BF16).reshape(Z, 2, 2, FK, SLAB, D)
    r_c(UB)
    r_c(DA)
    r_c(DB)
    r_c(O)
    zero = jnp.zeros((1, D), F32)
    for r in range(SLAB):
        sg[0, r : r + 1, :] = zero
    sg[0, 4:5, :] = col_sum(g_branch.astype(F32))
    sg[0, 5:6, :] = col_sum(g_second * n2)
    sg[0, 6:7, :] = col_sum(g_second)
    sg[0, 7:8, :] = col_sum(cot32)
    for r in range(FF // D):
        sg[0, 8 + r : 9 + r, :] = upg[:, r * D : (r + 1) * D]

    got(olr, r_y.at[2])
    for h in range(H):
        rows = slice(h * HD, (h + 1) * HD)
        w_head = w1[:, :, :, :, :, 0:D].reshape(D, D)[rows, :]
        ga = dot_nt(w_head, g_branch).astype(BF16).astype(F32)
        low = (ga * ot[h, HD : HD + 1, 0:R]).astype(BF16)
        exact = ot[h, 0:HD, 0:R] + olr[h].astype(F32) * ot[h, HD + 1 : HD + 2, 0:R]
        delta = col_sum(low.astype(F32) * exact)
        d1, d2, d3 = three_terms(delta)
        tail = jnp.where(
            row_tail == NT, -d1, jnp.where(row_tail == NT + 1, -d2, jnp.where(row_tail == NT + 2, -d3, 0.0))
        )
        dot_[h, 0:HD, 0:R] = low
        dot_[h, HD : HD + SLAB, 0:R] = tail.astype(BF16)
        dos[0:R, rows] = low.T
    push(dot_.at[:, 0 : HD + SLAB, 0:R], dot_.at[:, 0 : HD + SLAB, R : 2 * R], s_y.at[4], r_y.at[4], d_y)
    dqt[...] = jnp.zeros((H, HD, 2 * R), F32)
    dwkv[...] = jnp.zeros((D, 2 * D), F32)
    lacc[...] = jnp.zeros((3, 8, D), F32)

    def tok_sent():
        @pl.when(z < Z - 1)
        def _():
            for k in range(Z):
                @pl.when(z - k >= 0)
                def _():
                    sent(tokb.at[z - k, c], s_tz.at[0, z - k])

        @pl.when(z > 0)
        def _():
            for k in range(Z):
                @pl.when(z + k < Z)
                def _():
                    sent(tokb.at[z + k, c], s_tz.at[1, z + k])

        for zz in range(Z):
            sent(tokb.at[zz, c], s_tc.at[zz])
        sent(tokb.at[z, c], s_tp)

    tok_sent()
    r_1(UB)
    r_1(DA)
    r_1(DB)

    got(qt.at[:, HD : HD + SLAB, R : 2 * R], r_y.at[3])
    got(dot_.at[:, 0 : HD + SLAB, R : 2 * R], r_y.at[4])
    for h in range(H):
        dos[R : 2 * R, h * HD : (h + 1) * HD] = dot_[h, 0:HD, R : 2 * R].T

    turns = sorted(range(1, Z), key=lambda m: (m & -m, m)) + [0]

    def plane(n):
        m = jnp.int32(0)
        for k in range(Z - 1):
            m = jnp.where(n == k, turns[k], m)
        return zxor(m)

    def p_sum(m):
        zz = zxor(m)
        got(crf.at[zz], r_pc.at[zz])
        t = tokb[zz, c].astype(F32) + crf[zz].astype(F32)
        bit = 1
        while bit < Z and m % (2 * bit) == 0:
            at = zxor(m + bit - 1)
            got(zrf.at[at], r_pz.at[at])
            t = t + zrf[at].astype(F32)
            bit *= 2
        return t

    def p_z(s):
        m = turns[s]
        bit = m & -m
        zz, at = zxor(m), zxor(bit ^ (m - 1))
        tokb[zz, c] = p_sum(m).astype(BF16)
        push(tokb.at[zz, c], zrf.at[at], s_pz.at[zz], r_pz.at[at], d_z(zxor(bit)))

    if Z == 4:
        before = {
            1: [(r_1, O), (r_2, UA)],
            2: [(r_2, DB), (r_2, UB)],
            3: [(r_2, DA), (r_z, UA)],
        }
        between = {
            1: [(p_z, 0)],
            2: [(p_z, 1)],
            3: [(p_z, 2), (r_z, UB)],
        }
        late = [
            (r_c, K), (r_c, V), "queries", (r_c, Q), (r_z, DB), "sums", (r_1, V), (r_1, K), "gq", (r_z, DA), (r_2, O),
            "core", (r_1, Q), (r_zz, UA), "x", (r_2, K), (r_2, V), (r_z, O), (r_zz, UB), (r_2, Q), "y", (r_zz, DB),
            (r_z, K), (r_z, V), (r_zz, DA), (r_z, Q), (r_zz, O), "first",
            (r_end, UA), (r_end, UB), (r_end, DA), (r_end, DB), (r_end, O), (r_end, K), (r_end, V), (r_end, Q), "z",
        ]
    else:
        before = {1: [(r_1, O)]}
        between = {s + 1: [(p_z, s)] for s in range(Z - 1)}
        before[Z - 1] = [(r_2, UA), (r_2, UB), (r_2, DA), (r_2, DB), (r_2, O)]
        late = [(r_z, g) for g in (O, UA, UB, DA, DB)]
        late += ["queries", "sums", "gq", (r_c, Q), (r_c, K), (r_c, V), "core"]
        late += [(r_1, Q), (r_1, K), (r_1, V), "x", (r_2, Q), (r_2, K), (r_2, V), "y", (r_z, Q), (r_z, K), (r_z, V)]
        late += [(r_zz, g) for g in (O, UA, UB, DA, DB)] + ["first", "z"] + [(r_end, g) for g in range(8)]

    def behind(n, carry):
        zz = plane(n)
        run(before, n)
        keys, values, extra = kb[zz], vb[zz], eb[zz]
        dks, dvs = [], []
        for h in range(H):
            cols = slice(h * HD, (h + 1) * HD)
            s = dot_nn(jnp.concatenate([keys[:, cols], extra], axis=1), qt[h])
            dp = dot_nn(jnp.concatenate([values[:, cols], extra], axis=1), dot_[h])
            e = jnp.exp2(s).astype(BF16)
            ds = (e.astype(F32) * dp).astype(BF16)
            dvs.append(dot_nn(e, dos[:, cols]))
            dks.append(dot_nn(ds, qs[:, cols]) * LN2)
            dqt[h] += dot_tn(keys[:, cols], ds)
        dv = jnp.concatenate(dvs, axis=1)
        dkv = jnp.concatenate(dks + [dv], axis=1).astype(BF16)
        run(between, n)
        gp = dot_nt(dkv, w0[:, :, :, :, :, D : 3 * D].reshape(D, 2 * D))
        norm = (tokb[zz].reshape(2 * R, D).astype(F32) - stat[zz, :, 0:1]) * stat[zz, :, 1:2]
        tokb[zz] = gp.astype(BF16).reshape(2, R, D)
        push(tokb.at[zz, oc], crf.at[zz], s_pc.at[zz], r_pc.at[zz], d_core)
        x = (norm * par[0:1, :] + par[1:2, :]).astype(BF16)
        lacc[0] += fold_rows(gp * norm)
        lacc[1] += fold_rows(gp)
        lacc[2] += fold_rows(dv)
        dwkv[...] += dot_tn(x, dkv)
        return carry

    lax.fori_loop(0, Z, behind, 0)

    gs[K] = dwkv[:, 0:D].astype(BF16).reshape(Z, 2, 2, FK, SLAB, D)
    gs[V] = dwkv[:, D : 2 * D].astype(BF16).reshape(Z, 2, 2, FK, SLAB, D)

    def queries():
        dq = jnp.concatenate([(dqt[h] * (HD**-0.5)).T for h in range(H)], axis=1).astype(BF16)
        gs[Q] = dot_tn(xq[...], dq).astype(BF16).reshape(Z, 2, 2, FK, SLAB, D)
        gq = dot_nt(dq, w0[:, :, :, :, :, 0:D].reshape(D, D))
        acc[...] = gq[0:R]
        gqs[...] = gq[R : 2 * R].astype(BF16)
        both = jnp.concatenate([tok_ref[...], tokp[...]], axis=0).astype(F32)
        mean, centered, rstd = moments(both)
        sg[0, 0:1, :] = col_sum(lacc[0]) + col_sum(gq * (centered * rstd))
        sg[0, 1:2, :] = col_sum(lacc[1]) + col_sum(gq)
        sg[0, 2:3, :] = col_sum(dq.astype(F32))
        sg[0, 3:4, :] = col_sum(lacc[2])

    def queries_back():
        push(gqs, gqr, s_y.at[5], r_y.at[5], d_y)

    def sums():
        push(sg.at[0], src, s_sc, r_sc, d_core)

    def sums_core():
        got(src, r_sc)
        sg[1] = sg[0] + src[...]
        for k in range(1, FK):
            ff = fplus(k)
            push(sg.at[1], srx.at[f], s_sx.at[ff], r_sx.at[f], d_f(ff))

    def sums_x():
        t = sg[1]
        for k in range(1, FK):
            got(srx.at[fplus(k)], r_sx.at[fplus(k)])
            t = t + srx[fplus(k)]
        sg[2] = t
        push(sg.at[2], sry, s_sy, r_sy, d_y)

    def sums_y():
        got(sry, r_sy)
        sg[3] = sg[2] + sry[...]
        for k in range(1, Z):
            zz = zplus(k)
            push(sg.at[3], srz.at[z], s_sz.at[zz], r_sz.at[z], d_z(zz))

    def sums_z():
        t = sg[3]
        for k in range(1, Z):
            zz = zplus(k)
            got(srz.at[zz], r_sz.at[zz])
            t = t + srz[zz]
        gsm_ref[...] = t

    def first():
        got(gqr, r_y.at[5])
        t = p_sum(0) + acc[...] + gqr[...].astype(F32)
        mean, centered, rstd = moments(tok_ref[...].astype(F32))
        gtok_ref[...] = (hid[...] + norm_back(t * par[0:1, :], centered * rstd, rstd)).astype(BF16)

    named = {
        "queries": queries, "gq": queries_back, "sums": sums, "core": sums_core, "x": sums_x, "y": sums_y, "z": sums_z, "first": first,
    }
    for step in late:
        if isinstance(step, str):
            named[step]()
        else:
            step[0](step[1])

    for g in range(3):
        for k in range(1, Z):
            sent(wb[g].at[z, y, c, f], s_wz.at[g, zplus(k)])
        for zz in range(Z):
            sent(wb[g].at[zz, y, c, f], s_wy.at[g, zz, f])
            for k in range(1, FK):
                ff = fplus(k)
                sent(wb[g].at[zz, y, c, f], s_wx.at[g, ff, zz, y])
                if g in x_first:
                    sent(wb[g].at[zz, y, c, ff], s_wy.at[g, zz, ff])
                else:
                    sent(wb[g].at[zz, oy, c, f], s_wx.at[g, ff, zz, oy])
        for n in range(w_parts(g)):
            if g in x_first:
                sent(wb[g].at[:, y if n == 0 else oy, c], s_wc.at[g, n])
            else:
                sent(wb[g].at[:, :, c, fplus(n)], s_wc.at[g, n])
    for g in range(8):
        r_sent(g)
    for zz in range(Z):
        sent(tokb.at[zz, oc], s_pc.at[zz])
    for k in range(1, Z):
        sent(tokb.at[zplus(k), c], s_pz.at[zplus(k)])
        sent(sg.at[3], s_sz.at[zplus(k)])
    sent(oh, s_y.at[0])
    sent(ml, s_y.at[1])
    sent(ol, s_y.at[2])
    sent(qt.at[:, HD : HD + SLAB, 0:R], s_y.at[3])
    sent(dot_.at[:, 0 : HD + SLAB, 0:R], s_y.at[4])
    sent(gqs, s_y.at[5])
    sent(sg.at[0], s_sc)
    for k in range(1, FK):
        sent(sg.at[1], s_sx.at[fplus(k)])
    sent(sg.at[2], s_sy)


def layer(Z, FK, R, D, FF, NT, operands):
    vm = lambda shape, dtype: pltpu.VMEM(shape, dtype)
    dma = lambda *shape: pltpu.SemaphoreType.DMA(shape)
    lead = (Z, 2, 2, FK)
    slabs = ((SLAB, 3 * D + 128), (SLAB, D + FF), (4 * SLAB, D))
    gslabs = ((4, SLAB, D), (2, SLAB, FF // 2), (2, 2 * SLAB, D))
    scratch = [
        vm((Z, 2, R, D), BF16),
        vm((R, D), BF16),
        vm((Z, 2 * R, D), BF16),
        vm((Z, 2 * R, D), BF16),
        vm((Z, 2 * R, 128), BF16),
        vm((Z, 2 * R, 128), F32),
        *[vm(lead + s, BF16) for s in slabs],
        *[vm((s[0],) + lead + s[1:], BF16) for s in gslabs],
        *[vm((s[0], Z, 2, FK) + s[1:], BF16) for s in gslabs],
        *[vm((s[0], FK, Z, 2) + s[1:] if FK > 1 else (SLAB, 128), BF16) for s in gslabs],
        *[vm((s[0], Z, FK) + s[1:], BF16) for s in gslabs],
        *[vm((s[0], Z) + s[1:], BF16) for s in gslabs],
        vm((Z, R, D), BF16),
        vm((Z, R, D), BF16),
        vm((SLAB, D), F32),
        vm((1, FF), F32),
        vm((H, 2 * HD, 2 * R), BF16),
        vm((H, 2 * HD, 2 * R), BF16),
        vm((2 * R, D), BF16),
        vm((2 * R, D), BF16),
        vm((H, 2 * HD, 2 * R), F32),
        vm((H, 1, 2 * R), F32),
        vm((H, HD, 2 * R), F32),
        vm((H, HD, R), BF16),
        vm((H, HD, R), BF16),
        vm((2 * H, R), F32),
        vm((H, HD, R), BF16),
        vm((H, HD, R), BF16),
        vm((2 * H, R), F32),
        vm((R, D), BF16),
        vm((R, D), BF16),
        vm((R, D), BF16),
        vm((R, D), F32),
        vm((R, D), F32),
        vm((R, D), F32),
        vm((D, 2 * D), F32),
        vm((3, 8, D), F32),
        vm((1, FF), F32),
        vm((2 * R, D), BF16),
        vm((4, SLAB, D), F32),
        vm((SLAB, D), F32),
        vm((FK, SLAB, D), F32),
        vm((SLAB, D), F32),
        vm((Z, SLAB, D), F32),
        vm((SLAB, 128), F32),
        dma(2, Z), dma(Z), dma(Z, 2), pltpu.SemaphoreType.DMA, pltpu.SemaphoreType.DMA,
        dma(3, Z), dma(3, Z), dma(3, Z, FK), dma(3, Z, FK),
        dma(3, FK, Z, 2), dma(3, FK, Z, 2), dma(3, 2), dma(3, 2),
        dma(8), dma(8), dma(8, FK), dma(8, FK), dma(8), dma(8), dma(8, Z), dma(8, Z),
        dma(Z), dma(Z), dma(Z), dma(Z), dma(6), dma(6),
        pltpu.SemaphoreType.DMA, pltpu.SemaphoreType.DMA,
        dma(FK), dma(FK),
        pltpu.SemaphoreType.DMA, pltpu.SemaphoreType.DMA,
        dma(Z), dma(Z),
    ]
    vmem = pl.BlockSpec(memory_space=pltpu.VMEM)
    smem = pl.BlockSpec(memory_space=pltpu.SMEM)
    shape = jax.ShapeDtypeStruct
    return pl.pallas_call(
        functools.partial(body, Z, FK, R, D, NT),
        out_shape=(
            shape((R, D), BF16),
            shape((R, D), BF16),
            shape((SLAB, 3 * D), F32),
            shape((SLAB, D), F32),
            shape((SLAB, FF), F32),
            shape((4 * SLAB, D), F32),
            shape((SLAB, D), F32),
        ),
        in_specs=[vmem] * 15 + [smem] * 2,
        out_specs=[vmem] * 7,
        scratch_shapes=scratch,
        compiler_params=pltpu.CompilerParams(
            collective_id=0, has_side_effects=True, vmem_limit_bytes=63 * 2**20
        ),
        name="layer",
    )(*operands)


def finish(NSH, FK, *refs):
    big_in, small_in, big_out, small_out = refs[0:6], refs[6], refs[7:13], refs[13:22]
    for a, b in zip(big_in, big_out):
        b[...] = a[...]
    at = lax.axis_index("blk") * FK
    if FK > 1:
        at = at + lax.axis_index("fsdp")
    D = small_in.shape[1]
    piece = D // NSH
    lane = lax.broadcasted_iota(jnp.int32, (128, D), 1)
    take = lax.broadcasted_iota(jnp.int32, (128, D), 0)
    full = small_in[...]
    for r in range(8):
        chosen = jnp.where(lane == at * piece + take, full[r : r + 1, :], 0.0)
        small_out[r][...] = jnp.sum(chosen, axis=1).reshape(1, 128)[:, 0:piece]
    FF = D * 4
    total = jnp.zeros((128,), F32)
    for r in range(4):
        chosen = jnp.where(lane + r * D == at * 4 * piece + take, full[8 + r : 9 + r, :], 0.0)
        total = total + jnp.sum(chosen, axis=1)
    small_out[8][...] = total.reshape(1, 128)[:, 0 : 4 * piece]


def hand_over(NSH, FK, FF, results):
    *big, small = results
    D = small.shape[1]
    vmem = pl.BlockSpec(memory_space=pltpu.VMEM)
    shape = jax.ShapeDtypeStruct
    return pl.pallas_call(
        functools.partial(finish, NSH, FK),
        out_shape=(
            *[shape(v.shape, v.dtype) for v in big],
            *[shape((1, D // NSH), F32) for _ in range(8)],
            shape((1, FF // NSH), F32),
        ),
        in_specs=[vmem] * 7,
        out_specs=[vmem] * 15,
        name="finish",
    )(*results)


def shards(
    blocks, fsdp,
    tokens, ln1_gain, ln1_bias, qkv_weight, query_bias, value_bias, out_weight, out_bias,
    ln2_gain, ln2_bias, up_weight, up_bias, down_weight, down_bias,
    table_lengths, support_lengths, cotangent,
):
    R, D = tokens.shape[1:]
    FF = up_weight.shape[1]
    NT = table_lengths.shape[1]
    smalls = (ln1_gain, ln1_bias, query_bias, value_bias, out_bias, ln2_gain, ln2_bias, down_bias, up_bias)
    weights = (qkv_weight, out_weight, up_weight, down_weight)
    inside = qkv_weight.shape[0] == SLAB
    FK = fsdp if inside else 1
    if not inside:
        whole = lambda v: lax.all_gather(v, "fsdp", axis=0, tiled=True)
        smalls = tuple(whole(v) for v in smalls)
        weights = tuple(whole(v) for v in weights)
    results = layer(
        blocks // 4, FK, R, D, FF, NT,
        (tokens[0], cotangent[0], *weights, *[v[None] for v in smalls], table_lengths, support_lengths),
    )
    block_out, grad_tokens, g_qkv, g_out, g_up, g_down, *small_grads = hand_over(
        blocks * FK, FK, FF, results
    )
    small_grads = [v[0] for v in small_grads]
    weight_grads = [g_qkv, g_out, g_up, g_down]
    if not inside:
        spread = lambda v: lax.psum_scatter(v, "fsdp", scatter_dimension=0, tiled=True)
        small_grads = [spread(v) for v in small_grads]
        weight_grads = [spread(v) for v in weight_grads]
    g_ln1g, g_ln1b, g_qb, g_vb, g_ob, g_ln2g, g_ln2b, g_db, g_ub = small_grads
    g_qkv, g_out, g_up, g_down = weight_grads
    return (
        block_out[None], grad_tokens[None], g_ln1g, g_ln1b, g_qkv, g_qb, g_vb, g_out, g_ob,
        g_ln2g, g_ln2b, g_up, g_ub, g_down, g_db,
    )


def solution(mesh):
    both = ("blk", "fsdp")
    vec, mat, rows = P(both), P(both, None), P("fsdp", "blk", None)
    return jax.shard_map(
        functools.partial(shards, mesh.shape["blk"], mesh.shape["fsdp"]),
        mesh=mesh,
        in_specs=(
            rows, vec, vec, mat, vec, vec, mat, vec, vec, vec, mat, vec, mat, vec,
            P("fsdp", None), P("fsdp", None), rows,
        ),
        out_specs=(rows, rows, vec, vec, mat, vec, vec, mat, vec, vec, vec, mat, vec, mat, vec),
        check_vma=False,
    )
```

```python
import functools
import math

import jax
import jax.numpy as jnp
from jax import lax
from jax.experimental import pallas as pl
from jax.experimental.pallas import tpu as pltpu
from jax.sharding import PartitionSpec as P

H = 4
HD = 128
SLAB = 16
EPSILON = 1e-05
MASKED = -1e30
LN2 = math.log(2.0)
MESH = pl.DeviceIdType.MESH
F32 = jnp.float32
BF16 = jnp.bfloat16


def dot_nn(a, b):
    return lax.dot_general(a, b, (((1,), (0,)), ((), ())), preferred_element_type=F32)


def dot_nt(a, b):
    return lax.dot_general(a, b, (((1,), (1,)), ((), ())), preferred_element_type=F32)


def dot_tn(a, b):
    return lax.dot_general(a, b, (((0,), (0,)), ((), ())), preferred_element_type=F32)


def moments(v):
    mean = jnp.mean(v, axis=-1, keepdims=True)
    centered = v - mean
    rstd = lax.rsqrt(jnp.mean(centered * centered, axis=-1, keepdims=True) + EPSILON)
    return mean, centered, rstd


def norm_back(g, n, r):
    return r * (g - jnp.mean(g, axis=-1, keepdims=True) - n * jnp.mean(g * n, axis=-1, keepdims=True))


def three_terms(v):
    first = v.astype(BF16)
    rest = v - first.astype(F32)
    second = rest.astype(BF16)
    third = (rest - second.astype(F32)).astype(BF16)
    return first.astype(F32), second.astype(F32), third.astype(F32)


def col_sum(v):
    return jnp.sum(v, axis=0, keepdims=True)


def fold_rows(v):
    return jnp.sum(v.reshape(v.shape[0] // 8, 8, v.shape[1]), axis=0)


FOUR = {
    "masks": [("w_out_z", 0), ("tr",), ("tl",), ("w_own_x", 2), ("tp",), ("w_own_x", 0), ("w_own_y", 2)],
    "small": [
        ("gtokp",), ("w_out_z", 1), ("w_own_y", 0), ("w_z", 0), ("w_out_z", 2), ("w_m", 0), ("w_own_x", 1), ("tc",),
        ("w_z", 1), ("w_l", 0), ("w_c", 0), ("tok_z", 1),
    ],
    ("A", 0): [("w_z", 2)],
    ("A", 2): [("w_m", 1), ("tok_z", 2)],
    ("A", 3): [("w_own_y", 1), ("w_m", 2), ("tok_z", 3)],
    ("B", 0): [("o_hi",)],
    ("B", 1): [("w_l", 1)],
    ("B", 3): [("w_l", 2), ("o_lo",)],
    "merge": [("g_o",)],
    "out": [("qtail",), ("w_c", 1)],
    "ffn": [("w_c", 2)],
    "dOc": [("g_ol",)],
    "dwu": [("dO",)],
    "dwo": [("r_c", "db")],
    "sent": [("r_c", "da")],
    ("e", 1): [("r_1", "db"), ("r_c", "ub"), ("r_1", "da")],
    "dosT": [("r_c", "ua"), ("g_dO",)],
    ("t", 0): [("r_2", "da")],
    ("t", 1): [("r_2", "db"), ("r_z", "db")],
    ("h", 2): [("r_1", "ua"), ("r_c", "o"), ("p_z", 1)],
    ("t", 2): [("r_1", "o"), ("r_2", "ua"), ("p_z", 0), ("r_1", "ub")],
    ("h", 3): [("r_z", "da")],
    "q": [("r_2", "ub"), ("r_2", "o"), ("r_c", "k"), ("r_z", "ua"), ("r_c", "v")],
    "end": [
        ("p_z", 2), ("s", 0), ("r_zz", "db"), ("r_c", "q"), ("r_1", "k"), ("s", 1), ("r_1", "v"), ("r_end", "db"),
        ("r_1", "q"), ("r_2", "v"), ("r_2", "q"), ("r_zz", "ua"), ("s", 2), ("r_zz", "da"), ("gq",), ("r_end", "ua"),
        ("r_z", "ub"), ("r_2", "k"), ("r_z", "k"), ("r_z", "v"), ("r_z", "o"), ("r_zz", "k"), ("r_z", "q"), ("s", 3),
        ("r_zz", "ub"), ("r_end", "da"), ("r_zz", "q"), ("r_zz", "o"), ("r_end", "k"), ("r_zz", "v"), ("first",),
        ("r_end", "q"), ("r_end", "v"), ("r_end", "ub"), ("s_end",), ("r_end", "o"),
    ],
}
X_FIRST = {0, 1}
Y_FIRST = {0, 3, 6, 7}
DIRECT = {0, 1, 2, 3, 4, 5, 6, 7}
STRAIGHT = {1, 2, 4, 7}


def order_of(Z):
    if Z == 4:
        return FOUR
    most = ("ua", "ub", "da", "db", "o")
    last = ("q", "k", "v")
    plan = {
        "masks": [("w_out_z", 0), ("w_own_y", 0), ("w_own_x", 0), ("tr",), ("tl",), ("tp",), ("tc",)],
        "small": [("w_z", 0), ("w_m", 0), ("w_l", 0), ("gtokp",), ("w_c", 0)],
        ("A", 0): [(step, g) for g in (1, 2) for step in ("w_out_z", "w_own_y", "w_own_x")],
        ("B", 0): [("o_hi",), ("w_z", 1), ("w_z", 2), ("w_m", 1), ("w_m", 2)],
        "merge": [("o_lo",), ("g_o",), ("w_l", 1), ("w_l", 2)],
        "out": [("qtail",), ("w_c", 1), ("w_c", 2)],
        "dOc": [("g_ol",)],
        "dwu": [("dO",)],
        "sent": [("r_c", g) for g in most],
        "dosT": [("r_1", g) for g in most] + [("g_dO",)],
        ("h", Z - 1): [("r_2", g) for g in most],
        "kv": [("p_z", Z - 2)] + [("r_z", g) for g in most],
        "end": [("gq",)] + [(step, g) for step in ("r_c", "r_1", "r_2", "r_z") for g in last],
    }
    for k in range(1, Z):
        plan.setdefault(("A", k), []).append(("tok_z", k))
    for k in range(Z - 2):
        plan[("t", k + 1)] = [("p_z", k)]
    plan["end"] += [("r_zz", g) for g in most + last] + [("s", k) for k in range(4)] + [("first",), ("s_end",)]
    plan["end"] += [("r_end", g) for g in most + last]
    return plan


def body(
    Z, FK, R, D, NT,
    tok_in, cot_in, wq_in, wo_in, wu_in, wd_in,
    v0, v1, v2, v3, v4, v5, v6, v7, v8, len_ref, sup_ref,
    out_ref, gtok_ref, gqkv_ref, gout_ref, gup_ref, gdown_ref, gsm_ref,
    tokb, tokp, kb, vb, eb, stat, w0, w1, w2, gs, gu, gd,
    cs, cu, cd, xs, xu, xd, ys, yu, yd, zs, zu, zd,
    crf, zrf, par, upb, qt, dot_, qs, dos, ot, mrun, dqt,
    oh, ol, ml, ohr, olr, mlr, gqs, gqr,
    nrm2, hid, acc, gsec, dwkv, lacc, upg, xq,
    sg, src, srx, sry, srz, tile, tok_ref, cot_ref, act_all, gpre_all, early,
    s_in,
    s_tz, s_tc, r_t, s_tp, r_tp,
    s_wz, r_wz, s_wy, r_wy, s_wx, r_wx, s_wc, r_wc,
    s_gc, r_gc, s_gx, r_gx, s_gy, r_gy, s_gd, r_gd, s_gz, r_gz,
    s_pc, r_pc, s_pz, r_pz, s_y, r_y,
    s_sc, r_sc, s_sx, r_sx, s_sy, r_sy, s_sz, r_sz,
):
    i = lax.axis_index("blk")
    f = lax.axis_index("fsdp")
    c = lax.rem(i, 2)
    y = lax.rem(i // 2, 2)
    z = i // 4
    oc = 1 - c
    oy = 1 - y
    CH = 4 * FK * SLAB * 4
    FF = Z * CH
    NSH = Z * 4 * FK

    def dev(zz, yy, cc, ff):
        return ((zz * 2 + yy) * 2 + cc, ff)

    d_core = dev(z, y, oc, f)
    d_y = dev(z, oy, c, f)

    def zplus(k):
        return lax.rem(z + k, Z)

    def zxor(m):
        out, bit = z, 1
        while bit < Z:
            out = out + bit * ((m // bit) % 2) * (1 - 2 * lax.rem(z // bit, 2))
            bit *= 2
        return out

    def fplus(k):
        return lax.rem(f + k, FK)

    def d_z(zz):
        return dev(zz, y, c, f)

    def d_f(ff):
        return (i, ff)

    def d_diag(ff):
        return dev(z, oy, c, ff)

    def cp(s, d, ss, rs, to):
        return pltpu.make_async_remote_copy(
            src_ref=s, dst_ref=d, send_sem=ss, recv_sem=rs, device_id=to, device_id_type=MESH
        )

    def push(s, d, ss, rs, to):
        cp(s, d, ss, rs, to).start()

    def got(d, rs):
        cp(d, d, rs, rs, d_core).wait_recv()

    def sent(s, ss):
        cp(s, s, ss, ss, d_core).wait_send()

    arriving = [
        pltpu.make_async_copy(a, b, s_in.at[n])
        for n, (a, b) in enumerate((
            (wq_in, w0.at[z, y, c, f, :, 0 : 3 * D]),
            (tok_in, tokb.at[z, c]),
            (wo_in, w1.at[z, y, c, f, :, 0:D]),
            (wu_in, w1.at[z, y, c, f, :, D : D + FF]),
            (wd_in, w2.at[z, y, c, f]),
            (tok_in, tok_ref),
            (cot_in, cot_ref),
        ))
    ]
    for t in arriving:
        t.start()
    bar = pltpu.get_barrier_semaphore()
    partners = [d_core, d_y] + [d_z(zplus(k)) for k in range(1, Z)]
    partners += [to(fplus(k)) for k in range(1, FK) for to in (d_f, d_diag)]
    for to in partners:
        pl.semaphore_signal(bar, inc=1, device_id=to, device_id_type=MESH)
    tile[...] = jnp.zeros((SLAB, 128), F32)
    for r, v in enumerate((v0, v1, v2, v3, v4, v5, v6, v7, v8)):
        tile[r : r + 1, 0 : v.shape[1]] = v[...].astype(F32)
    w0[z, y, c, f, :, 3 * D : 3 * D + 128] = tile[...].astype(BF16)
    pl.semaphore_wait(bar, len(partners))

    def tok_push(zz, ss_z, to):
        t = tokb.at[zz, c]
        push(t, t, ss_z, r_t.at[zz, c], to)

    def tok_core(zz):
        t = tokb.at[zz, c]
        push(t, t, s_tc.at[zz], r_t.at[zz, c], d_core)

    def tok_right(zz):
        @pl.when(z < Z - 1)
        def _():
            tok_push(zz, s_tz.at[0, zz], d_z(z + 1))

    def tok_left(zz):
        @pl.when(z > 0)
        def _():
            tok_push(zz, s_tz.at[1, zz], d_z(z - 1))

    def tok_z(k):
        @pl.when(z - k >= 0)
        def _():
            zz = z - k
            got(tokb.at[zz, c], r_t.at[zz, c])
            tok_right(zz)
            tok_core(zz)

        @pl.when(z + k < Z)
        def _():
            zz = z + k
            got(tokb.at[zz, c], r_t.at[zz, c])
            tok_left(zz)
            tok_core(zz)

    wb = (w0, w1, w2)

    x_first = X_FIRST

    def w_push_x(g, zz, yy):
        for k in range(1, FK):
            ff = fplus(k)
            t = wb[g].at[zz, yy, c, f]
            push(t, t, s_wx.at[g, ff, zz, yy], r_wx.at[g, f, zz, yy], d_f(ff))

    def w_push_y(g, zz, ff):
        t = wb[g].at[zz, y, c, ff]
        push(t, t, s_wy.at[g, zz, ff], r_wy.at[g, zz, ff], d_y)

    def w_out_z(g):
        t = wb[g].at[z, y, c, f]
        for k in range(1, Z):
            zz = zplus(k)
            push(t, t, s_wz.at[g, zz], r_wz.at[g, z], d_z(zz))

    def w_own_y(g):
        w_push_y(g, z, f)

    def w_own_x(g):
        w_push_x(g, z, y)

    def w_z(g):
        for k in range(1, Z):
            zz = zplus(k)
            got(wb[g].at[zz, y, c, f], r_wz.at[g, zz])
            w_push_x(g, zz, y)
            w_push_y(g, zz, f)

    def w_to_core(g, n):
        if g in x_first:
            t = wb[g].at[:, y if n == 0 else oy, c]
        else:
            t = wb[g].at[:, :, c, fplus(n)]
        push(t, t, s_wc.at[g, n], r_wc.at[g, n], d_core)

    def w_m(g):
        if g in x_first:
            for zz in range(Z):
                for k in range(1, FK):
                    ff = fplus(k)
                    got(wb[g].at[zz, y, c, ff], r_wx.at[g, ff, zz, y])
                    w_push_y(g, zz, ff)
        else:
            for zz in range(Z):
                got(wb[g].at[zz, oy, c, f], r_wy.at[g, zz, f])
                w_push_x(g, zz, oy)
        w_to_core(g, 0)

    def w_l(g):
        if g in x_first:
            for zz in range(Z):
                for ff in range(FK):
                    got(wb[g].at[zz, oy, c, ff], r_wy.at[g, zz, ff])
            w_to_core(g, 1)
        else:
            for k in range(1, FK):
                ff = fplus(k)
                for zz in range(Z):
                    for yy in range(2):
                        got(wb[g].at[zz, yy, c, ff], r_wx.at[g, ff, zz, yy])
                w_to_core(g, k)

    def w_parts(g):
        return 2 if g in x_first else FK

    def w_c(g):
        for n in range(w_parts(g)):
            if g in x_first:
                got(wb[g].at[:, y if n == 0 else oy, oc], r_wc.at[g, n])
            else:
                got(wb[g].at[:, :, oc, fplus(n)], r_wc.at[g, n])

    HF = FF // 2
    store = (gs, gs, gs, gs, gu, gu, gd, gd)
    from_core = (cs, cs, cs, cs, cu, cu, cd, cd)
    from_x = (xs, xs, xs, xs, xu, xu, xd, xd)
    from_y = (ys, ys, ys, ys, yu, yu, yd, yd)
    from_z = (zs, zs, zs, zs, zu, zu, zd, zd)
    lead = (0, 1, 2, 3, 0, 1, 0, 1)
    Q, K, V, O, UA, UB, DA, DB = range(8)
    y_first = {(Q, K, V, O, UA, UB, DA, DB)[t] for t in Y_FIRST}
    direct = {(Q, K, V, O, UA, UB, DA, DB)[t] for t in DIRECT}
    straight = {(Q, K, V, O, UA, UB, DA, DB)[t] for t in STRAIGHT}

    def r_c(g):
        n = lead[g]
        push(store[g].at[n, :, :, oc], from_core[g].at[n], s_gc.at[g], r_gc.at[g], d_core)

    def r_push_x(g, whole):
        n = lead[g]
        for k in range(1, FK):
            ff = fplus(k)
            if whole:
                push(store[g].at[n, :, :, c, ff], from_x[g].at[n, f], s_gx.at[g, ff], r_gx.at[g, f], d_f(ff))
            else:
                push(store[g].at[n, :, y, c, ff], from_x[g].at[n, f, :, 0], s_gx.at[g, ff], r_gx.at[g, f], d_f(ff))

    def r_push_y(g, whole):
        n = lead[g]
        if whole:
            push(store[g].at[n, :, oy, c], from_y[g].at[n], s_gy.at[g], r_gy.at[g], d_y)
        else:
            push(store[g].at[n, :, oy, c, f], from_y[g].at[n, :, 0], s_gy.at[g], r_gy.at[g], d_y)

    def over_z(one):
        def step(zz, carry):
            one(zz)
            return carry

        lax.fori_loop(0, Z, step, 0)

    def r_1(g):
        n = lead[g]
        got(from_core[g].at[n], r_gc.at[g])

        def one(zz):
            t = store[g][n, zz, :, c].astype(F32) + from_core[g][n, zz].astype(F32)
            store[g][n, zz, :, c] = t.astype(BF16)

        over_z(one)
        if g in direct:
            r_push_x(g, False)
            r_push_y(g, False)
            for k in range(1, FK):
                ff = fplus(k)
                t = store[g].at[n, :, oy, c, ff]
                push(t, from_x[g].at[n, f, :, 1], s_gd.at[g, ff], r_gd.at[g, f], d_diag(ff))
        elif g in y_first:
            r_push_y(g, True)
        else:
            r_push_x(g, True)

    def r_2(g):
        n = lead[g]
        if g in direct:
            return
        if g in y_first:
            got(from_y[g].at[n], r_gy.at[g])

            def one(zz):
                t = store[g][n, zz, y, c].astype(F32) + from_y[g][n, zz].astype(F32)
                store[g][n, zz, y, c] = t.astype(BF16)

            over_z(one)
            r_push_x(g, False)
        else:
            for k in range(1, FK):
                got(from_x[g].at[n, fplus(k)], r_gx.at[g, fplus(k)])

            def one(zz):
                t = store[g][n, zz, :, c, f].astype(F32)
                for k in range(1, FK):
                    t = t + from_x[g][n, fplus(k), zz].astype(F32)
                store[g][n, zz, :, c, f] = t.astype(BF16)

            if FK > 1:
                over_z(one)
            r_push_y(g, False)

    def r_z(g):
        n = lead[g]
        if g in direct:
            got(from_y[g].at[n, :, 0], r_gy.at[g])
            for k in range(1, FK):
                got(from_x[g].at[n, fplus(k), :, 0], r_gx.at[g, fplus(k)])
                got(from_x[g].at[n, fplus(k), :, 1], r_gd.at[g, fplus(k)])

            def one(zz):
                t = store[g][n, zz, y, c, f].astype(F32) + from_y[g][n, zz, 0].astype(F32)
                for k in range(1, FK):
                    t = t + from_x[g][n, fplus(k), zz, 0].astype(F32) + from_x[g][n, fplus(k), zz, 1].astype(F32)
                store[g][n, zz, y, c, f] = t.astype(BF16)

            over_z(one)
        elif g in y_first:
            for k in range(1, FK):
                got(from_x[g].at[n, fplus(k), :, 0], r_gx.at[g, fplus(k)])

            def one(zz):
                t = store[g][n, zz, y, c, f].astype(F32)
                for k in range(1, FK):
                    t = t + from_x[g][n, fplus(k), zz, 0].astype(F32)
                store[g][n, zz, y, c, f] = t.astype(BF16)

            if FK > 1:
                over_z(one)
        else:
            got(from_y[g].at[n, :, 0], r_gy.at[g])

            def one(zz):
                t = store[g][n, zz, y, c, f].astype(F32) + from_y[g][n, zz, 0].astype(F32)
                store[g][n, zz, y, c, f] = t.astype(BF16)

            over_z(one)
        if g in straight:
            for k in range(1, Z):
                zz = zplus(k)
                push(store[g].at[n, zz, y, c, f], from_z[g].at[n, z], s_gz.at[g, zz], r_gz.at[g, z], d_z(zz))
        else:
            r_fold(g, 1)

    def r_fold(g, bit):
        n = lead[g]
        for m in range(bit, Z, 2 * bit):
            push(
                store[g].at[n, zxor(m), y, c, f], from_z[g].at[n, zxor(bit ^ (m - 1))],
                s_gz.at[g, zxor(m)], r_gz.at[g, zxor(bit ^ (m - 1))], d_z(zxor(bit)),
            )

    def r_zz(g):
        n = lead[g]
        bit = 1
        while g not in straight and 2 * bit < Z:
            for m in range(0, Z, 2 * bit):
                zz, at = zxor(m), zxor(m + bit - 1)
                got(from_z[g].at[n, at], r_gz.at[g, at])
                t = store[g][n, zz, y, c, f].astype(F32) + from_z[g][n, at].astype(F32)
                store[g][n, zz, y, c, f] = t.astype(BF16)
            bit *= 2
            r_fold(g, bit)

    def r_end(g):
        n = lead[g]
        t = store[g][n, z, y, c, f].astype(F32)
        if g in straight:
            for k in range(1, Z):
                zz = zplus(k)
                got(from_z[g].at[n, zz], r_gz.at[g, zz])
                t = t + from_z[g][n, zz].astype(F32)
        else:
            at = zxor(Z // 2 - 1)
            got(from_z[g].at[n, at], r_gz.at[g, at])
            t = t + from_z[g][n, at].astype(F32)
        if g <= V:
            gqkv_ref[:, g * D : (g + 1) * D] = t
        elif g == O:
            gout_ref[...] = t
        elif g <= UB:
            gup_ref[:, (g - UA) * HF : (g - UA + 1) * HF] = t
        else:
            gdown_ref[(g - DA) * 2 * SLAB : (g - DA + 1) * 2 * SLAB, :] = t

    def r_sent(g):
        n = lead[g]
        sent(store[g].at[n, :, :, oc], s_gc.at[g])
        for k in range(1, FK):
            ff = fplus(k)
            if g in y_first or g in direct:
                sent(store[g].at[n, :, y, c, ff], s_gx.at[g, ff])
            else:
                sent(store[g].at[n, :, :, c, ff], s_gx.at[g, ff])
            if g in direct:
                sent(store[g].at[n, :, oy, c, ff], s_gd.at[g, ff])
        if g in y_first and g not in direct:
            sent(store[g].at[n, :, oy, c], s_gy.at[g])
        else:
            sent(store[g].at[n, :, oy, c, f], s_gy.at[g])
        for k in range(1, Z):
            sent(store[g].at[n, zplus(k), y, c, f], s_gz.at[g, zplus(k)])

    turns = sorted(range(1, Z), key=lambda m: (m & -m, m)) + [0]

    def plane(n):
        m = jnp.int32(0)
        for k in range(Z - 1):
            m = jnp.where(n == k, turns[k], m)
        return zxor(m)

    def p_sum(m):
        zz = zxor(m)
        got(crf.at[zz], r_pc.at[zz])
        t = tokb[zz, c].astype(F32) + crf[zz].astype(F32)
        bit = 1
        while bit < Z and m % (2 * bit) == 0:
            at = zxor(m + bit - 1)
            got(zrf.at[at], r_pz.at[at])
            t = t + zrf[at].astype(F32)
            bit *= 2
        return t

    def p_z(s):
        m = turns[s]
        bit = m & -m
        zz, at = zxor(m), zxor(bit ^ (m - 1))
        tokb[zz, c] = p_sum(m).astype(BF16)
        push(tokb.at[zz, c], zrf.at[at], s_pz.at[zz], r_pz.at[at], d_z(zxor(bit)))

    def queries_back():
        push(gqs, gqr, s_y.at[5], r_y.at[5], d_y)

    def sums():
        push(sg.at[0], src, s_sc, r_sc, d_core)

    def sums_core():
        got(src, r_sc)
        sg[1] = sg[0] + src[...]
        for k in range(1, FK):
            ff = fplus(k)
            push(sg.at[1], srx.at[f], s_sx.at[ff], r_sx.at[f], d_f(ff))

    def sums_x():
        t = sg[1]
        for k in range(1, FK):
            got(srx.at[fplus(k)], r_sx.at[fplus(k)])
            t = t + srx[fplus(k)]
        sg[2] = t
        push(sg.at[2], sry, s_sy, r_sy, d_y)

    def sums_y():
        got(sry, r_sy)
        sg[3] = sg[2] + sry[...]
        for k in range(1, Z):
            zz = zplus(k)
            push(sg.at[3], srz.at[z], s_sz.at[zz], r_sz.at[z], d_z(zz))

    def sums_z():
        t = sg[3]
        for k in range(1, Z):
            zz = zplus(k)
            got(srz.at[zz], r_sz.at[zz])
            t = t + srz[zz]
        gsm_ref[...] = t

    def first():
        got(gqr, r_y.at[5])
        t = p_sum(0) + acc[...] + gqr[...].astype(F32)
        mean, centered, rstd = moments(tok_ref[...].astype(F32))
        gtok_ref[...] = (hid[...] + norm_back(t * par[0:1, :], centered * rstd, rstd)).astype(BF16)


    qrows = slice(HD, HD + SLAB)
    grows = slice(0, HD + SLAB)
    near_half, far_half = slice(0, R), slice(R, 2 * R)

    def far_out():
        push(oh, ohr, s_y.at[0], r_y.at[0], d_y)
        push(ml, mlr, s_y.at[1], r_y.at[1], d_y)

    def far_got():
        got(ohr, r_y.at[0])
        got(mlr, r_y.at[1])

    def back_got():
        got(qt.at[:, qrows, far_half], r_y.at[3])
        got(dot_.at[:, grows, far_half], r_y.at[4])

    events = {
        "tr": lambda: tok_right(z),
        "tl": lambda: tok_left(z),
        "tp": lambda: push(tokb.at[z, c], tokp, s_tp, r_tp, d_y),
        "tc": lambda: tok_core(z),
        "tok_z": tok_z,
        "gtokp": lambda: got(tokp, r_tp),
        "w_out_z": w_out_z, "w_own_y": w_own_y, "w_own_x": w_own_x, "w_z": w_z, "w_m": w_m, "w_l": w_l, "w_c": w_c,
        "o_hi": far_out,
        "o_lo": lambda: push(ol, olr, s_y.at[2], r_y.at[2], d_y),
        "g_o": far_got,
        "g_ol": lambda: got(olr, r_y.at[2]),
        "qtail": lambda: push(qt.at[:, qrows, near_half], qt.at[:, qrows, far_half], s_y.at[3], r_y.at[3], d_y),
        "dO": lambda: push(dot_.at[:, grows, near_half], dot_.at[:, grows, far_half], s_y.at[4], r_y.at[4], d_y),
        "g_dO": back_got,
        "gq": queries_back,
        "r_c": r_c, "r_1": r_1, "r_2": r_2, "r_z": r_z, "r_zz": r_zz, "r_end": r_end,
        "p_z": p_z,
        "first": first,
        "s": lambda k: (sums, sums_core, sums_x, sums_y)[k](),
        "s_end": sums_z,
    }
    chunks = {"q": Q, "k": K, "v": V, "o": O, "ua": UA, "ub": UB, "da": DA, "db": DB}
    plan = order_of(Z)

    def do(stage):
        for name, *which in plan.get(stage, ()):
            events[name](*[chunks.get(t, t) for t in which])

    def run(stage, n):
        for at in range(Z):
            if (stage, at) in plan:
                @pl.when(n == at)
                def _():
                    do((stage, at))

    for t in arriving:
        t.wait()
    do("masks")

    starts, ends, stops = [], [], []
    total = jnp.int32(0)
    for t in range(NT):
        starts.append(total)
        stops.append(total + sup_ref[0, t])
        total = total + len_ref[0, t]
        ends.append(total)

    lane = lax.broadcasted_iota(jnp.int32, (1, 128), 1)
    lane_start = jnp.zeros((1, 128), jnp.int32)
    lane_stop = jnp.zeros((1, 128), jnp.int32)
    for t in range(NT):
        lane_start = jnp.where(lane == t, starts[t], lane_start)
        lane_stop = jnp.where(lane == t, stops[t], lane_stop)
    lane_ones = jnp.where((lane >= NT) & (lane < NT + 3), 1.0, 0.0)

    def mask_of(n):
        pos = (n * 2 + y) * 2 * R + lax.broadcasted_iota(jnp.int32, (2 * R, 128), 0)
        seen = (pos >= lane_start) & (pos < lane_stop)
        extra = jnp.where(lane < NT, jnp.where(seen, 0.0, MASKED), lane_ones)
        return extra.astype(BF16)

    def mask_block(n, carry):
        eb[n] = mask_of(n)
        return carry

    lax.fori_loop(0, Z, mask_block, 0)

    row = lax.broadcasted_iota(jnp.int32, (HD, 2 * R), 0)
    col = lax.broadcasted_iota(jnp.int32, (HD, 2 * R), 1)
    qpos = jnp.where(col < R, i * R + col, ((z * 2 + oy) * 2 + c - 1) * R + col)
    onehot = jnp.zeros((HD, 2 * R), F32)
    for t in range(NT):
        onehot = jnp.where((row == t) & (qpos >= starts[t]) & (qpos < ends[t]), 1.0, onehot)
    for h in range(H):
        qt[h, HD : 2 * HD, :] = onehot.astype(BF16)
        dot_[h, HD + SLAB : 2 * HD, :] = jnp.zeros((HD - SLAB, 2 * R), BF16)
        ot[h] = jnp.zeros((2 * HD, 2 * R), F32)
        mrun[h] = jnp.full((1, 2 * R), MASKED, F32)

    do("small")

    piece = D // NSH
    small = w0[:, :, :, :, :, 3 * D : 3 * D + 128].reshape(NSH * SLAB, 128)
    spread = (
        lax.rem(lax.broadcasted_iota(jnp.int32, (128, D), 1), piece)
        == lax.broadcasted_iota(jnp.int32, (128, D), 0)
    )
    wide = dot_nn(small, spread.astype(BF16))
    mine = (
        lax.broadcasted_iota(jnp.int32, (NSH * SLAB, D), 1) // piece
        == lax.broadcasted_iota(jnp.int32, (NSH * SLAB, D), 0) // SLAB
    )
    wide = jnp.where(mine, wide, 0.0)
    par[...] = jnp.sum(wide.reshape(NSH, SLAB, D), axis=0)
    pick = (
        lax.broadcasted_iota(jnp.int32, (NSH, NSH * SLAB), 1)
        == lax.broadcasted_iota(jnp.int32, (NSH, NSH * SLAB), 0) * SLAB + 8
    )
    ups = dot_nn(pick.astype(BF16), small).astype(BF16)
    spread = (
        lax.rem(lax.broadcasted_iota(jnp.int32, (128, FF), 1), 4 * piece)
        == lax.broadcasted_iota(jnp.int32, (128, FF), 0)
    )
    wide = dot_nn(ups, spread.astype(BF16))
    mine = (
        lax.broadcasted_iota(jnp.int32, (NSH, FF), 1) // (4 * piece)
        == lax.broadcasted_iota(jnp.int32, (NSH, FF), 0)
    )
    upb[...] = col_sum(jnp.where(mine, wide, 0.0))
    ln1g, ln1b = par[0:1, :], par[1:2, :]

    tokens = tok_ref[...].astype(F32)
    mean, centered, rstd = moments(tokens)
    xq[0:R, :] = (centered * rstd * ln1g + ln1b).astype(BF16)
    mean, centered, rstd = moments(tokp[...].astype(F32))
    xq[R : 2 * R, :] = (centered * rstd * ln1g + ln1b).astype(BF16)
    wq = w0[:, :, :, :, :, 0:D].reshape(D, D)
    qscale = HD ** (-0.5) / LN2
    qs[...] = ((dot_nn(xq[...], wq) + par[2:3, :]) * qscale).astype(BF16)
    for h in range(H):
        qt[h, 0:HD, :] = qs[:, h * HD : (h + 1) * HD].T

    def near(s):
        inner = jnp.minimum(z, Z - 1 - z)
        odd = lax.rem(s, 2)
        paired = z + (1 - 2 * odd) * ((s + 1) // 2)
        rest = jnp.where(z < Z - 1 - z, s, Z - 1 - s)
        return jnp.where(s <= 2 * inner, paired, rest)

    def attend(h, keys, values, extra, span):
        cols = slice(h * HD, (h + 1) * HD)
        s = dot_nn(jnp.concatenate([keys[:, cols], extra], axis=1), qt[h, :, span])
        top0 = mrun[h, :, span]
        top = jnp.maximum(top0, jnp.ceil(jnp.max(s, axis=0, keepdims=True)))
        e = jnp.exp2(s - top).astype(BF16)
        grown = dot_tn(jnp.concatenate([values[:, cols], extra], axis=1), e)
        ot[h, :, span] = ot[h, :, span] * jnp.exp2(top0 - top) + grown
        mrun[h, :, span] = top

    def ahead(n, carry):
        zz = near(n)
        run("A", n)
        got(tokb.at[zz, oc], r_t.at[zz, oc])
        mean, centered, rstd = moments(tokb[zz].reshape(2 * R, D).astype(F32))
        stat[zz] = jnp.where(lax.broadcasted_iota(jnp.int32, (2 * R, 128), 1) == 0, mean, rstd)
        x = (centered * rstd * par[0:1, :] + par[1:2, :]).astype(BF16)
        kv = dot_nn(x, w0[:, :, :, :, :, D : 3 * D].reshape(D, 2 * D))
        keys = kv[:, 0:D].astype(BF16)
        values = (kv[:, D : 2 * D] + par[3:4, :]).astype(BF16)
        kb[zz] = keys
        vb[zz] = values
        extra = eb[zz]
        for h in range(H):
            attend(h, keys, values, extra, slice(R, 2 * R))
        return carry

    lax.fori_loop(0, Z, ahead, 0)

    do("osplit")
    for h in range(H):
        t = ot[h, 0:HD, R : 2 * R]
        first_part = t.astype(BF16)
        oh[h] = first_part
        ol[h] = (t - first_part.astype(F32)).astype(BF16)
        ml[h : h + 1, :] = mrun[h, :, R : 2 * R]
        ml[H + h : H + h + 1, :] = ot[h, HD + NT : HD + NT + 1, R : 2 * R]
    def ahead_own(n, carry):
        zz = near(n)
        run("B", n)
        for h in range(H):
            attend(h, kb[zz], vb[zz], eb[zz], slice(0, R))
        return carry

    lax.fori_loop(0, Z, ahead_own, 0)
    do("merge")
    parts = []
    row_tail = lax.broadcasted_iota(jnp.int32, (SLAB, R), 0)
    for h in range(H):
        m_own, m_far = mrun[h, :, 0:R], mlr[h : h + 1, :]
        top = jnp.maximum(m_own, m_far)
        a_own, a_far = jnp.exp2(m_own - top), jnp.exp2(m_far - top)
        total = a_own * ot[h, HD + NT : HD + NT + 1, 0:R] + a_far * mlr[H + h : H + h + 1, :]
        inverse = 1.0 / total
        attended = ot[h, 0:HD, 0:R] * (a_own * inverse) + ohr[h].astype(F32) * (a_far * inverse)
        ot[h, 0:HD, 0:R] = attended
        ot[h, HD : HD + 1, 0:R] = inverse
        ot[h, HD + 1 : HD + 2, 0:R] = a_far * inverse
        parts.append(attended.T.astype(BF16))
        m1, m2, m3 = three_terms(top)
        tail = jnp.where(
            row_tail == NT, -m1,
            jnp.where(row_tail == NT + 1, -m2, jnp.where(row_tail == NT + 2, -m3, onehot[0:SLAB, 0:R])),
        )
        qt[h, HD : HD + SLAB, 0:R] = tail.astype(BF16)
    do("out")
    attn_low = jnp.concatenate(parts, axis=1)
    w_out = w1[:, :, :, :, :, 0:D].reshape(D, D)
    hidden = tokens + (dot_nn(attn_low, w_out) + par[4:5, :])
    hid[...] = hidden
    mean2, centered, rstd2 = moments(hidden)
    n2 = centered * rstd2
    nrm2[...] = (n2 * par[5:6, :] + par[6:7, :]).astype(BF16)
    acc[...] = hidden + par[7:8, :]
    gsec[...] = jnp.zeros((R, D), F32)

    def chunk(j, carry):
        cols = pl.ds(pl.multiple_of(D + j * CH, 128), CH)
        bcols = pl.ds(pl.multiple_of(j * CH, 128), CH)
        up = w1[:, :, :, :, :, cols].reshape(D, CH)
        down = w2[j].reshape(CH, D)
        pre = dot_nn(nrm2[...], up) + upb[:, bcols]
        phi = 0.5 * (1.0 + lax.erf(pre * (0.5**0.5)))
        act = (pre * phi).astype(BF16)
        slope = phi + pre * (jnp.exp2(pre * pre * (-0.5 / LN2)) * ((2.0 * math.pi) ** -0.5))
        acc[...] += dot_nn(act, down)
        gpre = (dot_nt(cot_ref[...], down) * slope).astype(BF16)
        gsec[...] += dot_nt(gpre, up)
        upg[:, bcols] = col_sum(gpre.astype(F32))
        act_all[:, bcols] = act
        gpre_all[:, bcols] = gpre
        return carry

    do("ffn")
    lax.fori_loop(0, Z, chunk, 0)
    do("ln2")
    out_ref[...] = acc[...].astype(BF16)

    g_second = gsec[...]
    n2 = (hid[...] - mean2) * rstd2
    ln2g = par[5:6, :]
    cot32 = cot_ref[...].astype(F32)
    grad_hidden = cot32 + norm_back(g_second * ln2g, n2, rstd2)
    hid[...] = grad_hidden
    g_branch = grad_hidden.astype(BF16)
    do("dOc")
    for h in range(H):
        rows = slice(h * HD, (h + 1) * HD)
        w_head = w1[:, :, :, :, :, 0:D].reshape(D, D)[rows, :]
        ga = dot_nt(w_head, g_branch).astype(BF16).astype(F32)
        low = (ga * ot[h, HD : HD + 1, 0:R]).astype(BF16)
        exact = ot[h, 0:HD, 0:R] + olr[h].astype(F32) * ot[h, HD + 1 : HD + 2, 0:R]
        delta = col_sum(low.astype(F32) * exact)
        d1, d2, d3 = three_terms(delta)
        tail = jnp.where(
            row_tail == NT, -d1, jnp.where(row_tail == NT + 1, -d2, jnp.where(row_tail == NT + 2, -d3, 0.0))
        )
        dot_[h, 0:HD, 0:R] = low
        dot_[h, HD : HD + SLAB, 0:R] = tail.astype(BF16)
        dos[0:R, rows] = low.T

    def g_up(j, carry):
        bcols = pl.ds(pl.multiple_of(j * CH, 128), CH)
        t = dot_tn(nrm2[...], gpre_all[:, bcols]).astype(BF16).reshape(Z, 2, 2, FK, SLAB, CH)
        hh = j // (Z // 2)
        gu[hh, :, :, :, :, :, pl.ds(pl.multiple_of((j - hh * (Z // 2)) * CH, 128), CH)] = t
        return carry

    def g_down(j, carry):
        bcols = pl.ds(pl.multiple_of(j * CH, 128), CH)
        t = dot_tn(act_all[:, bcols], cot_ref[...]).astype(BF16).reshape(2, 2, FK, 4 * SLAB, D)
        gd[0, j] = t[:, :, :, 0 : 2 * SLAB]
        gd[1, j] = t[:, :, :, 2 * SLAB : 4 * SLAB]
        return carry

    do("dwu")
    lax.fori_loop(0, Z, g_up, 0)
    do("dwd")
    lax.fori_loop(0, Z, g_down, 0)
    do("dwo")
    gs[O] = dot_tn(attn_low, g_branch).astype(BF16).reshape(Z, 2, 2, FK, SLAB, D)
    zero = jnp.zeros((1, D), F32)
    for r in range(SLAB):
        sg[0, r : r + 1, :] = zero
    sg[0, 4:5, :] = col_sum(g_branch.astype(F32))
    sg[0, 5:6, :] = col_sum(g_second * n2)
    sg[0, 6:7, :] = col_sum(g_second)
    sg[0, 7:8, :] = col_sum(cot32)
    for r in range(FF // D):
        sg[0, 8 + r : 9 + r, :] = upg[:, r * D : (r + 1) * D]

    dqt[...] = jnp.zeros((H, HD, 2 * R), F32)
    dwkv[...] = jnp.zeros((D, 2 * D), F32)
    lacc[...] = jnp.zeros((3, 8, D), F32)

    def tok_sent():
        @pl.when(z < Z - 1)
        def _():
            for k in range(Z):
                @pl.when(z - k >= 0)
                def _():
                    sent(tokb.at[z - k, c], s_tz.at[0, z - k])

        @pl.when(z > 0)
        def _():
            for k in range(Z):
                @pl.when(z + k < Z)
                def _():
                    sent(tokb.at[z + k, c], s_tz.at[1, z + k])

        for zz in range(Z):
            sent(tokb.at[zz, c], s_tc.at[zz])
        sent(tokb.at[z, c], s_tp)

    def heads(zz, span):
        keys, values, extra = kb[zz], vb[zz], eb[zz]
        dks, dvs = [], []
        for h in range(H):
            cols = slice(h * HD, (h + 1) * HD)
            s = dot_nn(jnp.concatenate([keys[:, cols], extra], axis=1), qt[h, :, span])
            dp = dot_nn(jnp.concatenate([values[:, cols], extra], axis=1), dot_[h, :, span])
            e = jnp.exp2(s).astype(BF16)
            ds = (e.astype(F32) * dp).astype(BF16)
            dvs.append(dot_nn(e, dos[span, cols]))
            dks.append(dot_nn(ds, qs[span, cols]) * LN2)
            dqt[h, :, span] += dot_tn(keys[:, cols], ds)
        return jnp.concatenate(dks + dvs, axis=1)

    def rest(n, zz, dkv32):
        dkv = dkv32.astype(BF16)
        run("t", n)
        gp = dot_nt(dkv, w0[:, :, :, :, :, D : 3 * D].reshape(D, 2 * D))
        norm = (tokb[zz].reshape(2 * R, D).astype(F32) - stat[zz, :, 0:1]) * stat[zz, :, 1:2]
        tokb[zz] = gp.astype(BF16).reshape(2, R, D)
        push(tokb.at[zz, oc], crf.at[zz], s_pc.at[zz], r_pc.at[zz], d_core)
        x = (norm * par[0:1, :] + par[1:2, :]).astype(BF16)
        lacc[0] += fold_rows(gp * norm)
        lacc[1] += fold_rows(gp)
        lacc[2] += fold_rows(dkv32[:, D : 2 * D])
        dwkv[...] += dot_tn(x, dkv)

    def behind_early(n, carry):
        run("e", n)
        early[n] = heads(plane(n), near_half)
        return carry

    def behind_far(n, carry):
        run("h", n)
        zz = plane(n)
        rest(n, zz, early[n] + heads(zz, far_half))
        return carry

    def behind(n, carry):
        run("h", n)
        zz = plane(n)
        rest(n, zz, heads(zz, slice(0, 2 * R)))
        return carry

    do("sent")
    tok_sent()
    E = early.shape[0] if Z == 4 else 0
    if E:
        lax.fori_loop(0, E, behind_early, 0)
    do("dosT")
    for h in range(H):
        dos[R : 2 * R, h * HD : (h + 1) * HD] = dot_[h, 0:HD, R : 2 * R].T
    if E:
        lax.fori_loop(0, E, behind_far, 0)
    lax.fori_loop(E, Z, behind, 0)

    do("kv")
    gs[K] = dwkv[:, 0:D].astype(BF16).reshape(Z, 2, 2, FK, SLAB, D)
    gs[V] = dwkv[:, D : 2 * D].astype(BF16).reshape(Z, 2, 2, FK, SLAB, D)

    def queries():
        dq = jnp.concatenate([(dqt[h] * (HD**-0.5)).T for h in range(H)], axis=1).astype(BF16)
        gs[Q] = dot_tn(xq[...], dq).astype(BF16).reshape(Z, 2, 2, FK, SLAB, D)
        gq = dot_nt(dq, w0[:, :, :, :, :, 0:D].reshape(D, D))
        acc[...] = gq[0:R]
        gqs[...] = gq[R : 2 * R].astype(BF16)
        both = jnp.concatenate([tok_ref[...], tokp[...]], axis=0).astype(F32)
        mean, centered, rstd = moments(both)
        sg[0, 0:1, :] = col_sum(lacc[0]) + col_sum(gq * (centered * rstd))
        sg[0, 1:2, :] = col_sum(lacc[1]) + col_sum(gq)
        sg[0, 2:3, :] = col_sum(dq.astype(F32))
        sg[0, 3:4, :] = col_sum(lacc[2])

    do("q")
    queries()
    do("end")

    for g in range(3):
        for k in range(1, Z):
            sent(wb[g].at[z, y, c, f], s_wz.at[g, zplus(k)])
        for zz in range(Z):
            sent(wb[g].at[zz, y, c, f], s_wy.at[g, zz, f])
            for k in range(1, FK):
                ff = fplus(k)
                sent(wb[g].at[zz, y, c, f], s_wx.at[g, ff, zz, y])
                if g in x_first:
                    sent(wb[g].at[zz, y, c, ff], s_wy.at[g, zz, ff])
                else:
                    sent(wb[g].at[zz, oy, c, f], s_wx.at[g, ff, zz, oy])
        for n in range(w_parts(g)):
            if g in x_first:
                sent(wb[g].at[:, y if n == 0 else oy, c], s_wc.at[g, n])
            else:
                sent(wb[g].at[:, :, c, fplus(n)], s_wc.at[g, n])
    for g in range(8):
        r_sent(g)
    for zz in range(Z):
        sent(tokb.at[zz, oc], s_pc.at[zz])
    for k in range(1, Z):
        sent(tokb.at[zplus(k), c], s_pz.at[zplus(k)])
        sent(sg.at[3], s_sz.at[zplus(k)])
    sent(oh, s_y.at[0])
    sent(ml, s_y.at[1])
    sent(ol, s_y.at[2])
    sent(qt.at[:, HD : HD + SLAB, 0:R], s_y.at[3])
    sent(dot_.at[:, 0 : HD + SLAB, 0:R], s_y.at[4])
    sent(gqs, s_y.at[5])
    sent(sg.at[0], s_sc)
    for k in range(1, FK):
        sent(sg.at[1], s_sx.at[fplus(k)])
    sent(sg.at[2], s_sy)


def layer(Z, FK, R, D, FF, NT, operands):
    vm = lambda shape, dtype: pltpu.VMEM(shape, dtype)
    dma = lambda *shape: pltpu.SemaphoreType.DMA(shape)
    lead = (Z, 2, 2, FK)
    slabs = ((SLAB, 3 * D + 128), (SLAB, D + FF), (4 * SLAB, D))
    gslabs = ((4, SLAB, D), (2, SLAB, FF // 2), (2, 2 * SLAB, D))
    scratch = [
        vm((Z, 2, R, D), BF16),
        vm((R, D), BF16),
        vm((Z, 2 * R, D), BF16),
        vm((Z, 2 * R, D), BF16),
        vm((Z, 2 * R, 128), BF16),
        vm((Z, 2 * R, 128), F32),
        *[vm(lead + s, BF16) for s in slabs],
        *[vm((s[0],) + lead + s[1:], BF16) for s in gslabs],
        *[vm((s[0], Z, 2, FK) + s[1:], BF16) for s in gslabs],
        *[vm((s[0], FK, Z, 2) + s[1:] if FK > 1 else (SLAB, 128), BF16) for s in gslabs],
        *[vm((s[0], Z, FK) + s[1:], BF16) for s in gslabs],
        *[vm((s[0], Z) + s[1:], BF16) for s in gslabs],
        vm((Z, R, D), BF16),
        vm((Z, R, D), BF16),
        vm((SLAB, D), F32),
        vm((1, FF), F32),
        vm((H, 2 * HD, 2 * R), BF16),
        vm((H, 2 * HD, 2 * R), BF16),
        vm((2 * R, D), BF16),
        vm((2 * R, D), BF16),
        vm((H, 2 * HD, 2 * R), F32),
        vm((H, 1, 2 * R), F32),
        vm((H, HD, 2 * R), F32),
        vm((H, HD, R), BF16),
        vm((H, HD, R), BF16),
        vm((2 * H, R), F32),
        vm((H, HD, R), BF16),
        vm((H, HD, R), BF16),
        vm((2 * H, R), F32),
        vm((R, D), BF16),
        vm((R, D), BF16),
        vm((R, D), BF16),
        vm((R, D), F32),
        vm((R, D), F32),
        vm((R, D), F32),
        vm((D, 2 * D), F32),
        vm((3, 8, D), F32),
        vm((1, FF), F32),
        vm((2 * R, D), BF16),
        vm((4, SLAB, D), F32),
        vm((SLAB, D), F32),
        vm((FK, SLAB, D), F32),
        vm((SLAB, D), F32),
        vm((Z, SLAB, D), F32),
        vm((SLAB, 128), F32),
        vm((R, D), BF16),
        vm((R, D), BF16),
        vm((R, FF), BF16),
        vm((R, FF), BF16),
        vm((2, 2 * R, 2 * D) if Z == 4 else (1, 8, 128), F32),
        dma(7),
        dma(2, Z), dma(Z), dma(Z, 2), pltpu.SemaphoreType.DMA, pltpu.SemaphoreType.DMA,
        dma(3, Z), dma(3, Z), dma(3, Z, FK), dma(3, Z, FK),
        dma(3, FK, Z, 2), dma(3, FK, Z, 2), dma(3, 2), dma(3, 2),
        dma(8), dma(8), dma(8, FK), dma(8, FK), dma(8), dma(8), dma(8, FK), dma(8, FK), dma(8, Z), dma(8, Z),
        dma(Z), dma(Z), dma(Z), dma(Z), dma(6), dma(6),
        pltpu.SemaphoreType.DMA, pltpu.SemaphoreType.DMA,
        dma(FK), dma(FK),
        pltpu.SemaphoreType.DMA, pltpu.SemaphoreType.DMA,
        dma(Z), dma(Z),
    ]
    vmem = pl.BlockSpec(memory_space=pltpu.VMEM)
    smem = pl.BlockSpec(memory_space=pltpu.SMEM)
    shape = jax.ShapeDtypeStruct
    return pl.pallas_call(
        functools.partial(body, Z, FK, R, D, NT),
        out_shape=(
            shape((R, D), BF16),
            shape((R, D), BF16),
            shape((SLAB, 3 * D), F32),
            shape((SLAB, D), F32),
            shape((SLAB, FF), F32),
            shape((4 * SLAB, D), F32),
            shape((SLAB, D), F32),
        ),
        in_specs=[pl.BlockSpec(memory_space=pl.ANY)] * 6 + [vmem] * 9 + [smem] * 2,
        out_specs=[vmem] * 7,
        scratch_shapes=scratch,
        compiler_params=pltpu.CompilerParams(
            collective_id=0, has_side_effects=True, vmem_limit_bytes=63 * 2**20
        ),
        name="layer",
    )(*operands)


def finish(NSH, FK, *refs):
    big_in, small_in, big_out, small_out = refs[0:6], refs[6], refs[7:13], refs[13:22]
    for a, b in zip(big_in, big_out):
        b[...] = a[...]
    at = lax.axis_index("blk") * FK
    if FK > 1:
        at = at + lax.axis_index("fsdp")
    D = small_in.shape[1]
    piece = D // NSH
    lane = lax.broadcasted_iota(jnp.int32, (128, D), 1)
    take = lax.broadcasted_iota(jnp.int32, (128, D), 0)
    full = small_in[...]
    for r in range(8):
        chosen = jnp.where(lane == at * piece + take, full[r : r + 1, :], 0.0)
        small_out[r][...] = jnp.sum(chosen, axis=1).reshape(1, 128)[:, 0:piece]
    FF = D * 4
    total = jnp.zeros((128,), F32)
    for r in range(4):
        chosen = jnp.where(lane + r * D == at * 4 * piece + take, full[8 + r : 9 + r, :], 0.0)
        total = total + jnp.sum(chosen, axis=1)
    small_out[8][...] = total.reshape(1, 128)[:, 0 : 4 * piece]


def hand_over(NSH, FK, FF, results):
    *big, small = results
    D = small.shape[1]
    vmem = pl.BlockSpec(memory_space=pltpu.VMEM)
    shape = jax.ShapeDtypeStruct
    return pl.pallas_call(
        functools.partial(finish, NSH, FK),
        out_shape=(
            *[shape(v.shape, v.dtype) for v in big],
            *[shape((1, D // NSH), F32) for _ in range(8)],
            shape((1, FF // NSH), F32),
        ),
        in_specs=[vmem] * 7,
        out_specs=[vmem] * 15,
        name="finish",
    )(*results)


def shards(
    blocks, fsdp,
    tokens, ln1_gain, ln1_bias, qkv_weight, query_bias, value_bias, out_weight, out_bias,
    ln2_gain, ln2_bias, up_weight, up_bias, down_weight, down_bias,
    table_lengths, support_lengths, cotangent,
):
    R, D = tokens.shape[1:]
    FF = up_weight.shape[1]
    NT = table_lengths.shape[1]
    smalls = (ln1_gain, ln1_bias, query_bias, value_bias, out_bias, ln2_gain, ln2_bias, down_bias, up_bias)
    weights = (qkv_weight, out_weight, up_weight, down_weight)
    inside = qkv_weight.shape[0] == SLAB
    FK = fsdp if inside else 1
    if not inside:
        whole = lambda v: lax.all_gather(v, "fsdp", axis=0, tiled=True)
        smalls = tuple(whole(v) for v in smalls)
        weights = tuple(whole(v) for v in weights)
    results = layer(
        blocks // 4, FK, R, D, FF, NT,
        (tokens[0], cotangent[0], *weights, *[v[None] for v in smalls], table_lengths, support_lengths),
    )
    block_out, grad_tokens, g_qkv, g_out, g_up, g_down, *small_grads = hand_over(
        blocks * FK, FK, FF, results
    )
    small_grads = [v[0] for v in small_grads]
    weight_grads = [g_qkv, g_out, g_up, g_down]
    if not inside:
        spread = lambda v: lax.psum_scatter(v, "fsdp", scatter_dimension=0, tiled=True)
        small_grads = [spread(v) for v in small_grads]
        weight_grads = [spread(v) for v in weight_grads]
    g_ln1g, g_ln1b, g_qb, g_vb, g_ob, g_ln2g, g_ln2b, g_db, g_ub = small_grads
    g_qkv, g_out, g_up, g_down = weight_grads
    return (
        block_out[None], grad_tokens[None], g_ln1g, g_ln1b, g_qkv, g_qb, g_vb, g_out, g_ob,
        g_ln2g, g_ln2b, g_up, g_ub, g_down, g_db,
    )


def solution(mesh):
    both = ("blk", "fsdp")
    vec, mat, rows = P(both), P(both, None), P("fsdp", "blk", None)
    return jax.shard_map(
        functools.partial(shards, mesh.shape["blk"], mesh.shape["fsdp"]),
        mesh=mesh,
        in_specs=(
            rows, vec, vec, mat, vec, vec, mat, vec, vec, vec, mat, vec, mat, vec,
            P("fsdp", None), P("fsdp", None), rows,
        ),
        out_specs=(rows, rows, vec, vec, mat, vec, vec, mat, vec, vec, vec, mat, vec, mat, vec),
        check_vma=False,
    )
```

```python
import functools
import math

import jax
import jax.numpy as jnp
from jax import lax
from jax.experimental import pallas as pl
from jax.experimental.pallas import tpu as pltpu
from jax.sharding import PartitionSpec as P

H = 4
HD = 128
SLAB = 16
EPSILON = 1e-05
MASKED = -1e30
LN2 = math.log(2.0)
MESH = pl.DeviceIdType.MESH
F32 = jnp.float32
BF16 = jnp.bfloat16


def dot_nn(a, b):
    return lax.dot_general(a, b, (((1,), (0,)), ((), ())), preferred_element_type=F32)


def dot_nt(a, b):
    return lax.dot_general(a, b, (((1,), (1,)), ((), ())), preferred_element_type=F32)


def dot_tn(a, b):
    return lax.dot_general(a, b, (((0,), (0,)), ((), ())), preferred_element_type=F32)


def moments(v):
    mean = jnp.mean(v, axis=-1, keepdims=True)
    centered = v - mean
    rstd = lax.rsqrt(jnp.mean(centered * centered, axis=-1, keepdims=True) + EPSILON)
    return mean, centered, rstd


def norm_back(g, n, r):
    return r * (g - jnp.mean(g, axis=-1, keepdims=True) - n * jnp.mean(g * n, axis=-1, keepdims=True))


def three_terms(v):
    first = v.astype(BF16)
    rest = v - first.astype(F32)
    second = rest.astype(BF16)
    third = (rest - second.astype(F32)).astype(BF16)
    return first.astype(F32), second.astype(F32), third.astype(F32)


def col_sum(v):
    return jnp.sum(v, axis=0, keepdims=True)


def fold_rows(v):
    return jnp.sum(v.reshape(v.shape[0] // 8, 8, v.shape[1]), axis=0)


FOUR = {
    "masks": [("w_out_z", 0), ("tc",), ("w_own_y", 0), ("tp",), ("w_own_x", 2), ("w_own_x", 1), ("tl",), ("tr",)],
    "small": [
        ("w_z", 0), ("w_own_x", 4), ("w_out_z", 1), ("tok_z", 1), ("w_m", 0), ("gtokp",), ("w_own_x", 0), ("w_z", 1),
        ("w_own_y", 1), ("w_own_y", 4), ("w_out_z", 2), ("w_own_y", 2), ("w_l", 0), ("w_m", 1), ("tok_z", 2),
        ("w_own_y", 3), ("w_c", 0),
    ],
    ("A", 0): [("w_out_z", 4), ("w_z", 2), ("w_out_z", 3), ("w_own_x", 3)],
    ("A", 2): [("w_l", 1), ("w_m", 2)],
    ("A", 3): [("tok_z", 3), ("w_z", 4)],
    "osplit": [("w_z", 3), ("w_m", 4), ("w_l", 2)],
    ("B", 0): [("o_hi",)],
    ("B", 1): [("w_m", 3)],
    ("B", 3): [("w_c", 1), ("w_l", 4)],
    "merge": [("w_l", 3), ("o_lo",), ("g_o",), ("w_c", 4)],
    "ffn": [("w_c", 2)],
    "ffd": [("w_c", 3)],
    "dOc": [("qtail",), ("g_ol",)],
    "dwu": [("dO",)],
    "sent": [("r_c", "ub")],
    ("e", 2): [("r_1", "ub"), ("r_2", "ub")],
    "dosT": [("r_c", "o"), ("g_dO",)],
    ("h", 0): [("r_c", "db")],
    ("h", 1): [("r_1", "o"), ("r_2", "o"), ("p_z", 0), ("r_c", "da")],
    ("t", 1): [("r_1", "db")],
    ("h", 2): [("r_z", "ub"), ("r_1", "da"), ("r_c", "ua")],
    ("t", 2): [("r_2", "db"), ("p_z", 1), ("r_1", "ua")],
    ("h", 3): [("r_z", "o"), ("r_z", "db")],
    "kv": [("r_2", "da")],
    "q": [("r_c", "v"), ("p_z", 2), ("r_1", "v"), ("r_zz", "ub"), ("r_c", "k"), ("r_2", "ua")],
    "end": [
        ("r_zz", "db"), ("s", 0), ("r_1", "k"), ("s", 1), ("r_c", "q"), ("r_z", "da"), ("r_2", "k"), ("r_z", "ua"),
        ("r_2", "v"), ("r_end", "ub"), ("r_1", "q"), ("r_zz", "o"), ("r_zz", "da"), ("r_end", "db"), ("s", 2),
        ("r_z", "k"), ("r_2", "q"), ("gq",), ("r_z", "v"), ("r_zz", "ua"), ("r_z", "q"), ("r_zz", "k"), ("s", 3),
        ("r_zz", "v"), ("r_end", "ua"), ("r_end", "o"), ("r_zz", "q"), ("r_end", "da"), ("r_end", "k"), ("first",),
        ("s_end",), ("r_end", "v"), ("r_end", "q"),
    ],
}
Y_FIRST = {0, 1, 2, 3, 6}
DIRECT = {0, 1, 2, 3, 4, 5, 6, 7}
STRAIGHT = {3, 5, 7}


def order_of(Z):
    if Z == 4:
        return FOUR
    most = ("ua", "ub", "da", "db", "o")
    last = ("q", "k", "v")
    plan = {
        "masks": [("w_out_z", 0), ("w_own_y", 0), ("w_own_x", 0), ("tr",), ("tl",), ("tp",), ("tc",)],
        "small": [("w_z", 0), ("w_m", 0), ("w_l", 0), ("gtokp",), ("w_c", 0)],
        ("A", 0): [(step, g) for g in range(1, 5) for step in ("w_out_z", "w_own_y", "w_own_x")],
        ("B", 0): [("o_hi",)] + [(step, g) for step in ("w_z", "w_m") for g in range(1, 5)],
        "merge": [("o_lo",), ("g_o",)] + [("w_l", g) for g in range(1, 5)],
        "out": [("qtail",)] + [("w_c", g) for g in range(1, 5)],
        "dOc": [("g_ol",)],
        "dwu": [("dO",)],
        "sent": [("r_c", g) for g in most],
        "dosT": [("r_1", g) for g in most] + [("g_dO",)],
        ("h", Z - 1): [("r_2", g) for g in most],
        "kv": [("p_z", Z - 2)] + [("r_z", g) for g in most],
        "end": [("gq",)] + [(step, g) for step in ("r_c", "r_1", "r_2", "r_z") for g in last],
    }
    for k in range(1, Z):
        plan.setdefault(("A", k), []).append(("tok_z", k))
    for k in range(Z - 2):
        plan[("t", k + 1)] = [("p_z", k)]
    plan["end"] += [("r_zz", g) for g in most + last] + [("s", k) for k in range(4)] + [("first",), ("s_end",)]
    plan["end"] += [("r_end", g) for g in most + last]
    return plan


def body(
    Z, FK, R, D, NT,
    tok_in, cot_in, wq_in, wo_in, wu_in, wd_in,
    v0, v1, v2, v3, v4, v5, v6, v7, v8, len_ref, sup_ref,
    out_ref, gtok_ref, gqkv_ref, gout_ref, gup_ref, gdown_ref, gsm_ref,
    tokb, tokp, kb, vb, eb, stat, w0, w1, w2, gs, gu, gd,
    cs, cu, cd, xs, xu, xd, ys, yu, yd, zs, zu, zd,
    crf, zrf, par, upb, qt, dot_, qs, dos, ot, mrun, dqt,
    oh, ol, ml, ohr, olr, mlr, gqs, gqr,
    nrm2, hid, acc, gsec, lacc, upg, xq,
    sg, src, srx, sry, srz, tile, tok_ref, cot_ref, act_all, gpre_all, big,
    s_in,
    s_tz, s_tc, r_t, s_tp, r_tp,
    s_wz, r_wz, s_wy, r_wy, s_wx, r_wx, s_wc, r_wc,
    s_gc, r_gc, s_gx, r_gx, s_gy, r_gy, s_gd, r_gd, s_gz, r_gz,
    s_pc, r_pc, s_pz, r_pz, s_y, r_y,
    s_sc, r_sc, s_sx, r_sx, s_sy, r_sy, s_sz, r_sz,
):
    i = lax.axis_index("blk")
    f = lax.axis_index("fsdp")
    c = lax.rem(i, 2)
    y = lax.rem(i // 2, 2)
    z = i // 4
    oc = 1 - c
    oy = 1 - y
    CH = 4 * FK * SLAB * 4
    FF = Z * CH
    NSH = Z * 4 * FK

    def dev(zz, yy, cc, ff):
        return ((zz * 2 + yy) * 2 + cc, ff)

    d_core = dev(z, y, oc, f)
    d_y = dev(z, oy, c, f)

    def zplus(k):
        return lax.rem(z + k, Z)

    def zxor(m):
        out, bit = z, 1
        while bit < Z:
            out = out + bit * ((m // bit) % 2) * (1 - 2 * lax.rem(z // bit, 2))
            bit *= 2
        return out

    def fplus(k):
        return lax.rem(f + k, FK)

    def d_z(zz):
        return dev(zz, y, c, f)

    def d_f(ff):
        return (i, ff)

    def fminus(k):
        return lax.rem(f + FK - k, FK)

    def d_diag(ff):
        return dev(z, oy, c, ff)

    def cp(s, d, ss, rs, to):
        return pltpu.make_async_remote_copy(
            src_ref=s, dst_ref=d, send_sem=ss, recv_sem=rs, device_id=to, device_id_type=MESH
        )

    def push(s, d, ss, rs, to):
        cp(s, d, ss, rs, to).start()

    def got(d, rs):
        cp(d, d, rs, rs, d_core).wait_recv()

    def sent(s, ss):
        cp(s, s, ss, ss, d_core).wait_send()

    arriving = [
        pltpu.make_async_copy(a, b, s_in.at[n])
        for n, (a, b) in enumerate((
            (wq_in, w0.at[z, y, c, f, :, 0 : 3 * D]),
            (tok_in, tokb.at[z, c]),
            (wo_in, w1.at[z, y, c, f, :, 0:D]),
            (wu_in, w1.at[z, y, c, f, :, D : D + FF]),
            (wd_in, w2.at[z, y, c, f]),
            (tok_in, tok_ref),
            (cot_in, cot_ref),
        ))
    ]
    for t in arriving:
        t.start()
    bar = pltpu.get_barrier_semaphore()
    partners = [d_core, d_y] + [d_z(zplus(k)) for k in range(1, Z)]
    partners += [to(fplus(k)) for k in range(1, FK) for to in (d_f, d_diag)]
    for to in partners:
        pl.semaphore_signal(bar, inc=1, device_id=to, device_id_type=MESH)
    tile[...] = jnp.zeros((SLAB, 128), F32)
    for r, v in enumerate((v0, v1, v2, v3, v4, v5, v6, v7, v8)):
        tile[r : r + 1, 0 : v.shape[1]] = v[...].astype(F32)
    w0[z, y, c, f, :, 3 * D : 3 * D + 128] = tile[...].astype(BF16)
    pl.semaphore_wait(bar, len(partners))

    def tok_push(zz, ss_z, to):
        t = tokb.at[zz, c]
        push(t, t, ss_z, r_t.at[zz, c], to)

    def tok_core(zz):
        t = tokb.at[zz, c]
        push(t, t, s_tc, r_t.at[zz, c], d_core)

    def tok_right(zz):
        @pl.when(z < Z - 1)
        def _():
            tok_push(zz, s_tz.at[0, zz], d_z(z + 1))

    def tok_left(zz):
        @pl.when(z > 0)
        def _():
            tok_push(zz, s_tz.at[1, zz], d_z(z - 1))

    def tok_z(k):
        @pl.when(z - k >= 0)
        def _():
            zz = z - k
            got(tokb.at[zz, c], r_t.at[zz, c])
            tok_right(zz)
            tok_core(zz)

        @pl.when(z + k < Z)
        def _():
            zz = z + k
            got(tokb.at[zz, c], r_t.at[zz, c])
            tok_left(zz)
            tok_core(zz)

    HF = FF // 2
    everything = slice(None)
    groups = (
        (w0, everything, everything),
        (w1, everything, slice(0, D + HF)),
        (w1, everything, slice(D + HF, D + FF)),
        (w2, slice(0, 2 * SLAB), everything),
        (w2, slice(2 * SLAB, 4 * SLAB), everything),
    )

    def w_at(g, zz, yy, cc, ff):
        where, rows, cols = groups[g]
        return where.at[zz, yy, cc, ff, rows, cols]

    def w_push_x(g, zz, yy):
        t = w_at(g, zz, yy, c, f)
        for k in range(1, FK):
            push(t, t, s_wx.at[g, k - 1], r_wx.at[g, k - 1], d_f(fplus(k)))

    def w_push_y(g, zz):
        t = w_at(g, zz, y, c, f)
        push(t, t, s_wy.at[g], r_wy.at[g, zz], d_y)

    def w_out_z(g):
        t = w_at(g, z, y, c, f)
        for k in range(1, Z):
            push(t, t, s_wz.at[g], r_wz.at[g, z], d_z(zplus(k)))

    def w_own_y(g):
        w_push_y(g, z)

    def w_own_x(g):
        w_push_x(g, z, y)

    def w_z(g):
        for k in range(1, Z):
            zz = zplus(k)
            got(w_at(g, zz, y, c, f), r_wz.at[g, zz])
            w_push_x(g, zz, y)
            w_push_y(g, zz)

    def w_to_core(g, ff):
        t = w_at(g, everything, everything, c, ff)
        push(t, t, s_wc.at[g], r_wc.at[g], d_core)

    def w_m(g):
        for zz in range(Z):
            got(w_at(g, zz, oy, c, f), r_wy.at[g, zz])
            w_push_x(g, zz, oy)
        w_to_core(g, f)

    def w_l(g):
        for k in range(1, FK):
            got(w_at(g, everything, everything, c, fminus(k)), r_wx.at[g, k - 1])
            w_to_core(g, fminus(k))

    def w_c(g):
        got(w_at(g, everything, everything, oc, everything), r_wc.at[g])

    def w_sent(g):
        sent(w_at(g, slice(0, Z - 1), y, c, f), s_wz.at[g])
        sent(w_at(g, everything, y, c, f), s_wy.at[g])
        for k in range(1, FK):
            sent(w_at(g, everything, everything, c, f), s_wx.at[g, k - 1])
        sent(w_at(g, everything, everything, c, everything), s_wc.at[g])

    store = (gs, gs, gs, gs, gu, gu, gd, gd)
    from_core = (cs, cs, cs, cs, cu, cu, cd, cd)
    from_x = (xs, xs, xs, xs, xu, xu, xd, xd)
    from_y = (ys, ys, ys, ys, yu, yu, yd, yd)
    from_z = (zs, zs, zs, zs, zu, zu, zd, zd)
    lead = (0, 1, 2, 3, 0, 1, 0, 1)
    Q, K, V, O, UA, UB, DA, DB = range(8)
    y_first = {(Q, K, V, O, UA, UB, DA, DB)[t] for t in Y_FIRST}
    direct = {(Q, K, V, O, UA, UB, DA, DB)[t] for t in DIRECT}
    slot = {g: n for n, g in enumerate(sorted(direct))}
    straight = {(Q, K, V, O, UA, UB, DA, DB)[t] for t in STRAIGHT}

    def r_c(g):
        n = lead[g]
        push(store[g].at[n, :, :, oc], from_core[g].at[n], s_gc.at[(g > O) + (g > UB)], r_gc.at[g], d_core)

    def r_push_x(g, whole):
        n = lead[g]
        for k in range(1, FK):
            ff = fplus(k)
            if whole:
                push(store[g].at[n, :, :, c, ff], from_x[g].at[n, f], s_gx.at[g, k - 1], r_gx.at[g, k - 1], d_f(ff))
            else:
                t = store[g].at[n, :, y, c, ff]
                push(t, from_x[g].at[n, f, :, 0], s_gx.at[g, k - 1], r_gx.at[g, k - 1], d_f(ff))

    def r_push_y(g, whole):
        n = lead[g]
        if whole:
            push(store[g].at[n, :, oy, c], from_y[g].at[n], s_gy.at[g], r_gy.at[g], d_y)
        else:
            push(store[g].at[n, :, oy, c, f], from_y[g].at[n, :, 0], s_gy.at[g], r_gy.at[g], d_y)

    def over_z(one):
        def step(zz, carry):
            one(zz)
            return carry

        lax.fori_loop(0, Z, step, 0)

    def r_1(g):
        n = lead[g]
        got(from_core[g].at[n], r_gc.at[g])

        def one(zz):
            t = store[g][n, zz, :, c].astype(F32) + from_core[g][n, zz].astype(F32)
            store[g][n, zz, :, c] = t.astype(BF16)

        over_z(one)
        if g in direct:
            r_push_x(g, False)
            r_push_y(g, False)
            for k in range(1, FK):
                ff = fplus(k)
                t = store[g].at[n, :, oy, c, ff]
                push(t, from_x[g].at[n, f, :, 1], s_gd.at[slot[g], k - 1], r_gd.at[slot[g], k - 1], d_diag(ff))
        elif g in y_first:
            r_push_y(g, True)
        else:
            r_push_x(g, True)

    def r_2(g):
        n = lead[g]
        if g in direct:
            return
        if g in y_first:
            got(from_y[g].at[n], r_gy.at[g])

            def one(zz):
                t = store[g][n, zz, y, c].astype(F32) + from_y[g][n, zz].astype(F32)
                store[g][n, zz, y, c] = t.astype(BF16)

            over_z(one)
            r_push_x(g, False)
        else:
            for k in range(1, FK):
                got(from_x[g].at[n, fminus(k)], r_gx.at[g, k - 1])

            def one(zz):
                t = store[g][n, zz, :, c, f].astype(F32)
                for k in range(1, FK):
                    t = t + from_x[g][n, fplus(k), zz].astype(F32)
                store[g][n, zz, :, c, f] = t.astype(BF16)

            if FK > 1:
                over_z(one)
            r_push_y(g, False)

    def r_z(g):
        n = lead[g]
        if g in direct:
            got(from_y[g].at[n, :, 0], r_gy.at[g])
            for k in range(1, FK):
                got(from_x[g].at[n, fminus(k), :, 0], r_gx.at[g, k - 1])
                got(from_x[g].at[n, fminus(k), :, 1], r_gd.at[slot[g], k - 1])

            def one(zz):
                t = store[g][n, zz, y, c, f].astype(F32) + from_y[g][n, zz, 0].astype(F32)
                for k in range(1, FK):
                    t = t + from_x[g][n, fplus(k), zz, 0].astype(F32) + from_x[g][n, fplus(k), zz, 1].astype(F32)
                store[g][n, zz, y, c, f] = t.astype(BF16)

            over_z(one)
        elif g in y_first:
            for k in range(1, FK):
                got(from_x[g].at[n, fminus(k), :, 0], r_gx.at[g, k - 1])

            def one(zz):
                t = store[g][n, zz, y, c, f].astype(F32)
                for k in range(1, FK):
                    t = t + from_x[g][n, fplus(k), zz, 0].astype(F32)
                store[g][n, zz, y, c, f] = t.astype(BF16)

            if FK > 1:
                over_z(one)
        else:
            got(from_y[g].at[n, :, 0], r_gy.at[g])

            def one(zz):
                t = store[g][n, zz, y, c, f].astype(F32) + from_y[g][n, zz, 0].astype(F32)
                store[g][n, zz, y, c, f] = t.astype(BF16)

            over_z(one)
        if g in straight:
            for k in range(1, Z):
                zz = zplus(k)
                push(store[g].at[n, zz, y, c, f], from_z[g].at[n, z], s_gz.at[g], r_gz.at[g, 0], d_z(zz))
        else:
            r_fold(g, 1)

    def r_fold(g, bit):
        n = lead[g]
        for m in range(bit, Z, 2 * bit):
            push(
                store[g].at[n, zxor(m), y, c, f], from_z[g].at[n, zxor(bit ^ (m - 1))],
                s_gz.at[g], r_gz.at[g, bit.bit_length() - 1], d_z(zxor(bit)),
            )

    def r_zz(g):
        n = lead[g]
        bit = 1
        while g not in straight and 2 * bit < Z:
            got(from_z[g].at[n, 0 : Z // (2 * bit)], r_gz.at[g, bit.bit_length() - 1])
            for m in range(0, Z, 2 * bit):
                zz, at = zxor(m), zxor(m + bit - 1)
                t = store[g][n, zz, y, c, f].astype(F32) + from_z[g][n, at].astype(F32)
                store[g][n, zz, y, c, f] = t.astype(BF16)
            bit *= 2
            r_fold(g, bit)

    def r_end(g):
        n = lead[g]
        t = store[g][n, z, y, c, f].astype(F32)
        if g in straight:
            got(from_z[g].at[n, 0 : Z - 1], r_gz.at[g, 0])
            for k in range(1, Z):
                t = t + from_z[g][n, zplus(k)].astype(F32)
        else:
            at = zxor(Z // 2 - 1)
            got(from_z[g].at[n, at], r_gz.at[g, (Z // 2).bit_length() - 1])
            t = t + from_z[g][n, at].astype(F32)
        if g <= V:
            gqkv_ref[:, g * D : (g + 1) * D] = t
        elif g == O:
            gout_ref[...] = t
        elif g <= UB:
            gup_ref[:, (g - UA) * HF : (g - UA + 1) * HF] = t
        else:
            gdown_ref[(g - DA) * 2 * SLAB : (g - DA + 1) * 2 * SLAB, :] = t
        r_sent(g)

    def r_sent(g):
        n = lead[g]
        for k in range(1, FK):
            ff = fplus(k)
            if g in y_first or g in direct:
                sent(store[g].at[n, :, y, c, ff], s_gx.at[g, k - 1])
            else:
                sent(store[g].at[n, :, :, c, ff], s_gx.at[g, k - 1])
            if g in direct:
                sent(store[g].at[n, :, oy, c, ff], s_gd.at[slot[g], k - 1])
        if g in y_first and g not in direct:
            sent(store[g].at[n, :, oy, c], s_gy.at[g])
        else:
            sent(store[g].at[n, :, oy, c, f], s_gy.at[g])
        sent(store[g].at[n, 0 : Z - 1, y, c, f], s_gz.at[g])

    turns = sorted(range(1, Z), key=lambda m: (m & -m, m)) + [0]

    def plane(n):
        m = jnp.int32(0)
        for k in range(Z - 1):
            m = jnp.where(n == k, turns[k], m)
        return zxor(m)

    def p_sum(m):
        zz = zxor(m)
        got(crf.at[zz], r_pc.at[zz])
        t = tokb[zz, c].astype(F32) + crf[zz].astype(F32)
        bit = 1
        while bit < Z and m % (2 * bit) == 0:
            at = zxor(m + bit - 1)
            got(zrf.at[at], r_pz.at[at])
            t = t + zrf[at].astype(F32)
            bit *= 2
        return t

    def p_z(s):
        m = turns[s]
        bit = m & -m
        zz, at = zxor(m), zxor(bit ^ (m - 1))
        tokb[zz, c] = p_sum(m).astype(BF16)
        push(tokb.at[zz, c], zrf.at[at], s_pz, r_pz.at[at], d_z(zxor(bit)))

    def queries_back():
        push(gqs, gqr, s_y.at[5], r_y.at[5], d_y)

    def sums():
        push(sg.at[0], src, s_sc, r_sc, d_core)

    def sums_core():
        got(src, r_sc)
        sg[1] = sg[0] + src[...]
        for k in range(1, FK):
            push(sg.at[1], srx.at[f], s_sx.at[k - 1], r_sx.at[k - 1], d_f(fplus(k)))

    def sums_x():
        t = sg[1]
        for k in range(1, FK):
            got(srx.at[fminus(k)], r_sx.at[k - 1])
            t = t + srx[fminus(k)]
        sg[2] = t
        push(sg.at[2], sry, s_sy, r_sy, d_y)

    def sums_y():
        got(sry, r_sy)
        sg[3] = sg[2] + sry[...]
        for k in range(1, Z):
            zz = zplus(k)
            push(sg.at[3], srz.at[z], s_sz, r_sz, d_z(zz))

    def sums_z():
        sent(sg.at[0], s_sc)
        for k in range(1, FK):
            sent(sg.at[1], s_sx.at[k - 1])
        sent(sg.at[2], s_sy)
        sent(srz.at[0 : Z - 1], s_sz)
        t = sg[3]
        got(srz.at[0 : Z - 1], r_sz)
        for k in range(1, Z):
            t = t + srz[zplus(k)]
        gsm_ref[...] = t

    def first():
        for n, t in enumerate((gs, gu, gd)):
            sent(t.at[:, :, :, oc], s_gc.at[n])
        sent(tokb.at[:, oc], s_pc)
        sent(tokb.at[0 : Z - 1, c], s_pz)
        sent(dot_.at[:, grows, near_half], s_y.at[4])
        sent(gqs, s_y.at[5])
        got(gqr, r_y.at[5])
        t = p_sum(0) + acc[...] + gqr[...].astype(F32)
        mean, centered, rstd = moments(tok_ref[...].astype(F32))
        gtok_ref[...] = (hid[...] + norm_back(t * par[0:1, :], centered * rstd, rstd)).astype(BF16)


    qrows = slice(HD, HD + SLAB)
    grows = slice(0, HD + SLAB)
    near_half, far_half = slice(0, R), slice(R, 2 * R)

    def far_out():
        push(oh, ohr, s_y.at[0], r_y.at[0], d_y)
        push(ml, mlr, s_y.at[1], r_y.at[1], d_y)

    def far_got():
        got(ohr, r_y.at[0])
        got(mlr, r_y.at[1])

    def back_got():
        got(qt.at[:, qrows, far_half], r_y.at[3])
        got(dot_.at[:, grows, far_half], r_y.at[4])

    events = {
        "tr": lambda: tok_right(z),
        "tl": lambda: tok_left(z),
        "tp": lambda: push(tokb.at[z, c], tokp, s_tp, r_tp, d_y),
        "tc": lambda: tok_core(z),
        "tok_z": tok_z,
        "gtokp": lambda: got(tokp, r_tp),
        "w_out_z": w_out_z, "w_own_y": w_own_y, "w_own_x": w_own_x, "w_z": w_z, "w_m": w_m, "w_l": w_l, "w_c": w_c,
        "o_hi": far_out,
        "o_lo": lambda: push(ol, olr, s_y.at[2], r_y.at[2], d_y),
        "g_o": far_got,
        "g_ol": lambda: got(olr, r_y.at[2]),
        "qtail": lambda: push(qt.at[:, qrows, near_half], qt.at[:, qrows, far_half], s_y.at[3], r_y.at[3], d_y),
        "dO": lambda: push(dot_.at[:, grows, near_half], dot_.at[:, grows, far_half], s_y.at[4], r_y.at[4], d_y),
        "g_dO": back_got,
        "gq": queries_back,
        "r_c": r_c, "r_1": r_1, "r_2": r_2, "r_z": r_z, "r_zz": r_zz, "r_end": r_end,
        "p_z": p_z,
        "first": first,
        "s": lambda k: (sums, sums_core, sums_x, sums_y)[k](),
        "s_end": sums_z,
    }
    chunks = {"q": Q, "k": K, "v": V, "o": O, "ua": UA, "ub": UB, "da": DA, "db": DB}
    plan = order_of(Z)

    def do(stage):
        for name, *which in plan.get(stage, ()):
            events[name](*[chunks.get(t, t) for t in which])

    def run(stage, n):
        for at in range(Z):
            if (stage, at) in plan:
                @pl.when(n == at)
                def _():
                    do((stage, at))

    for t in arriving:
        t.wait()
    do("masks")

    starts, ends, stops = [], [], []
    total = jnp.int32(0)
    for t in range(NT):
        starts.append(total)
        stops.append(total + sup_ref[0, t])
        total = total + len_ref[0, t]
        ends.append(total)

    lane = lax.broadcasted_iota(jnp.int32, (1, 128), 1)
    lane_start = jnp.zeros((1, 128), jnp.int32)
    lane_stop = jnp.zeros((1, 128), jnp.int32)
    for t in range(NT):
        lane_start = jnp.where(lane == t, starts[t], lane_start)
        lane_stop = jnp.where(lane == t, stops[t], lane_stop)
    lane_ones = jnp.where((lane >= NT) & (lane < NT + 3), 1.0, 0.0)

    def mask_of(n):
        pos = (n * 2 + y) * 2 * R + lax.broadcasted_iota(jnp.int32, (2 * R, 128), 0)
        seen = (pos >= lane_start) & (pos < lane_stop)
        extra = jnp.where(lane < NT, jnp.where(seen, 0.0, MASKED), lane_ones)
        return extra.astype(BF16)

    def mask_block(n, carry):
        eb[n] = mask_of(n)
        return carry

    lax.fori_loop(0, Z, mask_block, 0)

    row = lax.broadcasted_iota(jnp.int32, (HD, 2 * R), 0)
    col = lax.broadcasted_iota(jnp.int32, (HD, 2 * R), 1)
    qpos = jnp.where(col < R, i * R + col, ((z * 2 + oy) * 2 + c - 1) * R + col)
    onehot = jnp.zeros((HD, 2 * R), F32)
    for t in range(NT):
        onehot = jnp.where((row == t) & (qpos >= starts[t]) & (qpos < ends[t]), 1.0, onehot)
    for h in range(H):
        qt[h, HD : 2 * HD, :] = onehot.astype(BF16)
        dot_[h, HD + SLAB : 2 * HD, :] = jnp.zeros((HD - SLAB, 2 * R), BF16)
        ot[h] = jnp.zeros((2 * HD, 2 * R), F32)
        mrun[h] = jnp.full((1, 2 * R), MASKED, F32)

    do("small")

    piece = D // NSH
    small = w0[:, :, :, :, :, 3 * D : 3 * D + 128].reshape(NSH * SLAB, 128)
    spread = (
        lax.rem(lax.broadcasted_iota(jnp.int32, (128, D), 1), piece)
        == lax.broadcasted_iota(jnp.int32, (128, D), 0)
    )
    wide = dot_nn(small, spread.astype(BF16))
    mine = (
        lax.broadcasted_iota(jnp.int32, (NSH * SLAB, D), 1) // piece
        == lax.broadcasted_iota(jnp.int32, (NSH * SLAB, D), 0) // SLAB
    )
    wide = jnp.where(mine, wide, 0.0)
    par[...] = jnp.sum(wide.reshape(NSH, SLAB, D), axis=0)
    pick = (
        lax.broadcasted_iota(jnp.int32, (NSH, NSH * SLAB), 1)
        == lax.broadcasted_iota(jnp.int32, (NSH, NSH * SLAB), 0) * SLAB + 8
    )
    ups = dot_nn(pick.astype(BF16), small).astype(BF16)
    spread = (
        lax.rem(lax.broadcasted_iota(jnp.int32, (128, FF), 1), 4 * piece)
        == lax.broadcasted_iota(jnp.int32, (128, FF), 0)
    )
    wide = dot_nn(ups, spread.astype(BF16))
    mine = (
        lax.broadcasted_iota(jnp.int32, (NSH, FF), 1) // (4 * piece)
        == lax.broadcasted_iota(jnp.int32, (NSH, FF), 0)
    )
    upb[...] = col_sum(jnp.where(mine, wide, 0.0))
    ln1g, ln1b = par[0:1, :], par[1:2, :]

    tokens = tok_ref[...].astype(F32)
    mean, centered, rstd = moments(tokens)
    xq[0:R, :] = (centered * rstd * ln1g + ln1b).astype(BF16)
    mean, centered, rstd = moments(tokp[...].astype(F32))
    xq[R : 2 * R, :] = (centered * rstd * ln1g + ln1b).astype(BF16)
    wq = w0[:, :, :, :, :, 0:D].reshape(D, D)
    qscale = HD ** (-0.5) / LN2
    qs[...] = ((dot_nn(xq[...], wq) + par[2:3, :]) * qscale).astype(BF16)
    for h in range(H):
        qt[h, 0:HD, :] = qs[:, h * HD : (h + 1) * HD].T

    def near(s):
        inner = jnp.minimum(z, Z - 1 - z)
        odd = lax.rem(s, 2)
        paired = z + (1 - 2 * odd) * ((s + 1) // 2)
        rest = jnp.where(z < Z - 1 - z, s, Z - 1 - s)
        return jnp.where(s <= 2 * inner, paired, rest)

    def attend(h, keys, values, extra, span):
        cols = slice(h * HD, (h + 1) * HD)
        s = dot_nn(jnp.concatenate([keys[:, cols], extra], axis=1), qt[h, :, span])
        top0 = mrun[h, :, span]
        top = jnp.maximum(top0, jnp.ceil(jnp.max(s, axis=0, keepdims=True)))
        e = jnp.exp2(s - top).astype(BF16)
        grown = dot_tn(jnp.concatenate([values[:, cols], extra], axis=1), e)
        ot[h, :, span] = ot[h, :, span] * jnp.exp2(top0 - top) + grown
        mrun[h, :, span] = top

    def ahead(n, carry):
        zz = near(n)
        run("A", n)
        got(tokb.at[zz, oc], r_t.at[zz, oc])
        mean, centered, rstd = moments(tokb[zz].reshape(2 * R, D).astype(F32))
        stat[zz] = jnp.where(lax.broadcasted_iota(jnp.int32, (2 * R, 128), 1) == 0, mean, rstd)
        x = (centered * rstd * par[0:1, :] + par[1:2, :]).astype(BF16)
        kv = dot_nn(x, w0[:, :, :, :, :, D : 3 * D].reshape(D, 2 * D))
        keys = kv[:, 0:D].astype(BF16)
        values = (kv[:, D : 2 * D] + par[3:4, :]).astype(BF16)
        kb[zz] = keys
        vb[zz] = values
        extra = eb[zz]
        for h in range(H):
            attend(h, keys, values, extra, slice(R, 2 * R))
        return carry

    lax.fori_loop(0, Z, ahead, 0)

    do("osplit")
    for h in range(H):
        t = ot[h, 0:HD, R : 2 * R]
        first_part = t.astype(BF16)
        oh[h] = first_part
        ol[h] = (t - first_part.astype(F32)).astype(BF16)
        ml[h : h + 1, :] = mrun[h, :, R : 2 * R]
        ml[H + h : H + h + 1, :] = ot[h, HD + NT : HD + NT + 1, R : 2 * R]
    def ahead_own(n, carry):
        zz = near(n)
        run("B", n)
        for h in range(H):
            attend(h, kb[zz], vb[zz], eb[zz], slice(0, R))
        return carry

    lax.fori_loop(0, Z, ahead_own, 0)
    do("merge")
    parts = []
    row_tail = lax.broadcasted_iota(jnp.int32, (SLAB, R), 0)
    for h in range(H):
        m_own, m_far = mrun[h, :, 0:R], mlr[h : h + 1, :]
        top = jnp.maximum(m_own, m_far)
        a_own, a_far = jnp.exp2(m_own - top), jnp.exp2(m_far - top)
        total = a_own * ot[h, HD + NT : HD + NT + 1, 0:R] + a_far * mlr[H + h : H + h + 1, :]
        inverse = 1.0 / total
        attended = ot[h, 0:HD, 0:R] * (a_own * inverse) + ohr[h].astype(F32) * (a_far * inverse)
        ot[h, 0:HD, 0:R] = attended
        ot[h, HD : HD + 1, 0:R] = inverse
        ot[h, HD + 1 : HD + 2, 0:R] = a_far * inverse
        parts.append(attended.T.astype(BF16))
        m1, m2, m3 = three_terms(top)
        tail = jnp.where(
            row_tail == NT, -m1,
            jnp.where(row_tail == NT + 1, -m2, jnp.where(row_tail == NT + 2, -m3, onehot[0:SLAB, 0:R])),
        )
        qt[h, HD : HD + SLAB, 0:R] = tail.astype(BF16)
    do("out")
    attn_low = jnp.concatenate(parts, axis=1)
    w_out = w1[:, :, :, :, :, 0:D].reshape(D, D)
    hidden = tokens + (dot_nn(attn_low, w_out) + par[4:5, :])
    hid[...] = hidden
    mean2, centered, rstd2 = moments(hidden)
    n2 = centered * rstd2
    nrm2[...] = (n2 * par[5:6, :] + par[6:7, :]).astype(BF16)
    acc[...] = hidden + par[7:8, :]
    gsec[...] = jnp.zeros((R, D), F32)

    def slope_at(j):
        hh = j // (Z // 2)
        return pl.ds(pl.multiple_of(hh * R, R), R), pl.ds(pl.multiple_of((j - hh * (Z // 2)) * CH, 128), CH)

    def forward(j, carry):
        cols = pl.ds(pl.multiple_of(D + j * CH, 128), CH)
        bcols = pl.ds(pl.multiple_of(j * CH, 128), CH)
        pre = dot_nn(nrm2[...], w1[:, :, :, :, :, cols].reshape(D, CH)) + upb[:, bcols]
        phi = 0.5 * (1.0 + lax.erf(pre * (0.5**0.5)))
        act_all[:, bcols] = (pre * phi).astype(BF16)
        slope = phi + pre * (jnp.exp2(pre * pre * (-0.5 / LN2)) * ((2.0 * math.pi) ** -0.5))
        big[1, *slope_at(j)] = slope
        return carry

    def backward(j, carry):
        cols = pl.ds(pl.multiple_of(D + j * CH, 128), CH)
        bcols = pl.ds(pl.multiple_of(j * CH, 128), CH)
        gpre = (dot_nt(cot_ref[...], w2[j].reshape(CH, D)) * big[1, *slope_at(j)]).astype(BF16)
        gsec[...] += dot_nt(gpre, w1[:, :, :, :, :, cols].reshape(D, CH))
        gpre_all[:, bcols] = gpre
        return carry

    do("ffn")
    lax.fori_loop(0, Z, forward, 0)
    do("ffd")
    lax.fori_loop(0, Z, backward, 0)
    do("ln2")

    g_second = gsec[...]
    n2 = (hid[...] - mean2) * rstd2
    ln2g = par[5:6, :]
    cot32 = cot_ref[...].astype(F32)
    grad_hidden = cot32 + norm_back(g_second * ln2g, n2, rstd2)
    hid[...] = grad_hidden
    g_branch = grad_hidden.astype(BF16)
    do("dOc")
    for h in range(H):
        rows = slice(h * HD, (h + 1) * HD)
        w_head = w1[:, :, :, :, :, 0:D].reshape(D, D)[rows, :]
        ga = dot_nt(w_head, g_branch).astype(BF16).astype(F32)
        low = (ga * ot[h, HD : HD + 1, 0:R]).astype(BF16)
        exact = ot[h, 0:HD, 0:R] + olr[h].astype(F32) * ot[h, HD + 1 : HD + 2, 0:R]
        delta = col_sum(low.astype(F32) * exact)
        d1, d2, d3 = three_terms(delta)
        tail = jnp.where(
            row_tail == NT, -d1, jnp.where(row_tail == NT + 1, -d2, jnp.where(row_tail == NT + 2, -d3, 0.0))
        )
        dot_[h, 0:HD, 0:R] = low
        dot_[h, HD : HD + SLAB, 0:R] = tail.astype(BF16)
        dos[0:R, rows] = low.T

    def g_up(j, carry):
        bcols = pl.ds(pl.multiple_of(j * CH, 128), CH)
        t = dot_tn(nrm2[...], gpre_all[:, bcols]).astype(BF16).reshape(Z, 2, 2, FK, SLAB, CH)
        hh = j // (Z // 2)
        upg[:, bcols] = col_sum(gpre_all[:, bcols].astype(F32))
        gu[hh, :, :, :, :, :, pl.ds(pl.multiple_of((j - hh * (Z // 2)) * CH, 128), CH)] = t
        return carry

    def g_down(j, carry):
        bcols = pl.ds(pl.multiple_of(j * CH, 128), CH)
        acc[...] += dot_nn(act_all[:, bcols], w2[j].reshape(CH, D))
        t = dot_tn(act_all[:, bcols], cot_ref[...]).astype(BF16).reshape(2, 2, FK, 4 * SLAB, D)
        gd[0, j] = t[:, :, :, 0 : 2 * SLAB]
        gd[1, j] = t[:, :, :, 2 * SLAB : 4 * SLAB]
        return carry

    do("dwu")
    lax.fori_loop(0, Z, g_up, 0)
    do("dwd")
    lax.fori_loop(0, Z, g_down, 0)
    out_ref[...] = acc[...].astype(BF16)
    do("dwo")
    gs[O] = dot_tn(attn_low, g_branch).astype(BF16).reshape(Z, 2, 2, FK, SLAB, D)
    zero = jnp.zeros((1, D), F32)
    for r in range(SLAB):
        sg[0, r : r + 1, :] = zero
    sg[0, 4:5, :] = col_sum(g_branch.astype(F32))
    sg[0, 5:6, :] = col_sum(g_second * n2)
    sg[0, 6:7, :] = col_sum(g_second)
    sg[0, 7:8, :] = col_sum(cot32)
    for r in range(FF // D):
        sg[0, 8 + r : 9 + r, :] = upg[:, r * D : (r + 1) * D]

    dqt[...] = jnp.zeros((H, HD, 2 * R), F32)
    lacc[...] = jnp.zeros((3, 8, D), F32)

    def tok_sent():
        @pl.when(z < Z - 1)
        def _():
            for k in range(Z):
                @pl.when(z - k >= 0)
                def _():
                    sent(tokb.at[z - k, c], s_tz.at[0, z - k])

        @pl.when(z > 0)
        def _():
            for k in range(Z):
                @pl.when(z + k < Z)
                def _():
                    sent(tokb.at[z + k, c], s_tz.at[1, z + k])

        sent(tokb.at[:, c], s_tc)
        sent(tokb.at[z, c], s_tp)

    def heads(zz, span):
        keys, values, extra = kb[zz], vb[zz], eb[zz]
        dks, dvs = [], []
        for h in range(H):
            cols = slice(h * HD, (h + 1) * HD)
            s = dot_nn(jnp.concatenate([keys[:, cols], extra], axis=1), qt[h, :, span])
            dp = dot_nn(jnp.concatenate([values[:, cols], extra], axis=1), dot_[h, :, span])
            e = jnp.exp2(s).astype(BF16)
            ds = (e.astype(F32) * dp).astype(BF16)
            dvs.append(dot_nn(e, dos[span, cols]))
            dks.append(dot_nn(ds, qs[span, cols]) * LN2)
            dqt[h, :, span] += dot_tn(keys[:, cols], ds)
        return jnp.concatenate(dks + dvs, axis=1)

    def rest(n, zz, dkv32):
        dkv = dkv32.astype(BF16)
        run("t", n)
        gp = dot_nt(dkv, w0[:, :, :, :, :, D : 3 * D].reshape(D, 2 * D))
        norm = (tokb[zz].reshape(2 * R, D).astype(F32) - stat[zz, :, 0:1]) * stat[zz, :, 1:2]
        tokb[zz] = gp.astype(BF16).reshape(2, R, D)
        push(tokb.at[zz, oc], crf.at[zz], s_pc, r_pc.at[zz], d_core)
        x = (norm * par[0:1, :] + par[1:2, :]).astype(BF16)
        lacc[0] += fold_rows(gp * norm)
        lacc[1] += fold_rows(gp)
        lacc[2] += fold_rows(dkv32[:, D : 2 * D])
        big[0] = jnp.where(n == 0, 0.0, big[0]) + dot_tn(x, dkv)

    def behind_early(n, carry):
        run("e", n)
        big[n] = heads(plane(n), near_half)
        return carry

    def behind_far(n, carry):
        run("h", n)
        zz = plane(n)
        rest(n, zz, big[n] + heads(zz, far_half))
        return carry

    def behind(n, carry):
        run("h", n)
        zz = plane(n)
        rest(n, zz, heads(zz, slice(0, 2 * R)))
        return carry

    do("sent")
    tok_sent()
    for g in range(len(groups)):
        w_sent(g)
    sent(oh, s_y.at[0])
    sent(ml, s_y.at[1])
    sent(ol, s_y.at[2])
    sent(qt.at[:, qrows, near_half], s_y.at[3])
    E = big.shape[0] if Z == 4 else 0
    if E:
        lax.fori_loop(0, E, behind_early, 0)
    do("dosT")
    for h in range(H):
        dos[R : 2 * R, h * HD : (h + 1) * HD] = dot_[h, 0:HD, R : 2 * R].T
    if E:
        lax.fori_loop(0, E, behind_far, 0)
    lax.fori_loop(E, Z, behind, 0)

    do("kv")
    gs[K] = big[0, :, 0:D].astype(BF16).reshape(Z, 2, 2, FK, SLAB, D)
    gs[V] = big[0, :, D : 2 * D].astype(BF16).reshape(Z, 2, 2, FK, SLAB, D)

    def queries():
        dq = jnp.concatenate([(dqt[h] * (HD**-0.5)).T for h in range(H)], axis=1).astype(BF16)
        gs[Q] = dot_tn(xq[...], dq).astype(BF16).reshape(Z, 2, 2, FK, SLAB, D)
        gq = dot_nt(dq, w0[:, :, :, :, :, 0:D].reshape(D, D))
        acc[...] = gq[0:R]
        gqs[...] = gq[R : 2 * R].astype(BF16)
        both = jnp.concatenate([tok_ref[...], tokp[...]], axis=0).astype(F32)
        mean, centered, rstd = moments(both)
        sg[0, 0:1, :] = col_sum(lacc[0]) + col_sum(gq * (centered * rstd))
        sg[0, 1:2, :] = col_sum(lacc[1]) + col_sum(gq)
        sg[0, 2:3, :] = col_sum(dq.astype(F32))
        sg[0, 3:4, :] = col_sum(lacc[2])

    do("q")
    queries()
    do("end")


def layer(Z, FK, R, D, FF, NT, operands):
    vm = lambda shape, dtype: pltpu.VMEM(shape, dtype)
    dma = lambda *shape: pltpu.SemaphoreType.DMA(shape)
    one = pltpu.SemaphoreType.DMA
    others = max(FK - 1, 1)
    lead = (Z, 2, 2, FK)
    slabs = ((SLAB, 3 * D + 128), (SLAB, D + FF), (4 * SLAB, D))
    gslabs = ((4, SLAB, D), (2, SLAB, FF // 2), (2, 2 * SLAB, D))
    scratch = [
        vm((Z, 2, R, D), BF16),
        vm((R, D), BF16),
        vm((Z, 2 * R, D), BF16),
        vm((Z, 2 * R, D), BF16),
        vm((Z, 2 * R, 128), BF16),
        vm((Z, 2 * R, 128), F32),
        *[vm(lead + s, BF16) for s in slabs],
        *[vm((s[0],) + lead + s[1:], BF16) for s in gslabs],
        *[vm((s[0], Z, 2, FK) + s[1:], BF16) for s in gslabs],
        *[vm((s[0], FK, Z, 2) + s[1:] if FK > 1 else (SLAB, 128), BF16) for s in gslabs],
        *[vm((s[0], Z, FK) + s[1:], BF16) for s in gslabs],
        *[vm((s[0], Z) + s[1:], BF16) for s in gslabs],
        vm((Z, R, D), BF16),
        vm((Z, R, D), BF16),
        vm((SLAB, D), F32),
        vm((1, FF), F32),
        vm((H, 2 * HD, 2 * R), BF16),
        vm((H, 2 * HD, 2 * R), BF16),
        vm((2 * R, D), BF16),
        vm((2 * R, D), BF16),
        vm((H, 2 * HD, 2 * R), F32),
        vm((H, 1, 2 * R), F32),
        vm((H, HD, 2 * R), F32),
        vm((H, HD, R), BF16),
        vm((H, HD, R), BF16),
        vm((2 * H, R), F32),
        vm((H, HD, R), BF16),
        vm((H, HD, R), BF16),
        vm((2 * H, R), F32),
        vm((R, D), BF16),
        vm((R, D), BF16),
        vm((R, D), BF16),
        vm((R, D), F32),
        vm((R, D), F32),
        vm((R, D), F32),
        vm((3, 8, D), F32),
        vm((1, FF), F32),
        vm((2 * R, D), BF16),
        vm((4, SLAB, D), F32),
        vm((SLAB, D), F32),
        vm((FK, SLAB, D), F32),
        vm((SLAB, D), F32),
        vm((Z, SLAB, D), F32),
        vm((SLAB, 128), F32),
        vm((R, D), BF16),
        vm((R, D), BF16),
        vm((R, FF), BF16),
        vm((R, FF), BF16),
        vm((3 if Z == 4 else 2, 2 * R, 2 * D), F32),
        dma(7),
        dma(2, Z), one, dma(Z, 2), one, one,
        dma(5), dma(5, Z), dma(5), dma(5, Z), dma(5, others), dma(5, others), dma(5), dma(5),
        dma(3), dma(8), dma(8, others), dma(8, others), dma(8), dma(8),
        dma(max(len(DIRECT), 1), others), dma(max(len(DIRECT), 1), others), dma(8), dma(8, Z.bit_length() - 1),
        one, dma(Z), one, dma(Z), dma(6), dma(6),
        one, one, dma(others), dma(others), one, one, one, one,
    ]
    vmem = pl.BlockSpec(memory_space=pltpu.VMEM)
    smem = pl.BlockSpec(memory_space=pltpu.SMEM)
    shape = jax.ShapeDtypeStruct
    return pl.pallas_call(
        functools.partial(body, Z, FK, R, D, NT),
        out_shape=(
            shape((R, D), BF16),
            shape((R, D), BF16),
            shape((SLAB, 3 * D), F32),
            shape((SLAB, D), F32),
            shape((SLAB, FF), F32),
            shape((4 * SLAB, D), F32),
            shape((SLAB, D), F32),
        ),
        in_specs=[pl.BlockSpec(memory_space=pl.ANY)] * 6 + [vmem] * 9 + [smem] * 2,
        out_specs=[vmem] * 7,
        scratch_shapes=scratch,
        compiler_params=pltpu.CompilerParams(
            collective_id=0, has_side_effects=True, vmem_limit_bytes=63 * 2**20
        ),
        name="layer",
    )(*operands)


def finish(NSH, FK, *refs):
    big_in, small_in, big_out, small_out = refs[0:6], refs[6], refs[7:13], refs[13:22]
    for a, b in zip(big_in, big_out):
        b[...] = a[...]
    at = lax.axis_index("blk") * FK
    if FK > 1:
        at = at + lax.axis_index("fsdp")
    D = small_in.shape[1]
    piece = D // NSH
    lane = lax.broadcasted_iota(jnp.int32, (128, D), 1)
    take = lax.broadcasted_iota(jnp.int32, (128, D), 0)
    full = small_in[...]
    for r in range(8):
        chosen = jnp.where(lane == at * piece + take, full[r : r + 1, :], 0.0)
        small_out[r][...] = jnp.sum(chosen, axis=1).reshape(1, 128)[:, 0:piece]
    FF = D * 4
    total = jnp.zeros((128,), F32)
    for r in range(4):
        chosen = jnp.where(lane + r * D == at * 4 * piece + take, full[8 + r : 9 + r, :], 0.0)
        total = total + jnp.sum(chosen, axis=1)
    small_out[8][...] = total.reshape(1, 128)[:, 0 : 4 * piece]


def hand_over(NSH, FK, FF, results):
    *big, small = results
    D = small.shape[1]
    vmem = pl.BlockSpec(memory_space=pltpu.VMEM)
    shape = jax.ShapeDtypeStruct
    return pl.pallas_call(
        functools.partial(finish, NSH, FK),
        out_shape=(
            *[shape(v.shape, v.dtype) for v in big],
            *[shape((1, D // NSH), F32) for _ in range(8)],
            shape((1, FF // NSH), F32),
        ),
        in_specs=[vmem] * 7,
        out_specs=[vmem] * 15,
        name="finish",
    )(*results)


def shards(
    blocks, fsdp,
    tokens, ln1_gain, ln1_bias, qkv_weight, query_bias, value_bias, out_weight, out_bias,
    ln2_gain, ln2_bias, up_weight, up_bias, down_weight, down_bias,
    table_lengths, support_lengths, cotangent,
):
    R, D = tokens.shape[1:]
    FF = up_weight.shape[1]
    NT = table_lengths.shape[1]
    smalls = (ln1_gain, ln1_bias, query_bias, value_bias, out_bias, ln2_gain, ln2_bias, down_bias, up_bias)
    weights = (qkv_weight, out_weight, up_weight, down_weight)
    inside = qkv_weight.shape[0] == SLAB
    FK = fsdp if inside else 1
    if not inside:
        whole = lambda v: lax.all_gather(v, "fsdp", axis=0, tiled=True)
        smalls = tuple(whole(v) for v in smalls)
        weights = tuple(whole(v) for v in weights)
    results = layer(
        blocks // 4, FK, R, D, FF, NT,
        (tokens[0], cotangent[0], *weights, *[v[None] for v in smalls], table_lengths, support_lengths),
    )
    block_out, grad_tokens, g_qkv, g_out, g_up, g_down, *small_grads = hand_over(
        blocks * FK, FK, FF, results
    )
    small_grads = [v[0] for v in small_grads]
    weight_grads = [g_qkv, g_out, g_up, g_down]
    if not inside:
        spread = lambda v: lax.psum_scatter(v, "fsdp", scatter_dimension=0, tiled=True)
        small_grads = [spread(v) for v in small_grads]
        weight_grads = [spread(v) for v in weight_grads]
    g_ln1g, g_ln1b, g_qb, g_vb, g_ob, g_ln2g, g_ln2b, g_db, g_ub = small_grads
    g_qkv, g_out, g_up, g_down = weight_grads
    return (
        block_out[None], grad_tokens[None], g_ln1g, g_ln1b, g_qkv, g_qb, g_vb, g_out, g_ob,
        g_ln2g, g_ln2b, g_up, g_ub, g_down, g_db,
    )


def solution(mesh):
    both = ("blk", "fsdp")
    vec, mat, rows = P(both), P(both, None), P("fsdp", "blk", None)
    return jax.shard_map(
        functools.partial(shards, mesh.shape["blk"], mesh.shape["fsdp"]),
        mesh=mesh,
        in_specs=(
            rows, vec, vec, mat, vec, vec, mat, vec, vec, vec, mat, vec, mat, vec,
            P("fsdp", None), P("fsdp", None), rows,
        ),
        out_specs=(rows, rows, vec, vec, mat, vec, vec, mat, vec, vec, vec, mat, vec, mat, vec),
        check_vma=False,
    )
```

```python
import functools
import math

import jax
import jax.numpy as jnp
from jax import lax
from jax.experimental import pallas as pl
from jax.experimental.pallas import tpu as pltpu
from jax.sharding import PartitionSpec as P

H = 4
HD = 128
SLAB = 16
EPSILON = 1e-05
MASKED = -1e30
LN2 = math.log(2.0)
MESH = pl.DeviceIdType.MESH
F32 = jnp.float32
BF16 = jnp.bfloat16


def dot_nn(a, b):
    return lax.dot_general(a, b, (((1,), (0,)), ((), ())), preferred_element_type=F32)


def dot_nt(a, b):
    return lax.dot_general(a, b, (((1,), (1,)), ((), ())), preferred_element_type=F32)


def dot_tn(a, b):
    return lax.dot_general(a, b, (((0,), (0,)), ((), ())), preferred_element_type=F32)


def moments(v):
    mean = jnp.mean(v, axis=-1, keepdims=True)
    centered = v - mean
    rstd = lax.rsqrt(jnp.mean(centered * centered, axis=-1, keepdims=True) + EPSILON)
    return mean, centered, rstd


def norm_back(g, n, r):
    return r * (g - jnp.mean(g, axis=-1, keepdims=True) - n * jnp.mean(g * n, axis=-1, keepdims=True))


def three_terms(v):
    first = v.astype(BF16)
    rest = v - first.astype(F32)
    second = rest.astype(BF16)
    third = (rest - second.astype(F32)).astype(BF16)
    return first.astype(F32), second.astype(F32), third.astype(F32)


def col_sum(v):
    return jnp.sum(v, axis=0, keepdims=True)


def fold_rows(v):
    return jnp.sum(v.reshape(v.shape[0] // 8, 8, v.shape[1]), axis=0)


FOUR = {
    "masks": [("w_out_z", 0), ("tc",), ("w_own_y", 0), ("tp",), ("w_own_x", 2), ("w_own_x", 1), ("tl",), ("tr",)],
    "small": [
        ("w_z", 0), ("w_own_x", 4), ("w_out_z", 1), ("tok_z", 1), ("w_m", 0), ("gtokp",), ("w_own_x", 0), ("w_z", 1),
        ("w_own_y", 1), ("w_own_y", 4), ("w_out_z", 2), ("w_own_y", 2), ("w_l", 0), ("w_m", 1), ("tok_z", 2),
        ("w_own_y", 3), ("w_c", 0),
    ],
    ("A", 0): [("w_out_z", 4), ("w_z", 2), ("w_out_z", 3), ("w_own_x", 3)],
    ("A", 2): [("w_l", 1), ("w_m", 2)],
    ("A", 3): [("tok_z", 3), ("w_z", 4)],
    "osplit": [("w_z", 3), ("w_m", 4), ("w_l", 2)],
    ("B", 0): [("o_hi",)],
    ("B", 1): [("w_m", 3)],
    ("B", 3): [("w_c", 1), ("w_l", 4)],
    "merge": [("w_l", 3), ("o_lo",), ("g_o",), ("w_c", 4)],
    "ffn": [("w_c", 2)],
    "ffd": [("w_c", 3)],
    "dOc": [("qtail",), ("g_ol",)],
    "dwu": [("dO",)],
    "sent": [("r_c", "ub")],
    ("e", 2): [("r_1", "ub"), ("r_2", "ub")],
    "dosT": [("r_c", "o"), ("g_dO",)],
    ("h", 0): [("r_c", "db")],
    ("h", 1): [("r_1", "o"), ("r_2", "o"), ("p_z", 0), ("r_c", "da")],
    ("t", 1): [("r_1", "db")],
    ("h", 2): [("r_z", "ub"), ("r_1", "da"), ("r_c", "ua")],
    ("t", 2): [("r_2", "db"), ("p_z", 1), ("r_1", "ua")],
    ("h", 3): [("r_z", "o"), ("r_z", "db")],
    "kv": [("r_2", "da")],
    "q": [("r_c", "v"), ("p_z", 2), ("r_1", "v"), ("r_zz", "ub"), ("r_c", "k"), ("r_2", "ua")],
    "end": [
        ("r_zz", "db"), ("s", 0), ("r_1", "k"), ("s", 1), ("r_c", "q"), ("r_z", "da"), ("r_2", "k"), ("r_z", "ua"),
        ("r_2", "v"), ("r_end", "ub"), ("r_1", "q"), ("r_zz", "o"), ("r_zz", "da"), ("r_end", "db"), ("s", 2),
        ("r_z", "k"), ("r_2", "q"), ("gq",), ("r_z", "v"), ("r_zz", "ua"), ("r_z", "q"), ("r_zz", "k"), ("s", 3),
        ("r_zz", "v"), ("r_end", "ua"), ("r_end", "o"), ("r_zz", "q"), ("r_end", "da"), ("r_end", "k"), ("first",),
        ("s_end",), ("r_end", "v"), ("r_end", "q"),
    ],
}
Y_FIRST = {0, 1, 2, 3, 6}
DIRECT = {0, 1, 2, 3, 4, 5, 6, 7}
STRAIGHT = {3, 5, 7}


def order_of(Z):
    if Z == 4:
        return FOUR
    most = ("ua", "ub", "da", "db", "o")
    last = ("q", "k", "v")
    plan = {
        "masks": [("w_out_z", 0), ("w_own_y", 0), ("w_own_x", 0), ("tr",), ("tl",), ("tp",), ("tc",)],
        "small": [("w_z", 0), ("w_m", 0), ("w_l", 0), ("gtokp",), ("w_c", 0)],
        ("A", 0): [(step, g) for g in range(1, 5) for step in ("w_out_z", "w_own_y", "w_own_x")],
        ("B", 0): [("o_hi",)] + [(step, g) for step in ("w_z", "w_m") for g in range(1, 5)],
        "merge": [("o_lo",), ("g_o",)] + [("w_l", g) for g in range(1, 5)],
        "out": [("qtail",)] + [("w_c", g) for g in range(1, 5)],
        "dOc": [("g_ol",)],
        "dwu": [("dO",)],
        "sent": [("r_c", g) for g in most],
        "dosT": [("r_1", g) for g in most] + [("g_dO",)],
        ("h", Z - 1): [("r_2", g) for g in most],
        "kv": [("p_z", Z - 2)] + [("r_z", g) for g in most],
        "end": [("gq",)] + [(step, g) for step in ("r_c", "r_1", "r_2", "r_z") for g in last],
    }
    for k in range(1, Z):
        plan.setdefault(("A", k), []).append(("tok_z", k))
    for k in range(Z - 2):
        plan[("t", k + 1)] = [("p_z", k)]
    plan["end"] += [("r_zz", g) for g in most + last] + [("s", k) for k in range(4)] + [("first",), ("s_end",)]
    plan["end"] += [("r_end", g) for g in most + last]
    return plan


def body(
    Z, FK, R, D, NT,
    tok_in, cot_in, wq_in, wo_in, wu_in, wd_in,
    v0, v1, v2, v3, v4, v5, v6, v7, v8, len_ref, sup_ref,
    out_ref, gtok_ref, gqkv_ref, gout_ref, gup_ref, gdown_ref, gsm_ref,
    tokb, tokp, kb, vb, eb, stat, w0, w1, w2, gs, gu, gd,
    cs, cu, cd, xs, xu, xd, ys, yu, yd, zs, zu, zd,
    crf, zrf, par, upb, qt, dot_, qs, dos, ot, mrun, dqt,
    oh, ol, ml, ohr, olr, mlr, gqs, gqr,
    nrm2, hid, acc, gsec, lacc, upg, xq,
    sg, src, srx, sry, srz, tile, tok_ref, cot_ref, act_all, gpre_all, big,
    s_in,
    s_tz, s_tc, r_t, s_tp, r_tp,
    s_wz, r_wz, s_wy, r_wy, s_wx, r_wx, s_wc, r_wc,
    s_gc, r_gc, s_gx, r_gx, s_gy, r_gy, s_gd, r_gd, s_gz, r_gz,
    s_pc, r_pc, s_pz, r_pz, s_y, r_y,
    s_sc, r_sc, s_sx, r_sx, s_sy, r_sy, s_sz, r_sz,
):
    i = lax.axis_index("blk")
    f = lax.axis_index("fsdp")
    c = lax.rem(i, 2)
    y = lax.rem(i // 2, 2)
    z = i // 4
    oc = 1 - c
    oy = 1 - y
    CH = 4 * FK * SLAB * 4
    FF = Z * CH
    NSH = Z * 4 * FK

    def dev(zz, yy, cc, ff):
        return ((zz * 2 + yy) * 2 + cc, ff)

    d_core = dev(z, y, oc, f)
    d_y = dev(z, oy, c, f)

    def zplus(k):
        return lax.rem(z + k, Z)

    def zxor(m):
        out, bit = z, 1
        while bit < Z:
            out = out + bit * ((m // bit) % 2) * (1 - 2 * lax.rem(z // bit, 2))
            bit *= 2
        return out

    def fplus(k):
        return lax.rem(f + k, FK)

    def d_z(zz):
        return dev(zz, y, c, f)

    def d_f(ff):
        return (i, ff)

    def fminus(k):
        return lax.rem(f + FK - k, FK)

    def d_diag(ff):
        return dev(z, oy, c, ff)

    def cp(s, d, ss, rs, to):
        return pltpu.make_async_remote_copy(
            src_ref=s, dst_ref=d, send_sem=ss, recv_sem=rs, device_id=to, device_id_type=MESH
        )

    def push(s, d, ss, rs, to):
        cp(s, d, ss, rs, to).start()

    def got(d, rs):
        cp(d, d, rs, rs, d_core).wait_recv()

    def sent(s, ss):
        cp(s, s, ss, ss, d_core).wait_send()

    arriving = [
        pltpu.make_async_copy(a, b, s_in.at[n])
        for n, (a, b) in enumerate((
            (wq_in, w0.at[z, y, c, f, :, 0 : 3 * D]),
            (tok_in, tokb.at[z, c]),
            (wo_in, w1.at[z, y, c, f, :, 0:D]),
            (wu_in, w1.at[z, y, c, f, :, D : D + FF]),
            (wd_in, w2.at[z, y, c, f]),
            (tok_in, tok_ref),
            (cot_in, cot_ref),
        ))
    ]
    for t in arriving:
        t.start()
    bar = pltpu.get_barrier_semaphore()
    partners = [d_core, d_y] + [d_z(zplus(k)) for k in range(1, Z)]
    partners += [to(fplus(k)) for k in range(1, FK) for to in (d_f, d_diag)]
    for to in partners:
        pl.semaphore_signal(bar, inc=1, device_id=to, device_id_type=MESH)
    tile[...] = jnp.zeros((SLAB, 128), F32)
    for r, v in enumerate((v0, v1, v2, v3, v4, v5, v6, v7, v8)):
        tile[r : r + 1, 0 : v.shape[1]] = v[...].astype(F32)
    w0[z, y, c, f, :, 3 * D : 3 * D + 128] = tile[...].astype(BF16)
    pl.semaphore_wait(bar, len(partners))

    def tok_push(zz, ss_z, to):
        t = tokb.at[zz, c]
        push(t, t, ss_z, r_t.at[zz, c], to)

    def tok_core(zz):
        t = tokb.at[zz, c]
        push(t, t, s_tc, r_t.at[zz, c], d_core)

    def tok_right(zz):
        @pl.when(z < Z - 1)
        def _():
            tok_push(zz, s_tz.at[0, zz], d_z(z + 1))

    def tok_left(zz):
        @pl.when(z > 0)
        def _():
            tok_push(zz, s_tz.at[1, zz], d_z(z - 1))

    def tok_z(k):
        @pl.when(z - k >= 0)
        def _():
            zz = z - k
            got(tokb.at[zz, c], r_t.at[zz, c])
            tok_right(zz)
            tok_core(zz)

        @pl.when(z + k < Z)
        def _():
            zz = z + k
            got(tokb.at[zz, c], r_t.at[zz, c])
            tok_left(zz)
            tok_core(zz)

    HF = FF // 2
    everything = slice(None)
    groups = (
        (w0, everything, everything),
        (w1, everything, slice(0, D + HF)),
        (w1, everything, slice(D + HF, D + FF)),
        (w2, slice(0, 2 * SLAB), everything),
        (w2, slice(2 * SLAB, 4 * SLAB), everything),
    )

    def w_at(g, zz, yy, cc, ff):
        where, rows, cols = groups[g]
        return where.at[zz, yy, cc, ff, rows, cols]

    def w_push_x(g, zz, yy):
        t = w_at(g, zz, yy, c, f)
        for k in range(1, FK):
            push(t, t, s_wx.at[g, k - 1], r_wx.at[g, k - 1], d_f(fplus(k)))

    def w_push_y(g, zz):
        t = w_at(g, zz, y, c, f)
        push(t, t, s_wy.at[g], r_wy.at[g, zz], d_y)

    def w_out_z(g):
        t = w_at(g, z, y, c, f)
        for k in range(1, Z):
            push(t, t, s_wz.at[g], r_wz.at[g, z], d_z(zplus(k)))

    def w_own_y(g):
        w_push_y(g, z)

    def w_own_x(g):
        w_push_x(g, z, y)

    def w_z(g):
        for k in range(1, Z):
            zz = zplus(k)
            got(w_at(g, zz, y, c, f), r_wz.at[g, zz])
            w_push_x(g, zz, y)
            w_push_y(g, zz)

    def w_to_core(g, ff):
        t = w_at(g, everything, everything, c, ff)
        push(t, t, s_wc.at[g], r_wc.at[g], d_core)

    def w_m(g):
        for zz in range(Z):
            got(w_at(g, zz, oy, c, f), r_wy.at[g, zz])
            w_push_x(g, zz, oy)
        w_to_core(g, f)

    def w_l(g):
        for k in range(1, FK):
            got(w_at(g, everything, everything, c, fminus(k)), r_wx.at[g, k - 1])
            w_to_core(g, fminus(k))

    def w_c(g):
        got(w_at(g, everything, everything, oc, everything), r_wc.at[g])

    def w_sent(g):
        sent(w_at(g, slice(0, Z - 1), y, c, f), s_wz.at[g])
        sent(w_at(g, everything, y, c, f), s_wy.at[g])
        for k in range(1, FK):
            sent(w_at(g, everything, everything, c, f), s_wx.at[g, k - 1])
        sent(w_at(g, everything, everything, c, everything), s_wc.at[g])

    store = (gs, gs, gs, gs, gu, gu, gd, gd)
    from_core = (cs, cs, cs, cs, cu, cu, cd, cd)
    from_x = (xs, xs, xs, xs, xu, xu, xd, xd)
    from_y = (ys, ys, ys, ys, yu, yu, yd, yd)
    from_z = (zs, zs, zs, zs, zu, zu, zd, zd)
    lead = (0, 1, 2, 3, 0, 1, 0, 1)
    Q, K, V, O, UA, UB, DA, DB = range(8)
    y_first = {(Q, K, V, O, UA, UB, DA, DB)[t] for t in Y_FIRST}
    direct = {(Q, K, V, O, UA, UB, DA, DB)[t] for t in DIRECT}
    slot = {g: n for n, g in enumerate(sorted(direct))}
    straight = {(Q, K, V, O, UA, UB, DA, DB)[t] for t in STRAIGHT}

    def r_c(g):
        n = lead[g]
        push(store[g].at[n, :, :, oc], from_core[g].at[n], s_gc.at[(g > O) + (g > UB)], r_gc.at[g], d_core)

    def r_push_x(g, whole):
        n = lead[g]
        for k in range(1, FK):
            ff = fplus(k)
            if whole:
                push(store[g].at[n, :, :, c, ff], from_x[g].at[n, f], s_gx.at[g, k - 1], r_gx.at[g, k - 1], d_f(ff))
            else:
                t = store[g].at[n, :, y, c, ff]
                push(t, from_x[g].at[n, f, :, 0], s_gx.at[g, k - 1], r_gx.at[g, k - 1], d_f(ff))

    def r_push_y(g, whole):
        n = lead[g]
        if whole:
            push(store[g].at[n, :, oy, c], from_y[g].at[n], s_gy.at[g], r_gy.at[g], d_y)
        else:
            push(store[g].at[n, :, oy, c, f], from_y[g].at[n, :, 0], s_gy.at[g], r_gy.at[g], d_y)

    def over_z(one):
        def step(zz, carry):
            one(zz)
            return carry

        lax.fori_loop(0, Z, step, 0)

    def r_1(g):
        n = lead[g]
        got(from_core[g].at[n], r_gc.at[g])

        def one(zz):
            t = store[g][n, zz, :, c].astype(F32) + from_core[g][n, zz].astype(F32)
            store[g][n, zz, :, c] = t.astype(BF16)

        over_z(one)
        if g in direct:
            r_push_x(g, False)
            r_push_y(g, False)
            for k in range(1, FK):
                ff = fplus(k)
                t = store[g].at[n, :, oy, c, ff]
                push(t, from_x[g].at[n, f, :, 1], s_gd.at[slot[g], k - 1], r_gd.at[slot[g], k - 1], d_diag(ff))
        elif g in y_first:
            r_push_y(g, True)
        else:
            r_push_x(g, True)

    def r_2(g):
        n = lead[g]
        if g in direct:
            return
        if g in y_first:
            got(from_y[g].at[n], r_gy.at[g])

            def one(zz):
                t = store[g][n, zz, y, c].astype(F32) + from_y[g][n, zz].astype(F32)
                store[g][n, zz, y, c] = t.astype(BF16)

            over_z(one)
            r_push_x(g, False)
        else:
            for k in range(1, FK):
                got(from_x[g].at[n, fminus(k)], r_gx.at[g, k - 1])

            def one(zz):
                t = store[g][n, zz, :, c, f].astype(F32)
                for k in range(1, FK):
                    t = t + from_x[g][n, fplus(k), zz].astype(F32)
                store[g][n, zz, :, c, f] = t.astype(BF16)

            if FK > 1:
                over_z(one)
            r_push_y(g, False)

    def r_z(g):
        n = lead[g]
        if g in direct:
            got(from_y[g].at[n, :, 0], r_gy.at[g])
            for k in range(1, FK):
                got(from_x[g].at[n, fminus(k), :, 0], r_gx.at[g, k - 1])
                got(from_x[g].at[n, fminus(k), :, 1], r_gd.at[slot[g], k - 1])

            def one(zz):
                t = store[g][n, zz, y, c, f].astype(F32) + from_y[g][n, zz, 0].astype(F32)
                for k in range(1, FK):
                    t = t + from_x[g][n, fplus(k), zz, 0].astype(F32) + from_x[g][n, fplus(k), zz, 1].astype(F32)
                store[g][n, zz, y, c, f] = t.astype(BF16)

            over_z(one)
        elif g in y_first:
            for k in range(1, FK):
                got(from_x[g].at[n, fminus(k), :, 0], r_gx.at[g, k - 1])

            def one(zz):
                t = store[g][n, zz, y, c, f].astype(F32)
                for k in range(1, FK):
                    t = t + from_x[g][n, fplus(k), zz, 0].astype(F32)
                store[g][n, zz, y, c, f] = t.astype(BF16)

            if FK > 1:
                over_z(one)
        else:
            got(from_y[g].at[n, :, 0], r_gy.at[g])

            def one(zz):
                t = store[g][n, zz, y, c, f].astype(F32) + from_y[g][n, zz, 0].astype(F32)
                store[g][n, zz, y, c, f] = t.astype(BF16)

            over_z(one)
        if g in straight:
            for k in range(1, Z):
                zz = zplus(k)
                push(store[g].at[n, zz, y, c, f], from_z[g].at[n, z], s_gz.at[g], r_gz.at[g, 0], d_z(zz))
        else:
            r_fold(g, 1)

    def r_fold(g, bit):
        n = lead[g]
        for m in range(bit, Z, 2 * bit):
            push(
                store[g].at[n, zxor(m), y, c, f], from_z[g].at[n, zxor(bit ^ (m - 1))],
                s_gz.at[g], r_gz.at[g, bit.bit_length() - 1], d_z(zxor(bit)),
            )

    def r_zz(g):
        n = lead[g]
        bit = 1
        while g not in straight and 2 * bit < Z:
            got(from_z[g].at[n, 0 : Z // (2 * bit)], r_gz.at[g, bit.bit_length() - 1])
            for m in range(0, Z, 2 * bit):
                zz, at = zxor(m), zxor(m + bit - 1)
                t = store[g][n, zz, y, c, f].astype(F32) + from_z[g][n, at].astype(F32)
                store[g][n, zz, y, c, f] = t.astype(BF16)
            bit *= 2
            r_fold(g, bit)

    def r_end(g):
        n = lead[g]
        t = store[g][n, z, y, c, f].astype(F32)
        if g in straight:
            got(from_z[g].at[n, 0 : Z - 1], r_gz.at[g, 0])
            for k in range(1, Z):
                t = t + from_z[g][n, zplus(k)].astype(F32)
        else:
            at = zxor(Z // 2 - 1)
            got(from_z[g].at[n, at], r_gz.at[g, (Z // 2).bit_length() - 1])
            t = t + from_z[g][n, at].astype(F32)
        if g <= V:
            gqkv_ref[:, g * D : (g + 1) * D] = t
        elif g == O:
            gout_ref[...] = t
        elif g <= UB:
            gup_ref[:, (g - UA) * HF : (g - UA + 1) * HF] = t
        else:
            gdown_ref[(g - DA) * 2 * SLAB : (g - DA + 1) * 2 * SLAB, :] = t
        r_sent(g)

    def r_sent(g):
        n = lead[g]
        for k in range(1, FK):
            ff = fplus(k)
            if g in y_first or g in direct:
                sent(store[g].at[n, :, y, c, ff], s_gx.at[g, k - 1])
            else:
                sent(store[g].at[n, :, :, c, ff], s_gx.at[g, k - 1])
            if g in direct:
                sent(store[g].at[n, :, oy, c, ff], s_gd.at[slot[g], k - 1])
        if g in y_first and g not in direct:
            sent(store[g].at[n, :, oy, c], s_gy.at[g])
        else:
            sent(store[g].at[n, :, oy, c, f], s_gy.at[g])
        sent(store[g].at[n, 0 : Z - 1, y, c, f], s_gz.at[g])

    turns = sorted(range(1, Z), key=lambda m: (m & -m, m)) + [0]

    def plane(n):
        m = jnp.int32(0)
        for k in range(Z - 1):
            m = jnp.where(n == k, turns[k], m)
        return zxor(m)

    def p_sum(m):
        zz = zxor(m)
        got(crf.at[zz], r_pc.at[zz])
        t = tokb[zz, c].astype(F32) + crf[zz].astype(F32)
        bit = 1
        while bit < Z and m % (2 * bit) == 0:
            at = zxor(m + bit - 1)
            got(zrf.at[at], r_pz.at[at])
            t = t + zrf[at].astype(F32)
            bit *= 2
        return t

    def p_z(s):
        m = turns[s]
        bit = m & -m
        zz, at = zxor(m), zxor(bit ^ (m - 1))
        tokb[zz, c] = p_sum(m).astype(BF16)
        push(tokb.at[zz, c], zrf.at[at], s_pz, r_pz.at[at], d_z(zxor(bit)))

    def queries_back():
        push(gqs, gqr, s_y.at[5], r_y.at[5], d_y)

    def sums():
        push(sg.at[0], src, s_sc, r_sc, d_core)

    def sums_core():
        got(src, r_sc)
        sg[1] = sg[0] + src[...]
        for k in range(1, FK):
            push(sg.at[1], srx.at[f], s_sx.at[k - 1], r_sx.at[k - 1], d_f(fplus(k)))

    def sums_x():
        t = sg[1]
        for k in range(1, FK):
            got(srx.at[fminus(k)], r_sx.at[k - 1])
            t = t + srx[fminus(k)]
        sg[2] = t
        push(sg.at[2], sry, s_sy, r_sy, d_y)

    def sums_y():
        got(sry, r_sy)
        sg[3] = sg[2] + sry[...]
        for k in range(1, Z):
            zz = zplus(k)
            push(sg.at[3], srz.at[z], s_sz, r_sz, d_z(zz))

    def sums_z():
        sent(sg.at[0], s_sc)
        for k in range(1, FK):
            sent(sg.at[1], s_sx.at[k - 1])
        sent(sg.at[2], s_sy)
        sent(srz.at[0 : Z - 1], s_sz)
        t = sg[3]
        got(srz.at[0 : Z - 1], r_sz)
        for k in range(1, Z):
            t = t + srz[zplus(k)]
        gsm_ref[...] = t

    def first():
        for n, t in enumerate((gs, gu, gd)):
            sent(t.at[:, :, :, oc], s_gc.at[n])
        sent(tokb.at[:, oc], s_pc)
        sent(tokb.at[0 : Z - 1, c], s_pz)
        sent(dot_.at[:, grows, near_half], s_y.at[4])
        sent(gqs, s_y.at[5])
        got(gqr, r_y.at[5])
        t = p_sum(0) + acc[...] + gqr[...].astype(F32)
        mean, centered, rstd = moments(tok_ref[...].astype(F32))
        gtok_ref[...] = (hid[...] + norm_back(t * par[0:1, :], centered * rstd, rstd)).astype(BF16)


    qrows = slice(HD, HD + SLAB)
    grows = slice(0, HD + SLAB)
    near_half, far_half = slice(0, R), slice(R, 2 * R)

    def far_out():
        push(oh, ohr, s_y.at[0], r_y.at[0], d_y)
        push(ml, mlr, s_y.at[1], r_y.at[1], d_y)

    def far_got():
        got(ohr, r_y.at[0])
        got(mlr, r_y.at[1])

    def back_got():
        got(qt.at[:, qrows, far_half], r_y.at[3])
        got(dot_.at[:, grows, far_half], r_y.at[4])

    events = {
        "tr": lambda: tok_right(z),
        "tl": lambda: tok_left(z),
        "tp": lambda: push(tokb.at[z, c], tokp, s_tp, r_tp, d_y),
        "tc": lambda: tok_core(z),
        "tok_z": tok_z,
        "gtokp": lambda: got(tokp, r_tp),
        "w_out_z": w_out_z, "w_own_y": w_own_y, "w_own_x": w_own_x, "w_z": w_z, "w_m": w_m, "w_l": w_l, "w_c": w_c,
        "o_hi": far_out,
        "o_lo": lambda: push(ol, olr, s_y.at[2], r_y.at[2], d_y),
        "g_o": far_got,
        "g_ol": lambda: got(olr, r_y.at[2]),
        "qtail": lambda: push(qt.at[:, qrows, near_half], qt.at[:, qrows, far_half], s_y.at[3], r_y.at[3], d_y),
        "dO": lambda: push(dot_.at[:, grows, near_half], dot_.at[:, grows, far_half], s_y.at[4], r_y.at[4], d_y),
        "g_dO": back_got,
        "gq": queries_back,
        "r_c": r_c, "r_1": r_1, "r_2": r_2, "r_z": r_z, "r_zz": r_zz, "r_end": r_end,
        "p_z": p_z,
        "first": first,
        "s": lambda k: (sums, sums_core, sums_x, sums_y)[k](),
        "s_end": sums_z,
    }
    chunks = {"q": Q, "k": K, "v": V, "o": O, "ua": UA, "ub": UB, "da": DA, "db": DB}
    plan = order_of(Z)

    def do(stage):
        for name, *which in plan.get(stage, ()):
            events[name](*[chunks.get(t, t) for t in which])

    def run(stage, n):
        for at in range(Z):
            if (stage, at) in plan:
                @pl.when(n == at)
                def _():
                    do((stage, at))

    for t in arriving:
        t.wait()
    do("masks")

    starts, ends, stops = [], [], []
    total = jnp.int32(0)
    for t in range(NT):
        starts.append(total)
        stops.append(total + sup_ref[0, t])
        total = total + len_ref[0, t]
        ends.append(total)

    lane = lax.broadcasted_iota(jnp.int32, (1, 128), 1)
    lane_start = jnp.zeros((1, 128), jnp.int32)
    lane_stop = jnp.zeros((1, 128), jnp.int32)
    for t in range(NT):
        lane_start = jnp.where(lane == t, starts[t], lane_start)
        lane_stop = jnp.where(lane == t, stops[t], lane_stop)
    lane_ones = jnp.where((lane >= NT) & (lane < NT + 3), 1.0, 0.0)

    def mask_of(n):
        pos = (n * 2 + y) * 2 * R + lax.broadcasted_iota(jnp.int32, (2 * R, 128), 0)
        seen = (pos >= lane_start) & (pos < lane_stop)
        extra = jnp.where(lane < NT, jnp.where(seen, 0.0, MASKED), lane_ones)
        return extra.astype(BF16)

    def mask_block(n, carry):
        eb[n] = mask_of(n)
        return carry

    lax.fori_loop(0, Z, mask_block, 0)

    row = lax.broadcasted_iota(jnp.int32, (HD, 2 * R), 0)
    col = lax.broadcasted_iota(jnp.int32, (HD, 2 * R), 1)
    qpos = jnp.where(col < R, i * R + col, ((z * 2 + oy) * 2 + c - 1) * R + col)
    onehot = jnp.zeros((HD, 2 * R), F32)
    for t in range(NT):
        onehot = jnp.where((row == t) & (qpos >= starts[t]) & (qpos < ends[t]), 1.0, onehot)
    for h in range(H):
        qt[h, HD : 2 * HD, :] = onehot.astype(BF16)
        dot_[h, HD + SLAB : 2 * HD, :] = jnp.zeros((HD - SLAB, 2 * R), BF16)
        ot[h] = jnp.zeros((2 * HD, 2 * R), F32)
        mrun[h] = jnp.full((1, 2 * R), MASKED, F32)

    do("small")

    piece = D // NSH
    small = w0[:, :, :, :, :, 3 * D : 3 * D + 128].reshape(NSH * SLAB, 128)
    spread = (
        lax.rem(lax.broadcasted_iota(jnp.int32, (128, D), 1), piece)
        == lax.broadcasted_iota(jnp.int32, (128, D), 0)
    )
    wide = dot_nn(small, spread.astype(BF16))
    mine = (
        lax.broadcasted_iota(jnp.int32, (NSH * SLAB, D), 1) // piece
        == lax.broadcasted_iota(jnp.int32, (NSH * SLAB, D), 0) // SLAB
    )
    wide = jnp.where(mine, wide, 0.0)
    par[...] = jnp.sum(wide.reshape(NSH, SLAB, D), axis=0)
    pick = (
        lax.broadcasted_iota(jnp.int32, (NSH, NSH * SLAB), 1)
        == lax.broadcasted_iota(jnp.int32, (NSH, NSH * SLAB), 0) * SLAB + 8
    )
    ups = dot_nn(pick.astype(BF16), small).astype(BF16)
    spread = (
        lax.rem(lax.broadcasted_iota(jnp.int32, (128, FF), 1), 4 * piece)
        == lax.broadcasted_iota(jnp.int32, (128, FF), 0)
    )
    wide = dot_nn(ups, spread.astype(BF16))
    mine = (
        lax.broadcasted_iota(jnp.int32, (NSH, FF), 1) // (4 * piece)
        == lax.broadcasted_iota(jnp.int32, (NSH, FF), 0)
    )
    upb[...] = col_sum(jnp.where(mine, wide, 0.0))
    ln1g, ln1b = par[0:1, :], par[1:2, :]

    tokens = tok_ref[...].astype(F32)
    mean, centered, rstd = moments(tokens)
    xq[0:R, :] = (centered * rstd * ln1g + ln1b).astype(BF16)
    mean, centered, rstd = moments(tokp[...].astype(F32))
    xq[R : 2 * R, :] = (centered * rstd * ln1g + ln1b).astype(BF16)
    wq = w0[:, :, :, :, :, 0:D].reshape(D, D)
    qscale = HD ** (-0.5) / LN2
    qs[...] = ((dot_nn(xq[...], wq) + par[2:3, :]) * qscale).astype(BF16)
    for h in range(H):
        qt[h, 0:HD, :] = qs[:, h * HD : (h + 1) * HD].T

    def near(s):
        inner = jnp.minimum(z, Z - 1 - z)
        odd = lax.rem(s, 2)
        paired = z + (1 - 2 * odd) * ((s + 1) // 2)
        rest = jnp.where(z < Z - 1 - z, s, Z - 1 - s)
        return jnp.where(s <= 2 * inner, paired, rest)

    def attend(h, keys, values, extra, span):
        cols = slice(h * HD, (h + 1) * HD)
        s = dot_nn(jnp.concatenate([keys[:, cols], extra], axis=1), qt[h, :, span])
        top0 = mrun[h, :, span]
        top = jnp.maximum(top0, jnp.ceil(jnp.max(s, axis=0, keepdims=True)))
        e = jnp.exp2(s - top).astype(BF16)
        grown = dot_tn(jnp.concatenate([values[:, cols], extra], axis=1), e)
        ot[h, :, span] = ot[h, :, span] * jnp.exp2(top0 - top) + grown
        mrun[h, :, span] = top

    def ahead(n, carry):
        zz = near(n)
        run("A", n)
        got(tokb.at[zz, oc], r_t.at[zz, oc])
        mean, centered, rstd = moments(tokb[zz].reshape(2 * R, D).astype(F32))
        stat[zz] = jnp.where(lax.broadcasted_iota(jnp.int32, (2 * R, 128), 1) == 0, mean, rstd)
        x = (centered * rstd * par[0:1, :] + par[1:2, :]).astype(BF16)
        kv = dot_nn(x, w0[:, :, :, :, :, D : 3 * D].reshape(D, 2 * D))
        keys = kv[:, 0:D].astype(BF16)
        values = (kv[:, D : 2 * D] + par[3:4, :]).astype(BF16)
        kb[zz] = keys
        vb[zz] = values
        extra = eb[zz]
        for h in range(H):
            attend(h, keys, values, extra, slice(R, 2 * R))
        return carry

    lax.fori_loop(0, Z, ahead, 0)

    do("osplit")
    for h in range(H):
        t = ot[h, 0:HD, R : 2 * R]
        first_part = t.astype(BF16)
        oh[h] = first_part
        ol[h] = (t - first_part.astype(F32)).astype(BF16)
        ml[h : h + 1, :] = mrun[h, :, R : 2 * R]
        ml[H + h : H + h + 1, :] = ot[h, HD + NT : HD + NT + 1, R : 2 * R]
    def ahead_own(n, carry):
        zz = near(n)
        run("B", n)
        for h in range(H):
            attend(h, kb[zz], vb[zz], eb[zz], slice(0, R))
        return carry

    lax.fori_loop(0, Z, ahead_own, 0)
    do("merge")
    parts = []
    row_tail = lax.broadcasted_iota(jnp.int32, (SLAB, R), 0)
    for h in range(H):
        m_own, m_far = mrun[h, :, 0:R], mlr[h : h + 1, :]
        top = jnp.maximum(m_own, m_far)
        a_own, a_far = jnp.exp2(m_own - top), jnp.exp2(m_far - top)
        total = a_own * ot[h, HD + NT : HD + NT + 1, 0:R] + a_far * mlr[H + h : H + h + 1, :]
        inverse = 1.0 / total
        attended = ot[h, 0:HD, 0:R] * (a_own * inverse) + ohr[h].astype(F32) * (a_far * inverse)
        ot[h, 0:HD, 0:R] = attended
        ot[h, HD : HD + 1, 0:R] = inverse
        ot[h, HD + 1 : HD + 2, 0:R] = a_far * inverse
        parts.append(attended.T.astype(BF16))
        m1, m2, m3 = three_terms(top)
        tail = jnp.where(
            row_tail == NT, -m1,
            jnp.where(row_tail == NT + 1, -m2, jnp.where(row_tail == NT + 2, -m3, onehot[0:SLAB, 0:R])),
        )
        qt[h, HD : HD + SLAB, 0:R] = tail.astype(BF16)
    do("out")
    attn_low = jnp.concatenate(parts, axis=1)
    w_out = w1[:, :, :, :, :, 0:D].reshape(D, D)
    hidden = tokens + (dot_nn(attn_low, w_out) + par[4:5, :])
    hid[...] = hidden
    mean2, centered, rstd2 = moments(hidden)
    n2 = centered * rstd2
    nrm2[...] = (n2 * par[5:6, :] + par[6:7, :]).astype(BF16)
    acc[...] = hidden + par[7:8, :]
    gsec[...] = jnp.zeros((R, D), F32)

    def slope_at(j):
        hh = j // (Z // 2)
        return pl.ds(pl.multiple_of(hh * R, R), R), pl.ds(pl.multiple_of((j - hh * (Z // 2)) * CH, 128), CH)

    def forward(j, carry):
        cols = pl.ds(pl.multiple_of(D + j * CH, 128), CH)
        bcols = pl.ds(pl.multiple_of(j * CH, 128), CH)
        pre = dot_nn(nrm2[...], w1[:, :, :, :, :, cols].reshape(D, CH)) + upb[:, bcols]
        phi = 0.5 * (1.0 + lax.erf(pre * (0.5**0.5)))
        act_all[:, bcols] = (pre * phi).astype(BF16)
        slope = phi + pre * (jnp.exp2(pre * pre * (-0.5 / LN2)) * ((2.0 * math.pi) ** -0.5))
        big[1, *slope_at(j)] = slope
        return carry

    def backward(j, carry):
        cols = pl.ds(pl.multiple_of(D + j * CH, 128), CH)
        bcols = pl.ds(pl.multiple_of(j * CH, 128), CH)
        gpre = (dot_nt(cot_ref[...], w2[j].reshape(CH, D)) * big[1, *slope_at(j)]).astype(BF16)
        gsec[...] += dot_nt(gpre, w1[:, :, :, :, :, cols].reshape(D, CH))
        gpre_all[:, bcols] = gpre
        return carry

    do("ffn")
    lax.fori_loop(0, Z, forward, 0)
    do("ffd")
    lax.fori_loop(0, Z, backward, 0)
    do("ln2")

    g_second = gsec[...]
    n2 = (hid[...] - mean2) * rstd2
    ln2g = par[5:6, :]
    cot32 = cot_ref[...].astype(F32)
    grad_hidden = cot32 + norm_back(g_second * ln2g, n2, rstd2)
    hid[...] = grad_hidden
    g_branch = grad_hidden.astype(BF16)
    do("dOc")
    for h in range(H):
        rows = slice(h * HD, (h + 1) * HD)
        w_head = w1[:, :, :, :, :, 0:D].reshape(D, D)[rows, :]
        ga = dot_nt(w_head, g_branch).astype(BF16).astype(F32)
        low = (ga * ot[h, HD : HD + 1, 0:R]).astype(BF16)
        exact = ot[h, 0:HD, 0:R] + olr[h].astype(F32) * ot[h, HD + 1 : HD + 2, 0:R]
        delta = col_sum(low.astype(F32) * exact)
        d1, d2, d3 = three_terms(delta)
        tail = jnp.where(
            row_tail == NT, -d1, jnp.where(row_tail == NT + 1, -d2, jnp.where(row_tail == NT + 2, -d3, 0.0))
        )
        dot_[h, 0:HD, 0:R] = low
        dot_[h, HD : HD + SLAB, 0:R] = tail.astype(BF16)
        dos[0:R, rows] = low.T

    def g_up(j, carry):
        bcols = pl.ds(pl.multiple_of(j * CH, 128), CH)
        t = dot_tn(nrm2[...], gpre_all[:, bcols]).astype(BF16).reshape(Z, 2, 2, FK, SLAB, CH)
        hh = j // (Z // 2)
        upg[:, bcols] = col_sum(gpre_all[:, bcols].astype(F32))
        gu[hh, :, :, :, :, :, pl.ds(pl.multiple_of((j - hh * (Z // 2)) * CH, 128), CH)] = t
        return carry

    def g_down(j, carry):
        bcols = pl.ds(pl.multiple_of(j * CH, 128), CH)
        acc[...] += dot_nn(act_all[:, bcols], w2[j].reshape(CH, D))
        t = dot_tn(act_all[:, bcols], cot_ref[...]).astype(BF16).reshape(2, 2, FK, 4 * SLAB, D)
        gd[0, j] = t[:, :, :, 0 : 2 * SLAB]
        gd[1, j] = t[:, :, :, 2 * SLAB : 4 * SLAB]
        return carry

    do("dwu")
    lax.fori_loop(0, Z, g_up, 0)
    do("dwd")
    lax.fori_loop(0, Z, g_down, 0)
    out_ref[...] = acc[...].astype(BF16)
    do("dwo")
    gs[O] = dot_tn(attn_low, g_branch).astype(BF16).reshape(Z, 2, 2, FK, SLAB, D)
    zero = jnp.zeros((1, D), F32)
    for r in range(SLAB):
        sg[0, r : r + 1, :] = zero
    sg[0, 4:5, :] = col_sum(g_branch.astype(F32))
    sg[0, 5:6, :] = col_sum(g_second * n2)
    sg[0, 6:7, :] = col_sum(g_second)
    sg[0, 7:8, :] = col_sum(cot32)
    for r in range(FF // D):
        sg[0, 8 + r : 9 + r, :] = upg[:, r * D : (r + 1) * D]

    dqt[...] = jnp.zeros((H, HD, 2 * R), F32)
    lacc[...] = jnp.zeros((3, 8, D), F32)

    def tok_sent():
        @pl.when(z < Z - 1)
        def _():
            for k in range(Z):
                @pl.when(z - k >= 0)
                def _():
                    sent(tokb.at[z - k, c], s_tz.at[0, z - k])

        @pl.when(z > 0)
        def _():
            for k in range(Z):
                @pl.when(z + k < Z)
                def _():
                    sent(tokb.at[z + k, c], s_tz.at[1, z + k])

        sent(tokb.at[:, c], s_tc)
        sent(tokb.at[z, c], s_tp)

    def heads(zz, span):
        keys, values, extra = kb[zz], vb[zz], eb[zz]
        dks, dvs = [], []
        for h in range(H):
            cols = slice(h * HD, (h + 1) * HD)
            s = dot_nn(jnp.concatenate([keys[:, cols], extra], axis=1), qt[h, :, span])
            dp = dot_nn(jnp.concatenate([values[:, cols], extra], axis=1), dot_[h, :, span])
            e = jnp.exp2(s).astype(BF16)
            ds = (e.astype(F32) * dp).astype(BF16)
            dvs.append(dot_nn(e, dos[span, cols]))
            dks.append(dot_nn(ds, qs[span, cols]) * LN2)
            dqt[h, :, span] += dot_tn(keys[:, cols], ds)
        return jnp.concatenate(dks + dvs, axis=1)

    def rest(n, zz, dkv32):
        dkv = dkv32.astype(BF16)
        run("t", n)
        gp = dot_nt(dkv, w0[:, :, :, :, :, D : 3 * D].reshape(D, 2 * D))
        norm = (tokb[zz].reshape(2 * R, D).astype(F32) - stat[zz, :, 0:1]) * stat[zz, :, 1:2]
        tokb[zz] = gp.astype(BF16).reshape(2, R, D)
        push(tokb.at[zz, oc], crf.at[zz], s_pc, r_pc.at[zz], d_core)
        x = (norm * par[0:1, :] + par[1:2, :]).astype(BF16)
        lacc[0] += fold_rows(gp * norm)
        lacc[1] += fold_rows(gp)
        lacc[2] += fold_rows(dkv32[:, D : 2 * D])
        big[0] = jnp.where(n == 0, 0.0, big[0]) + dot_tn(x, dkv)

    def behind_early(n, carry):
        run("e", n)
        big[n] = heads(plane(n), near_half)
        return carry

    def behind_far(n, carry):
        run("h", n)
        zz = plane(n)
        rest(n, zz, big[n] + heads(zz, far_half))
        return carry

    def behind(n, carry):
        run("h", n)
        zz = plane(n)
        rest(n, zz, heads(zz, slice(0, 2 * R)))
        return carry

    do("sent")
    tok_sent()
    for g in range(len(groups)):
        w_sent(g)
    sent(oh, s_y.at[0])
    sent(ml, s_y.at[1])
    sent(ol, s_y.at[2])
    sent(qt.at[:, qrows, near_half], s_y.at[3])
    E = big.shape[0] if Z == 4 else 0
    if E:
        lax.fori_loop(0, E, behind_early, 0)
    do("dosT")
    for h in range(H):
        dos[R : 2 * R, h * HD : (h + 1) * HD] = dot_[h, 0:HD, R : 2 * R].T
    if E:
        lax.fori_loop(0, E, behind_far, 0)
    lax.fori_loop(E, Z, behind, 0)

    do("kv")
    gs[K] = big[0, :, 0:D].astype(BF16).reshape(Z, 2, 2, FK, SLAB, D)
    gs[V] = big[0, :, D : 2 * D].astype(BF16).reshape(Z, 2, 2, FK, SLAB, D)

    def queries():
        dq = jnp.concatenate([(dqt[h] * (HD**-0.5)).T for h in range(H)], axis=1).astype(BF16)
        gs[Q] = dot_tn(xq[...], dq).astype(BF16).reshape(Z, 2, 2, FK, SLAB, D)
        gq = dot_nt(dq, w0[:, :, :, :, :, 0:D].reshape(D, D))
        acc[...] = gq[0:R]
        gqs[...] = gq[R : 2 * R].astype(BF16)
        both = jnp.concatenate([tok_ref[...], tokp[...]], axis=0).astype(F32)
        mean, centered, rstd = moments(both)
        sg[0, 0:1, :] = col_sum(lacc[0]) + col_sum(gq * (centered * rstd))
        sg[0, 1:2, :] = col_sum(lacc[1]) + col_sum(gq)
        sg[0, 2:3, :] = col_sum(dq.astype(F32))
        sg[0, 3:4, :] = col_sum(lacc[2])

    do("q")
    queries()
    do("end")


def layer(Z, FK, R, D, FF, NT, operands):
    vm = lambda shape, dtype: pltpu.VMEM(shape, dtype)
    dma = lambda *shape: pltpu.SemaphoreType.DMA(shape)
    one = pltpu.SemaphoreType.DMA
    others = max(FK - 1, 1)
    lead = (Z, 2, 2, FK)
    slabs = ((SLAB, 3 * D + 128), (SLAB, D + FF), (4 * SLAB, D))
    gslabs = ((4, SLAB, D), (2, SLAB, FF // 2), (2, 2 * SLAB, D))
    scratch = [
        vm((Z, 2, R, D), BF16),
        vm((R, D), BF16),
        vm((Z, 2 * R, D), BF16),
        vm((Z, 2 * R, D), BF16),
        vm((Z, 2 * R, 128), BF16),
        vm((Z, 2 * R, 128), F32),
        *[vm(lead + s, BF16) for s in slabs],
        *[vm((s[0],) + lead + s[1:], BF16) for s in gslabs],
        *[vm((s[0], Z, 2, FK) + s[1:], BF16) for s in gslabs],
        *[vm((s[0], FK, Z, 2) + s[1:] if FK > 1 else (SLAB, 128), BF16) for s in gslabs],
        *[vm((s[0], Z, FK) + s[1:], BF16) for s in gslabs],
        *[vm((s[0], Z) + s[1:], BF16) for s in gslabs],
        vm((Z, R, D), BF16),
        vm((Z, R, D), BF16),
        vm((SLAB, D), F32),
        vm((1, FF), F32),
        vm((H, 2 * HD, 2 * R), BF16),
        vm((H, 2 * HD, 2 * R), BF16),
        vm((2 * R, D), BF16),
        vm((2 * R, D), BF16),
        vm((H, 2 * HD, 2 * R), F32),
        vm((H, 1, 2 * R), F32),
        vm((H, HD, 2 * R), F32),
        vm((H, HD, R), BF16),
        vm((H, HD, R), BF16),
        vm((2 * H, R), F32),
        vm((H, HD, R), BF16),
        vm((H, HD, R), BF16),
        vm((2 * H, R), F32),
        vm((R, D), BF16),
        vm((R, D), BF16),
        vm((R, D), BF16),
        vm((R, D), F32),
        vm((R, D), F32),
        vm((R, D), F32),
        vm((3, 8, D), F32),
        vm((1, FF), F32),
        vm((2 * R, D), BF16),
        vm((4, SLAB, D), F32),
        vm((SLAB, D), F32),
        vm((FK, SLAB, D), F32),
        vm((SLAB, D), F32),
        vm((Z, SLAB, D), F32),
        vm((SLAB, 128), F32),
        vm((R, D), BF16),
        vm((R, D), BF16),
        vm((R, FF), BF16),
        vm((R, FF), BF16),
        vm((3 if Z == 4 else 2, 2 * R, 2 * D), F32),
        dma(7),
        dma(2, Z), one, dma(Z, 2), one, one,
        dma(5), dma(5, Z), dma(5), dma(5, Z), dma(5, others), dma(5, others), dma(5), dma(5),
        dma(3), dma(8), dma(8, others), dma(8, others), dma(8), dma(8),
        dma(max(len(DIRECT), 1), others), dma(max(len(DIRECT), 1), others), dma(8), dma(8, Z.bit_length() - 1),
        one, dma(Z), one, dma(Z), dma(6), dma(6),
        one, one, dma(others), dma(others), one, one, one, one,
    ]
    vmem = pl.BlockSpec(memory_space=pltpu.VMEM)
    smem = pl.BlockSpec(memory_space=pltpu.SMEM)
    shape = jax.ShapeDtypeStruct
    return pl.pallas_call(
        functools.partial(body, Z, FK, R, D, NT),
        out_shape=(
            pltpu.VMEM((R, D), BF16),
            pltpu.VMEM((R, D), BF16),
            pltpu.VMEM((SLAB, 3 * D), F32),
            pltpu.VMEM((SLAB, D), F32),
            pltpu.VMEM((SLAB, FF), F32),
            pltpu.VMEM((4 * SLAB, D), F32),
            pltpu.VMEM((SLAB, D), F32),
        ),
        in_specs=[pl.BlockSpec(memory_space=pl.ANY)] * 6 + [vmem] * 9 + [smem] * 2,
        out_specs=[vmem] * 7,
        scratch_shapes=scratch,
        compiler_params=pltpu.CompilerParams(
            collective_id=0, has_side_effects=True, vmem_limit_bytes=63 * 2**20
        ),
        name="layer",
    )(*operands)


def finish(NSH, FK, *refs):
    big_in, small_in, big_out, small_out = refs[0:6], refs[6], refs[7:13], refs[13:22]
    for a, b in zip(big_in, big_out):
        b[...] = a[...]
    at = lax.axis_index("blk") * FK
    if FK > 1:
        at = at + lax.axis_index("fsdp")
    D = small_in.shape[1]
    piece = D // NSH
    lane = lax.broadcasted_iota(jnp.int32, (128, D), 1)
    take = lax.broadcasted_iota(jnp.int32, (128, D), 0)
    full = small_in[...]
    for r in range(8):
        chosen = jnp.where(lane == at * piece + take, full[r : r + 1, :], 0.0)
        small_out[r][...] = jnp.sum(chosen, axis=1).reshape(1, 128)[:, 0:piece]
    FF = D * 4
    total = jnp.zeros((128,), F32)
    for r in range(4):
        chosen = jnp.where(lane + r * D == at * 4 * piece + take, full[8 + r : 9 + r, :], 0.0)
        total = total + jnp.sum(chosen, axis=1)
    small_out[8][...] = total.reshape(1, 128)[:, 0 : 4 * piece]


def hand_over(NSH, FK, FF, results):
    *big, small = results
    D = small.shape[1]
    vmem = pl.BlockSpec(memory_space=pltpu.VMEM)
    shape = jax.ShapeDtypeStruct
    return pl.pallas_call(
        functools.partial(finish, NSH, FK),
        out_shape=(
            *[shape(v.shape, v.dtype) for v in big],
            *[shape((1, D // NSH), F32) for _ in range(8)],
            shape((1, FF // NSH), F32),
        ),
        in_specs=[vmem] * 7,
        out_specs=[vmem] * 15,
        name="finish",
    )(*[pltpu.with_memory_space_constraint(v, pltpu.VMEM) for v in results])


def shards(
    blocks, fsdp,
    tokens, ln1_gain, ln1_bias, qkv_weight, query_bias, value_bias, out_weight, out_bias,
    ln2_gain, ln2_bias, up_weight, up_bias, down_weight, down_bias,
    table_lengths, support_lengths, cotangent,
):
    R, D = tokens.shape[1:]
    FF = up_weight.shape[1]
    NT = table_lengths.shape[1]
    smalls = (ln1_gain, ln1_bias, query_bias, value_bias, out_bias, ln2_gain, ln2_bias, down_bias, up_bias)
    weights = (qkv_weight, out_weight, up_weight, down_weight)
    inside = qkv_weight.shape[0] == SLAB
    FK = fsdp if inside else 1
    if not inside:
        whole = lambda v: lax.all_gather(v, "fsdp", axis=0, tiled=True)
        smalls = tuple(whole(v) for v in smalls)
        weights = tuple(whole(v) for v in weights)
    results = layer(
        blocks // 4, FK, R, D, FF, NT,
        (tokens[0], cotangent[0], *weights, *[v[None] for v in smalls], table_lengths, support_lengths),
    )
    block_out, grad_tokens, g_qkv, g_out, g_up, g_down, *small_grads = hand_over(
        blocks * FK, FK, FF, results
    )
    small_grads = [v[0] for v in small_grads]
    weight_grads = [g_qkv, g_out, g_up, g_down]
    if not inside:
        spread = lambda v: lax.psum_scatter(v, "fsdp", scatter_dimension=0, tiled=True)
        small_grads = [spread(v) for v in small_grads]
        weight_grads = [spread(v) for v in weight_grads]
    g_ln1g, g_ln1b, g_qb, g_vb, g_ob, g_ln2g, g_ln2b, g_db, g_ub = small_grads
    g_qkv, g_out, g_up, g_down = weight_grads
    return (
        block_out[None], grad_tokens[None], g_ln1g, g_ln1b, g_qkv, g_qb, g_vb, g_out, g_ob,
        g_ln2g, g_ln2b, g_up, g_ub, g_down, g_db,
    )


def solution(mesh):
    both = ("blk", "fsdp")
    vec, mat, rows = P(both), P(both, None), P("fsdp", "blk", None)
    return jax.shard_map(
        functools.partial(shards, mesh.shape["blk"], mesh.shape["fsdp"]),
        mesh=mesh,
        in_specs=(
            rows, vec, vec, mat, vec, vec, mat, vec, vec, vec, mat, vec, mat, vec,
            P("fsdp", None), P("fsdp", None), rows,
        ),
        out_specs=(rows, rows, vec, vec, mat, vec, vec, mat, vec, vec, vec, mat, vec, mat, vec),
        check_vma=False,
    )
```

```python
import functools
import math

import jax
import jax.numpy as jnp
from jax import lax
from jax.experimental import pallas as pl
from jax.experimental.pallas import tpu as pltpu
from jax.sharding import PartitionSpec as P

H = 4
HD = 128
SLAB = 16
EPSILON = 1e-05
MASKED = -1e30
LN2 = math.log(2.0)
MESH = pl.DeviceIdType.MESH
F32 = jnp.float32
BF16 = jnp.bfloat16


def dot_nn(a, b):
    return lax.dot_general(a, b, (((1,), (0,)), ((), ())), preferred_element_type=F32)


def dot_nt(a, b):
    return lax.dot_general(a, b, (((1,), (1,)), ((), ())), preferred_element_type=F32)


def dot_tn(a, b):
    return lax.dot_general(a, b, (((0,), (0,)), ((), ())), preferred_element_type=F32)


def moments(v):
    mean = jnp.mean(v, axis=-1, keepdims=True)
    centered = v - mean
    rstd = lax.rsqrt(jnp.mean(centered * centered, axis=-1, keepdims=True) + EPSILON)
    return mean, centered, rstd


def norm_back(g, n, r):
    return r * (g - jnp.mean(g, axis=-1, keepdims=True) - n * jnp.mean(g * n, axis=-1, keepdims=True))


def three_terms(v):
    first = v.astype(BF16)
    rest = v - first.astype(F32)
    second = rest.astype(BF16)
    third = (rest - second.astype(F32)).astype(BF16)
    return first.astype(F32), second.astype(F32), third.astype(F32)


def col_sum(v):
    return jnp.sum(v, axis=0, keepdims=True)


def fold_rows(v):
    return jnp.sum(v.reshape(v.shape[0] // 8, 8, v.shape[1]), axis=0)


FOUR = {
    "masks": [
        ("w_out_z", 0), ("w_own_x", 2), ("w_own_y", 0), ("tr",), ("w_out_z", 1), ("tl",), ("tp",), ("w_out_z", 2),
    ],
    "small": [
        ("w_z", 0), ("tc",), ("w_own_x", 0), ("w_m", 0), ("w_own_y", 1), ("w_own_y", 4), ("gtokp",), ("w_z", 1),
        ("tok_z", 1), ("w_l", 0), ("w_m", 1), ("w_z", 2), ("w_own_y", 3), ("w_own_y", 2), ("w_c", 0), ("w_own_x", 3),
        ("w_out_z", 4),
    ],
    ("A", 0): [("w_own_x", 1), ("w_own_x", 4), ("tok_z", 2)],
    ("A", 1): [("w_z", 4), ("w_m", 2), ("w_out_z", 3)],
    ("A", 3): [("tok_z", 3), ("w_l", 1), ("w_m", 4), ("w_z", 3)],
    ("B", 0): [("o_hi",)],
    ("B", 1): [("o_lo",)],
    ("B", 2): [("w_m", 3), ("w_l", 4), ("w_l", 2)],
    "merge": [("w_c", 2), ("w_c", 1), ("w_l", 3), ("w_c", 4), ("g_o",)],
    "out": [("qtail",)],
    "ffn": [("w_c", 3)],
    "dOc": [("g_ol",)],
    "dwu": [("dO",)],
    "dwd": [("r_c", "ub")],
    "sent": [("r_1", "ub"), ("r_c", "db")],
    "dosT": [("r_1", "db"), ("g_dO",), ("r_2", "ub")],
    ("h", 1): [("r_c", "ua")],
    ("t", 1): [("r_2", "db"), ("r_c", "o"), ("r_z", "ub")],
    ("h", 2): [("r_zz", "ub"), ("r_1", "ua"), ("p_z", 1)],
    ("t", 2): [("r_c", "da"), ("r_z", "db"), ("p_z", 0)],
    ("h", 3): [("r_1", "da"), ("r_1", "o"), ("r_zz", "db")],
    "kv": [("r_2", "ua"), ("p_z", 2)],
    "q": [("r_2", "da"), ("r_c", "v"), ("r_c", "k")],
    "end": [
        ("r_1", "v"), ("r_1", "k"), ("r_2", "o"), ("r_c", "q"), ("r_z", "ua"), ("r_1", "q"), ("s", 0), ("r_z", "da"),
        ("r_end", "db"), ("s", 1), ("r_2", "v"), ("r_z", "o"), ("r_zz", "o"), ("r_2", "k"), ("r_zz", "da"), ("s", 2),
        ("r_2", "q"), ("r_end", "ub"), ("r_z", "k"), ("gq",), ("r_zz", "ua"), ("r_z", "v"), ("r_z", "q"), ("s", 3),
        ("r_zz", "v"), ("r_end", "ua"), ("r_zz", "k"), ("r_zz", "q"), ("r_end", "da"), ("r_end", "o"), ("first",),
        ("r_end", "v"), ("r_end", "k"), ("s_end",), ("r_end", "q"),
    ],
}
Y_FIRST = {0, 2, 5, 6, 7}
DIRECT = {0, 1, 3, 4, 5, 6, 7}
STRAIGHT = {3, 5, 6, 7}


def order_of(Z):
    if Z == 4:
        return FOUR
    most = ("ua", "ub", "da", "db", "o")
    last = ("q", "k", "v")
    plan = {
        "masks": [("w_out_z", 0), ("w_own_y", 0), ("w_own_x", 0), ("tr",), ("tl",), ("tp",), ("tc",)],
        "small": [("w_z", 0), ("w_m", 0), ("w_l", 0), ("gtokp",), ("w_c", 0)],
        ("A", 0): [(step, g) for g in range(1, 5) for step in ("w_out_z", "w_own_y", "w_own_x")],
        ("B", 0): [("o_hi",)] + [(step, g) for step in ("w_z", "w_m") for g in range(1, 5)],
        "merge": [("o_lo",), ("g_o",)] + [("w_l", g) for g in range(1, 5)],
        "out": [("qtail",)] + [("w_c", g) for g in range(1, 5)],
        "dOc": [("g_ol",)],
        "dwu": [("dO",)],
        "sent": [("r_c", g) for g in most],
        "dosT": [("r_1", g) for g in most] + [("g_dO",)],
        ("h", Z - 1): [("r_2", g) for g in most],
        "kv": [("p_z", Z - 2)] + [("r_z", g) for g in most],
        "end": [("gq",)] + [(step, g) for step in ("r_c", "r_1", "r_2", "r_z") for g in last],
    }
    for k in range(1, Z):
        plan.setdefault(("A", k), []).append(("tok_z", k))
    for k in range(Z - 2):
        plan[("t", k + 1)] = [("p_z", k)]
    plan["end"] += [("r_zz", g) for g in most + last] + [("s", k) for k in range(4)] + [("first",), ("s_end",)]
    plan["end"] += [("r_end", g) for g in most + last]
    return plan


def body(
    Z, FK, R, D, NT,
    tok_in, cot_in, wq_in, wo_in, wu_in, wd_in,
    v0, v1, v2, v3, v4, v5, v6, v7, v8, len_ref, sup_ref,
    out_ref, gtok_ref, gqkv_ref, gout_ref, gup_ref, gdown_ref, gsm_ref,
    tokb, tokp, kb, vb, eb, stat, w0, w1, w2, gs, gu, gd,
    cs, cu, cd, xs, xu, xd, ys, yu, yd, zs, zu, zd,
    crf, zrf, par, upb, qt, dot_, qs, dos, ot, mrun, dqt,
    oh, ol, ml, ohr, olr, mlr, gqs, gqr,
    nrm2, hid, acc, gsec, lacc, upg, xq,
    sg, src, srx, sry, srz, tile, tok_ref, cot_ref, act_all, gpre_all, big,
    s_in,
    s_tz, s_tc, r_t, s_tp, r_tp,
    s_wz, r_wz, s_wy, r_wy, s_wx, r_wx, s_wc, r_wc,
    s_gc, r_gc, s_gx, r_gx, s_gy, r_gy, s_gd, r_gd, s_gz, r_gz,
    s_pc, r_pc, s_pz, r_pz, s_y, r_y,
    s_sc, r_sc, s_sx, r_sx, s_sy, r_sy, s_sz, r_sz,
):
    i = lax.axis_index("blk")
    f = lax.axis_index("fsdp")
    c = lax.rem(i, 2)
    y = lax.rem(i // 2, 2)
    z = i // 4
    oc = 1 - c
    oy = 1 - y
    CH = 4 * FK * SLAB * 4
    FF = Z * CH
    NSH = Z * 4 * FK

    def dev(zz, yy, cc, ff):
        return ((zz * 2 + yy) * 2 + cc, ff)

    d_core = dev(z, y, oc, f)
    d_y = dev(z, oy, c, f)

    def zplus(k):
        return lax.rem(z + k, Z)

    def zxor(m):
        out, bit = z, 1
        while bit < Z:
            out = out + bit * ((m // bit) % 2) * (1 - 2 * lax.rem(z // bit, 2))
            bit *= 2
        return out

    def fplus(k):
        return lax.rem(f + k, FK)

    def d_z(zz):
        return dev(zz, y, c, f)

    def d_f(ff):
        return (i, ff)

    def fminus(k):
        return lax.rem(f + FK - k, FK)

    def d_diag(ff):
        return dev(z, oy, c, ff)

    def cp(s, d, ss, rs, to):
        return pltpu.make_async_remote_copy(
            src_ref=s, dst_ref=d, send_sem=ss, recv_sem=rs, device_id=to, device_id_type=MESH
        )

    def push(s, d, ss, rs, to):
        cp(s, d, ss, rs, to).start()

    def got(d, rs):
        cp(d, d, rs, rs, d_core).wait_recv()

    def sent(s, ss):
        cp(s, s, ss, ss, d_core).wait_send()

    arriving = [
        pltpu.make_async_copy(a, b, s_in.at[n])
        for n, (a, b) in enumerate((
            (wq_in, w0.at[z, y, c, f, :, 0 : 3 * D]),
            (tok_in, tokb.at[z, c]),
            (wo_in, w1.at[z, y, c, f, :, 0:D]),
            (wu_in, w1.at[z, y, c, f, :, D : D + FF]),
            (wd_in, w2.at[z, y, c, f]),
            (tok_in, tok_ref),
            (cot_in, cot_ref),
        ))
    ]
    for t in arriving:
        t.start()
    bar = pltpu.get_barrier_semaphore()
    partners = [d_core, d_y] + [d_z(zplus(k)) for k in range(1, Z)]
    partners += [to(fplus(k)) for k in range(1, FK) for to in (d_f, d_diag)]
    for to in partners:
        pl.semaphore_signal(bar, inc=1, device_id=to, device_id_type=MESH)
    tile[...] = jnp.zeros((SLAB, 128), F32)
    for r, v in enumerate((v0, v1, v2, v3, v4, v5, v6, v7, v8)):
        tile[r : r + 1, 0 : v.shape[1]] = v[...].astype(F32)
    w0[z, y, c, f, :, 3 * D : 3 * D + 128] = tile[...].astype(BF16)
    pl.semaphore_wait(bar, len(partners))

    def tok_push(zz, ss_z, to):
        t = tokb.at[zz, c]
        push(t, t, ss_z, r_t.at[zz, c], to)

    def tok_core(zz):
        t = tokb.at[zz, c]
        push(t, t, s_tc, r_t.at[zz, c], d_core)

    def tok_right(zz):
        @pl.when(z < Z - 1)
        def _():
            tok_push(zz, s_tz.at[0, zz], d_z(z + 1))

    def tok_left(zz):
        @pl.when(z > 0)
        def _():
            tok_push(zz, s_tz.at[1, zz], d_z(z - 1))

    def tok_z(k):
        @pl.when(z - k >= 0)
        def _():
            zz = z - k
            got(tokb.at[zz, c], r_t.at[zz, c])
            tok_right(zz)
            tok_core(zz)

        @pl.when(z + k < Z)
        def _():
            zz = z + k
            got(tokb.at[zz, c], r_t.at[zz, c])
            tok_left(zz)
            tok_core(zz)

    HF = FF // 2
    everything = slice(None)
    groups = (
        (w0, everything, everything),
        (w1, everything, slice(0, D + HF)),
        (w1, everything, slice(D + HF, D + FF)),
        (w2, slice(0, 2 * SLAB), everything),
        (w2, slice(2 * SLAB, 4 * SLAB), everything),
    )

    def w_at(g, zz, yy, cc, ff):
        where, rows, cols = groups[g]
        return where.at[zz, yy, cc, ff, rows, cols]

    def w_push_x(g, zz, yy):
        t = w_at(g, zz, yy, c, f)
        for k in range(1, FK):
            push(t, t, s_wx.at[g, k - 1], r_wx.at[g, k - 1], d_f(fplus(k)))

    def w_push_y(g, zz):
        t = w_at(g, zz, y, c, f)
        push(t, t, s_wy.at[g], r_wy.at[g, zz], d_y)

    def w_out_z(g):
        t = w_at(g, z, y, c, f)
        for k in range(1, Z):
            push(t, t, s_wz.at[g], r_wz.at[g, z], d_z(zplus(k)))

    def w_own_y(g):
        w_push_y(g, z)

    def w_own_x(g):
        w_push_x(g, z, y)

    def w_z(g):
        for k in range(1, Z):
            zz = zplus(k)
            got(w_at(g, zz, y, c, f), r_wz.at[g, zz])
            w_push_x(g, zz, y)
            w_push_y(g, zz)

    def w_to_core(g, ff):
        t = w_at(g, everything, everything, c, ff)
        push(t, t, s_wc.at[g], r_wc.at[g], d_core)

    def w_m(g):
        for zz in range(Z):
            got(w_at(g, zz, oy, c, f), r_wy.at[g, zz])
            w_push_x(g, zz, oy)
        w_to_core(g, f)

    def w_l(g):
        for k in range(1, FK):
            got(w_at(g, everything, everything, c, fminus(k)), r_wx.at[g, k - 1])
            w_to_core(g, fminus(k))

    def w_c(g):
        got(w_at(g, everything, everything, oc, everything), r_wc.at[g])

    def w_sent(g):
        sent(w_at(g, slice(0, Z - 1), y, c, f), s_wz.at[g])
        sent(w_at(g, everything, y, c, f), s_wy.at[g])
        for k in range(1, FK):
            sent(w_at(g, everything, everything, c, f), s_wx.at[g, k - 1])
        sent(w_at(g, everything, everything, c, everything), s_wc.at[g])

    store = (gs, gs, gs, gs, gu, gu, gd, gd)
    from_core = (cs, cs, cs, cs, cu, cu, cd, cd)
    from_x = (xs, xs, xs, xs, xu, xu, xd, xd)
    from_y = (ys, ys, ys, ys, yu, yu, yd, yd)
    from_z = (zs, zs, zs, zs, zu, zu, zd, zd)
    lead = (0, 1, 2, 3, 0, 1, 0, 1)
    Q, K, V, O, UA, UB, DA, DB = range(8)
    y_first = {(Q, K, V, O, UA, UB, DA, DB)[t] for t in Y_FIRST}
    direct = {(Q, K, V, O, UA, UB, DA, DB)[t] for t in DIRECT}
    slot = {g: n for n, g in enumerate(sorted(direct))}
    straight = {(Q, K, V, O, UA, UB, DA, DB)[t] for t in STRAIGHT}

    def r_c(g):
        n = lead[g]
        push(store[g].at[n, :, :, oc], from_core[g].at[n], s_gc.at[(g > O) + (g > UB)], r_gc.at[g], d_core)

    def r_push_x(g, whole):
        n = lead[g]
        for k in range(1, FK):
            ff = fplus(k)
            if whole:
                push(store[g].at[n, :, :, c, ff], from_x[g].at[n, f], s_gx.at[g, k - 1], r_gx.at[g, k - 1], d_f(ff))
            else:
                t = store[g].at[n, :, y, c, ff]
                push(t, from_x[g].at[n, f, :, 0], s_gx.at[g, k - 1], r_gx.at[g, k - 1], d_f(ff))

    def r_push_y(g, whole):
        n = lead[g]
        if whole:
            push(store[g].at[n, :, oy, c], from_y[g].at[n], s_gy.at[g], r_gy.at[g], d_y)
        else:
            push(store[g].at[n, :, oy, c, f], from_y[g].at[n, :, 0], s_gy.at[g], r_gy.at[g], d_y)

    def over_z(one):
        def step(zz, carry):
            one(zz)
            return carry

        lax.fori_loop(0, Z, step, 0)

    def r_1(g):
        n = lead[g]
        got(from_core[g].at[n], r_gc.at[g])

        def one(zz):
            t = store[g][n, zz, :, c].astype(F32) + from_core[g][n, zz].astype(F32)
            store[g][n, zz, :, c] = t.astype(BF16)

        over_z(one)
        if g in direct:
            r_push_x(g, False)
            r_push_y(g, False)
            for k in range(1, FK):
                ff = fplus(k)
                t = store[g].at[n, :, oy, c, ff]
                push(t, from_x[g].at[n, f, :, 1], s_gd.at[slot[g], k - 1], r_gd.at[slot[g], k - 1], d_diag(ff))
        elif g in y_first:
            r_push_y(g, True)
        else:
            r_push_x(g, True)

    def r_2(g):
        n = lead[g]
        if g in direct:
            return
        if g in y_first:
            got(from_y[g].at[n], r_gy.at[g])

            def one(zz):
                t = store[g][n, zz, y, c].astype(F32) + from_y[g][n, zz].astype(F32)
                store[g][n, zz, y, c] = t.astype(BF16)

            over_z(one)
            r_push_x(g, False)
        else:
            for k in range(1, FK):
                got(from_x[g].at[n, fminus(k)], r_gx.at[g, k - 1])

            def one(zz):
                t = store[g][n, zz, :, c, f].astype(F32)
                for k in range(1, FK):
                    t = t + from_x[g][n, fplus(k), zz].astype(F32)
                store[g][n, zz, :, c, f] = t.astype(BF16)

            if FK > 1:
                over_z(one)
            r_push_y(g, False)

    def r_z(g):
        n = lead[g]
        if g in direct:
            got(from_y[g].at[n, :, 0], r_gy.at[g])
            for k in range(1, FK):
                got(from_x[g].at[n, fminus(k), :, 0], r_gx.at[g, k - 1])
                got(from_x[g].at[n, fminus(k), :, 1], r_gd.at[slot[g], k - 1])

            def one(zz):
                t = store[g][n, zz, y, c, f].astype(F32) + from_y[g][n, zz, 0].astype(F32)
                for k in range(1, FK):
                    t = t + from_x[g][n, fplus(k), zz, 0].astype(F32) + from_x[g][n, fplus(k), zz, 1].astype(F32)
                store[g][n, zz, y, c, f] = t.astype(BF16)

            over_z(one)
        elif g in y_first:
            for k in range(1, FK):
                got(from_x[g].at[n, fminus(k), :, 0], r_gx.at[g, k - 1])

            def one(zz):
                t = store[g][n, zz, y, c, f].astype(F32)
                for k in range(1, FK):
                    t = t + from_x[g][n, fplus(k), zz, 0].astype(F32)
                store[g][n, zz, y, c, f] = t.astype(BF16)

            if FK > 1:
                over_z(one)
        else:
            got(from_y[g].at[n, :, 0], r_gy.at[g])

            def one(zz):
                t = store[g][n, zz, y, c, f].astype(F32) + from_y[g][n, zz, 0].astype(F32)
                store[g][n, zz, y, c, f] = t.astype(BF16)

            over_z(one)
        if g in straight:
            for k in range(1, Z):
                zz = zplus(k)
                push(store[g].at[n, zz, y, c, f], from_z[g].at[n, z], s_gz.at[g], r_gz.at[g, 0], d_z(zz))
        else:
            r_fold(g, 1)

    def r_fold(g, bit):
        n = lead[g]
        for m in range(bit, Z, 2 * bit):
            push(
                store[g].at[n, zxor(m), y, c, f], from_z[g].at[n, zxor(bit ^ (m - 1))],
                s_gz.at[g], r_gz.at[g, bit.bit_length() - 1], d_z(zxor(bit)),
            )

    def r_zz(g):
        n = lead[g]
        bit = 1
        while g not in straight and 2 * bit < Z:
            got(from_z[g].at[n, 0 : Z // (2 * bit)], r_gz.at[g, bit.bit_length() - 1])
            for m in range(0, Z, 2 * bit):
                zz, at = zxor(m), zxor(m + bit - 1)
                t = store[g][n, zz, y, c, f].astype(F32) + from_z[g][n, at].astype(F32)
                store[g][n, zz, y, c, f] = t.astype(BF16)
            bit *= 2
            r_fold(g, bit)

    def r_end(g):
        n = lead[g]
        t = store[g][n, z, y, c, f].astype(F32)
        if g in straight:
            got(from_z[g].at[n, 0 : Z - 1], r_gz.at[g, 0])
            for k in range(1, Z):
                t = t + from_z[g][n, zplus(k)].astype(F32)
        else:
            at = zxor(Z // 2 - 1)
            got(from_z[g].at[n, at], r_gz.at[g, (Z // 2).bit_length() - 1])
            t = t + from_z[g][n, at].astype(F32)
        if g <= V:
            gqkv_ref[:, g * D : (g + 1) * D] = t
        elif g == O:
            gout_ref[...] = t
        elif g <= UB:
            gup_ref[:, (g - UA) * HF : (g - UA + 1) * HF] = t
        else:
            gdown_ref[(g - DA) * 2 * SLAB : (g - DA + 1) * 2 * SLAB, :] = t
        r_sent(g)

    def r_sent(g):
        n = lead[g]
        for k in range(1, FK):
            ff = fplus(k)
            if g in y_first or g in direct:
                sent(store[g].at[n, :, y, c, ff], s_gx.at[g, k - 1])
            else:
                sent(store[g].at[n, :, :, c, ff], s_gx.at[g, k - 1])
            if g in direct:
                sent(store[g].at[n, :, oy, c, ff], s_gd.at[slot[g], k - 1])
        if g in y_first and g not in direct:
            sent(store[g].at[n, :, oy, c], s_gy.at[g])
        else:
            sent(store[g].at[n, :, oy, c, f], s_gy.at[g])
        sent(store[g].at[n, 0 : Z - 1, y, c, f], s_gz.at[g])

    turns = sorted(range(1, Z), key=lambda m: (m & -m, m)) + [0]

    def plane(n):
        m = jnp.int32(0)
        for k in range(Z - 1):
            m = jnp.where(n == k, turns[k], m)
        return zxor(m)

    def p_sum(m):
        zz = zxor(m)
        got(crf.at[zz], r_pc.at[zz])
        t = tokb[zz, c].astype(F32) + crf[zz].astype(F32)
        bit = 1
        while bit < Z and m % (2 * bit) == 0:
            at = zxor(m + bit - 1)
            got(zrf.at[at], r_pz.at[at])
            t = t + zrf[at].astype(F32)
            bit *= 2
        return t

    def p_z(s):
        m = turns[s]
        bit = m & -m
        zz, at = zxor(m), zxor(bit ^ (m - 1))
        tokb[zz, c] = p_sum(m).astype(BF16)
        push(tokb.at[zz, c], zrf.at[at], s_pz, r_pz.at[at], d_z(zxor(bit)))

    def queries_back():
        push(gqs, gqr, s_y.at[5], r_y.at[5], d_y)

    def sums():
        push(sg.at[0], src, s_sc, r_sc, d_core)

    def sums_core():
        got(src, r_sc)
        sg[1] = sg[0] + src[...]
        for k in range(1, FK):
            push(sg.at[1], srx.at[f], s_sx.at[k - 1], r_sx.at[k - 1], d_f(fplus(k)))

    def sums_x():
        t = sg[1]
        for k in range(1, FK):
            got(srx.at[fminus(k)], r_sx.at[k - 1])
            t = t + srx[fminus(k)]
        sg[2] = t
        push(sg.at[2], sry, s_sy, r_sy, d_y)

    def sums_y():
        got(sry, r_sy)
        sg[3] = sg[2] + sry[...]
        for k in range(1, Z):
            zz = zplus(k)
            push(sg.at[3], srz.at[z], s_sz, r_sz, d_z(zz))

    def sums_z():
        sent(sg.at[0], s_sc)
        for k in range(1, FK):
            sent(sg.at[1], s_sx.at[k - 1])
        sent(sg.at[2], s_sy)
        sent(srz.at[0 : Z - 1], s_sz)
        t = sg[3]
        got(srz.at[0 : Z - 1], r_sz)
        for k in range(1, Z):
            t = t + srz[zplus(k)]
        gsm_ref[...] = t

    def first():
        for n, t in enumerate((gs, gu, gd)):
            sent(t.at[:, :, :, oc], s_gc.at[n])
        sent(tokb.at[:, oc], s_pc)
        sent(tokb.at[0 : Z - 1, c], s_pz)
        sent(dot_.at[:, grows, near_half], s_y.at[4])
        sent(gqs, s_y.at[5])
        got(gqr, r_y.at[5])
        t = p_sum(0) + acc[...] + gqr[...].astype(F32)
        mean, centered, rstd = moments(tok_ref[...].astype(F32))
        gtok_ref[...] = (hid[...] + norm_back(t * par[0:1, :], centered * rstd, rstd)).astype(BF16)


    qrows = slice(HD, HD + SLAB)
    grows = slice(0, HD + SLAB)
    near_half, far_half = slice(0, R), slice(R, 2 * R)

    def far_out():
        push(oh, ohr, s_y.at[0], r_y.at[0], d_y)
        push(ml, mlr, s_y.at[1], r_y.at[1], d_y)

    def far_got():
        got(ohr, r_y.at[0])
        got(mlr, r_y.at[1])

    def back_got():
        got(qt.at[:, qrows, far_half], r_y.at[3])
        got(dot_.at[:, grows, far_half], r_y.at[4])

    events = {
        "tr": lambda: tok_right(z),
        "tl": lambda: tok_left(z),
        "tp": lambda: push(tokb.at[z, c], tokp, s_tp, r_tp, d_y),
        "tc": lambda: tok_core(z),
        "tok_z": tok_z,
        "gtokp": lambda: got(tokp, r_tp),
        "w_out_z": w_out_z, "w_own_y": w_own_y, "w_own_x": w_own_x, "w_z": w_z, "w_m": w_m, "w_l": w_l, "w_c": w_c,
        "o_hi": far_out,
        "o_lo": lambda: push(ol, olr, s_y.at[2], r_y.at[2], d_y),
        "g_o": far_got,
        "g_ol": lambda: got(olr, r_y.at[2]),
        "qtail": lambda: push(qt.at[:, qrows, near_half], qt.at[:, qrows, far_half], s_y.at[3], r_y.at[3], d_y),
        "dO": lambda: push(dot_.at[:, grows, near_half], dot_.at[:, grows, far_half], s_y.at[4], r_y.at[4], d_y),
        "g_dO": back_got,
        "gq": queries_back,
        "r_c": r_c, "r_1": r_1, "r_2": r_2, "r_z": r_z, "r_zz": r_zz, "r_end": r_end,
        "p_z": p_z,
        "first": first,
        "s": lambda k: (sums, sums_core, sums_x, sums_y)[k](),
        "s_end": sums_z,
    }
    chunks = {"q": Q, "k": K, "v": V, "o": O, "ua": UA, "ub": UB, "da": DA, "db": DB}
    plan = order_of(Z)

    def do(stage):
        for name, *which in plan.get(stage, ()):
            events[name](*[chunks.get(t, t) for t in which])

    def run(stage, n):
        for at in range(Z):
            if (stage, at) in plan:
                @pl.when(n == at)
                def _():
                    do((stage, at))

    for t in arriving:
        t.wait()
    do("masks")

    starts, ends, stops = [], [], []
    total = jnp.int32(0)
    for t in range(NT):
        starts.append(total)
        stops.append(total + sup_ref[0, t])
        total = total + len_ref[0, t]
        ends.append(total)

    lane = lax.broadcasted_iota(jnp.int32, (1, 128), 1)
    lane_start = jnp.zeros((1, 128), jnp.int32)
    lane_stop = jnp.zeros((1, 128), jnp.int32)
    for t in range(NT):
        lane_start = jnp.where(lane == t, starts[t], lane_start)
        lane_stop = jnp.where(lane == t, stops[t], lane_stop)
    lane_ones = jnp.where((lane >= NT) & (lane < NT + 3), 1.0, 0.0)

    def mask_of(n):
        pos = (n * 2 + y) * 2 * R + lax.broadcasted_iota(jnp.int32, (2 * R, 128), 0)
        seen = (pos >= lane_start) & (pos < lane_stop)
        extra = jnp.where(lane < NT, jnp.where(seen, 0.0, MASKED), lane_ones)
        return extra.astype(BF16)

    def mask_block(n, carry):
        eb[n] = mask_of(n)
        return carry

    lax.fori_loop(0, Z, mask_block, 0)

    row = lax.broadcasted_iota(jnp.int32, (HD, 2 * R), 0)
    col = lax.broadcasted_iota(jnp.int32, (HD, 2 * R), 1)
    qpos = jnp.where(col < R, i * R + col, ((z * 2 + oy) * 2 + c - 1) * R + col)
    onehot = jnp.zeros((HD, 2 * R), F32)
    for t in range(NT):
        onehot = jnp.where((row == t) & (qpos >= starts[t]) & (qpos < ends[t]), 1.0, onehot)
    for h in range(H):
        qt[h, HD : 2 * HD, :] = onehot.astype(BF16)
        dot_[h, HD + SLAB : 2 * HD, :] = jnp.zeros((HD - SLAB, 2 * R), BF16)
        ot[h] = jnp.zeros((2 * HD, 2 * R), F32)
        mrun[h] = jnp.full((1, 2 * R), MASKED, F32)

    do("small")

    piece = D // NSH
    small = w0[:, :, :, :, :, 3 * D : 3 * D + 128].reshape(NSH * SLAB, 128)
    spread = (
        lax.rem(lax.broadcasted_iota(jnp.int32, (128, D), 1), piece)
        == lax.broadcasted_iota(jnp.int32, (128, D), 0)
    )
    wide = dot_nn(small, spread.astype(BF16))
    mine = (
        lax.broadcasted_iota(jnp.int32, (NSH * SLAB, D), 1) // piece
        == lax.broadcasted_iota(jnp.int32, (NSH * SLAB, D), 0) // SLAB
    )
    wide = jnp.where(mine, wide, 0.0)
    par[...] = jnp.sum(wide.reshape(NSH, SLAB, D), axis=0)
    pick = (
        lax.broadcasted_iota(jnp.int32, (NSH, NSH * SLAB), 1)
        == lax.broadcasted_iota(jnp.int32, (NSH, NSH * SLAB), 0) * SLAB + 8
    )
    ups = dot_nn(pick.astype(BF16), small).astype(BF16)
    spread = (
        lax.rem(lax.broadcasted_iota(jnp.int32, (128, FF), 1), 4 * piece)
        == lax.broadcasted_iota(jnp.int32, (128, FF), 0)
    )
    wide = dot_nn(ups, spread.astype(BF16))
    mine = (
        lax.broadcasted_iota(jnp.int32, (NSH, FF), 1) // (4 * piece)
        == lax.broadcasted_iota(jnp.int32, (NSH, FF), 0)
    )
    upb[...] = col_sum(jnp.where(mine, wide, 0.0))
    ln1g, ln1b = par[0:1, :], par[1:2, :]

    tokens = tok_ref[...].astype(F32)
    mean, centered, rstd = moments(tokens)
    xq[0:R, :] = (centered * rstd * ln1g + ln1b).astype(BF16)
    mean, centered, rstd = moments(tokp[...].astype(F32))
    xq[R : 2 * R, :] = (centered * rstd * ln1g + ln1b).astype(BF16)
    wq = w0[:, :, :, :, :, 0:D].reshape(D, D)
    qscale = HD ** (-0.5) / LN2
    qs[...] = ((dot_nn(xq[...], wq) + par[2:3, :]) * qscale).astype(BF16)
    for h in range(H):
        qt[h, 0:HD, :] = qs[:, h * HD : (h + 1) * HD].T

    def near(s):
        inner = jnp.minimum(z, Z - 1 - z)
        odd = lax.rem(s, 2)
        paired = z + (1 - 2 * odd) * ((s + 1) // 2)
        rest = jnp.where(z < Z - 1 - z, s, Z - 1 - s)
        return jnp.where(s <= 2 * inner, paired, rest)

    def attend(h, keys, values, extra, span):
        cols = slice(h * HD, (h + 1) * HD)
        s = dot_nn(jnp.concatenate([keys[:, cols], extra], axis=1), qt[h, :, span])
        top0 = mrun[h, :, span]
        top = jnp.maximum(top0, jnp.ceil(jnp.max(s, axis=0, keepdims=True)))
        e = jnp.exp2(s - top).astype(BF16)
        grown = dot_tn(jnp.concatenate([values[:, cols], extra], axis=1), e)
        ot[h, :, span] = ot[h, :, span] * jnp.exp2(top0 - top) + grown
        mrun[h, :, span] = top

    def ahead(n, carry):
        zz = near(n)
        run("A", n)
        got(tokb.at[zz, oc], r_t.at[zz, oc])
        mean, centered, rstd = moments(tokb[zz].reshape(2 * R, D).astype(F32))
        stat[zz] = jnp.where(lax.broadcasted_iota(jnp.int32, (2 * R, 128), 1) == 0, mean, rstd)
        x = (centered * rstd * par[0:1, :] + par[1:2, :]).astype(BF16)
        kv = dot_nn(x, w0[:, :, :, :, :, D : 3 * D].reshape(D, 2 * D))
        keys = kv[:, 0:D].astype(BF16)
        values = (kv[:, D : 2 * D] + par[3:4, :]).astype(BF16)
        kb[zz] = keys
        vb[zz] = values
        extra = eb[zz]
        for h in range(H):
            attend(h, keys, values, extra, slice(R, 2 * R))
        return carry

    lax.fori_loop(0, Z, ahead, 0)

    do("osplit")
    for h in range(H):
        t = ot[h, 0:HD, R : 2 * R]
        first_part = t.astype(BF16)
        oh[h] = first_part
        ol[h] = (t - first_part.astype(F32)).astype(BF16)
        ml[h : h + 1, :] = mrun[h, :, R : 2 * R]
        ml[H + h : H + h + 1, :] = ot[h, HD + NT : HD + NT + 1, R : 2 * R]
    def ahead_own(n, carry):
        zz = near(n)
        run("B", n)
        for h in range(H):
            attend(h, kb[zz], vb[zz], eb[zz], slice(0, R))
        return carry

    lax.fori_loop(0, Z, ahead_own, 0)
    do("merge")
    parts = []
    row_tail = lax.broadcasted_iota(jnp.int32, (SLAB, R), 0)
    for h in range(H):
        m_own, m_far = mrun[h, :, 0:R], mlr[h : h + 1, :]
        top = jnp.maximum(m_own, m_far)
        a_own, a_far = jnp.exp2(m_own - top), jnp.exp2(m_far - top)
        total = a_own * ot[h, HD + NT : HD + NT + 1, 0:R] + a_far * mlr[H + h : H + h + 1, :]
        inverse = 1.0 / total
        attended = ot[h, 0:HD, 0:R] * (a_own * inverse) + ohr[h].astype(F32) * (a_far * inverse)
        ot[h, 0:HD, 0:R] = attended
        ot[h, HD : HD + 1, 0:R] = inverse
        ot[h, HD + 1 : HD + 2, 0:R] = a_far * inverse
        parts.append(attended.T.astype(BF16))
        m1, m2, m3 = three_terms(top)
        tail = jnp.where(
            row_tail == NT, -m1,
            jnp.where(row_tail == NT + 1, -m2, jnp.where(row_tail == NT + 2, -m3, onehot[0:SLAB, 0:R])),
        )
        qt[h, HD : HD + SLAB, 0:R] = tail.astype(BF16)
    do("out")
    attn_low = jnp.concatenate(parts, axis=1)
    w_out = w1[:, :, :, :, :, 0:D].reshape(D, D)
    hidden = tokens + (dot_nn(attn_low, w_out) + par[4:5, :])
    hid[...] = hidden
    mean2, centered, rstd2 = moments(hidden)
    n2 = centered * rstd2
    nrm2[...] = (n2 * par[5:6, :] + par[6:7, :]).astype(BF16)
    acc[...] = hidden + par[7:8, :]
    gsec[...] = jnp.zeros((R, D), F32)

    def slope_at(j):
        hh = j // (Z // 2)
        return pl.ds(pl.multiple_of(hh * R, R), R), pl.ds(pl.multiple_of((j - hh * (Z // 2)) * CH, 128), CH)

    def forward(j, carry):
        cols = pl.ds(pl.multiple_of(D + j * CH, 128), CH)
        bcols = pl.ds(pl.multiple_of(j * CH, 128), CH)
        pre = dot_nn(nrm2[...], w1[:, :, :, :, :, cols].reshape(D, CH)) + upb[:, bcols]
        phi = 0.5 * (1.0 + lax.erf(pre * (0.5**0.5)))
        act_all[:, bcols] = (pre * phi).astype(BF16)
        slope = phi + pre * (jnp.exp2(pre * pre * (-0.5 / LN2)) * ((2.0 * math.pi) ** -0.5))
        big[1, *slope_at(j)] = slope
        return carry

    def backward(j, carry):
        cols = pl.ds(pl.multiple_of(D + j * CH, 128), CH)
        bcols = pl.ds(pl.multiple_of(j * CH, 128), CH)
        gpre = (dot_nt(cot_ref[...], w2[j].reshape(CH, D)) * big[1, *slope_at(j)]).astype(BF16)
        gsec[...] += dot_nt(gpre, w1[:, :, :, :, :, cols].reshape(D, CH))
        gpre_all[:, bcols] = gpre
        return carry

    do("ffn")
    lax.fori_loop(0, Z, forward, 0)
    do("ffd")
    lax.fori_loop(0, Z, backward, 0)
    do("ln2")

    g_second = gsec[...]
    n2 = (hid[...] - mean2) * rstd2
    ln2g = par[5:6, :]
    cot32 = cot_ref[...].astype(F32)
    grad_hidden = cot32 + norm_back(g_second * ln2g, n2, rstd2)
    hid[...] = grad_hidden
    g_branch = grad_hidden.astype(BF16)
    do("dOc")
    for h in range(H):
        rows = slice(h * HD, (h + 1) * HD)
        w_head = w1[:, :, :, :, :, 0:D].reshape(D, D)[rows, :]
        ga = dot_nt(w_head, g_branch).astype(BF16).astype(F32)
        low = (ga * ot[h, HD : HD + 1, 0:R]).astype(BF16)
        exact = ot[h, 0:HD, 0:R] + olr[h].astype(F32) * ot[h, HD + 1 : HD + 2, 0:R]
        delta = col_sum(low.astype(F32) * exact)
        d1, d2, d3 = three_terms(delta)
        tail = jnp.where(
            row_tail == NT, -d1, jnp.where(row_tail == NT + 1, -d2, jnp.where(row_tail == NT + 2, -d3, 0.0))
        )
        dot_[h, 0:HD, 0:R] = low
        dot_[h, HD : HD + SLAB, 0:R] = tail.astype(BF16)
        dos[0:R, rows] = low.T

    def g_up(j, carry):
        bcols = pl.ds(pl.multiple_of(j * CH, 128), CH)
        t = dot_tn(nrm2[...], gpre_all[:, bcols]).astype(BF16).reshape(Z, 2, 2, FK, SLAB, CH)
        hh = j // (Z // 2)
        upg[:, bcols] = col_sum(gpre_all[:, bcols].astype(F32))
        gu[hh, :, :, :, :, :, pl.ds(pl.multiple_of((j - hh * (Z // 2)) * CH, 128), CH)] = t
        return carry

    def g_down(j, carry):
        bcols = pl.ds(pl.multiple_of(j * CH, 128), CH)
        acc[...] += dot_nn(act_all[:, bcols], w2[j].reshape(CH, D))
        t = dot_tn(act_all[:, bcols], cot_ref[...]).astype(BF16).reshape(2, 2, FK, 4 * SLAB, D)
        gd[0, j] = t[:, :, :, 0 : 2 * SLAB]
        gd[1, j] = t[:, :, :, 2 * SLAB : 4 * SLAB]
        return carry

    do("dwu")
    lax.fori_loop(0, Z, g_up, 0)
    do("dwd")
    lax.fori_loop(0, Z, g_down, 0)
    out_ref[...] = acc[...].astype(BF16)
    do("dwo")
    gs[O] = dot_tn(attn_low, g_branch).astype(BF16).reshape(Z, 2, 2, FK, SLAB, D)
    zero = jnp.zeros((1, D), F32)
    for r in range(SLAB):
        sg[0, r : r + 1, :] = zero
    sg[0, 4:5, :] = col_sum(g_branch.astype(F32))
    sg[0, 5:6, :] = col_sum(g_second * n2)
    sg[0, 6:7, :] = col_sum(g_second)
    sg[0, 7:8, :] = col_sum(cot32)
    for r in range(FF // D):
        sg[0, 8 + r : 9 + r, :] = upg[:, r * D : (r + 1) * D]

    dqt[...] = jnp.zeros((H, HD, 2 * R), F32)
    lacc[...] = jnp.zeros((3, 8, D), F32)

    def tok_sent():
        @pl.when(z < Z - 1)
        def _():
            for k in range(Z):
                @pl.when(z - k >= 0)
                def _():
                    sent(tokb.at[z - k, c], s_tz.at[0, z - k])

        @pl.when(z > 0)
        def _():
            for k in range(Z):
                @pl.when(z + k < Z)
                def _():
                    sent(tokb.at[z + k, c], s_tz.at[1, z + k])

        sent(tokb.at[:, c], s_tc)
        sent(tokb.at[z, c], s_tp)

    def heads(zz, span):
        keys, values, extra = kb[zz], vb[zz], eb[zz]
        dks, dvs = [], []
        for h in range(H):
            cols = slice(h * HD, (h + 1) * HD)
            s = dot_nn(jnp.concatenate([keys[:, cols], extra], axis=1), qt[h, :, span])
            dp = dot_nn(jnp.concatenate([values[:, cols], extra], axis=1), dot_[h, :, span])
            e = jnp.exp2(s).astype(BF16)
            ds = (e.astype(F32) * dp).astype(BF16)
            dvs.append(dot_nn(e, dos[span, cols]))
            dks.append(dot_nn(ds, qs[span, cols]) * LN2)
            dqt[h, :, span] += dot_tn(keys[:, cols], ds)
        return jnp.concatenate(dks + dvs, axis=1)

    def rest(n, zz, dkv32):
        dkv = dkv32.astype(BF16)
        run("t", n)
        gp = dot_nt(dkv, w0[:, :, :, :, :, D : 3 * D].reshape(D, 2 * D))
        norm = (tokb[zz].reshape(2 * R, D).astype(F32) - stat[zz, :, 0:1]) * stat[zz, :, 1:2]
        tokb[zz] = gp.astype(BF16).reshape(2, R, D)
        push(tokb.at[zz, oc], crf.at[zz], s_pc, r_pc.at[zz], d_core)
        x = (norm * par[0:1, :] + par[1:2, :]).astype(BF16)
        lacc[0] += fold_rows(gp * norm)
        lacc[1] += fold_rows(gp)
        lacc[2] += fold_rows(dkv32[:, D : 2 * D])
        big[0] = jnp.where(n == 0, 0.0, big[0]) + dot_tn(x, dkv)

    def behind_early(n, carry):
        run("e", n)
        big[n] = heads(plane(n), near_half)
        return carry

    def behind_far(n, carry):
        run("h", n)
        zz = plane(n)
        rest(n, zz, big[n] + heads(zz, far_half))
        return carry

    def behind(n, carry):
        run("h", n)
        zz = plane(n)
        rest(n, zz, heads(zz, slice(0, 2 * R)))
        return carry

    do("sent")
    tok_sent()
    for g in range(len(groups)):
        w_sent(g)
    sent(oh, s_y.at[0])
    sent(ml, s_y.at[1])
    sent(ol, s_y.at[2])
    sent(qt.at[:, qrows, near_half], s_y.at[3])
    E = big.shape[0] if Z == 4 else 0
    if E:
        lax.fori_loop(0, E, behind_early, 0)
    do("dosT")
    for h in range(H):
        dos[R : 2 * R, h * HD : (h + 1) * HD] = dot_[h, 0:HD, R : 2 * R].T
    if E:
        lax.fori_loop(0, E, behind_far, 0)
    lax.fori_loop(E, Z, behind, 0)

    do("kv")
    gs[K] = big[0, :, 0:D].astype(BF16).reshape(Z, 2, 2, FK, SLAB, D)
    gs[V] = big[0, :, D : 2 * D].astype(BF16).reshape(Z, 2, 2, FK, SLAB, D)

    def queries():
        dq = jnp.concatenate([(dqt[h] * (HD**-0.5)).T for h in range(H)], axis=1).astype(BF16)
        gs[Q] = dot_tn(xq[...], dq).astype(BF16).reshape(Z, 2, 2, FK, SLAB, D)
        gq = dot_nt(dq, w0[:, :, :, :, :, 0:D].reshape(D, D))
        acc[...] = gq[0:R]
        gqs[...] = gq[R : 2 * R].astype(BF16)
        both = jnp.concatenate([tok_ref[...], tokp[...]], axis=0).astype(F32)
        mean, centered, rstd = moments(both)
        sg[0, 0:1, :] = col_sum(lacc[0]) + col_sum(gq * (centered * rstd))
        sg[0, 1:2, :] = col_sum(lacc[1]) + col_sum(gq)
        sg[0, 2:3, :] = col_sum(dq.astype(F32))
        sg[0, 3:4, :] = col_sum(lacc[2])

    do("q")
    queries()
    do("end")


def layer(Z, FK, R, D, FF, NT, operands):
    vm = lambda shape, dtype: pltpu.VMEM(shape, dtype)
    dma = lambda *shape: pltpu.SemaphoreType.DMA(shape)
    one = pltpu.SemaphoreType.DMA
    others = max(FK - 1, 1)
    lead = (Z, 2, 2, FK)
    slabs = ((SLAB, 3 * D + 128), (SLAB, D + FF), (4 * SLAB, D))
    gslabs = ((4, SLAB, D), (2, SLAB, FF // 2), (2, 2 * SLAB, D))
    scratch = [
        vm((Z, 2, R, D), BF16),
        vm((R, D), BF16),
        vm((Z, 2 * R, D), BF16),
        vm((Z, 2 * R, D), BF16),
        vm((Z, 2 * R, 128), BF16),
        vm((Z, 2 * R, 128), F32),
        *[vm(lead + s, BF16) for s in slabs],
        *[vm((s[0],) + lead + s[1:], BF16) for s in gslabs],
        *[vm((s[0], Z, 2, FK) + s[1:], BF16) for s in gslabs],
        *[vm((s[0], FK, Z, 2) + s[1:] if FK > 1 else (SLAB, 128), BF16) for s in gslabs],
        *[vm((s[0], Z, FK) + s[1:], BF16) for s in gslabs],
        *[vm((s[0], Z) + s[1:], BF16) for s in gslabs],
        vm((Z, R, D), BF16),
        vm((Z, R, D), BF16),
        vm((SLAB, D), F32),
        vm((1, FF), F32),
        vm((H, 2 * HD, 2 * R), BF16),
        vm((H, 2 * HD, 2 * R), BF16),
        vm((2 * R, D), BF16),
        vm((2 * R, D), BF16),
        vm((H, 2 * HD, 2 * R), F32),
        vm((H, 1, 2 * R), F32),
        vm((H, HD, 2 * R), F32),
        vm((H, HD, R), BF16),
        vm((H, HD, R), BF16),
        vm((2 * H, R), F32),
        vm((H, HD, R), BF16),
        vm((H, HD, R), BF16),
        vm((2 * H, R), F32),
        vm((R, D), BF16),
        vm((R, D), BF16),
        vm((R, D), BF16),
        vm((R, D), F32),
        vm((R, D), F32),
        vm((R, D), F32),
        vm((3, 8, D), F32),
        vm((1, FF), F32),
        vm((2 * R, D), BF16),
        vm((4, SLAB, D), F32),
        vm((SLAB, D), F32),
        vm((FK, SLAB, D), F32),
        vm((SLAB, D), F32),
        vm((Z, SLAB, D), F32),
        vm((SLAB, 128), F32),
        vm((R, D), BF16),
        vm((R, D), BF16),
        vm((R, FF), BF16),
        vm((R, FF), BF16),
        vm((3 if Z == 4 else 2, 2 * R, 2 * D), F32),
        dma(7),
        dma(2, Z), one, dma(Z, 2), one, one,
        dma(5), dma(5, Z), dma(5), dma(5, Z), dma(5, others), dma(5, others), dma(5), dma(5),
        dma(3), dma(8), dma(8, others), dma(8, others), dma(8), dma(8),
        dma(max(len(DIRECT), 1), others), dma(max(len(DIRECT), 1), others), dma(8), dma(8, Z.bit_length() - 1),
        one, dma(Z), one, dma(Z), dma(6), dma(6),
        one, one, dma(others), dma(others), one, one, one, one,
    ]
    vmem = pl.BlockSpec(memory_space=pltpu.VMEM)
    smem = pl.BlockSpec(memory_space=pltpu.SMEM)
    shape = jax.ShapeDtypeStruct
    return pl.pallas_call(
        functools.partial(body, Z, FK, R, D, NT),
        out_shape=(
            pltpu.VMEM((R, D), BF16),
            pltpu.VMEM((R, D), BF16),
            pltpu.VMEM((SLAB, 3 * D), F32),
            pltpu.VMEM((SLAB, D), F32),
            pltpu.VMEM((SLAB, FF), F32),
            pltpu.VMEM((4 * SLAB, D), F32),
            pltpu.VMEM((SLAB, D), F32),
        ),
        in_specs=[pl.BlockSpec(memory_space=pl.ANY)] * 6 + [vmem] * 9 + [smem] * 2,
        out_specs=[vmem] * 7,
        scratch_shapes=scratch,
        compiler_params=pltpu.CompilerParams(
            collective_id=0, has_side_effects=True, vmem_limit_bytes=63 * 2**20
        ),
        name="layer",
    )(*operands)


def finish(NSH, FK, *refs):
    big_in, small_in, big_out, small_out = refs[0:6], refs[6], refs[7:13], refs[13:22]
    for a, b in zip(big_in, big_out):
        b[...] = a[...]
    at = lax.axis_index("blk") * FK
    if FK > 1:
        at = at + lax.axis_index("fsdp")
    D = small_in.shape[1]
    piece = D // NSH
    lane = lax.broadcasted_iota(jnp.int32, (128, D), 1)
    take = lax.broadcasted_iota(jnp.int32, (128, D), 0)
    full = small_in[...]
    for r in range(8):
        chosen = jnp.where(lane == at * piece + take, full[r : r + 1, :], 0.0)
        small_out[r][...] = jnp.sum(chosen, axis=1).reshape(1, 128)[:, 0:piece]
    FF = D * 4
    total = jnp.zeros((128,), F32)
    for r in range(4):
        chosen = jnp.where(lane + r * D == at * 4 * piece + take, full[8 + r : 9 + r, :], 0.0)
        total = total + jnp.sum(chosen, axis=1)
    small_out[8][...] = total.reshape(1, 128)[:, 0 : 4 * piece]


def hand_over(NSH, FK, FF, results):
    *big, small = results
    D = small.shape[1]
    vmem = pl.BlockSpec(memory_space=pltpu.VMEM)
    shape = jax.ShapeDtypeStruct
    return pl.pallas_call(
        functools.partial(finish, NSH, FK),
        out_shape=(
            *[shape(v.shape, v.dtype) for v in big],
            *[shape((1, D // NSH), F32) for _ in range(8)],
            shape((1, FF // NSH), F32),
        ),
        in_specs=[vmem] * 7,
        out_specs=[vmem] * 15,
        name="finish",
    )(*[pltpu.with_memory_space_constraint(v, pltpu.VMEM) for v in results])


def shards(
    blocks, fsdp,
    tokens, ln1_gain, ln1_bias, qkv_weight, query_bias, value_bias, out_weight, out_bias,
    ln2_gain, ln2_bias, up_weight, up_bias, down_weight, down_bias,
    table_lengths, support_lengths, cotangent,
):
    R, D = tokens.shape[1:]
    FF = up_weight.shape[1]
    NT = table_lengths.shape[1]
    smalls = (ln1_gain, ln1_bias, query_bias, value_bias, out_bias, ln2_gain, ln2_bias, down_bias, up_bias)
    weights = (qkv_weight, out_weight, up_weight, down_weight)
    inside = qkv_weight.shape[0] == SLAB
    FK = fsdp if inside else 1
    if not inside:
        whole = lambda v: lax.all_gather(v, "fsdp", axis=0, tiled=True)
        smalls = tuple(whole(v) for v in smalls)
        weights = tuple(whole(v) for v in weights)
    results = layer(
        blocks // 4, FK, R, D, FF, NT,
        (tokens[0], cotangent[0], *weights, *[v[None] for v in smalls], table_lengths, support_lengths),
    )
    block_out, grad_tokens, g_qkv, g_out, g_up, g_down, *small_grads = hand_over(
        blocks * FK, FK, FF, results
    )
    small_grads = [v[0] for v in small_grads]
    weight_grads = [g_qkv, g_out, g_up, g_down]
    if not inside:
        spread = lambda v: lax.psum_scatter(v, "fsdp", scatter_dimension=0, tiled=True)
        small_grads = [spread(v) for v in small_grads]
        weight_grads = [spread(v) for v in weight_grads]
    g_ln1g, g_ln1b, g_qb, g_vb, g_ob, g_ln2g, g_ln2b, g_db, g_ub = small_grads
    g_qkv, g_out, g_up, g_down = weight_grads
    return (
        block_out[None], grad_tokens[None], g_ln1g, g_ln1b, g_qkv, g_qb, g_vb, g_out, g_ob,
        g_ln2g, g_ln2b, g_up, g_ub, g_down, g_db,
    )


def solution(mesh):
    both = ("blk", "fsdp")
    vec, mat, rows = P(both), P(both, None), P("fsdp", "blk", None)
    return jax.shard_map(
        functools.partial(shards, mesh.shape["blk"], mesh.shape["fsdp"]),
        mesh=mesh,
        in_specs=(
            rows, vec, vec, mat, vec, vec, mat, vec, vec, vec, mat, vec, mat, vec,
            P("fsdp", None), P("fsdp", None), rows,
        ),
        out_specs=(rows, rows, vec, vec, mat, vec, vec, mat, vec, vec, vec, mat, vec, mat, vec),
        check_vma=False,
    )
```

```python
import functools
import math

import jax
import jax.numpy as jnp
from jax import lax
from jax.experimental import pallas as pl
from jax.experimental.pallas import tpu as pltpu
from jax.sharding import PartitionSpec as P

H = 4
HD = 128
SLAB = 16
EPSILON = 1e-05
MASKED = -1e30
LN2 = math.log(2.0)
BINARY = HD ** (-0.5) / LN2
MESH = pl.DeviceIdType.MESH
F32 = jnp.float32
BF16 = jnp.bfloat16


def dot_nn(a, b):
    return lax.dot_general(a, b, (((1,), (0,)), ((), ())), preferred_element_type=F32)


def dot_nt(a, b):
    return lax.dot_general(a, b, (((1,), (1,)), ((), ())), preferred_element_type=F32)


def dot_tn(a, b):
    return lax.dot_general(a, b, (((0,), (0,)), ((), ())), preferred_element_type=F32)


def moments(v):
    mean = jnp.mean(v, axis=-1, keepdims=True)
    centered = v - mean
    rstd = lax.rsqrt(jnp.mean(centered * centered, axis=-1, keepdims=True) + EPSILON)
    return mean, centered, rstd


def norm_back(g, n, r):
    return r * (g - jnp.mean(g, axis=-1, keepdims=True) - n * jnp.mean(g * n, axis=-1, keepdims=True))


def three_terms(v):
    first = v.astype(BF16)
    rest = v - first.astype(F32)
    second = rest.astype(BF16)
    third = (rest - second.astype(F32)).astype(BF16)
    return first.astype(F32), second.astype(F32), third.astype(F32)


def col_sum(v):
    return jnp.sum(v, axis=0, keepdims=True)


def fold_rows(v):
    return jnp.sum(v.reshape(v.shape[0] // 8, 8, v.shape[1]), axis=0)


FOUR = {
    "masks": [
        ("w_out_z", 0), ("w_own_x", 2), ("w_own_y", 0), ("tr",), ("w_out_z", 1), ("tl",), ("tp",), ("w_out_z", 2),
    ],
    "small": [
        ("w_z", 0), ("tc",), ("w_own_x", 0), ("w_m", 0), ("w_own_y", 1), ("w_own_y", 4), ("gtokp",), ("w_z", 1),
        ("tok_z", 1), ("w_l", 0), ("w_m", 1), ("w_z", 2), ("w_own_y", 3), ("w_own_y", 2), ("w_c", 0), ("w_own_x", 3),
        ("w_out_z", 4),
    ],
    ("A", 0): [("w_own_x", 1), ("w_own_x", 4), ("tok_z", 2)],
    ("A", 1): [("w_z", 4), ("w_m", 2), ("w_out_z", 3)],
    ("A", 3): [("tok_z", 3), ("w_l", 1), ("w_m", 4), ("w_z", 3)],
    ("B", 0): [("o_hi",)],
    ("B", 1): [("o_lo",)],
    ("B", 2): [("w_m", 3), ("w_l", 4), ("w_l", 2)],
    "merge": [("w_c", 2), ("w_c", 1), ("w_l", 3), ("w_c", 4), ("g_o",)],
    "out": [("qtail",)],
    "ffn": [("w_c", 3)],
    "dOc": [("g_ol",)],
    "dwu": [("dO",)],
    "dwd": [("r_c", "ub")],
    "sent": [("r_1", "ub"), ("r_c", "db")],
    "dosT": [("r_1", "db"), ("g_dO",), ("r_2", "ub")],
    ("h", 1): [("r_c", "ua")],
    ("t", 1): [("r_2", "db"), ("r_c", "o"), ("r_z", "ub")],
    ("h", 2): [("r_zz", "ub"), ("r_1", "ua"), ("p_z", 1)],
    ("t", 2): [("r_c", "da"), ("r_z", "db"), ("p_z", 0)],
    ("h", 3): [("r_1", "da"), ("r_1", "o"), ("r_zz", "db")],
    "kv": [("r_2", "ua"), ("p_z", 2)],
    "q": [("r_2", "da"), ("r_c", "v"), ("r_c", "k")],
    "end": [
        ("r_1", "v"), ("r_1", "k"), ("r_2", "o"), ("r_c", "q"), ("r_z", "ua"), ("r_1", "q"), ("s", 0), ("r_z", "da"),
        ("r_end", "db"), ("s", 1), ("r_2", "v"), ("r_z", "o"), ("r_zz", "o"), ("r_2", "k"), ("r_zz", "da"), ("s", 2),
        ("r_2", "q"), ("r_end", "ub"), ("r_z", "k"), ("gq",), ("r_zz", "ua"), ("r_z", "v"), ("r_z", "q"), ("s", 3),
        ("r_zz", "v"), ("r_end", "ua"), ("r_zz", "k"), ("r_zz", "q"), ("r_end", "da"), ("r_end", "o"), ("first",),
        ("r_end", "v"), ("r_end", "k"), ("s_end",), ("r_end", "q"),
    ],
}
Y_FIRST = {0, 2, 5, 6, 7}
DIRECT = {0, 1, 3, 4, 5, 6, 7}
STRAIGHT = {3, 5, 6, 7}


def order_of(Z):
    if Z == 4:
        return FOUR
    most = ("ua", "ub", "da", "db", "o")
    last = ("q", "k", "v")
    plan = {
        "masks": [("w_out_z", 0), ("w_own_y", 0), ("w_own_x", 0), ("tr",), ("tl",), ("tp",), ("tc",)],
        "small": [("w_z", 0), ("w_m", 0), ("w_l", 0), ("gtokp",), ("w_c", 0)],
        ("A", 0): [(step, g) for g in range(1, 5) for step in ("w_out_z", "w_own_y", "w_own_x")],
        ("B", 0): [("o_hi",)] + [(step, g) for step in ("w_z", "w_m") for g in range(1, 5)],
        "merge": [("o_lo",), ("g_o",)] + [("w_l", g) for g in range(1, 5)],
        "out": [("qtail",)] + [("w_c", g) for g in range(1, 5)],
        "dOc": [("g_ol",)],
        "dwu": [("dO",)],
        "sent": [("r_c", g) for g in most],
        "dosT": [("r_1", g) for g in most] + [("g_dO",)],
        ("h", Z - 1): [("r_2", g) for g in most],
        "kv": [("p_z", Z - 2)] + [("r_z", g) for g in most],
        "end": [("gq",)] + [(step, g) for step in ("r_c", "r_1", "r_2", "r_z") for g in last],
    }
    for k in range(1, Z):
        plan.setdefault(("A", k), []).append(("tok_z", k))
    for k in range(Z - 2):
        plan[("t", k + 1)] = [("p_z", k)]
    plan["end"] += [("r_zz", g) for g in most + last] + [("s", k) for k in range(4)] + [("first",), ("s_end",)]
    plan["end"] += [("r_end", g) for g in most + last]
    return plan


def body(
    Z, FK, R, D, NT,
    tok_in, cot_in, wq_in, wo_in, wu_in, wd_in,
    v0, v1, v2, v3, v4, v5, v6, v7, v8, len_ref, sup_ref,
    out_ref, gtok_ref, gqkv_ref, gout_ref, gup_ref, gdown_ref, gsm_ref,
    tokb, tokp, kb, vb, eb, stat, w0, w1, w2, gs, gu, gd,
    cs, cu, cd, xs, xu, xd, ys, yu, yd, zs, zu, zd,
    crf, zrf, par, upb, qt, dot_, qs, dos, ot, mrun, dqt,
    oh, ol, ml, ohr, olr, mlr, gqs, gqr,
    nrm2, hid, acc, gsec, lacc, upg, xq,
    sg, src, srx, sry, srz, tile, tok_ref, cot_ref, act_all, gpre_all, big,
    s_in,
    s_tz, s_tc, r_t, s_tp, r_tp,
    s_wz, r_wz, s_wy, r_wy, s_wx, r_wx, s_wc, r_wc,
    s_gc, r_gc, s_gx, r_gx, s_gy, r_gy, s_gd, r_gd, s_gz, r_gz,
    s_pc, r_pc, s_pz, r_pz, s_y, r_y,
    s_sc, r_sc, s_sx, r_sx, s_sy, r_sy, s_sz, r_sz,
):
    i = lax.axis_index("blk")
    f = lax.axis_index("fsdp")
    c = lax.rem(i, 2)
    y = lax.rem(i // 2, 2)
    z = i // 4
    oc = 1 - c
    oy = 1 - y
    CH = 4 * FK * SLAB * 4
    FF = Z * CH
    NSH = Z * 4 * FK

    def dev(zz, yy, cc, ff):
        return ((zz * 2 + yy) * 2 + cc, ff)

    d_core = dev(z, y, oc, f)
    d_y = dev(z, oy, c, f)

    def zplus(k):
        return lax.rem(z + k, Z)

    def zxor(m):
        out, bit = z, 1
        while bit < Z:
            out = out + bit * ((m // bit) % 2) * (1 - 2 * lax.rem(z // bit, 2))
            bit *= 2
        return out

    def fplus(k):
        return lax.rem(f + k, FK)

    def d_z(zz):
        return dev(zz, y, c, f)

    def d_f(ff):
        return (i, ff)

    def fminus(k):
        return lax.rem(f + FK - k, FK)

    def d_diag(ff):
        return dev(z, oy, c, ff)

    def cp(s, d, ss, rs, to):
        return pltpu.make_async_remote_copy(
            src_ref=s, dst_ref=d, send_sem=ss, recv_sem=rs, device_id=to, device_id_type=MESH
        )

    def push(s, d, ss, rs, to):
        cp(s, d, ss, rs, to).start()

    def got(d, rs):
        cp(d, d, rs, rs, d_core).wait_recv()

    def sent(s, ss):
        cp(s, s, ss, ss, d_core).wait_send()

    arriving = [
        pltpu.make_async_copy(a, b, s_in.at[n])
        for n, (a, b) in enumerate((
            (wq_in, w0.at[z, y, c, f, :, 0 : 3 * D]),
            (tok_in, tokb.at[z, c]),
            (wo_in, w1.at[z, y, c, f, :, 0:D]),
            (wu_in, w1.at[z, y, c, f, :, D : D + FF]),
            (wd_in, w2.at[z, y, c, f]),
            (tok_in, tok_ref),
            (cot_in, cot_ref),
        ))
    ]
    for t in arriving:
        t.start()
    bar = pltpu.get_barrier_semaphore()
    partners = [d_core, d_y] + [d_z(zplus(k)) for k in range(1, Z)]
    partners += [to(fplus(k)) for k in range(1, FK) for to in (d_f, d_diag)]
    for to in partners:
        pl.semaphore_signal(bar, inc=1, device_id=to, device_id_type=MESH)
    tile[...] = jnp.zeros((SLAB, 128), F32)
    for r, v in enumerate((v0, v1, v2, v3, v4, v5, v6, v7, v8)):
        tile[r : r + 1, 0 : v.shape[1]] = v[...].astype(F32)
    w0[z, y, c, f, :, 3 * D : 3 * D + 128] = tile[...].astype(BF16)
    pl.semaphore_wait(bar, len(partners))

    def tok_push(zz, ss_z, to):
        t = tokb.at[zz, c]
        push(t, t, ss_z, r_t.at[zz, c], to)

    def tok_core(zz):
        t = tokb.at[zz, c]
        push(t, t, s_tc, r_t.at[zz, c], d_core)

    def tok_right(zz):
        @pl.when(z < Z - 1)
        def _():
            tok_push(zz, s_tz.at[0, zz], d_z(z + 1))

    def tok_left(zz):
        @pl.when(z > 0)
        def _():
            tok_push(zz, s_tz.at[1, zz], d_z(z - 1))

    def tok_z(k):
        @pl.when(z - k >= 0)
        def _():
            zz = z - k
            got(tokb.at[zz, c], r_t.at[zz, c])
            tok_right(zz)
            tok_core(zz)

        @pl.when(z + k < Z)
        def _():
            zz = z + k
            got(tokb.at[zz, c], r_t.at[zz, c])
            tok_left(zz)
            tok_core(zz)

    HF = FF // 2
    everything = slice(None)
    groups = (
        (w0, everything, everything),
        (w1, everything, slice(0, D + HF)),
        (w1, everything, slice(D + HF, D + FF)),
        (w2, slice(0, 2 * SLAB), everything),
        (w2, slice(2 * SLAB, 4 * SLAB), everything),
    )

    def w_at(g, zz, yy, cc, ff):
        where, rows, cols = groups[g]
        return where.at[zz, yy, cc, ff, rows, cols]

    def w_push_x(g, zz, yy):
        t = w_at(g, zz, yy, c, f)
        for k in range(1, FK):
            push(t, t, s_wx.at[g, k - 1], r_wx.at[g, k - 1], d_f(fplus(k)))

    def w_push_y(g, zz):
        t = w_at(g, zz, y, c, f)
        push(t, t, s_wy.at[g], r_wy.at[g, zz], d_y)

    def w_out_z(g):
        t = w_at(g, z, y, c, f)
        for k in range(1, Z):
            push(t, t, s_wz.at[g], r_wz.at[g, z], d_z(zplus(k)))

    def w_own_y(g):
        w_push_y(g, z)

    def w_own_x(g):
        w_push_x(g, z, y)

    def w_z(g):
        for k in range(1, Z):
            zz = zplus(k)
            got(w_at(g, zz, y, c, f), r_wz.at[g, zz])
            w_push_x(g, zz, y)
            w_push_y(g, zz)

    def w_to_core(g, ff):
        t = w_at(g, everything, everything, c, ff)
        push(t, t, s_wc.at[g], r_wc.at[g], d_core)

    def w_m(g):
        for zz in range(Z):
            got(w_at(g, zz, oy, c, f), r_wy.at[g, zz])
            w_push_x(g, zz, oy)
        w_to_core(g, f)

    def w_l(g):
        for k in range(1, FK):
            got(w_at(g, everything, everything, c, fminus(k)), r_wx.at[g, k - 1])
            w_to_core(g, fminus(k))

    def w_c(g):
        got(w_at(g, everything, everything, oc, everything), r_wc.at[g])

    def w_sent(g):
        sent(w_at(g, slice(0, Z - 1), y, c, f), s_wz.at[g])
        sent(w_at(g, everything, y, c, f), s_wy.at[g])
        for k in range(1, FK):
            sent(w_at(g, everything, everything, c, f), s_wx.at[g, k - 1])
        sent(w_at(g, everything, everything, c, everything), s_wc.at[g])

    store = (gs, gs, gs, gs, gu, gu, gd, gd)
    from_core = (cs, cs, cs, cs, cu, cu, cd, cd)
    from_x = (xs, xs, xs, xs, xu, xu, xd, xd)
    from_y = (ys, ys, ys, ys, yu, yu, yd, yd)
    from_z = (zs, zs, zs, zs, zu, zu, zd, zd)
    lead = (0, 1, 2, 3, 0, 1, 0, 1)
    Q, K, V, O, UA, UB, DA, DB = range(8)
    y_first = {(Q, K, V, O, UA, UB, DA, DB)[t] for t in Y_FIRST}
    direct = {(Q, K, V, O, UA, UB, DA, DB)[t] for t in DIRECT}
    slot = {g: n for n, g in enumerate(sorted(direct))}
    straight = {(Q, K, V, O, UA, UB, DA, DB)[t] for t in STRAIGHT}

    def r_c(g):
        n = lead[g]
        push(store[g].at[n, :, :, oc], from_core[g].at[n], s_gc.at[(g > O) + (g > UB)], r_gc.at[g], d_core)

    def r_push_x(g, whole):
        n = lead[g]
        for k in range(1, FK):
            ff = fplus(k)
            if whole:
                push(store[g].at[n, :, :, c, ff], from_x[g].at[n, f], s_gx.at[g, k - 1], r_gx.at[g, k - 1], d_f(ff))
            else:
                t = store[g].at[n, :, y, c, ff]
                push(t, from_x[g].at[n, f, :, 0], s_gx.at[g, k - 1], r_gx.at[g, k - 1], d_f(ff))

    def r_push_y(g, whole):
        n = lead[g]
        if whole:
            push(store[g].at[n, :, oy, c], from_y[g].at[n], s_gy.at[g], r_gy.at[g], d_y)
        else:
            push(store[g].at[n, :, oy, c, f], from_y[g].at[n, :, 0], s_gy.at[g], r_gy.at[g], d_y)

    def over_z(one):
        def step(zz, carry):
            one(zz)
            return carry

        lax.fori_loop(0, Z, step, 0)

    def r_1(g):
        n = lead[g]
        got(from_core[g].at[n], r_gc.at[g])

        def one(zz):
            t = store[g][n, zz, :, c].astype(F32) + from_core[g][n, zz].astype(F32)
            store[g][n, zz, :, c] = t.astype(BF16)

        over_z(one)
        if g in direct:
            r_push_x(g, False)
            r_push_y(g, False)
            for k in range(1, FK):
                ff = fplus(k)
                t = store[g].at[n, :, oy, c, ff]
                push(t, from_x[g].at[n, f, :, 1], s_gd.at[slot[g], k - 1], r_gd.at[slot[g], k - 1], d_diag(ff))
        elif g in y_first:
            r_push_y(g, True)
        else:
            r_push_x(g, True)

    def r_2(g):
        n = lead[g]
        if g in direct:
            return
        if g in y_first:
            got(from_y[g].at[n], r_gy.at[g])

            def one(zz):
                t = store[g][n, zz, y, c].astype(F32) + from_y[g][n, zz].astype(F32)
                store[g][n, zz, y, c] = t.astype(BF16)

            over_z(one)
            r_push_x(g, False)
        else:
            for k in range(1, FK):
                got(from_x[g].at[n, fminus(k)], r_gx.at[g, k - 1])

            def one(zz):
                t = store[g][n, zz, :, c, f].astype(F32)
                for k in range(1, FK):
                    t = t + from_x[g][n, fplus(k), zz].astype(F32)
                store[g][n, zz, :, c, f] = t.astype(BF16)

            if FK > 1:
                over_z(one)
            r_push_y(g, False)

    def r_z(g):
        n = lead[g]
        if g in direct:
            got(from_y[g].at[n, :, 0], r_gy.at[g])
            for k in range(1, FK):
                got(from_x[g].at[n, fminus(k), :, 0], r_gx.at[g, k - 1])
                got(from_x[g].at[n, fminus(k), :, 1], r_gd.at[slot[g], k - 1])

            def one(zz):
                t = store[g][n, zz, y, c, f].astype(F32) + from_y[g][n, zz, 0].astype(F32)
                for k in range(1, FK):
                    t = t + from_x[g][n, fplus(k), zz, 0].astype(F32) + from_x[g][n, fplus(k), zz, 1].astype(F32)
                store[g][n, zz, y, c, f] = t.astype(BF16)

            over_z(one)
        elif g in y_first:
            for k in range(1, FK):
                got(from_x[g].at[n, fminus(k), :, 0], r_gx.at[g, k - 1])

            def one(zz):
                t = store[g][n, zz, y, c, f].astype(F32)
                for k in range(1, FK):
                    t = t + from_x[g][n, fplus(k), zz, 0].astype(F32)
                store[g][n, zz, y, c, f] = t.astype(BF16)

            if FK > 1:
                over_z(one)
        else:
            got(from_y[g].at[n, :, 0], r_gy.at[g])

            def one(zz):
                t = store[g][n, zz, y, c, f].astype(F32) + from_y[g][n, zz, 0].astype(F32)
                store[g][n, zz, y, c, f] = t.astype(BF16)

            over_z(one)
        if g in straight:
            for k in range(1, Z):
                zz = zplus(k)
                push(store[g].at[n, zz, y, c, f], from_z[g].at[n, z], s_gz.at[g], r_gz.at[g, 0], d_z(zz))
        else:
            r_fold(g, 1)

    def r_fold(g, bit):
        n = lead[g]
        for m in range(bit, Z, 2 * bit):
            push(
                store[g].at[n, zxor(m), y, c, f], from_z[g].at[n, zxor(bit ^ (m - 1))],
                s_gz.at[g], r_gz.at[g, bit.bit_length() - 1], d_z(zxor(bit)),
            )

    def r_zz(g):
        n = lead[g]
        bit = 1
        while g not in straight and 2 * bit < Z:
            got(from_z[g].at[n, 0 : Z // (2 * bit)], r_gz.at[g, bit.bit_length() - 1])
            for m in range(0, Z, 2 * bit):
                zz, at = zxor(m), zxor(m + bit - 1)
                t = store[g][n, zz, y, c, f].astype(F32) + from_z[g][n, at].astype(F32)
                store[g][n, zz, y, c, f] = t.astype(BF16)
            bit *= 2
            r_fold(g, bit)

    def r_end(g):
        n = lead[g]
        t = store[g][n, z, y, c, f].astype(F32)
        if g in straight:
            got(from_z[g].at[n, 0 : Z - 1], r_gz.at[g, 0])
            for k in range(1, Z):
                t = t + from_z[g][n, zplus(k)].astype(F32)
        else:
            at = zxor(Z // 2 - 1)
            got(from_z[g].at[n, at], r_gz.at[g, (Z // 2).bit_length() - 1])
            t = t + from_z[g][n, at].astype(F32)
        if g <= V:
            gqkv_ref[:, g * D : (g + 1) * D] = t
        elif g == O:
            gout_ref[...] = t
        elif g <= UB:
            gup_ref[:, (g - UA) * HF : (g - UA + 1) * HF] = t
        else:
            gdown_ref[(g - DA) * 2 * SLAB : (g - DA + 1) * 2 * SLAB, :] = t
        r_sent(g)

    def r_sent(g):
        n = lead[g]
        for k in range(1, FK):
            ff = fplus(k)
            if g in y_first or g in direct:
                sent(store[g].at[n, :, y, c, ff], s_gx.at[g, k - 1])
            else:
                sent(store[g].at[n, :, :, c, ff], s_gx.at[g, k - 1])
            if g in direct:
                sent(store[g].at[n, :, oy, c, ff], s_gd.at[slot[g], k - 1])
        if g in y_first and g not in direct:
            sent(store[g].at[n, :, oy, c], s_gy.at[g])
        else:
            sent(store[g].at[n, :, oy, c, f], s_gy.at[g])
        sent(store[g].at[n, 0 : Z - 1, y, c, f], s_gz.at[g])

    turns = sorted(range(1, Z), key=lambda m: (m & -m, m)) + [0]

    def plane(n):
        m = jnp.int32(0)
        for k in range(Z - 1):
            m = jnp.where(n == k, turns[k], m)
        return zxor(m)

    def p_sum(m):
        zz = zxor(m)
        got(crf.at[zz], r_pc.at[zz])
        t = tokb[zz, c].astype(F32) + crf[zz].astype(F32)
        bit = 1
        while bit < Z and m % (2 * bit) == 0:
            at = zxor(m + bit - 1)
            got(zrf.at[at], r_pz.at[at])
            t = t + zrf[at].astype(F32)
            bit *= 2
        return t

    def p_z(s):
        m = turns[s]
        bit = m & -m
        zz, at = zxor(m), zxor(bit ^ (m - 1))
        tokb[zz, c] = p_sum(m).astype(BF16)
        push(tokb.at[zz, c], zrf.at[at], s_pz, r_pz.at[at], d_z(zxor(bit)))

    def queries_back():
        push(gqs, gqr, s_y.at[5], r_y.at[5], d_y)

    def sums():
        push(sg.at[0], src, s_sc, r_sc, d_core)

    def sums_core():
        got(src, r_sc)
        sg[1] = sg[0] + src[...]
        for k in range(1, FK):
            push(sg.at[1], srx.at[f], s_sx.at[k - 1], r_sx.at[k - 1], d_f(fplus(k)))

    def sums_x():
        t = sg[1]
        for k in range(1, FK):
            got(srx.at[fminus(k)], r_sx.at[k - 1])
            t = t + srx[fminus(k)]
        sg[2] = t
        push(sg.at[2], sry, s_sy, r_sy, d_y)

    def sums_y():
        got(sry, r_sy)
        sg[3] = sg[2] + sry[...]
        for k in range(1, Z):
            zz = zplus(k)
            push(sg.at[3], srz.at[z], s_sz, r_sz, d_z(zz))

    def sums_z():
        sent(sg.at[0], s_sc)
        for k in range(1, FK):
            sent(sg.at[1], s_sx.at[k - 1])
        sent(sg.at[2], s_sy)
        sent(srz.at[0 : Z - 1], s_sz)
        t = sg[3]
        got(srz.at[0 : Z - 1], r_sz)
        for k in range(1, Z):
            t = t + srz[zplus(k)]
        gsm_ref[...] = t

    def first():
        for n, t in enumerate((gs, gu, gd)):
            sent(t.at[:, :, :, oc], s_gc.at[n])
        sent(tokb.at[:, oc], s_pc)
        sent(tokb.at[0 : Z - 1, c], s_pz)
        sent(dot_.at[:, grows, near_half], s_y.at[4])
        sent(gqs, s_y.at[5])
        got(gqr, r_y.at[5])
        t = p_sum(0) + acc[...] + gqr[...].astype(F32)
        mean, centered, rstd = moments(tok_ref[...].astype(F32))
        gtok_ref[...] = (hid[...] + norm_back(t * par[0:1, :], centered * rstd, rstd)).astype(BF16)


    qrows = slice(HD, HD + SLAB)
    grows = slice(0, HD + SLAB)
    near_half, far_half = slice(0, R), slice(R, 2 * R)

    def far_out():
        push(oh, ohr, s_y.at[0], r_y.at[0], d_y)
        push(ml, mlr, s_y.at[1], r_y.at[1], d_y)

    def far_got():
        got(ohr, r_y.at[0])
        got(mlr, r_y.at[1])

    def back_got():
        got(qt.at[:, qrows, far_half], r_y.at[3])
        got(dot_.at[:, grows, far_half], r_y.at[4])

    events = {
        "tr": lambda: tok_right(z),
        "tl": lambda: tok_left(z),
        "tp": lambda: push(tokb.at[z, c], tokp, s_tp, r_tp, d_y),
        "tc": lambda: tok_core(z),
        "tok_z": tok_z,
        "gtokp": lambda: got(tokp, r_tp),
        "w_out_z": w_out_z, "w_own_y": w_own_y, "w_own_x": w_own_x, "w_z": w_z, "w_m": w_m, "w_l": w_l, "w_c": w_c,
        "o_hi": far_out,
        "o_lo": lambda: push(ol, olr, s_y.at[2], r_y.at[2], d_y),
        "g_o": far_got,
        "g_ol": lambda: got(olr, r_y.at[2]),
        "qtail": lambda: push(qt.at[:, qrows, near_half], qt.at[:, qrows, far_half], s_y.at[3], r_y.at[3], d_y),
        "dO": lambda: push(dot_.at[:, grows, near_half], dot_.at[:, grows, far_half], s_y.at[4], r_y.at[4], d_y),
        "g_dO": back_got,
        "gq": queries_back,
        "r_c": r_c, "r_1": r_1, "r_2": r_2, "r_z": r_z, "r_zz": r_zz, "r_end": r_end,
        "p_z": p_z,
        "first": first,
        "s": lambda k: (sums, sums_core, sums_x, sums_y)[k](),
        "s_end": sums_z,
    }
    chunks = {"q": Q, "k": K, "v": V, "o": O, "ua": UA, "ub": UB, "da": DA, "db": DB}
    plan = order_of(Z)

    def do(stage):
        for name, *which in plan.get(stage, ()):
            events[name](*[chunks.get(t, t) for t in which])

    def run(stage, n):
        for at in range(Z):
            if (stage, at) in plan:
                @pl.when(n == at)
                def _():
                    do((stage, at))

    for t in arriving:
        t.wait()
    do("masks")

    starts, ends, stops = [], [], []
    total = jnp.int32(0)
    for t in range(NT):
        starts.append(total)
        stops.append(total + sup_ref[0, t])
        total = total + len_ref[0, t]
        ends.append(total)

    lane = lax.broadcasted_iota(jnp.int32, (1, 128), 1)
    lane_start = jnp.zeros((1, 128), jnp.int32)
    lane_stop = jnp.zeros((1, 128), jnp.int32)
    for t in range(NT):
        lane_start = jnp.where(lane == t, starts[t], lane_start)
        lane_stop = jnp.where(lane == t, stops[t], lane_stop)
    lane_ones = jnp.where((lane >= NT) & (lane < NT + 3), 1.0, 0.0)

    def mask_of(n):
        pos = (n * 2 + y) * 2 * R + lax.broadcasted_iota(jnp.int32, (2 * R, 128), 0)
        seen = (pos >= lane_start) & (pos < lane_stop)
        extra = jnp.where(lane < NT, jnp.where(seen, 0.0, MASKED), lane_ones)
        return extra.astype(BF16)

    def mask_block(n, carry):
        eb[n] = mask_of(n)
        return carry

    lax.fori_loop(0, Z, mask_block, 0)

    row = lax.broadcasted_iota(jnp.int32, (HD, 2 * R), 0)
    col = lax.broadcasted_iota(jnp.int32, (HD, 2 * R), 1)
    qpos = jnp.where(col < R, i * R + col, ((z * 2 + oy) * 2 + c - 1) * R + col)
    onehot = jnp.zeros((HD, 2 * R), F32)
    for t in range(NT):
        onehot = jnp.where((row == t) & (qpos >= starts[t]) & (qpos < ends[t]), 1.0, onehot)
    for h in range(H):
        qt[h, HD : 2 * HD, :] = onehot.astype(BF16)
        dot_[h, HD + SLAB : 2 * HD, :] = jnp.zeros((HD - SLAB, 2 * R), BF16)
        ot[h] = jnp.zeros((2 * HD, 2 * R), F32)
        mrun[h] = jnp.full((1, 2 * R), MASKED, F32)

    do("small")

    piece = D // NSH
    small = w0[:, :, :, :, :, 3 * D : 3 * D + 128].reshape(NSH * SLAB, 128)
    spread = (
        lax.rem(lax.broadcasted_iota(jnp.int32, (128, D), 1), piece)
        == lax.broadcasted_iota(jnp.int32, (128, D), 0)
    )
    wide = dot_nn(small, spread.astype(BF16))
    mine = (
        lax.broadcasted_iota(jnp.int32, (NSH * SLAB, D), 1) // piece
        == lax.broadcasted_iota(jnp.int32, (NSH * SLAB, D), 0) // SLAB
    )
    wide = jnp.where(mine, wide, 0.0)
    par[...] = jnp.sum(wide.reshape(NSH, SLAB, D), axis=0)
    pick = (
        lax.broadcasted_iota(jnp.int32, (NSH, NSH * SLAB), 1)
        == lax.broadcasted_iota(jnp.int32, (NSH, NSH * SLAB), 0) * SLAB + 8
    )
    ups = dot_nn(pick.astype(BF16), small).astype(BF16)
    spread = (
        lax.rem(lax.broadcasted_iota(jnp.int32, (128, FF), 1), 4 * piece)
        == lax.broadcasted_iota(jnp.int32, (128, FF), 0)
    )
    wide = dot_nn(ups, spread.astype(BF16))
    mine = (
        lax.broadcasted_iota(jnp.int32, (NSH, FF), 1) // (4 * piece)
        == lax.broadcasted_iota(jnp.int32, (NSH, FF), 0)
    )
    upb[...] = col_sum(jnp.where(mine, wide, 0.0))
    ln1g, ln1b = par[0:1, :], par[1:2, :]

    tokens = tok_ref[...].astype(F32)
    mean, centered, rstd = moments(tokens)
    xq[0:R, :] = (centered * rstd * ln1g + ln1b).astype(BF16)
    mean, centered, rstd = moments(tokp[...].astype(F32))
    xq[R : 2 * R, :] = (centered * rstd * ln1g + ln1b).astype(BF16)
    wq = w0[:, :, :, :, :, 0:D].reshape(D, D)
    qs[...] = (dot_nn(xq[...], wq) + par[2:3, :]).astype(BF16)
    for h in range(H):
        qt[h, 0:HD, :] = qs[:, h * HD : (h + 1) * HD].T

    def near(s):
        inner = jnp.minimum(z, Z - 1 - z)
        odd = lax.rem(s, 2)
        paired = z + (1 - 2 * odd) * ((s + 1) // 2)
        rest = jnp.where(z < Z - 1 - z, s, Z - 1 - s)
        return jnp.where(s <= 2 * inner, paired, rest)

    def attend(h, keys, values, extra, span):
        cols = slice(h * HD, (h + 1) * HD)
        s = dot_nn(jnp.concatenate([keys[:, cols], extra], axis=1), qt[h, :, span]) * BINARY
        top0 = mrun[h, :, span]
        top = jnp.maximum(top0, jnp.ceil(jnp.max(s, axis=0, keepdims=True)))
        e = jnp.exp2(s - top).astype(BF16)
        grown = dot_tn(jnp.concatenate([values[:, cols], extra], axis=1), e)
        ot[h, :, span] = ot[h, :, span] * jnp.exp2(top0 - top) + grown
        mrun[h, :, span] = top

    def ahead(n, carry):
        zz = near(n)
        run("A", n)
        got(tokb.at[zz, oc], r_t.at[zz, oc])
        mean, centered, rstd = moments(tokb[zz].reshape(2 * R, D).astype(F32))
        stat[zz] = jnp.where(lax.broadcasted_iota(jnp.int32, (2 * R, 128), 1) == 0, mean, rstd)
        x = (centered * rstd * par[0:1, :] + par[1:2, :]).astype(BF16)
        kv = dot_nn(x, w0[:, :, :, :, :, D : 3 * D].reshape(D, 2 * D))
        keys = kv[:, 0:D].astype(BF16)
        values = (kv[:, D : 2 * D] + par[3:4, :]).astype(BF16)
        kb[zz] = keys
        vb[zz] = values
        extra = eb[zz]
        for h in range(H):
            attend(h, keys, values, extra, slice(R, 2 * R))
        return carry

    lax.fori_loop(0, Z, ahead, 0)

    do("osplit")
    for h in range(H):
        t = ot[h, 0:HD, R : 2 * R]
        first_part = t.astype(BF16)
        oh[h] = first_part
        ol[h] = (t - first_part.astype(F32)).astype(BF16)
        ml[h : h + 1, :] = mrun[h, :, R : 2 * R]
        ml[H + h : H + h + 1, :] = ot[h, HD + NT : HD + NT + 1, R : 2 * R]
    def ahead_own(n, carry):
        zz = near(n)
        run("B", n)
        for h in range(H):
            attend(h, kb[zz], vb[zz], eb[zz], slice(0, R))
        return carry

    lax.fori_loop(0, Z, ahead_own, 0)
    do("merge")
    parts = []
    row_tail = lax.broadcasted_iota(jnp.int32, (SLAB, R), 0)
    for h in range(H):
        m_own, m_far = mrun[h, :, 0:R], mlr[h : h + 1, :]
        top = jnp.maximum(m_own, m_far)
        a_own, a_far = jnp.exp2(m_own - top), jnp.exp2(m_far - top)
        total = a_own * ot[h, HD + NT : HD + NT + 1, 0:R] + a_far * mlr[H + h : H + h + 1, :]
        inverse = 1.0 / total
        attended = ot[h, 0:HD, 0:R] * (a_own * inverse) + ohr[h].astype(F32) * (a_far * inverse)
        ot[h, 0:HD, 0:R] = attended
        ot[h, HD : HD + 1, 0:R] = inverse
        ot[h, HD + 1 : HD + 2, 0:R] = a_far * inverse
        parts.append(attended.T.astype(BF16))
        m1, m2, m3 = three_terms(top)
        tail = jnp.where(
            row_tail == NT + 3, m1,
            jnp.where(row_tail == NT + 4, m2, jnp.where(row_tail == NT + 5, m3, onehot[0:SLAB, 0:R])),
        )
        qt[h, HD : HD + SLAB, 0:R] = tail.astype(BF16)
    do("out")
    attn_low = jnp.concatenate(parts, axis=1)
    w_out = w1[:, :, :, :, :, 0:D].reshape(D, D)
    hidden = tokens + (dot_nn(attn_low, w_out) + par[4:5, :])
    hid[...] = hidden
    mean2, centered, rstd2 = moments(hidden)
    n2 = centered * rstd2
    nrm2[...] = (n2 * par[5:6, :] + par[6:7, :]).astype(BF16)
    acc[...] = hidden + par[7:8, :]
    gsec[...] = jnp.zeros((R, D), F32)

    def slope_at(j):
        hh = j // (Z // 2)
        return pl.ds(pl.multiple_of(hh * R, R), R), pl.ds(pl.multiple_of((j - hh * (Z // 2)) * CH, 128), CH)

    def forward(j, carry):
        cols = pl.ds(pl.multiple_of(D + j * CH, 128), CH)
        bcols = pl.ds(pl.multiple_of(j * CH, 128), CH)
        pre = dot_nn(nrm2[...], w1[:, :, :, :, :, cols].reshape(D, CH)) + upb[:, bcols]
        phi = 0.5 * (1.0 + lax.erf(pre * (0.5**0.5)))
        act_all[:, bcols] = (pre * phi).astype(BF16)
        slope = phi + pre * (jnp.exp2(pre * pre * (-0.5 / LN2)) * ((2.0 * math.pi) ** -0.5))
        big[1, *slope_at(j)] = slope
        return carry

    def backward(j, carry):
        cols = pl.ds(pl.multiple_of(D + j * CH, 128), CH)
        bcols = pl.ds(pl.multiple_of(j * CH, 128), CH)
        gpre = (dot_nt(cot_ref[...], w2[j].reshape(CH, D)) * big[1, *slope_at(j)]).astype(BF16)
        gsec[...] += dot_nt(gpre, w1[:, :, :, :, :, cols].reshape(D, CH))
        gpre_all[:, bcols] = gpre
        return carry

    do("ffn")
    lax.fori_loop(0, Z, forward, 0)
    do("ffd")
    lax.fori_loop(0, Z, backward, 0)
    do("ln2")

    g_second = gsec[...]
    n2 = (hid[...] - mean2) * rstd2
    ln2g = par[5:6, :]
    cot32 = cot_ref[...].astype(F32)
    grad_hidden = cot32 + norm_back(g_second * ln2g, n2, rstd2)
    hid[...] = grad_hidden
    g_branch = grad_hidden.astype(BF16)
    do("dOc")
    for h in range(H):
        rows = slice(h * HD, (h + 1) * HD)
        w_head = w1[:, :, :, :, :, 0:D].reshape(D, D)[rows, :]
        ga = dot_nt(w_head, g_branch).astype(BF16).astype(F32)
        low = (ga * ot[h, HD : HD + 1, 0:R]).astype(BF16)
        exact = ot[h, 0:HD, 0:R] + olr[h].astype(F32) * ot[h, HD + 1 : HD + 2, 0:R]
        delta = col_sum(low.astype(F32) * exact)
        d1, d2, d3 = three_terms(delta)
        tail = jnp.where(
            row_tail == NT, -d1, jnp.where(row_tail == NT + 1, -d2, jnp.where(row_tail == NT + 2, -d3, 0.0))
        )
        dot_[h, 0:HD, 0:R] = low
        dot_[h, HD : HD + SLAB, 0:R] = tail.astype(BF16)
        dos[0:R, rows] = low.T

    def g_up(j, carry):
        bcols = pl.ds(pl.multiple_of(j * CH, 128), CH)
        t = dot_tn(nrm2[...], gpre_all[:, bcols]).astype(BF16).reshape(Z, 2, 2, FK, SLAB, CH)
        hh = j // (Z // 2)
        upg[:, bcols] = col_sum(gpre_all[:, bcols].astype(F32))
        gu[hh, :, :, :, :, :, pl.ds(pl.multiple_of((j - hh * (Z // 2)) * CH, 128), CH)] = t
        return carry

    def g_down(j, carry):
        bcols = pl.ds(pl.multiple_of(j * CH, 128), CH)
        acc[...] += dot_nn(act_all[:, bcols], w2[j].reshape(CH, D))
        t = dot_tn(act_all[:, bcols], cot_ref[...]).astype(BF16).reshape(2, 2, FK, 4 * SLAB, D)
        gd[0, j] = t[:, :, :, 0 : 2 * SLAB]
        gd[1, j] = t[:, :, :, 2 * SLAB : 4 * SLAB]
        return carry

    do("dwu")
    lax.fori_loop(0, Z, g_up, 0)
    do("dwd")
    lax.fori_loop(0, Z, g_down, 0)
    out_ref[...] = acc[...].astype(BF16)
    do("dwo")
    gs[O] = dot_tn(attn_low, g_branch).astype(BF16).reshape(Z, 2, 2, FK, SLAB, D)
    zero = jnp.zeros((1, D), F32)
    for r in range(SLAB):
        sg[0, r : r + 1, :] = zero
    sg[0, 4:5, :] = col_sum(g_branch.astype(F32))
    sg[0, 5:6, :] = col_sum(g_second * n2)
    sg[0, 6:7, :] = col_sum(g_second)
    sg[0, 7:8, :] = col_sum(cot32)
    for r in range(FF // D):
        sg[0, 8 + r : 9 + r, :] = upg[:, r * D : (r + 1) * D]

    dqt[...] = jnp.zeros((H, HD, 2 * R), F32)
    lacc[...] = jnp.zeros((3, 8, D), F32)

    def tok_sent():
        @pl.when(z < Z - 1)
        def _():
            for k in range(Z):
                @pl.when(z - k >= 0)
                def _():
                    sent(tokb.at[z - k, c], s_tz.at[0, z - k])

        @pl.when(z > 0)
        def _():
            for k in range(Z):
                @pl.when(z + k < Z)
                def _():
                    sent(tokb.at[z + k, c], s_tz.at[1, z + k])

        sent(tokb.at[:, c], s_tc)
        sent(tokb.at[z, c], s_tp)

    def heads(zz, span):
        keys, values, extra = kb[zz], vb[zz], eb[zz]
        dks, dvs = [], []
        for h in range(H):
            cols = slice(h * HD, (h + 1) * HD)
            s = dot_nn(jnp.concatenate([keys[:, cols], extra], axis=1), qt[h, :, span]) * BINARY
            tail = qt[h, HD : HD + SLAB, span].astype(F32)
            at = lax.broadcasted_iota(jnp.int32, tail.shape, 0)
            top = col_sum(jnp.where((at >= NT + 3) & (at < NT + 6), tail, 0.0))
            dp = dot_nn(jnp.concatenate([values[:, cols], extra], axis=1), dot_[h, :, span])
            e = jnp.exp2(s - top).astype(BF16)
            ds = (e.astype(F32) * dp).astype(BF16)
            dvs.append(dot_nn(e, dos[span, cols]))
            dks.append(dot_nn(ds, qs[span, cols]) * HD ** (-0.5))
            dqt[h, :, span] += dot_tn(keys[:, cols], ds)
        return jnp.concatenate(dks + dvs, axis=1)

    def rest(n, zz, dkv32):
        dkv = dkv32.astype(BF16)
        run("t", n)
        gp = dot_nt(dkv, w0[:, :, :, :, :, D : 3 * D].reshape(D, 2 * D))
        norm = (tokb[zz].reshape(2 * R, D).astype(F32) - stat[zz, :, 0:1]) * stat[zz, :, 1:2]
        tokb[zz] = gp.astype(BF16).reshape(2, R, D)
        push(tokb.at[zz, oc], crf.at[zz], s_pc, r_pc.at[zz], d_core)
        x = (norm * par[0:1, :] + par[1:2, :]).astype(BF16)
        lacc[0] += fold_rows(gp * norm)
        lacc[1] += fold_rows(gp)
        lacc[2] += fold_rows(dkv32[:, D : 2 * D])
        big[0] = jnp.where(n == 0, 0.0, big[0]) + dot_tn(x, dkv)

    def behind_early(n, carry):
        run("e", n)
        big[n] = heads(plane(n), near_half)
        return carry

    def behind_far(n, carry):
        run("h", n)
        zz = plane(n)
        rest(n, zz, big[n] + heads(zz, far_half))
        return carry

    def behind(n, carry):
        run("h", n)
        zz = plane(n)
        rest(n, zz, heads(zz, slice(0, 2 * R)))
        return carry

    do("sent")
    tok_sent()
    for g in range(len(groups)):
        w_sent(g)
    sent(oh, s_y.at[0])
    sent(ml, s_y.at[1])
    sent(ol, s_y.at[2])
    sent(qt.at[:, qrows, near_half], s_y.at[3])
    E = big.shape[0] if Z == 4 else 0
    if E:
        lax.fori_loop(0, E, behind_early, 0)
    do("dosT")
    for h in range(H):
        dos[R : 2 * R, h * HD : (h + 1) * HD] = dot_[h, 0:HD, R : 2 * R].T
    if E:
        lax.fori_loop(0, E, behind_far, 0)
    lax.fori_loop(E, Z, behind, 0)

    do("kv")
    gs[K] = big[0, :, 0:D].astype(BF16).reshape(Z, 2, 2, FK, SLAB, D)
    gs[V] = big[0, :, D : 2 * D].astype(BF16).reshape(Z, 2, 2, FK, SLAB, D)

    def queries():
        dq = jnp.concatenate([(dqt[h] * (HD**-0.5)).T for h in range(H)], axis=1).astype(BF16)
        gs[Q] = dot_tn(xq[...], dq).astype(BF16).reshape(Z, 2, 2, FK, SLAB, D)
        gq = dot_nt(dq, w0[:, :, :, :, :, 0:D].reshape(D, D))
        acc[...] = gq[0:R]
        gqs[...] = gq[R : 2 * R].astype(BF16)
        both = jnp.concatenate([tok_ref[...], tokp[...]], axis=0).astype(F32)
        mean, centered, rstd = moments(both)
        sg[0, 0:1, :] = col_sum(lacc[0]) + col_sum(gq * (centered * rstd))
        sg[0, 1:2, :] = col_sum(lacc[1]) + col_sum(gq)
        sg[0, 2:3, :] = col_sum(dq.astype(F32))
        sg[0, 3:4, :] = col_sum(lacc[2])

    do("q")
    queries()
    do("end")


def layer(Z, FK, R, D, FF, NT, operands):
    vm = lambda shape, dtype: pltpu.VMEM(shape, dtype)
    dma = lambda *shape: pltpu.SemaphoreType.DMA(shape)
    one = pltpu.SemaphoreType.DMA
    others = max(FK - 1, 1)
    lead = (Z, 2, 2, FK)
    slabs = ((SLAB, 3 * D + 128), (SLAB, D + FF), (4 * SLAB, D))
    gslabs = ((4, SLAB, D), (2, SLAB, FF // 2), (2, 2 * SLAB, D))
    scratch = [
        vm((Z, 2, R, D), BF16),
        vm((R, D), BF16),
        vm((Z, 2 * R, D), BF16),
        vm((Z, 2 * R, D), BF16),
        vm((Z, 2 * R, 128), BF16),
        vm((Z, 2 * R, 128), F32),
        *[vm(lead + s, BF16) for s in slabs],
        *[vm((s[0],) + lead + s[1:], BF16) for s in gslabs],
        *[vm((s[0], Z, 2, FK) + s[1:], BF16) for s in gslabs],
        *[vm((s[0], FK, Z, 2) + s[1:] if FK > 1 else (SLAB, 128), BF16) for s in gslabs],
        *[vm((s[0], Z, FK) + s[1:], BF16) for s in gslabs],
        *[vm((s[0], Z) + s[1:], BF16) for s in gslabs],
        vm((Z, R, D), BF16),
        vm((Z, R, D), BF16),
        vm((SLAB, D), F32),
        vm((1, FF), F32),
        vm((H, 2 * HD, 2 * R), BF16),
        vm((H, 2 * HD, 2 * R), BF16),
        vm((2 * R, D), BF16),
        vm((2 * R, D), BF16),
        vm((H, 2 * HD, 2 * R), F32),
        vm((H, 1, 2 * R), F32),
        vm((H, HD, 2 * R), F32),
        vm((H, HD, R), BF16),
        vm((H, HD, R), BF16),
        vm((2 * H, R), F32),
        vm((H, HD, R), BF16),
        vm((H, HD, R), BF16),
        vm((2 * H, R), F32),
        vm((R, D), BF16),
        vm((R, D), BF16),
        vm((R, D), BF16),
        vm((R, D), F32),
        vm((R, D), F32),
        vm((R, D), F32),
        vm((3, 8, D), F32),
        vm((1, FF), F32),
        vm((2 * R, D), BF16),
        vm((4, SLAB, D), F32),
        vm((SLAB, D), F32),
        vm((FK, SLAB, D), F32),
        vm((SLAB, D), F32),
        vm((Z, SLAB, D), F32),
        vm((SLAB, 128), F32),
        vm((R, D), BF16),
        vm((R, D), BF16),
        vm((R, FF), BF16),
        vm((R, FF), BF16),
        vm((3 if Z == 4 else 2, 2 * R, 2 * D), F32),
        dma(7),
        dma(2, Z), one, dma(Z, 2), one, one,
        dma(5), dma(5, Z), dma(5), dma(5, Z), dma(5, others), dma(5, others), dma(5), dma(5),
        dma(3), dma(8), dma(8, others), dma(8, others), dma(8), dma(8),
        dma(max(len(DIRECT), 1), others), dma(max(len(DIRECT), 1), others), dma(8), dma(8, Z.bit_length() - 1),
        one, dma(Z), one, dma(Z), dma(6), dma(6),
        one, one, dma(others), dma(others), one, one, one, one,
    ]
    vmem = pl.BlockSpec(memory_space=pltpu.VMEM)
    smem = pl.BlockSpec(memory_space=pltpu.SMEM)
    shape = jax.ShapeDtypeStruct
    return pl.pallas_call(
        functools.partial(body, Z, FK, R, D, NT),
        out_shape=(
            pltpu.VMEM((R, D), BF16),
            pltpu.VMEM((R, D), BF16),
            pltpu.VMEM((SLAB, 3 * D), F32),
            pltpu.VMEM((SLAB, D), F32),
            pltpu.VMEM((SLAB, FF), F32),
            pltpu.VMEM((4 * SLAB, D), F32),
            pltpu.VMEM((SLAB, D), F32),
        ),
        in_specs=[pl.BlockSpec(memory_space=pl.ANY)] * 6 + [vmem] * 9 + [smem] * 2,
        out_specs=[vmem] * 7,
        scratch_shapes=scratch,
        compiler_params=pltpu.CompilerParams(
            collective_id=0, has_side_effects=True, vmem_limit_bytes=63 * 2**20
        ),
        name="layer",
    )(*operands)


def finish(NSH, FK, *refs):
    big_in, small_in, big_out, small_out = refs[0:6], refs[6], refs[7:13], refs[13:22]
    for a, b in zip(big_in, big_out):
        b[...] = a[...]
    at = lax.axis_index("blk") * FK
    if FK > 1:
        at = at + lax.axis_index("fsdp")
    D = small_in.shape[1]
    piece = D // NSH
    lane = lax.broadcasted_iota(jnp.int32, (128, D), 1)
    take = lax.broadcasted_iota(jnp.int32, (128, D), 0)
    full = small_in[...]
    for r in range(8):
        chosen = jnp.where(lane == at * piece + take, full[r : r + 1, :], 0.0)
        small_out[r][...] = jnp.sum(chosen, axis=1).reshape(1, 128)[:, 0:piece]
    FF = D * 4
    total = jnp.zeros((128,), F32)
    for r in range(4):
        chosen = jnp.where(lane + r * D == at * 4 * piece + take, full[8 + r : 9 + r, :], 0.0)
        total = total + jnp.sum(chosen, axis=1)
    small_out[8][...] = total.reshape(1, 128)[:, 0 : 4 * piece]


def hand_over(NSH, FK, FF, results):
    *big, small = results
    D = small.shape[1]
    vmem = pl.BlockSpec(memory_space=pltpu.VMEM)
    shape = jax.ShapeDtypeStruct
    return pl.pallas_call(
        functools.partial(finish, NSH, FK),
        out_shape=(
            *[shape(v.shape, v.dtype) for v in big],
            *[shape((1, D // NSH), F32) for _ in range(8)],
            shape((1, FF // NSH), F32),
        ),
        in_specs=[vmem] * 7,
        out_specs=[vmem] * 15,
        name="finish",
    )(*[pltpu.with_memory_space_constraint(v, pltpu.VMEM) for v in results])


def shards(
    blocks, fsdp,
    tokens, ln1_gain, ln1_bias, qkv_weight, query_bias, value_bias, out_weight, out_bias,
    ln2_gain, ln2_bias, up_weight, up_bias, down_weight, down_bias,
    table_lengths, support_lengths, cotangent,
):
    R, D = tokens.shape[1:]
    FF = up_weight.shape[1]
    NT = table_lengths.shape[1]
    smalls = (ln1_gain, ln1_bias, query_bias, value_bias, out_bias, ln2_gain, ln2_bias, down_bias, up_bias)
    weights = (qkv_weight, out_weight, up_weight, down_weight)
    inside = qkv_weight.shape[0] == SLAB
    FK = fsdp if inside else 1
    if not inside:
        whole = lambda v: lax.all_gather(v, "fsdp", axis=0, tiled=True)
        smalls = tuple(whole(v) for v in smalls)
        weights = tuple(whole(v) for v in weights)
    results = layer(
        blocks // 4, FK, R, D, FF, NT,
        (tokens[0], cotangent[0], *weights, *[v[None] for v in smalls], table_lengths, support_lengths),
    )
    block_out, grad_tokens, g_qkv, g_out, g_up, g_down, *small_grads = hand_over(
        blocks * FK, FK, FF, results
    )
    small_grads = [v[0] for v in small_grads]
    weight_grads = [g_qkv, g_out, g_up, g_down]
    if not inside:
        spread = lambda v: lax.psum_scatter(v, "fsdp", scatter_dimension=0, tiled=True)
        small_grads = [spread(v) for v in small_grads]
        weight_grads = [spread(v) for v in weight_grads]
    g_ln1g, g_ln1b, g_qb, g_vb, g_ob, g_ln2g, g_ln2b, g_db, g_ub = small_grads
    g_qkv, g_out, g_up, g_down = weight_grads
    return (
        block_out[None], grad_tokens[None], g_ln1g, g_ln1b, g_qkv, g_qb, g_vb, g_out, g_ob,
        g_ln2g, g_ln2b, g_up, g_ub, g_down, g_db,
    )


def solution(mesh):
    both = ("blk", "fsdp")
    vec, mat, rows = P(both), P(both, None), P("fsdp", "blk", None)
    return jax.shard_map(
        functools.partial(shards, mesh.shape["blk"], mesh.shape["fsdp"]),
        mesh=mesh,
        in_specs=(
            rows, vec, vec, mat, vec, vec, mat, vec, vec, vec, mat, vec, mat, vec,
            P("fsdp", None), P("fsdp", None), rows,
        ),
        out_specs=(rows, rows, vec, vec, mat, vec, vec, mat, vec, vec, vec, mat, vec, mat, vec),
        check_vma=False,
    )
```

```python
import functools
import math

import jax
import jax.numpy as jnp
from jax import lax
from jax.experimental import pallas as pl
from jax.experimental.pallas import tpu as pltpu
from jax.sharding import PartitionSpec as P

H = 4
HD = 128
SLAB = 16
EPSILON = 1e-05
MASKED = -1e30
LN2 = math.log(2.0)
BINARY = HD ** (-0.5) / LN2
MESH = pl.DeviceIdType.MESH
F32 = jnp.float32
BF16 = jnp.bfloat16


def dot_nn(a, b):
    return lax.dot_general(a, b, (((1,), (0,)), ((), ())), preferred_element_type=F32)


def dot_nt(a, b):
    return lax.dot_general(a, b, (((1,), (1,)), ((), ())), preferred_element_type=F32)


def dot_tn(a, b):
    return lax.dot_general(a, b, (((0,), (0,)), ((), ())), preferred_element_type=F32)


def moments(v):
    mean = jnp.mean(v, axis=-1, keepdims=True)
    centered = v - mean
    rstd = lax.rsqrt(jnp.mean(centered * centered, axis=-1, keepdims=True) + EPSILON)
    return mean, centered, rstd


def norm_back(g, n, r):
    return r * (g - jnp.mean(g, axis=-1, keepdims=True) - n * jnp.mean(g * n, axis=-1, keepdims=True))


def three_terms(v):
    first = v.astype(BF16)
    rest = v - first.astype(F32)
    second = rest.astype(BF16)
    third = (rest - second.astype(F32)).astype(BF16)
    return first.astype(F32), second.astype(F32), third.astype(F32)


def col_sum(v):
    return jnp.sum(v, axis=0, keepdims=True)


def fold_rows(v):
    return jnp.sum(v.reshape(v.shape[0] // 8, 8, v.shape[1]), axis=0)


FOUR = {
    "masks": [
        ("w_out_z", 0), ("w_own_x", 2), ("w_own_y", 0), ("tr",), ("w_out_z", 1), ("tl",), ("tp",), ("w_out_z", 2),
    ],
    "small": [
        ("w_z", 0), ("tc",), ("w_own_x", 0), ("w_m", 0), ("w_own_y", 1), ("w_own_y", 4), ("gtokp",), ("w_z", 1),
        ("tok_z", 1), ("w_l", 0), ("w_m", 1), ("w_z", 2), ("w_own_y", 3), ("w_own_y", 2), ("w_c", 0), ("w_own_x", 3),
        ("w_out_z", 4),
    ],
    ("A", 0): [("w_own_x", 1), ("w_own_x", 4), ("tok_z", 2)],
    ("A", 1): [("w_z", 4), ("w_m", 2), ("w_out_z", 3)],
    ("A", 3): [("tok_z", 3), ("w_l", 1), ("w_m", 4), ("w_z", 3)],
    ("B", 0): [("o_hi",)],
    ("B", 1): [("o_lo",)],
    ("B", 2): [("w_m", 3), ("w_l", 4), ("w_l", 2)],
    "merge": [("w_c", 2), ("w_c", 1), ("w_l", 3), ("w_c", 4), ("g_o",)],
    "out": [("qtail",)],
    "ffn": [("w_c", 3)],
    "dOc": [("g_ol",)],
    "dwu": [("dO",)],
    "dwd": [("r_c", "ub")],
    "sent": [("r_1", "ub"), ("r_c", "db")],
    "dosT": [("r_1", "db"), ("g_dO",), ("r_2", "ub")],
    ("h", 1): [("r_c", "ua")],
    ("t", 1): [("r_2", "db"), ("r_c", "o"), ("r_z", "ub")],
    ("h", 2): [("r_zz", "ub"), ("r_1", "ua"), ("p_z", 1)],
    ("t", 2): [("r_c", "da"), ("r_z", "db"), ("p_z", 0)],
    ("h", 3): [("r_1", "da"), ("r_1", "o"), ("r_zz", "db")],
    "kv": [("r_2", "ua"), ("p_z", 2)],
    "q": [("r_2", "da"), ("r_c", "v"), ("r_c", "k")],
    "end": [
        ("r_1", "v"), ("r_1", "k"), ("r_2", "o"), ("r_c", "q"), ("r_z", "ua"), ("r_1", "q"), ("s", 0), ("r_z", "da"),
        ("r_end", "db"), ("s", 1), ("r_2", "v"), ("r_z", "o"), ("r_zz", "o"), ("r_2", "k"), ("r_zz", "da"), ("s", 2),
        ("r_2", "q"), ("r_end", "ub"), ("r_z", "k"), ("gq",), ("r_zz", "ua"), ("r_z", "v"), ("r_z", "q"), ("s", 3),
        ("r_zz", "v"), ("r_end", "ua"), ("r_zz", "k"), ("r_zz", "q"), ("r_end", "da"), ("r_end", "o"), ("first",),
        ("r_end", "v"), ("r_end", "k"), ("s_end",), ("r_end", "q"),
    ],
}
Y_FIRST = {0, 2, 5, 6, 7}
DIRECT = {0, 1, 3, 4, 5, 6, 7}
STRAIGHT = {3, 5, 6, 7}


def order_of(Z):
    if Z == 4:
        return FOUR
    most = ("ua", "ub", "da", "db", "o")
    last = ("q", "k", "v")
    plan = {
        "masks": [("w_out_z", 0), ("w_own_y", 0), ("w_own_x", 0), ("tr",), ("tl",), ("tp",), ("tc",)],
        "small": [("w_z", 0), ("w_m", 0), ("w_l", 0), ("gtokp",), ("w_c", 0)],
        ("A", 0): [(step, g) for g in range(1, 5) for step in ("w_out_z", "w_own_y", "w_own_x")],
        ("B", 0): [("o_hi",)] + [(step, g) for step in ("w_z", "w_m") for g in range(1, 5)],
        "merge": [("o_lo",), ("g_o",)] + [("w_l", g) for g in range(1, 5)],
        "out": [("qtail",)] + [("w_c", g) for g in range(1, 5)],
        "dOc": [("g_ol",)],
        "dwu": [("dO",)],
        "sent": [("r_c", g) for g in most],
        "dosT": [("r_1", g) for g in most] + [("g_dO",)],
        ("h", Z - 1): [("r_2", g) for g in most],
        "kv": [("p_z", Z - 2)] + [("r_z", g) for g in most],
        "end": [("gq",)] + [(step, g) for step in ("r_c", "r_1", "r_2", "r_z") for g in last],
    }
    for k in range(1, Z):
        plan.setdefault(("A", k), []).append(("tok_z", k))
    for k in range(Z - 2):
        plan[("t", k + 1)] = [("p_z", k)]
    plan["end"] += [("r_zz", g) for g in most + last] + [("s", k) for k in range(4)] + [("first",), ("s_end",)]
    plan["end"] += [("r_end", g) for g in most + last]
    return plan


def body(
    Z, FK, R, D, NT,
    tok_in, cot_in, wq_in, wo_in, wu_in, wd_in,
    v0, v1, v2, v3, v4, v5, v6, v7, v8, len_ref, sup_ref,
    out_ref, gtok_ref, gqkv_ref, gout_ref, gup_ref, gdown_ref, gsm_ref,
    tokb, tokp, kb, vb, eb, stat, w0, w1, w2, gs, gu, gd,
    cs, cu, cd, xs, xu, xd, ys, yu, yd, zs, zu, zd,
    crf, zrf, par, upb, qt, dot_, qs, dos, ot, mrun, dqt,
    oh, ol, ml, ohr, olr, mlr, gqs, gqr,
    nrm2, hid, acc, gsec, lacc, upg, xq,
    sg, src, srx, sry, srz, tile, tok_ref, cot_ref, act_all, gpre_all, big,
    s_in,
    s_tz, s_tc, r_t, s_tp, r_tp,
    s_wz, r_wz, s_wy, r_wy, s_wx, r_wx, s_wc, r_wc,
    s_gc, r_gc, s_gx, r_gx, s_gy, r_gy, s_gd, r_gd, s_gz, r_gz,
    s_pc, r_pc, s_pz, r_pz, s_y, r_y,
    s_sc, r_sc, s_sx, r_sx, s_sy, r_sy, s_sz, r_sz,
):
    i = lax.axis_index("blk")
    f = lax.axis_index("fsdp")
    c = lax.rem(i, 2)
    y = lax.rem(i // 2, 2)
    z = i // 4
    oc = 1 - c
    oy = 1 - y
    CH = 4 * FK * SLAB * 4
    FF = Z * CH
    NSH = Z * 4 * FK

    def dev(zz, yy, cc, ff):
        return ((zz * 2 + yy) * 2 + cc, ff)

    d_core = dev(z, y, oc, f)
    d_y = dev(z, oy, c, f)

    def zplus(k):
        return lax.rem(z + k, Z)

    def zxor(m):
        out, bit = z, 1
        while bit < Z:
            out = out + bit * ((m // bit) % 2) * (1 - 2 * lax.rem(z // bit, 2))
            bit *= 2
        return out

    def fplus(k):
        return lax.rem(f + k, FK)

    def d_z(zz):
        return dev(zz, y, c, f)

    def d_f(ff):
        return (i, ff)

    def fminus(k):
        return lax.rem(f + FK - k, FK)

    def d_diag(ff):
        return dev(z, oy, c, ff)

    def cp(s, d, ss, rs, to):
        return pltpu.make_async_remote_copy(
            src_ref=s, dst_ref=d, send_sem=ss, recv_sem=rs, device_id=to, device_id_type=MESH
        )

    def push(s, d, ss, rs, to):
        cp(s, d, ss, rs, to).start()

    def got(d, rs):
        cp(d, d, rs, rs, d_core).wait_recv()

    def sent(s, ss):
        cp(s, s, ss, ss, d_core).wait_send()

    arriving = [
        pltpu.make_async_copy(a, b, s_in.at[n])
        for n, (a, b) in enumerate((
            (wq_in, w0.at[z, y, c, f, :, 0 : 3 * D]),
            (tok_in, tokb.at[z, c]),
            (wo_in, w1.at[z, y, c, f, :, 0:D]),
            (wu_in, w1.at[z, y, c, f, :, D : D + FF]),
            (wd_in, w2.at[z, y, c, f]),
            (tok_in, tok_ref),
            (cot_in, cot_ref),
        ))
    ]
    for t in arriving:
        t.start()
    bar = pltpu.get_barrier_semaphore()
    partners = [d_core, d_y] + [d_z(zplus(k)) for k in range(1, Z)]
    partners += [to(fplus(k)) for k in range(1, FK) for to in (d_f, d_diag)]
    for to in partners:
        pl.semaphore_signal(bar, inc=1, device_id=to, device_id_type=MESH)
    tile[...] = jnp.zeros((SLAB, 128), F32)
    for r, v in enumerate((v0, v1, v2, v3, v4, v5, v6, v7, v8)):
        tile[r : r + 1, 0 : v.shape[1]] = v[...].astype(F32)
    w0[z, y, c, f, :, 3 * D : 3 * D + 128] = tile[...].astype(BF16)
    pl.semaphore_wait(bar, len(partners))

    def tok_push(zz, ss_z, to):
        t = tokb.at[zz, c]
        push(t, t, ss_z, r_t.at[zz, c], to)

    def tok_core(zz):
        t = tokb.at[zz, c]
        push(t, t, s_tc, r_t.at[zz, c], d_core)

    def tok_right(zz):
        @pl.when(z < Z - 1)
        def _():
            tok_push(zz, s_tz.at[0, zz], d_z(z + 1))

    def tok_left(zz):
        @pl.when(z > 0)
        def _():
            tok_push(zz, s_tz.at[1, zz], d_z(z - 1))

    def tok_z(k):
        @pl.when(z - k >= 0)
        def _():
            zz = z - k
            got(tokb.at[zz, c], r_t.at[zz, c])
            tok_right(zz)
            tok_core(zz)

        @pl.when(z + k < Z)
        def _():
            zz = z + k
            got(tokb.at[zz, c], r_t.at[zz, c])
            tok_left(zz)
            tok_core(zz)

    HF = FF // 2
    everything = slice(None)
    groups = (
        (w0, everything, everything),
        (w1, everything, slice(0, D + HF)),
        (w1, everything, slice(D + HF, D + FF)),
        (w2, slice(0, 2 * SLAB), everything),
        (w2, slice(2 * SLAB, 4 * SLAB), everything),
    )

    def w_at(g, zz, yy, cc, ff):
        where, rows, cols = groups[g]
        return where.at[zz, yy, cc, ff, rows, cols]

    def w_push_x(g, zz, yy):
        t = w_at(g, zz, yy, c, f)
        for k in range(1, FK):
            push(t, t, s_wx.at[g, k - 1], r_wx.at[g, k - 1], d_f(fplus(k)))

    def w_push_y(g, zz):
        t = w_at(g, zz, y, c, f)
        push(t, t, s_wy.at[g], r_wy.at[g, zz], d_y)

    def w_out_z(g):
        t = w_at(g, z, y, c, f)
        for k in range(1, Z):
            push(t, t, s_wz.at[g], r_wz.at[g, z], d_z(zplus(k)))

    def w_own_y(g):
        w_push_y(g, z)

    def w_own_x(g):
        w_push_x(g, z, y)

    def w_z(g):
        for k in range(1, Z):
            zz = zplus(k)
            got(w_at(g, zz, y, c, f), r_wz.at[g, zz])
            w_push_x(g, zz, y)
            w_push_y(g, zz)

    def w_to_core(g, ff):
        t = w_at(g, everything, everything, c, ff)
        push(t, t, s_wc.at[g], r_wc.at[g], d_core)

    def w_m(g):
        for zz in range(Z):
            got(w_at(g, zz, oy, c, f), r_wy.at[g, zz])
            w_push_x(g, zz, oy)
        w_to_core(g, f)

    def w_l(g):
        for k in range(1, FK):
            got(w_at(g, everything, everything, c, fminus(k)), r_wx.at[g, k - 1])
            w_to_core(g, fminus(k))

    def w_c(g):
        got(w_at(g, everything, everything, oc, everything), r_wc.at[g])

    def w_sent(g):
        sent(w_at(g, slice(0, Z - 1), y, c, f), s_wz.at[g])
        sent(w_at(g, everything, y, c, f), s_wy.at[g])
        for k in range(1, FK):
            sent(w_at(g, everything, everything, c, f), s_wx.at[g, k - 1])
        sent(w_at(g, everything, everything, c, everything), s_wc.at[g])

    store = (gs, gs, gs, gs, gu, gu, gd, gd)
    from_core = (cs, cs, cs, cs, cu, cu, cd, cd)
    from_x = (xs, xs, xs, xs, xu, xu, xd, xd)
    from_y = (ys, ys, ys, ys, yu, yu, yd, yd)
    from_z = (zs, zs, zs, zs, zu, zu, zd, zd)
    lead = (0, 1, 2, 3, 0, 1, 0, 1)
    Q, K, V, O, UA, UB, DA, DB = range(8)
    y_first = {(Q, K, V, O, UA, UB, DA, DB)[t] for t in Y_FIRST}
    direct = {(Q, K, V, O, UA, UB, DA, DB)[t] for t in DIRECT}
    slot = {g: n for n, g in enumerate(sorted(direct))}
    straight = {(Q, K, V, O, UA, UB, DA, DB)[t] for t in STRAIGHT}

    def r_c(g):
        n = lead[g]
        push(store[g].at[n, :, :, oc], from_core[g].at[n], s_gc.at[(g > O) + (g > UB)], r_gc.at[g], d_core)

    def r_push_x(g, whole):
        n = lead[g]
        for k in range(1, FK):
            ff = fplus(k)
            if whole:
                push(store[g].at[n, :, :, c, ff], from_x[g].at[n, f], s_gx.at[g, k - 1], r_gx.at[g, k - 1], d_f(ff))
            else:
                t = store[g].at[n, :, y, c, ff]
                push(t, from_x[g].at[n, f, :, 0], s_gx.at[g, k - 1], r_gx.at[g, k - 1], d_f(ff))

    def r_push_y(g, whole):
        n = lead[g]
        if whole:
            push(store[g].at[n, :, oy, c], from_y[g].at[n], s_gy.at[g], r_gy.at[g], d_y)
        else:
            push(store[g].at[n, :, oy, c, f], from_y[g].at[n, :, 0], s_gy.at[g], r_gy.at[g], d_y)

    def over_z(one):
        def step(zz, carry):
            one(zz)
            return carry

        lax.fori_loop(0, Z, step, 0)

    def r_1(g):
        n = lead[g]
        got(from_core[g].at[n], r_gc.at[g])

        def one(zz):
            t = store[g][n, zz, :, c].astype(F32) + from_core[g][n, zz].astype(F32)
            store[g][n, zz, :, c] = t.astype(BF16)

        over_z(one)
        if g in direct:
            r_push_x(g, False)
            r_push_y(g, False)
            for k in range(1, FK):
                ff = fplus(k)
                t = store[g].at[n, :, oy, c, ff]
                push(t, from_x[g].at[n, f, :, 1], s_gd.at[slot[g], k - 1], r_gd.at[slot[g], k - 1], d_diag(ff))
        elif g in y_first:
            r_push_y(g, True)
        else:
            r_push_x(g, True)

    def r_2(g):
        n = lead[g]
        if g in direct:
            return
        if g in y_first:
            got(from_y[g].at[n], r_gy.at[g])

            def one(zz):
                t = store[g][n, zz, y, c].astype(F32) + from_y[g][n, zz].astype(F32)
                store[g][n, zz, y, c] = t.astype(BF16)

            over_z(one)
            r_push_x(g, False)
        else:
            for k in range(1, FK):
                got(from_x[g].at[n, fminus(k)], r_gx.at[g, k - 1])

            def one(zz):
                t = store[g][n, zz, :, c, f].astype(F32)
                for k in range(1, FK):
                    t = t + from_x[g][n, fplus(k), zz].astype(F32)
                store[g][n, zz, :, c, f] = t.astype(BF16)

            if FK > 1:
                over_z(one)
            r_push_y(g, False)

    def r_z(g):
        n = lead[g]
        if g in direct:
            got(from_y[g].at[n, :, 0], r_gy.at[g])
            for k in range(1, FK):
                got(from_x[g].at[n, fminus(k), :, 0], r_gx.at[g, k - 1])
                got(from_x[g].at[n, fminus(k), :, 1], r_gd.at[slot[g], k - 1])

            def one(zz):
                t = store[g][n, zz, y, c, f].astype(F32) + from_y[g][n, zz, 0].astype(F32)
                for k in range(1, FK):
                    t = t + from_x[g][n, fplus(k), zz, 0].astype(F32) + from_x[g][n, fplus(k), zz, 1].astype(F32)
                store[g][n, zz, y, c, f] = t.astype(BF16)

            over_z(one)
        elif g in y_first:
            for k in range(1, FK):
                got(from_x[g].at[n, fminus(k), :, 0], r_gx.at[g, k - 1])

            def one(zz):
                t = store[g][n, zz, y, c, f].astype(F32)
                for k in range(1, FK):
                    t = t + from_x[g][n, fplus(k), zz, 0].astype(F32)
                store[g][n, zz, y, c, f] = t.astype(BF16)

            if FK > 1:
                over_z(one)
        else:
            got(from_y[g].at[n, :, 0], r_gy.at[g])

            def one(zz):
                t = store[g][n, zz, y, c, f].astype(F32) + from_y[g][n, zz, 0].astype(F32)
                store[g][n, zz, y, c, f] = t.astype(BF16)

            over_z(one)
        if g in straight:
            for k in range(1, Z):
                zz = zplus(k)
                push(store[g].at[n, zz, y, c, f], from_z[g].at[n, z], s_gz.at[g], r_gz.at[g, 0], d_z(zz))
        else:
            r_fold(g, 1)

    def r_fold(g, bit):
        n = lead[g]
        for m in range(bit, Z, 2 * bit):
            push(
                store[g].at[n, zxor(m), y, c, f], from_z[g].at[n, zxor(bit ^ (m - 1))],
                s_gz.at[g], r_gz.at[g, bit.bit_length() - 1], d_z(zxor(bit)),
            )

    def r_zz(g):
        n = lead[g]
        bit = 1
        while g not in straight and 2 * bit < Z:
            got(from_z[g].at[n, 0 : Z // (2 * bit)], r_gz.at[g, bit.bit_length() - 1])
            for m in range(0, Z, 2 * bit):
                zz, at = zxor(m), zxor(m + bit - 1)
                t = store[g][n, zz, y, c, f].astype(F32) + from_z[g][n, at].astype(F32)
                store[g][n, zz, y, c, f] = t.astype(BF16)
            bit *= 2
            r_fold(g, bit)

    def r_end(g):
        n = lead[g]
        t = store[g][n, z, y, c, f].astype(F32)
        if g in straight:
            got(from_z[g].at[n, 0 : Z - 1], r_gz.at[g, 0])
            for k in range(1, Z):
                t = t + from_z[g][n, zplus(k)].astype(F32)
        else:
            at = zxor(Z // 2 - 1)
            got(from_z[g].at[n, at], r_gz.at[g, (Z // 2).bit_length() - 1])
            t = t + from_z[g][n, at].astype(F32)
        if g <= V:
            gqkv_ref[:, g * D : (g + 1) * D] = t
        elif g == O:
            gout_ref[...] = t
        elif g <= UB:
            gup_ref[:, (g - UA) * HF : (g - UA + 1) * HF] = t
        else:
            gdown_ref[(g - DA) * 2 * SLAB : (g - DA + 1) * 2 * SLAB, :] = t
        r_sent(g)

    def r_sent(g):
        n = lead[g]
        for k in range(1, FK):
            ff = fplus(k)
            if g in y_first or g in direct:
                sent(store[g].at[n, :, y, c, ff], s_gx.at[g, k - 1])
            else:
                sent(store[g].at[n, :, :, c, ff], s_gx.at[g, k - 1])
            if g in direct:
                sent(store[g].at[n, :, oy, c, ff], s_gd.at[slot[g], k - 1])
        if g in y_first and g not in direct:
            sent(store[g].at[n, :, oy, c], s_gy.at[g])
        else:
            sent(store[g].at[n, :, oy, c, f], s_gy.at[g])
        sent(store[g].at[n, 0 : Z - 1, y, c, f], s_gz.at[g])

    turns = sorted(range(1, Z), key=lambda m: (m & -m, m)) + [0]

    def plane(n):
        m = jnp.int32(0)
        for k in range(Z - 1):
            m = jnp.where(n == k, turns[k], m)
        return zxor(m)

    def p_sum(m):
        zz = zxor(m)
        got(crf.at[zz], r_pc.at[zz])
        t = tokb[zz, c].astype(F32) + crf[zz].astype(F32)
        bit = 1
        while bit < Z and m % (2 * bit) == 0:
            at = zxor(m + bit - 1)
            got(zrf.at[at], r_pz.at[at])
            t = t + zrf[at].astype(F32)
            bit *= 2
        return t

    def p_z(s):
        m = turns[s]
        bit = m & -m
        zz, at = zxor(m), zxor(bit ^ (m - 1))
        tokb[zz, c] = p_sum(m).astype(BF16)
        push(tokb.at[zz, c], zrf.at[at], s_pz, r_pz.at[at], d_z(zxor(bit)))

    def queries_back():
        push(gqs, gqr, s_y.at[5], r_y.at[5], d_y)

    def sums():
        push(sg.at[0], src, s_sc, r_sc, d_core)

    def sums_core():
        got(src, r_sc)
        sg[1] = sg[0] + src[...]
        for k in range(1, FK):
            push(sg.at[1], srx.at[f], s_sx.at[k - 1], r_sx.at[k - 1], d_f(fplus(k)))

    def sums_x():
        t = sg[1]
        for k in range(1, FK):
            got(srx.at[fminus(k)], r_sx.at[k - 1])
            t = t + srx[fminus(k)]
        sg[2] = t
        push(sg.at[2], sry, s_sy, r_sy, d_y)

    def sums_y():
        got(sry, r_sy)
        sg[3] = sg[2] + sry[...]
        for k in range(1, Z):
            zz = zplus(k)
            push(sg.at[3], srz.at[z], s_sz, r_sz, d_z(zz))

    def sums_z():
        sent(sg.at[0], s_sc)
        for k in range(1, FK):
            sent(sg.at[1], s_sx.at[k - 1])
        sent(sg.at[2], s_sy)
        sent(srz.at[0 : Z - 1], s_sz)
        t = sg[3]
        got(srz.at[0 : Z - 1], r_sz)
        for k in range(1, Z):
            t = t + srz[zplus(k)]
        gsm_ref[...] = t

    def first():
        for n, t in enumerate((gs, gu, gd)):
            sent(t.at[:, :, :, oc], s_gc.at[n])
        sent(tokb.at[:, oc], s_pc)
        sent(tokb.at[0 : Z - 1, c], s_pz)
        sent(dot_.at[:, grows, near_half], s_y.at[4])
        sent(dot_.at[:, qrows, near_half], s_y.at[6])
        sent(gqs, s_y.at[5])
        got(gqr, r_y.at[5])
        t = p_sum(0) + acc[...] + gqr[...].astype(F32)
        mean, centered, rstd = moments(tok_ref[...].astype(F32))
        gtok_ref[...] = (hid[...] + norm_back(t * par[0:1, :], centered * rstd, rstd)).astype(BF16)


    qrows = slice(HD, HD + SLAB)
    grows = slice(0, HD)
    near_half, far_half = slice(0, R), slice(R, 2 * R)

    def far_out():
        push(oh, ohr, s_y.at[0], r_y.at[0], d_y)
        push(ml, mlr, s_y.at[1], r_y.at[1], d_y)

    def far_got():
        got(ohr, r_y.at[0])
        got(mlr, r_y.at[1])

    def back_got():
        got(qt.at[:, qrows, far_half], r_y.at[3])
        got(dot_.at[:, grows, far_half], r_y.at[4])
        got(dot_.at[:, qrows, far_half], r_y.at[6])

    events = {
        "tr": lambda: tok_right(z),
        "tl": lambda: tok_left(z),
        "tp": lambda: push(tokb.at[z, c], tokp, s_tp, r_tp, d_y),
        "tc": lambda: tok_core(z),
        "tok_z": tok_z,
        "gtokp": lambda: got(tokp, r_tp),
        "w_out_z": w_out_z, "w_own_y": w_own_y, "w_own_x": w_own_x, "w_z": w_z, "w_m": w_m, "w_l": w_l, "w_c": w_c,
        "o_hi": far_out,
        "o_lo": lambda: push(ol, olr, s_y.at[2], r_y.at[2], d_y),
        "g_o": far_got,
        "g_ol": lambda: None,
        "qtail": lambda: push(qt.at[:, qrows, near_half], qt.at[:, qrows, far_half], s_y.at[3], r_y.at[3], d_y),
        "dO": lambda: push(dot_.at[:, qrows, near_half], dot_.at[:, qrows, far_half], s_y.at[6], r_y.at[6], d_y),
        "g_dO": back_got,
        "gq": queries_back,
        "r_c": r_c, "r_1": r_1, "r_2": r_2, "r_z": r_z, "r_zz": r_zz, "r_end": r_end,
        "p_z": p_z,
        "first": first,
        "s": lambda k: (sums, sums_core, sums_x, sums_y)[k](),
        "s_end": sums_z,
    }
    chunks = {"q": Q, "k": K, "v": V, "o": O, "ua": UA, "ub": UB, "da": DA, "db": DB}
    plan = order_of(Z)

    def do(stage):
        for name, *which in plan.get(stage, ()):
            events[name](*[chunks.get(t, t) for t in which])

    def run(stage, n):
        for at in range(Z):
            if (stage, at) in plan:
                @pl.when(n == at)
                def _():
                    do((stage, at))

    for t in arriving:
        t.wait()
    do("masks")

    starts, ends, stops = [], [], []
    total = jnp.int32(0)
    for t in range(NT):
        starts.append(total)
        stops.append(total + sup_ref[0, t])
        total = total + len_ref[0, t]
        ends.append(total)

    lane = lax.broadcasted_iota(jnp.int32, (1, 128), 1)
    lane_start = jnp.zeros((1, 128), jnp.int32)
    lane_stop = jnp.zeros((1, 128), jnp.int32)
    for t in range(NT):
        lane_start = jnp.where(lane == t, starts[t], lane_start)
        lane_stop = jnp.where(lane == t, stops[t], lane_stop)
    lane_ones = jnp.where((lane >= NT) & (lane < NT + 3), 1.0, 0.0)

    def mask_of(n):
        pos = (n * 2 + y) * 2 * R + lax.broadcasted_iota(jnp.int32, (2 * R, 128), 0)
        seen = (pos >= lane_start) & (pos < lane_stop)
        extra = jnp.where(lane < NT, jnp.where(seen, 0.0, MASKED), lane_ones)
        return extra.astype(BF16)

    def mask_block(n, carry):
        eb[n] = mask_of(n)
        return carry

    lax.fori_loop(0, Z, mask_block, 0)

    row = lax.broadcasted_iota(jnp.int32, (HD, 2 * R), 0)
    col = lax.broadcasted_iota(jnp.int32, (HD, 2 * R), 1)
    qpos = jnp.where(col < R, i * R + col, ((z * 2 + oy) * 2 + c - 1) * R + col)
    onehot = jnp.zeros((HD, 2 * R), F32)
    for t in range(NT):
        onehot = jnp.where((row == t) & (qpos >= starts[t]) & (qpos < ends[t]), 1.0, onehot)
    for h in range(H):
        qt[h, HD : 2 * HD, :] = onehot.astype(BF16)
        dot_[h, HD + SLAB : 2 * HD, :] = jnp.zeros((HD - SLAB, 2 * R), BF16)
        ot[h] = jnp.zeros((2 * HD, 2 * R), F32)
        mrun[h] = jnp.full((1, 2 * R), MASKED, F32)

    do("small")

    piece = D // NSH
    small = w0[:, :, :, :, :, 3 * D : 3 * D + 128].reshape(NSH * SLAB, 128)
    spread = (
        lax.rem(lax.broadcasted_iota(jnp.int32, (128, D), 1), piece)
        == lax.broadcasted_iota(jnp.int32, (128, D), 0)
    )
    wide = dot_nn(small, spread.astype(BF16))
    mine = (
        lax.broadcasted_iota(jnp.int32, (NSH * SLAB, D), 1) // piece
        == lax.broadcasted_iota(jnp.int32, (NSH * SLAB, D), 0) // SLAB
    )
    wide = jnp.where(mine, wide, 0.0)
    par[...] = jnp.sum(wide.reshape(NSH, SLAB, D), axis=0)
    pick = (
        lax.broadcasted_iota(jnp.int32, (NSH, NSH * SLAB), 1)
        == lax.broadcasted_iota(jnp.int32, (NSH, NSH * SLAB), 0) * SLAB + 8
    )
    ups = dot_nn(pick.astype(BF16), small).astype(BF16)
    spread = (
        lax.rem(lax.broadcasted_iota(jnp.int32, (128, FF), 1), 4 * piece)
        == lax.broadcasted_iota(jnp.int32, (128, FF), 0)
    )
    wide = dot_nn(ups, spread.astype(BF16))
    mine = (
        lax.broadcasted_iota(jnp.int32, (NSH, FF), 1) // (4 * piece)
        == lax.broadcasted_iota(jnp.int32, (NSH, FF), 0)
    )
    upb[...] = col_sum(jnp.where(mine, wide, 0.0))
    ln1g, ln1b = par[0:1, :], par[1:2, :]

    tokens = tok_ref[...].astype(F32)
    mean, centered, rstd = moments(tokens)
    xq[0:R, :] = (centered * rstd * ln1g + ln1b).astype(BF16)
    mean, centered, rstd = moments(tokp[...].astype(F32))
    xq[R : 2 * R, :] = (centered * rstd * ln1g + ln1b).astype(BF16)
    wq = w0[:, :, :, :, :, 0:D].reshape(D, D)
    qs[...] = (dot_nn(xq[...], wq) + par[2:3, :]).astype(BF16)
    for h in range(H):
        qt[h, 0:HD, :] = qs[:, h * HD : (h + 1) * HD].T

    def near(s):
        inner = jnp.minimum(z, Z - 1 - z)
        odd = lax.rem(s, 2)
        paired = z + (1 - 2 * odd) * ((s + 1) // 2)
        rest = jnp.where(z < Z - 1 - z, s, Z - 1 - s)
        return jnp.where(s <= 2 * inner, paired, rest)

    def attend(h, keys, values, extra, span):
        cols = slice(h * HD, (h + 1) * HD)
        s = dot_nn(jnp.concatenate([keys[:, cols], extra], axis=1), qt[h, :, span]) * BINARY
        top0 = mrun[h, :, span]
        top = jnp.maximum(top0, jnp.ceil(jnp.max(s, axis=0, keepdims=True)))
        e = jnp.exp2(s - top).astype(BF16)
        grown = dot_tn(jnp.concatenate([values[:, cols], extra], axis=1), e)
        ot[h, :, span] = ot[h, :, span] * jnp.exp2(top0 - top) + grown
        mrun[h, :, span] = top

    def ahead(n, carry):
        zz = near(n)
        run("A", n)
        got(tokb.at[zz, oc], r_t.at[zz, oc])
        mean, centered, rstd = moments(tokb[zz].reshape(2 * R, D).astype(F32))
        stat[zz] = jnp.where(lax.broadcasted_iota(jnp.int32, (2 * R, 128), 1) == 0, mean, rstd)
        x = (centered * rstd * par[0:1, :] + par[1:2, :]).astype(BF16)
        kv = dot_nn(x, w0[:, :, :, :, :, D : 3 * D].reshape(D, 2 * D))
        keys = kv[:, 0:D].astype(BF16)
        values = (kv[:, D : 2 * D] + par[3:4, :]).astype(BF16)
        kb[zz] = keys
        vb[zz] = values
        extra = eb[zz]
        for h in range(H):
            attend(h, keys, values, extra, slice(R, 2 * R))
        return carry

    lax.fori_loop(0, Z, ahead, 0)

    do("osplit")
    for h in range(H):
        t = ot[h, 0:HD, R : 2 * R]
        first_part = t.astype(BF16)
        oh[h] = first_part
        ol[h] = (t - first_part.astype(F32)).astype(BF16)
        ml[h : h + 1, :] = mrun[h, :, R : 2 * R]
        ml[H + h : H + h + 1, :] = ot[h, HD + NT : HD + NT + 1, R : 2 * R]
    def ahead_own(n, carry):
        zz = near(n)
        run("B", n)
        for h in range(H):
            attend(h, kb[zz], vb[zz], eb[zz], slice(0, R))
        return carry

    lax.fori_loop(0, Z, ahead_own, 0)
    do("merge")
    parts = []
    row_tail = lax.broadcasted_iota(jnp.int32, (SLAB, R), 0)
    for h in range(H):
        m_own, m_far = mrun[h, :, 0:R], mlr[h : h + 1, :]
        top = jnp.maximum(m_own, m_far)
        a_own, a_far = jnp.exp2(m_own - top), jnp.exp2(m_far - top)
        total = a_own * ot[h, HD + NT : HD + NT + 1, 0:R] + a_far * mlr[H + h : H + h + 1, :]
        inverse = 1.0 / total
        attended = ot[h, 0:HD, 0:R] * (a_own * inverse) + ohr[h].astype(F32) * (a_far * inverse)
        ot[h, 0:HD, 0:R] = attended
        ot[h, HD : HD + 1, 0:R] = inverse
        ot[h, HD + 1 : HD + 2, 0:R] = a_far * inverse
        parts.append(attended.T.astype(BF16))
        m1, m2, m3 = three_terms(top)
        tail = jnp.where(
            row_tail == NT + 3, m1,
            jnp.where(row_tail == NT + 4, m2, jnp.where(row_tail == NT + 5, m3, onehot[0:SLAB, 0:R])),
        )
        qt[h, HD : HD + SLAB, 0:R] = tail.astype(BF16)
    do("out")
    attn_low = jnp.concatenate(parts, axis=1)
    w_out = w1[:, :, :, :, :, 0:D].reshape(D, D)
    hidden = tokens + (dot_nn(attn_low, w_out) + par[4:5, :])
    hid[...] = hidden
    mean2, centered, rstd2 = moments(hidden)
    n2 = centered * rstd2
    nrm2[...] = (n2 * par[5:6, :] + par[6:7, :]).astype(BF16)
    acc[...] = hidden + par[7:8, :]
    gsec[...] = jnp.zeros((R, D), F32)

    def slope_at(j):
        hh = j // (Z // 2)
        return pl.ds(pl.multiple_of(hh * R, R), R), pl.ds(pl.multiple_of((j - hh * (Z // 2)) * CH, 128), CH)

    def forward(j, carry):
        cols = pl.ds(pl.multiple_of(D + j * CH, 128), CH)
        bcols = pl.ds(pl.multiple_of(j * CH, 128), CH)
        pre = dot_nn(nrm2[...], w1[:, :, :, :, :, cols].reshape(D, CH)) + upb[:, bcols]
        phi = 0.5 * (1.0 + lax.erf(pre * (0.5**0.5)))
        act_all[:, bcols] = (pre * phi).astype(BF16)
        slope = phi + pre * (jnp.exp2(pre * pre * (-0.5 / LN2)) * ((2.0 * math.pi) ** -0.5))
        big[1, *slope_at(j)] = slope
        return carry

    def backward(j, carry):
        cols = pl.ds(pl.multiple_of(D + j * CH, 128), CH)
        bcols = pl.ds(pl.multiple_of(j * CH, 128), CH)
        gpre = (dot_nt(cot_ref[...], w2[j].reshape(CH, D)) * big[1, *slope_at(j)]).astype(BF16)
        gsec[...] += dot_nt(gpre, w1[:, :, :, :, :, cols].reshape(D, CH))
        gpre_all[:, bcols] = gpre
        return carry

    do("ffn")
    lax.fori_loop(0, Z, forward, 0)
    do("ffd")
    lax.fori_loop(0, Z, backward, 0)
    do("ln2")

    g_second = gsec[...]
    n2 = (hid[...] - mean2) * rstd2
    ln2g = par[5:6, :]
    cot32 = cot_ref[...].astype(F32)
    grad_hidden = cot32 + norm_back(g_second * ln2g, n2, rstd2)
    hid[...] = grad_hidden
    g_branch = grad_hidden.astype(BF16)
    do("dOc")
    for h in range(H):
        rows = slice(h * HD, (h + 1) * HD)
        w_head = w1[:, :, :, :, :, 0:D].reshape(D, D)[rows, :]
        ga = dot_nt(w_head, g_branch).astype(BF16).astype(F32)
        dot_[h, 0:HD, 0:R] = (ga * ot[h, HD : HD + 1, 0:R]).astype(BF16)
    push(dot_.at[:, grows, near_half], dot_.at[:, grows, far_half], s_y.at[4], r_y.at[4], d_y)
    got(olr, r_y.at[2])
    for h in range(H):
        rows = slice(h * HD, (h + 1) * HD)
        low = dot_[h, 0:HD, 0:R]
        exact = ot[h, 0:HD, 0:R] + olr[h].astype(F32) * ot[h, HD + 1 : HD + 2, 0:R]
        delta = col_sum(low.astype(F32) * exact)
        d1, d2, d3 = three_terms(delta)
        tail = jnp.where(
            row_tail == NT, -d1, jnp.where(row_tail == NT + 1, -d2, jnp.where(row_tail == NT + 2, -d3, 0.0))
        )
        dot_[h, HD : HD + SLAB, 0:R] = tail.astype(BF16)
        dos[0:R, rows] = low.T

    def g_up(j, carry):
        bcols = pl.ds(pl.multiple_of(j * CH, 128), CH)
        t = dot_tn(nrm2[...], gpre_all[:, bcols]).astype(BF16).reshape(Z, 2, 2, FK, SLAB, CH)
        hh = j // (Z // 2)
        upg[:, bcols] = col_sum(gpre_all[:, bcols].astype(F32))
        gu[hh, :, :, :, :, :, pl.ds(pl.multiple_of((j - hh * (Z // 2)) * CH, 128), CH)] = t
        return carry

    def g_down(j, carry):
        bcols = pl.ds(pl.multiple_of(j * CH, 128), CH)
        acc[...] += dot_nn(act_all[:, bcols], w2[j].reshape(CH, D))
        t = dot_tn(act_all[:, bcols], cot_ref[...]).astype(BF16).reshape(2, 2, FK, 4 * SLAB, D)
        gd[0, j] = t[:, :, :, 0 : 2 * SLAB]
        gd[1, j] = t[:, :, :, 2 * SLAB : 4 * SLAB]
        return carry

    do("dwu")
    lax.fori_loop(0, Z, g_up, 0)
    do("dwd")
    lax.fori_loop(0, Z, g_down, 0)
    out_ref[...] = acc[...].astype(BF16)
    do("dwo")
    gs[O] = dot_tn(attn_low, g_branch).astype(BF16).reshape(Z, 2, 2, FK, SLAB, D)
    zero = jnp.zeros((1, D), F32)
    for r in range(SLAB):
        sg[0, r : r + 1, :] = zero
    sg[0, 4:5, :] = col_sum(g_branch.astype(F32))
    sg[0, 5:6, :] = col_sum(g_second * n2)
    sg[0, 6:7, :] = col_sum(g_second)
    sg[0, 7:8, :] = col_sum(cot32)
    for r in range(FF // D):
        sg[0, 8 + r : 9 + r, :] = upg[:, r * D : (r + 1) * D]

    dqt[...] = jnp.zeros((H, HD, 2 * R), F32)
    lacc[...] = jnp.zeros((3, 8, D), F32)

    def tok_sent():
        @pl.when(z < Z - 1)
        def _():
            for k in range(Z):
                @pl.when(z - k >= 0)
                def _():
                    sent(tokb.at[z - k, c], s_tz.at[0, z - k])

        @pl.when(z > 0)
        def _():
            for k in range(Z):
                @pl.when(z + k < Z)
                def _():
                    sent(tokb.at[z + k, c], s_tz.at[1, z + k])

        sent(tokb.at[:, c], s_tc)
        sent(tokb.at[z, c], s_tp)

    def heads(zz, span):
        keys, values, extra = kb[zz], vb[zz], eb[zz]
        dks, dvs = [], []
        for h in range(H):
            cols = slice(h * HD, (h + 1) * HD)
            s = dot_nn(jnp.concatenate([keys[:, cols], extra], axis=1), qt[h, :, span]) * BINARY
            tail = qt[h, HD : HD + SLAB, span].astype(F32)
            at = lax.broadcasted_iota(jnp.int32, tail.shape, 0)
            top = col_sum(jnp.where((at >= NT + 3) & (at < NT + 6), tail, 0.0))
            dp = dot_nn(jnp.concatenate([values[:, cols], extra], axis=1), dot_[h, :, span])
            e = jnp.exp2(s - top).astype(BF16)
            ds = (e.astype(F32) * dp).astype(BF16)
            dvs.append(dot_nn(e, dos[span, cols]))
            dks.append(dot_nn(ds, qs[span, cols]) * HD ** (-0.5))
            dqt[h, :, span] += dot_tn(keys[:, cols], ds)
        return jnp.concatenate(dks + dvs, axis=1)

    def rest(n, zz, dkv32):
        dkv = dkv32.astype(BF16)
        run("t", n)
        gp = dot_nt(dkv, w0[:, :, :, :, :, D : 3 * D].reshape(D, 2 * D))
        norm = (tokb[zz].reshape(2 * R, D).astype(F32) - stat[zz, :, 0:1]) * stat[zz, :, 1:2]
        tokb[zz] = gp.astype(BF16).reshape(2, R, D)
        push(tokb.at[zz, oc], crf.at[zz], s_pc, r_pc.at[zz], d_core)
        x = (norm * par[0:1, :] + par[1:2, :]).astype(BF16)
        lacc[0] += fold_rows(gp * norm)
        lacc[1] += fold_rows(gp)
        lacc[2] += fold_rows(dkv32[:, D : 2 * D])
        big[0] = jnp.where(n == 0, 0.0, big[0]) + dot_tn(x, dkv)

    def behind_early(n, carry):
        run("e", n)
        big[n] = heads(plane(n), near_half)
        return carry

    def behind_far(n, carry):
        run("h", n)
        zz = plane(n)
        rest(n, zz, big[n] + heads(zz, far_half))
        return carry

    def behind(n, carry):
        run("h", n)
        zz = plane(n)
        rest(n, zz, heads(zz, slice(0, 2 * R)))
        return carry

    do("sent")
    tok_sent()
    for g in range(len(groups)):
        w_sent(g)
    sent(oh, s_y.at[0])
    sent(ml, s_y.at[1])
    sent(ol, s_y.at[2])
    sent(qt.at[:, qrows, near_half], s_y.at[3])
    E = big.shape[0] if Z == 4 else 0
    if E:
        lax.fori_loop(0, E, behind_early, 0)
    do("dosT")
    for h in range(H):
        dos[R : 2 * R, h * HD : (h + 1) * HD] = dot_[h, 0:HD, R : 2 * R].T
    if E:
        lax.fori_loop(0, E, behind_far, 0)
    lax.fori_loop(E, Z, behind, 0)

    do("kv")
    gs[K] = big[0, :, 0:D].astype(BF16).reshape(Z, 2, 2, FK, SLAB, D)
    gs[V] = big[0, :, D : 2 * D].astype(BF16).reshape(Z, 2, 2, FK, SLAB, D)

    def queries():
        dq = jnp.concatenate([(dqt[h] * (HD**-0.5)).T for h in range(H)], axis=1).astype(BF16)
        gs[Q] = dot_tn(xq[...], dq).astype(BF16).reshape(Z, 2, 2, FK, SLAB, D)
        gq = dot_nt(dq, w0[:, :, :, :, :, 0:D].reshape(D, D))
        acc[...] = gq[0:R]
        gqs[...] = gq[R : 2 * R].astype(BF16)
        both = jnp.concatenate([tok_ref[...], tokp[...]], axis=0).astype(F32)
        mean, centered, rstd = moments(both)
        sg[0, 0:1, :] = col_sum(lacc[0]) + col_sum(gq * (centered * rstd))
        sg[0, 1:2, :] = col_sum(lacc[1]) + col_sum(gq)
        sg[0, 2:3, :] = col_sum(dq.astype(F32))
        sg[0, 3:4, :] = col_sum(lacc[2])

    do("q")
    queries()
    do("end")


def layer(Z, FK, R, D, FF, NT, operands):
    vm = lambda shape, dtype: pltpu.VMEM(shape, dtype)
    dma = lambda *shape: pltpu.SemaphoreType.DMA(shape)
    one = pltpu.SemaphoreType.DMA
    others = max(FK - 1, 1)
    lead = (Z, 2, 2, FK)
    slabs = ((SLAB, 3 * D + 128), (SLAB, D + FF), (4 * SLAB, D))
    gslabs = ((4, SLAB, D), (2, SLAB, FF // 2), (2, 2 * SLAB, D))
    scratch = [
        vm((Z, 2, R, D), BF16),
        vm((R, D), BF16),
        vm((Z, 2 * R, D), BF16),
        vm((Z, 2 * R, D), BF16),
        vm((Z, 2 * R, 128), BF16),
        vm((Z, 2 * R, 128), F32),
        *[vm(lead + s, BF16) for s in slabs],
        *[vm((s[0],) + lead + s[1:], BF16) for s in gslabs],
        *[vm((s[0], Z, 2, FK) + s[1:], BF16) for s in gslabs],
        *[vm((s[0], FK, Z, 2) + s[1:] if FK > 1 else (SLAB, 128), BF16) for s in gslabs],
        *[vm((s[0], Z, FK) + s[1:], BF16) for s in gslabs],
        *[vm((s[0], Z) + s[1:], BF16) for s in gslabs],
        vm((Z, R, D), BF16),
        vm((Z, R, D), BF16),
        vm((SLAB, D), F32),
        vm((1, FF), F32),
        vm((H, 2 * HD, 2 * R), BF16),
        vm((H, 2 * HD, 2 * R), BF16),
        vm((2 * R, D), BF16),
        vm((2 * R, D), BF16),
        vm((H, 2 * HD, 2 * R), F32),
        vm((H, 1, 2 * R), F32),
        vm((H, HD, 2 * R), F32),
        vm((H, HD, R), BF16),
        vm((H, HD, R), BF16),
        vm((2 * H, R), F32),
        vm((H, HD, R), BF16),
        vm((H, HD, R), BF16),
        vm((2 * H, R), F32),
        vm((R, D), BF16),
        vm((R, D), BF16),
        vm((R, D), BF16),
        vm((R, D), F32),
        vm((R, D), F32),
        vm((R, D), F32),
        vm((3, 8, D), F32),
        vm((1, FF), F32),
        vm((2 * R, D), BF16),
        vm((4, SLAB, D), F32),
        vm((SLAB, D), F32),
        vm((FK, SLAB, D), F32),
        vm((SLAB, D), F32),
        vm((Z, SLAB, D), F32),
        vm((SLAB, 128), F32),
        vm((R, D), BF16),
        vm((R, D), BF16),
        vm((R, FF), BF16),
        vm((R, FF), BF16),
        vm((3 if Z == 4 else 2, 2 * R, 2 * D), F32),
        dma(7),
        dma(2, Z), one, dma(Z, 2), one, one,
        dma(5), dma(5, Z), dma(5), dma(5, Z), dma(5, others), dma(5, others), dma(5), dma(5),
        dma(3), dma(8), dma(8, others), dma(8, others), dma(8), dma(8),
        dma(max(len(DIRECT), 1), others), dma(max(len(DIRECT), 1), others), dma(8), dma(8, Z.bit_length() - 1),
        one, dma(Z), one, dma(Z), dma(7), dma(7),
        one, one, dma(others), dma(others), one, one, one, one,
    ]
    vmem = pl.BlockSpec(memory_space=pltpu.VMEM)
    smem = pl.BlockSpec(memory_space=pltpu.SMEM)
    shape = jax.ShapeDtypeStruct
    return pl.pallas_call(
        functools.partial(body, Z, FK, R, D, NT),
        out_shape=(
            pltpu.VMEM((R, D), BF16),
            pltpu.VMEM((R, D), BF16),
            pltpu.VMEM((SLAB, 3 * D), F32),
            pltpu.VMEM((SLAB, D), F32),
            pltpu.VMEM((SLAB, FF), F32),
            pltpu.VMEM((4 * SLAB, D), F32),
            pltpu.VMEM((SLAB, D), F32),
        ),
        in_specs=[pl.BlockSpec(memory_space=pl.ANY)] * 6 + [vmem] * 9 + [smem] * 2,
        out_specs=[vmem] * 7,
        scratch_shapes=scratch,
        compiler_params=pltpu.CompilerParams(
            collective_id=0, has_side_effects=True, vmem_limit_bytes=63 * 2**20
        ),
        name="layer",
    )(*operands)


def finish(NSH, FK, *refs):
    big_in, small_in, big_out, small_out = refs[0:6], refs[6], refs[7:13], refs[13:22]
    for a, b in zip(big_in, big_out):
        b[...] = a[...]
    at = lax.axis_index("blk") * FK
    if FK > 1:
        at = at + lax.axis_index("fsdp")
    D = small_in.shape[1]
    piece = D // NSH
    lane = lax.broadcasted_iota(jnp.int32, (128, D), 1)
    take = lax.broadcasted_iota(jnp.int32, (128, D), 0)
    full = small_in[...]
    for r in range(8):
        chosen = jnp.where(lane == at * piece + take, full[r : r + 1, :], 0.0)
        small_out[r][...] = jnp.sum(chosen, axis=1).reshape(1, 128)[:, 0:piece]
    FF = D * 4
    total = jnp.zeros((128,), F32)
    for r in range(4):
        chosen = jnp.where(lane + r * D == at * 4 * piece + take, full[8 + r : 9 + r, :], 0.0)
        total = total + jnp.sum(chosen, axis=1)
    small_out[8][...] = total.reshape(1, 128)[:, 0 : 4 * piece]


def hand_over(NSH, FK, FF, results):
    *big, small = results
    D = small.shape[1]
    vmem = pl.BlockSpec(memory_space=pltpu.VMEM)
    shape = jax.ShapeDtypeStruct
    return pl.pallas_call(
        functools.partial(finish, NSH, FK),
        out_shape=(
            *[shape(v.shape, v.dtype) for v in big],
            *[shape((1, D // NSH), F32) for _ in range(8)],
            shape((1, FF // NSH), F32),
        ),
        in_specs=[vmem] * 7,
        out_specs=[vmem] * 15,
        name="finish",
    )(*[pltpu.with_memory_space_constraint(v, pltpu.VMEM) for v in results])


def shards(
    blocks, fsdp,
    tokens, ln1_gain, ln1_bias, qkv_weight, query_bias, value_bias, out_weight, out_bias,
    ln2_gain, ln2_bias, up_weight, up_bias, down_weight, down_bias,
    table_lengths, support_lengths, cotangent,
):
    R, D = tokens.shape[1:]
    FF = up_weight.shape[1]
    NT = table_lengths.shape[1]
    smalls = (ln1_gain, ln1_bias, query_bias, value_bias, out_bias, ln2_gain, ln2_bias, down_bias, up_bias)
    weights = (qkv_weight, out_weight, up_weight, down_weight)
    inside = qkv_weight.shape[0] == SLAB
    FK = fsdp if inside else 1
    if not inside:
        whole = lambda v: lax.all_gather(v, "fsdp", axis=0, tiled=True)
        smalls = tuple(whole(v) for v in smalls)
        weights = tuple(whole(v) for v in weights)
    results = layer(
        blocks // 4, FK, R, D, FF, NT,
        (tokens[0], cotangent[0], *weights, *[v[None] for v in smalls], table_lengths, support_lengths),
    )
    block_out, grad_tokens, g_qkv, g_out, g_up, g_down, *small_grads = hand_over(
        blocks * FK, FK, FF, results
    )
    small_grads = [v[0] for v in small_grads]
    weight_grads = [g_qkv, g_out, g_up, g_down]
    if not inside:
        spread = lambda v: lax.psum_scatter(v, "fsdp", scatter_dimension=0, tiled=True)
        small_grads = [spread(v) for v in small_grads]
        weight_grads = [spread(v) for v in weight_grads]
    g_ln1g, g_ln1b, g_qb, g_vb, g_ob, g_ln2g, g_ln2b, g_db, g_ub = small_grads
    g_qkv, g_out, g_up, g_down = weight_grads
    return (
        block_out[None], grad_tokens[None], g_ln1g, g_ln1b, g_qkv, g_qb, g_vb, g_out, g_ob,
        g_ln2g, g_ln2b, g_up, g_ub, g_down, g_db,
    )


def solution(mesh):
    both = ("blk", "fsdp")
    vec, mat, rows = P(both), P(both, None), P("fsdp", "blk", None)
    return jax.shard_map(
        functools.partial(shards, mesh.shape["blk"], mesh.shape["fsdp"]),
        mesh=mesh,
        in_specs=(
            rows, vec, vec, mat, vec, vec, mat, vec, vec, vec, mat, vec, mat, vec,
            P("fsdp", None), P("fsdp", None), rows,
        ),
        out_specs=(rows, rows, vec, vec, mat, vec, vec, mat, vec, vec, vec, mat, vec, mat, vec),
        check_vma=False,
    )
```
